128 devices in a mesh: seq: 16 (over y, z), expert: 8 (over x, core).
Axes of the slice: x: 4, y: 4, z: 4, core: 2. Of those that a mesh axis runs over, the one named last changes fastest.
Arguments:
- tokens: bfloat16 [8, 4096, 1152], P('expert', 'seq'), may hold values from -6 to 6
- expert_index: int32 [8, 4096, 1], P('expert', 'seq'), may hold values from 0 to 7; in each aligned block of 256 rows (0 to 255, 256 to 511, ..., all dimensions but the last counted through in order) at most 64 rows name the same one
- cotangent: bfloat16 [8, 4096, 1152], P('expert', 'seq'), may hold values from -6 to 6
- first_gain: float32 [1152], replicated, may hold values from 0.5 to 1.5
- in_weight: bfloat16 [1152, 4608], replicated, may hold values from -0.1875 to 0.1875
- conv_weight: float32 [4, 2304], replicated, may hold values from -3 to 3
- conv_bias: float32 [2304], replicated, may hold values from -3 to 3
- select_weight: bfloat16 [2304, 104], replicated, may hold values from -0.125 to 0.125
- step_weight: bfloat16 [72, 2304], replicated, may hold values from -0.75 to 0.75
- step_bias: float32 [2304], replicated, may hold values from -4 to -2.5
- decay_log: float32 [16, 2304], replicated, may hold values from -9 to 1
- skip_gain: float32 [2304], replicated, may hold values from 0.5 to 1.5
- out_weight: bfloat16 [2304, 1152], replicated, may hold values from -0.125 to 0.125
- second_gain: float32 [1152], replicated, may hold values from 0.5 to 1.5
- router_weight: bfloat16 [1152, 8], replicated, may hold values from -0.125 to 0.125
- expert_first: bfloat16 [8, 1152, 3072], P('expert'), may hold values from -0.1875 to 0.1875
- expert_second: bfloat16 [8, 3072, 1152], P('expert'), may hold values from -0.875 to 0.875
Outputs:
- mixed: bfloat16 [8, 4096, 1152], P('expert', 'seq')
- grad_tokens: float32 [8, 4096, 1152], P('expert', 'seq')
- grad_first_gain: float32 [1152], P(('seq', 'expert'))
- grad_in_weight: float32 [1152, 4608], P(None, ('seq', 'expert'))
- grad_conv_weight: float32 [4, 2304], P(None, ('seq', 'expert'))
- grad_conv_bias: float32 [2304], P(('seq', 'expert'))
- grad_select_weight: float32 [2304, 104], P(('seq', 'expert'))
- grad_step_weight: float32 [72, 2304], P(None, ('seq', 'expert'))
- grad_step_bias: float32 [2304], P(('seq', 'expert'))
- grad_decay_log: float32 [16, 2304], P(None, ('seq', 'expert'))
- grad_skip_gain: float32 [2304], P(('seq', 'expert'))
- grad_out_weight: float32 [2304, 1152], P(('seq', 'expert'))
- grad_second_gain: float32 [1152], P(('seq', 'expert'))
- grad_router_weight: float32 [1152, 8], P(('seq', 'expert'))
- grad_expert_first: float32 [8, 1152, 3072], P('expert', None, 'seq')
- grad_expert_second: float32 [8, 3072, 1152], P('expert', 'seq')
The draws below stay inside these ranges and needn't reach their ends.
Inputs may be any that keep to these rules, and one draw needn't show every extreme that they name: `expert_index`: in each aligned block of 256 tokens of a sequence no expert is named more than 64 times, a bound that some block reaches.
All inputs are finite; a program needn't handle non-finite values.
Results may differ from the reference program's by a relative error of at most 0.038.
Values may be sent and summed in bfloat16 or wider, within the bound.
A program may use at most 256 MiB of HBM per device.

```python
import math
import jax
import jax.numpy as jnp
import numpy as np
from jax import lax

D = 1152
EINNER = 2304
STATE = 16
DTRANK = 72
KCONV = 4
FF = 3072
TOK_DEV = 256
EXPERTS = 8
SEQS = 8
LENGTH = 4096
CAP = 64
N_SEQ = 16


def draw_decay_log(key, part):
    key = jax.random.fold_in(key, 11)
    key_kind, key_state, key_channel = jax.random.split(key, 3)
    slow_share = 0.5
    slow_mask = jax.random.uniform(key_kind, (EINNER,), jnp.float32) < slow_share
    level = jnp.where(slow_mask, math.log(10.0 / LENGTH), math.log(0.5))
    spread = jax.random.uniform(key_state, (STATE, EINNER), jnp.float32, -0.7, 0.7)
    jitter = jax.random.uniform(key_channel, (EINNER,), jnp.float32, -0.5, 0.5)
    return (level[None, :] + spread + jitter[None, :]).astype(jnp.float32)


def shard_levels(own_key, extent, shards, least, largest):
    level, own = 1.0, jax.random.fold_in(own_key, 6)
    for dim, blocks in shards:
        heights = jnp.exp(jax.random.uniform(jax.random.fold_in(own, dim), (blocks,), jnp.float32, least / len(shards), largest / len(shards)))
        level = level * jnp.repeat(heights, extent[dim] // blocks).reshape([-1 if axis == dim else 1 for axis in range(len(extent))])
    return level


def routed_block(stream_key, own, number, rows, count, top, bound, skew):
    order = jax.random.permutation(stream_key, count)
    crowded, usual = load_shares(count, rows * top, bound, skew, True), load_shares(count, rows * top, bound, skew, False)
    places = jnp.arange(count)

    def named(lengths, offset_by):
        used = int((lengths > 0).sum())
        fixed = max(1, used // 4)
        shifted = fixed + (places - fixed + offset_by * (used - fixed)) % max(1, count - fixed)
        return jnp.zeros((count,), jnp.int32).at[order[jnp.where(places < fixed, places, shifted)]].set(jnp.asarray(lengths, jnp.int32))

    lengths = jnp.where(number % 4 == 0, named(crowded, number // 4), named(usual, number - number // 4 - 1))
    mixed = jax.random.permutation(jax.random.fold_in(own, 3), count)
    donor, sink = mixed[0:count // 2 * 2:2], mixed[1:count // 2 * 2:2]
    room = jnp.minimum(lengths[donor] - 1, bound - lengths[sink]) // 2
    room = jnp.where((donor == order[0]) | (sink == order[0]) | (lengths[sink] == 0), 0, jnp.maximum(room, 0))
    shifted = jax.random.randint(jax.random.fold_in(own, 4), (count // 2,), 0, 1 << 20) % (room + 1)
    lengths = lengths.at[donor].add(-shifted).at[sink].add(shifted)
    labels = jnp.searchsorted(jnp.cumsum(lengths), jnp.arange(rows * top), side="right").astype(jnp.int32)
    table = labels.reshape(top, rows).T
    table = table[jax.random.permutation(jax.random.fold_in(own, 1), rows)]
    offset_by = jax.random.randint(jax.random.fold_in(own, 2), (rows, 1), 0, top)
    return jnp.take_along_axis(table, (jnp.arange(top)[None, :] + offset_by) % top, axis=1)


def load_shares(count, total, limit, skew, full):
    portions = [(1 << 20) // math.isqrt(grade ** skew) + 1 for grade in range(1, count + 1)]
    largest = limit if full else min(limit, max(-(-total // count), total * portions[0] // sum(portions)))
    least = 1 if total - largest >= count - 1 else 0
    holding, surplus = [largest] + [least] * (count - 1), total - largest - least * (count - 1)
    while surplus > 0:
        movable = [i for i in range(1, count) if holding[i] < largest] or [i for i in range(1, count) if holding[i] < limit]
        mass, remaining = sum([portions[i] for i in movable]), surplus
        for i in movable:
            extra = min(limit - holding[i], max(1, remaining * portions[i] // mass), surplus)
            holding[i] = holding[i] + extra
            surplus = surplus - extra
    return np.array(holding)


def bell_draw(stream_key, dims, deviation, limit, cuts=(), held_as=jnp.bfloat16):
    result = deviation * jax.random.normal(stream_key, dims, jnp.float32)
    if cuts:
        result = result * shard_levels(stream_key, dims, cuts, -0.22, 0.18)
    return jnp.clip(result, -limit, limit).astype(held_as)


def setup_inputs(seed: int = 0) -> dict:
    key_of = jax.random.split(jax.random.key(seed), 18)
    tokens = bell_draw(key_of[0], (SEQS, LENGTH, D), 1.0, 6.0, ((0, 8), (1, 16)))
    expert_index_keys = jax.random.split(jax.random.fold_in(key_of[1], 1), SEQS * LENGTH // TOK_DEV)
    expert_index_turns = jax.random.permutation(jax.random.fold_in(key_of[1], 3), SEQS * LENGTH // TOK_DEV)
    expert_index = jax.vmap(lambda own, number: routed_block(jax.random.fold_in(key_of[1], 2), own, number, TOK_DEV, EXPERTS, 1, CAP, 2))(expert_index_keys, expert_index_turns).reshape((SEQS, LENGTH, 1))
    cotangent = bell_draw(key_of[2], (SEQS, LENGTH, D), 1.0, 6.0, ((0, 8), (1, 16)))
    first_gain = jnp.clip(1.0 + 0.1 * jax.random.normal(key_of[3], (D,), jnp.float32), 0.5, 1.5)
    in_weight = bell_draw(key_of[4], (D, 2 * EINNER), D ** -0.5, 0.1875)
    conv_weight = bell_draw(key_of[5], (KCONV, EINNER), KCONV ** -0.5, 3.0, (), jnp.float32)
    conv_bias = bell_draw(key_of[6], (EINNER,), 0.5, 3.0, (), jnp.float32)
    select_weight = bell_draw(key_of[7], (EINNER, DTRANK + 2 * STATE), EINNER ** -0.5, 0.125)
    step_weight = bell_draw(key_of[8], (DTRANK, EINNER), DTRANK ** -0.5, 0.75)
    step_bias = jnp.clip(jax.random.uniform(key_of[9], (EINNER,), jnp.float32, -4.0, -2.5), -4.0, -2.5)
    decay_log = draw_decay_log(jax.random.fold_in(key_of[17], 71), 0)
    skip_gain = jnp.clip(jax.random.uniform(key_of[11], (EINNER,), jnp.float32, 0.5, 1.5), 0.5, 1.5)
    out_weight = bell_draw(key_of[12], (EINNER, D), EINNER ** -0.5, 0.125)
    second_gain = jnp.clip(1.0 + 0.1 * jax.random.normal(key_of[13], (D,), jnp.float32), 0.5, 1.5)
    router_weight = bell_draw(key_of[14], (D, EXPERTS), (2 * D) ** -0.5, 0.125)
    expert_first = bell_draw(key_of[15], (EXPERTS, D, FF), D ** -0.5, 0.1875, ((0, 8),))
    expert_second = bell_draw(key_of[16], (EXPERTS, FF, D), (FF // 64) ** -0.5, 0.875, ((0, 8),))
    return dict(tokens=tokens, expert_index=expert_index, cotangent=cotangent, first_gain=first_gain, in_weight=in_weight, conv_weight=conv_weight, conv_bias=conv_bias, select_weight=select_weight, step_weight=step_weight, step_bias=step_bias, decay_log=decay_log, skip_gain=skip_gain, out_weight=out_weight, second_gain=second_gain, router_weight=router_weight, expert_first=expert_first, expert_second=expert_second)


@jax.custom_vjp
def low(v):
    return lax.optimization_barrier(v.astype(jnp.bfloat16)).astype(jnp.float32)

@jax.custom_vjp
def low_back(v):
    return v

def low_keep(v):
    return (low(v), None)

def low_pass(kept, grad):
    return (grad,)

def back_keep(v):
    return (v, None)

def back_low(kept, grad):
    return (low(grad),)
low.defvjp(low_keep, low_pass)
low_back.defvjp(back_keep, back_low)

def product(left, right):
    return jnp.dot(left, right, precision=lax.Precision.HIGHEST, preferred_element_type=jnp.float32)

def rms_norm(stream, norm_gain):
    return stream * lax.rsqrt(lax.optimization_barrier(jnp.mean(stream * stream, axis=-1, keepdims=True)) + 1e-05) * norm_gain

def conv_silu(padded, conv_weight, conv_bias):
    tap_count = conv_weight.shape[0]
    out_rows = padded.shape[0] - tap_count + 1
    summed = conv_bias[None, :]
    for offset in range(tap_count):
        summed = summed + conv_weight[offset][None, :] * padded[offset:offset + out_rows]
    return jax.nn.silu(summed)

def run_scan(step_size, input_map, output_map, conv_out, decay_log, carried):
    decay_rate = -jnp.exp(decay_log)
    row_count = step_size.shape[0]
    block_rows = math.gcd(row_count, 32)

    def advance(memory, item_now):
        step_now, input_now, output_now, value_now = item_now
        memory = jnp.exp(step_now[None, :] * decay_rate) * memory + input_now[:, None] * (step_now * value_now)[None, :]
        return (memory, lax.optimization_barrier(jnp.sum(output_now[:, None] * memory, axis=0)))

    def sweep(memory, block_items):
        return lax.scan(advance, memory, block_items, unroll=True)
    shaped = tuple((array_now.reshape(row_count // block_rows, block_rows, array_now.shape[1]) for array_now in (step_size, input_map, output_map, conv_out)))
    last_state, outputs = lax.scan(jax.checkpoint(sweep), carried, shaped)
    return (outputs.reshape(row_count, outputs.shape[2]), last_state)

def layer(params, stream, routes):
    first_gain, in_weight, conv_weight, conv_bias, select_weight, step_weight, step_bias, decay_log, skip_gain, out_weight, second_gain, router_weight, expert_first, expert_second = params
    inner_width = conv_bias.shape[0]
    rank_width = step_weight.shape[0]
    state_width = decay_log.shape[0]
    expert_count = expert_first.shape[0]
    model_width = stream.shape[1]
    tap_count = conv_weight.shape[0]
    normed_in = low(rms_norm(stream, first_gain))
    projected = low_back(product(normed_in, in_weight))
    conv_input = projected[:, :inner_width]
    gate_input = projected[:, inner_width:]
    padded = jnp.concatenate([jnp.zeros((tap_count - 1, inner_width), jnp.float32), conv_input], axis=0)
    conv_out = conv_silu(padded, conv_weight, conv_bias)
    conv_low = low(conv_out)
    selection = low_back(product(conv_low, select_weight))
    step_low = low(selection[:, :rank_width])
    input_map = selection[:, rank_width:rank_width + state_width]
    output_map = selection[:, rank_width + state_width:]
    step_size = jax.nn.softplus(low_back(product(step_low, step_weight)) + step_bias)
    scanned, unused = run_scan(step_size, input_map, output_map, conv_out, decay_log, jnp.zeros((state_width, inner_width), jnp.float32))
    mixer_out = scanned + skip_gain * conv_out
    gated = low(mixer_out * jax.nn.silu(gate_input))
    middle = stream + low_back(product(gated, out_weight))
    normed_mid = low(rms_norm(middle, second_gain))
    logits = low_back(product(normed_mid, router_weight))
    router_probs = jax.nn.softmax(logits, axis=-1)
    picks = (routes[:, None] == jnp.arange(expert_count, dtype=jnp.int32)[None, :]).astype(jnp.int32)
    gate_value = lax.optimization_barrier(jnp.sum(router_probs * picks.astype(jnp.float32), axis=1))
    slot_rank = lax.optimization_barrier(jnp.sum((jnp.cumsum(picks, axis=0) - 1) * picks, axis=1)).astype(jnp.int32)
    seq_capacity = N_SEQ * CAP
    slot_index = (routes * seq_capacity + slot_rank).astype(jnp.int32)
    expert_rows = jnp.zeros((expert_count * seq_capacity, model_width), jnp.float32).at[slot_index].set(low_back(normed_mid))
    expert_rows = expert_rows.reshape(expert_count, seq_capacity, model_width)
    hidden_pre = low_back(jnp.einsum('ecd,edf->ecf', expert_rows, expert_first, precision=lax.Precision.HIGHEST))
    activated = low(jax.nn.gelu(hidden_pre))
    returned = low_back(low(jnp.einsum('ecf,efd->ecd', activated, expert_second, precision=lax.Precision.HIGHEST)))
    expert_value = returned.reshape(expert_count * seq_capacity, model_width)[slot_index]
    return middle + gate_value[:, None] * expert_value

def reference(tokens, expert_index, cotangent, first_gain, in_weight, conv_weight, conv_bias, select_weight, step_weight, step_bias, decay_log, skip_gain, out_weight, second_gain, router_weight, expert_first, expert_second):
    params = tuple((weight_now.astype(jnp.float32) for weight_now in (first_gain, in_weight, conv_weight, conv_bias, select_weight, step_weight, step_bias, decay_log, skip_gain, out_weight, second_gain, router_weight, expert_first, expert_second)))
    stream = tokens.astype(jnp.float32)
    routes = expert_index[:, :, 0]

    def forward(params_now, stream_now):

        def single(sequence_pair):
            return layer(params_now, sequence_pair[0], sequence_pair[1])
        return lax.map(jax.checkpoint(single), (stream_now, routes))
    mixed, pullback = jax.vjp(forward, params, stream)
    weight_grads, grad_tokens = pullback(cotangent.astype(jnp.float32))
    return (mixed.astype(jnp.bfloat16), grad_tokens, weight_grads[0], weight_grads[1], weight_grads[2], weight_grads[3], weight_grads[4], weight_grads[5], weight_grads[6], weight_grads[7], weight_grads[8], weight_grads[9], weight_grads[10], weight_grads[11], weight_grads[12], weight_grads[13])
```

```python
import functools
import math

import jax
import jax.numpy as jnp
from jax import lax
from jax.experimental import pallas as pl
from jax.experimental.pallas import tpu as pltpu
from jax.sharding import PartitionSpec as P

LANES = 128
SEGS = 8
LOG2E = math.log2(math.e)


def fill_maps(sel_ref, wide_ref, steps, column, states):
    def fill(j, unused):
        rows = sel_ref[pl.ds(pl.multiple_of(j * SEGS, SEGS), SEGS), :]
        for n in range(states):
            wide_ref[j * states + n] = jnp.broadcast_to(
                rows[:, column + n : column + n + 1], (SEGS, LANES)
            )
        return unused

    lax.fori_loop(0, steps, fill, 0)


def segment_prefix(value, span, rate, later):
    place = lax.broadcasted_iota(jnp.int32, (SEGS, LANES), 0)
    hop = 1
    while hop < SEGS:
        turn = SEGS - hop if later else hop
        has = (place < SEGS - hop) if later else (place >= hop)
        before = jnp.where(has, pltpu.roll(value, turn, 0), 0.0)
        value = value + jnp.exp2(rate * span) * before
        span = span + jnp.where(has, pltpu.roll(span, turn, 0), 0.0)
        hop *= 2
    return value


def span_prefix(span, later):
    place = lax.broadcasted_iota(jnp.int32, (SEGS, LANES), 0)
    hop = 1
    while hop < SEGS:
        turn = SEGS - hop if later else hop
        has = (place < SEGS - hop) if later else (place >= hop)
        span = span + jnp.where(has, pltpu.roll(span, turn, 0), 0.0)
        hop *= 2
    return span


def rates_of(log_ref, lanes, states):
    return [
        jnp.broadcast_to(-LOG2E * jnp.exp(log_ref[n : n + 1, lanes]), (SEGS, LANES))
        for n in range(states)
    ]


def summary_kernel(later, column, step_ref, other_ref, sel_ref, log_ref, part_ref, span_ref, msg_ref, wide):
    rows, width = step_ref.shape
    steps, states = rows // SEGS, log_ref.shape[0]
    fill_maps(sel_ref, wide, steps, column, states)

    def block(eb, unused):
        lanes = pl.ds(pl.multiple_of(eb * LANES, LANES), LANES)
        rate = rates_of(log_ref, lanes, states)

        def advance(i, carry):
            span, memory = carry
            j = steps - 1 - i if later else i
            here = pl.ds(pl.multiple_of(j * SEGS, SEGS), SEGS)
            step = step_ref[here, lanes]
            other = other_ref[here, lanes]
            if not later:
                other = step * other
            new = []
            for n in range(states):
                decay = jnp.exp2(step * rate[n])
                fresh = wide[j * states + n] * other
                if later:
                    new.append(decay * (memory[n] + fresh))
                else:
                    new.append(decay * memory[n] + fresh)
            return span + step, tuple(new)

        zero = jnp.zeros((SEGS, LANES), jnp.float32)
        span, memory = lax.fori_loop(0, steps, advance, (zero, (zero,) * states), unroll=2)
        total = span_prefix(span, later)
        span_ref[:, lanes] = total
        end = 0 if later else SEGS - 1
        for n in range(states):
            value = segment_prefix(memory[n], span, rate[n], later)
            part_ref[n, :, lanes] = value
            msg_ref[n, pl.ds(eb, 1), :] = value[end : end + 1]
            msg_ref[n, pl.ds(24 + eb, 1), :] = total[end : end + 1]
        return unused

    lax.fori_loop(0, width // LANES, block, 0)


def entering(part, span_total, rate, carried, later):
    place = lax.broadcasted_iota(jnp.int32, (SEGS, LANES), 0)
    ends = part + jnp.exp2(rate * span_total) * carried
    if later:
        return jnp.where(place == SEGS - 1, carried, pltpu.roll(ends, SEGS - 1, 0))
    return jnp.where(place == 0, carried, pltpu.roll(ends, 1, 0))


def forward_kernel(column, step_ref, conv_ref, sel_ref, log_ref, part_ref, span_ref, in_ref, y_ref, entry_ref, wide_in, wide_out):
    rows, width = step_ref.shape
    steps, states = rows // SEGS, log_ref.shape[0]
    fill_maps(sel_ref, wide_in, steps, column, states)
    fill_maps(sel_ref, wide_out, steps, column + states, states)

    def block(eb, unused):
        lanes = pl.ds(pl.multiple_of(eb * LANES, LANES), LANES)
        rate = rates_of(log_ref, lanes, states)
        first = []
        for n in range(states):
            carried = jnp.broadcast_to(in_ref[n, pl.ds(eb, 1), :], (SEGS, LANES))
            first.append(entering(part_ref[n, :, lanes], span_ref[:, lanes], rate[n], carried, False))
            entry_ref[n, :, lanes] = first[n]

        def advance(j, memory):
            here = pl.ds(pl.multiple_of(j * SEGS, SEGS), SEGS)
            step = step_ref[here, lanes]
            fresh = step * conv_ref[here, lanes]
            new, terms = [], []
            for n in range(states):
                value = jnp.exp2(step * rate[n]) * memory[n] + wide_in[j * states + n] * fresh
                new.append(value)
                terms.append(wide_out[j * states + n] * value)
            while len(terms) > 1:
                terms = [a + b for a, b in zip(terms[::2], terms[1::2])]
            y_ref[here, lanes] = terms[0]
            return tuple(new)

        lax.fori_loop(0, steps, advance, tuple(first), unroll=2)
        return unused

    lax.fori_loop(0, width // LANES, block, 0)


def backward_kernel(column, step_ref, conv_ref, grad_ref, sel_ref, log_ref, entry_ref, part_ref, span_ref, in_ref,
                    gstep_ref, gconv_ref, gmaps_ref, glog_ref, wide_in, wide_out, sum_in, sum_out, states_ref, decays_ref):
    rows, width = step_ref.shape
    steps, states = rows // SEGS, log_ref.shape[0]
    fill_maps(sel_ref, wide_in, steps, column, states)
    fill_maps(sel_ref, wide_out, steps, column + states, states)
    sum_in[...] = jnp.zeros_like(sum_in)
    sum_out[...] = jnp.zeros_like(sum_out)

    def block(eb, unused):
        lanes = pl.ds(pl.multiple_of(eb * LANES, LANES), LANES)
        rate = rates_of(log_ref, lanes, states)

        def advance(j, memory):
            here = pl.ds(pl.multiple_of(j * SEGS, SEGS), SEGS)
            step = step_ref[here, lanes]
            fresh = step * conv_ref[here, lanes]
            new = []
            for n in range(states):
                decay = jnp.exp2(step * rate[n])
                value = decay * memory[n] + wide_in[j * states + n] * fresh
                decays_ref[j * states + n] = decay
                states_ref[(j + 1) * states + n] = value
                new.append(value)
            return tuple(new)

        first = []
        for n in range(states):
            first.append(entry_ref[n, :, lanes])
            states_ref[n] = first[n]
        lax.fori_loop(0, steps, advance, tuple(first), unroll=2)

        def retreat(i, carry):
            j = steps - 1 - i
            mu, slow = carry
            here = pl.ds(pl.multiple_of(j * SEGS, SEGS), SEGS)
            step = step_ref[here, lanes]
            conv = conv_ref[here, lanes]
            grad = grad_ref[here, lanes]
            fresh = step * conv
            new_mu, new_slow, by_in, by_rate = [], [], [], []
            for n in range(states):
                k = j * states + n
                lam = wide_out[k] * grad + mu[n]
                sum_out[k] += grad * states_ref[k + states]
                sum_in[k] += lam * fresh
                by_in.append(lam * wide_in[k])
                turned = lam * decays_ref[k]
                new_mu.append(turned)
                kept = turned * states_ref[k]
                by_rate.append(kept * rate[n])
                new_slow.append(slow[n] + kept * step)
            while len(by_in) > 1:
                by_in = [a + b for a, b in zip(by_in[::2], by_in[1::2])]
                by_rate = [a + b for a, b in zip(by_rate[::2], by_rate[1::2])]
            gstep_ref[here, lanes] = by_in[0] * conv + (1.0 / LOG2E) * by_rate[0]
            gconv_ref[here, lanes] = by_in[0] * step
            return tuple(new_mu), tuple(new_slow)

        last = []
        for n in range(states):
            carried = jnp.broadcast_to(in_ref[n, pl.ds(eb, 1), :], (SEGS, LANES))
            last.append(entering(part_ref[n, :, lanes], span_ref[:, lanes], rate[n], carried, True))
        zero = jnp.zeros((SEGS, LANES), jnp.float32)
        unused_mu, slow = lax.fori_loop(0, steps, retreat, (tuple(last), (zero,) * states))
        for n in range(states):
            glog_ref[n : n + 1, lanes] = (1.0 / LOG2E) * jnp.sum(slow[n] * rate[n], axis=0, keepdims=True)
        return unused

    lax.fori_loop(0, width // LANES, block, 0)

    def collect(j, unused):
        spot = lax.broadcasted_iota(jnp.int32, (SEGS, LANES), 1)
        row = jnp.zeros((SEGS, LANES), jnp.float32)
        for n in range(states):
            row = jnp.where(spot == column + n, jnp.sum(sum_in[j * states + n], axis=1, keepdims=True), row)
            row = jnp.where(spot == column + states + n, jnp.sum(sum_out[j * states + n], axis=1, keepdims=True), row)
        gmaps_ref[pl.ds(pl.multiple_of(j * SEGS, SEGS), SEGS), :] = row
        return unused

    lax.fori_loop(0, steps, collect, 0)


def exchange_kernel(later, size, msg_ref, log_ref, in_ref, taken, made, send_first, recv_first, send_second, recv_second):
    me = lax.axis_index("seq")
    barrier = pltpu.get_barrier_semaphore()
    for k in range(1, size):
        pl.semaphore_signal(
            barrier, inc=1, device_id={"seq": lax.rem(me + k, size)}, device_id_type=pl.DeviceIdType.MESH
        )
    pl.semaphore_wait(barrier, size - 1)

    def first(k):
        peer = lax.rem(me + k, size)
        return pltpu.make_async_remote_copy(
            src_ref=msg_ref.at[peer], dst_ref=taken.at[k], send_sem=send_first.at[k], recv_sem=recv_first.at[k],
            device_id={"seq": peer}, device_id_type=pl.DeviceIdType.MESH,
        )

    def second(k):
        peer = lax.rem(me + k, size)
        return pltpu.make_async_remote_copy(
            src_ref=made.at[peer], dst_ref=in_ref.at[me], send_sem=send_second.at[k], recv_sem=recv_second.at[k],
            device_id={"seq": peer}, device_id_type=pl.DeviceIdType.MESH,
        )

    outward = [first(k) for k in range(1, size)]
    for copy in outward:
        copy.start()
    taken[0] = msg_ref[me]
    rate = -LOG2E * jnp.exp(log_ref[me])
    for copy in outward:
        copy.wait()
    state = jnp.zeros(rate.shape, jnp.float32)
    for turn in range(size):
        d = size - 1 - turn if later else turn
        made[d] = state
        slot = lax.rem(me - d + size, size)
        state = jnp.exp2(rate * taken[slot, 24:48, :]) * state + taken[slot, 0:24, :]
    homeward = [second(k) for k in range(1, size)]
    for copy in homeward:
        copy.start()
    in_ref[me] = made[me]
    for copy in homeward:
        copy.wait()


WHOLE = pl.BlockSpec(memory_space=pltpu.VMEM)


def shaped(*dims, dtype=jnp.float32):
    return jax.ShapeDtypeStruct(dims, dtype)


def roomy(mebibytes, **more):
    return pltpu.CompilerParams(vmem_limit_bytes=mebibytes << 20, **more)


def summarize(step, other, selection, decay_log, later, column):
    rows, width = step.shape
    states, steps = decay_log.shape[0], rows // SEGS
    return pl.pallas_call(
        functools.partial(summary_kernel, later, column),
        out_shape=(shaped(states, SEGS, width), shaped(SEGS, width), shaped(states, 48, LANES)),
        in_specs=[WHOLE] * 4,
        out_specs=(WHOLE,) * 3,
        scratch_shapes=[pltpu.VMEM((steps * states, SEGS, LANES), jnp.float32)],
        compiler_params=roomy(24),
        name="summary_later" if later else "summary_earlier",
    )(step, other, selection, decay_log)


def exchange(message, log_rows, later):
    states = message.shape[0]
    return pl.pallas_call(
        functools.partial(exchange_kernel, later, states),
        out_shape=shaped(states, 24, LANES),
        in_specs=[WHOLE] * 2,
        out_specs=WHOLE,
        scratch_shapes=[
            pltpu.VMEM((states, 48, LANES), jnp.float32),
            pltpu.VMEM((states, 24, LANES), jnp.float32),
        ]
        + [pltpu.SemaphoreType.DMA((states,))] * 4,
        compiler_params=roomy(16, collective_id=1 if later else 0, has_side_effects=True),
        name="exchange_later" if later else "exchange_earlier",
    )(message, log_rows)


def scan_forward(step, conv, selection, decay_log, part, span, entry, column):
    rows, width = step.shape
    states, steps = decay_log.shape[0], rows // SEGS
    wide = pltpu.VMEM((steps * states, SEGS, LANES), jnp.float32)
    return pl.pallas_call(
        functools.partial(forward_kernel, column),
        out_shape=(shaped(rows, width), shaped(states, SEGS, width)),
        in_specs=[WHOLE] * 7,
        out_specs=(WHOLE,) * 2,
        scratch_shapes=[wide] * 2,
        compiler_params=roomy(28),
        name="scan_forward",
    )(step, conv, selection, decay_log, part, span, entry)


def scan_backward(step, conv, grad, selection, decay_log, first, part, span, entry, column):
    rows, width = step.shape
    states, steps = decay_log.shape[0], rows // SEGS
    wide = pltpu.VMEM((steps * states, SEGS, LANES), jnp.float32)
    longer = pltpu.VMEM(((steps + 1) * states, SEGS, LANES), jnp.float32)
    return pl.pallas_call(
        functools.partial(backward_kernel, column),
        out_shape=(shaped(rows, width), shaped(rows, width), shaped(rows, LANES), shaped(states, width)),
        in_specs=[WHOLE] * 9,
        out_specs=(WHOLE,) * 4,
        scratch_shapes=[wide] * 4 + [longer, wide],
        compiler_params=roomy(44),
        name="scan_backward",
    )(step, conv, grad, selection, decay_log, first, part, span, entry)


def segmented(block):
    rows = block.shape[0]
    return block.reshape(SEGS, rows // SEGS, -1).transpose(1, 0, 2).reshape(rows, -1)


def in_order(block):
    rows = block.shape[0]
    return block.reshape(rows // SEGS, SEGS, -1).transpose(1, 0, 2).reshape(rows, -1)


def rms_scale(stream):
    return lax.rsqrt(jnp.mean(stream * stream, axis=-1, keepdims=True) + 1e-05)


def rms_back(stream, scale, gain, grad):
    grown = grad * gain
    along = jnp.mean(stream * grown, axis=-1, keepdims=True)
    return scale * grown - stream * (scale * scale * scale * along), jnp.sum(grad * stream * scale, axis=0)


def silu_slope(value):
    gate = jax.nn.sigmoid(value)
    return gate * (1.0 + value * (1.0 - gate))


def product(left, right):
    return jnp.dot(left, right, preferred_element_type=jnp.float32)


def across(left, right):
    return jnp.einsum("tk,dk->td", left, right, preferred_element_type=jnp.float32)


def summed_rows(left, right):
    return jnp.einsum("tk,td->kd", left, right, preferred_element_type=jnp.float32)


def expert_sums_kernel(hidden_ref, received_ref, active_ref, grad_ref, out_ref):
    pair = out_ref.shape[0]
    half = out_ref.shape[2]

    def emit(left_ref, right_ref, which):
        total = lax.dot_general(
            left_ref[...], right_ref[...], (((0,), (0,)), ((), ())), preferred_element_type=jnp.float32
        ).astype(jnp.bfloat16)
        for i in range(pair):
            out_ref[i, which] = total[i * half : (i + 1) * half]

    emit(hidden_ref, received_ref, 0)
    emit(active_ref, grad_ref, 1)


def expert_sums(grad_hidden, received, activated, grad_received, owners):
    rows, hidden = grad_hidden.shape
    width = received.shape[1]
    pair = 2
    cols = pair * hidden // owners
    chunk = pl.BlockSpec((rows, cols), lambda i: (0, i))
    fixed = pl.BlockSpec((rows, width), lambda i: (0, 0))
    return pl.pallas_call(
        expert_sums_kernel,
        grid=(owners // pair,),
        out_shape=shaped(owners, 2, hidden // owners, width, dtype=jnp.bfloat16),
        in_specs=[chunk, fixed, chunk, fixed],
        out_specs=pl.BlockSpec((pair, 2, hidden // owners, width), lambda i: (i, 0, 0, 0)),
        compiler_params=roomy(32),
        name="expert_sums",
    )(grad_hidden, received, activated, grad_received)


def total_over(block, seqs, experts):
    rows, width = block.shape
    mine = lax.psum_scatter(block.astype(jnp.bfloat16), "seq", scatter_dimension=0, tiled=True)
    parts = mine.reshape(experts, rows // (seqs * experts), width)
    parts = lax.all_to_all(parts, "expert", split_axis=0, concat_axis=0, tiled=True)
    return jnp.sum(parts.astype(jnp.float32), axis=0)


def local(
    tokens,
    expert_index,
    cotangent,
    first_gain,
    in_weight,
    conv_weight,
    conv_bias,
    select_weight,
    step_weight,
    step_bias,
    decay_log,
    skip_gain,
    out_weight,
    second_gain,
    router_weight,
    expert_first,
    expert_second,
):
    bf16, f32 = jnp.bfloat16, jnp.float32
    stream = segmented(tokens[0]).astype(f32)
    routes = segmented(expert_index[0])[:, 0]
    upstream = segmented(cotangent[0]).astype(f32)
    row_count, model_width = stream.shape
    inner = conv_bias.shape[0]
    rank = step_weight.shape[0]
    states = decay_log.shape[0]
    taps = conv_weight.shape[0]
    expert_count = router_weight.shape[1]
    capacity = 2 * row_count // expert_count
    seqs, experts = lax.axis_size("seq"), lax.axis_size("expert")
    reach = (taps - 1) * SEGS
    onward = [(i, i + 1) for i in range(seqs - 1)]
    backward = [(i + 1, i) for i in range(seqs - 1)]

    first_scale = rms_scale(stream)
    normed_in = (stream * first_scale * first_gain).astype(bf16)
    projected = product(normed_in, in_weight)
    conv_input = projected[:, :inner]
    gate_input = projected[:, inner:]

    ends = conv_input[row_count - reach :].reshape(taps - 1, SEGS, inner)
    arrived = lax.ppermute(ends[:, SEGS - 1], "seq", onward)
    front = jnp.concatenate([arrived[:, None], ends[:, : SEGS - 1]], axis=1).reshape(reach, inner)
    padded = jnp.concatenate([front, conv_input], axis=0)
    preact = conv_bias[None, :]
    for k in range(taps):
        preact = preact + conv_weight[k][None, :] * padded[k * SEGS : k * SEGS + row_count]
    conv_out = jax.nn.silu(preact)
    conv_low = conv_out.astype(bf16)
    selection = product(conv_low, jnp.pad(select_weight, ((0, 0), (0, LANES - select_weight.shape[1]))))
    step_low = selection[:, :rank].astype(bf16)
    step_raw = product(step_low, step_weight) + step_bias
    step_size = jax.nn.softplus(step_raw)

    log_rows = jnp.pad(decay_log.reshape(states, inner // LANES, LANES), ((0, 0), (0, 24 - inner // LANES), (0, 0)))
    part, span, message = summarize(step_size, conv_out, selection, decay_log, False, rank)
    entry = exchange(message, log_rows, False)
    scanned, first = scan_forward(step_size, conv_out, selection, decay_log, part, span, entry, rank)

    mixer_out = scanned + skip_gain * conv_out
    gated = (mixer_out * jax.nn.silu(gate_input)).astype(bf16)
    middle = stream + product(gated, out_weight)
    second_scale = rms_scale(middle)
    normed_mid = (middle * second_scale * second_gain).astype(bf16)
    router_probs = jax.nn.softmax(product(normed_mid, router_weight), axis=-1)
    picks = (routes[:, None] == jnp.arange(expert_count, dtype=jnp.int32)[None, :]).astype(jnp.int32)
    chosen = picks.astype(f32)
    gate_value = jnp.sum(router_probs * chosen, axis=1)
    slot_rank = jnp.sum((jnp.cumsum(picks, axis=0) - 1) * picks, axis=1)
    slot_index = routes * capacity + slot_rank

    def dispatch(rows):
        blank = jnp.zeros((expert_count * capacity, model_width), bf16)
        placed = blank.at[slot_index].set(rows).reshape(expert_count, capacity, model_width)
        return lax.all_to_all(placed, "expert", split_axis=0, concat_axis=0, tiled=True).reshape(-1, model_width)

    def combine(rows):
        home = lax.all_to_all(
            rows.reshape(expert_count, capacity, model_width), "expert", split_axis=0, concat_axis=0, tiled=True
        )
        return home.reshape(-1, model_width)[slot_index].astype(f32)

    first_matrix, second_matrix = expert_first[0], expert_second[0]
    received = dispatch(normed_mid)
    grad_value = (gate_value[:, None] * upstream).astype(bf16)
    grad_received = dispatch(grad_value)
    hidden_pre = product(received, first_matrix)
    activated = jax.nn.gelu(hidden_pre).astype(bf16)
    result = product(activated, second_matrix).astype(bf16)
    grad_act = across(grad_received, second_matrix)
    grad_hidden = jax.vjp(jax.nn.gelu, hidden_pre)[1](grad_act)[0].astype(bf16)
    grad_sent = across(grad_hidden, first_matrix).astype(bf16)
    expert_value = combine(result)
    grad_mid_expert = combine(grad_sent)
    expert_grads = expert_sums(grad_hidden, received, activated, grad_received, seqs)

    mixed = middle + gate_value[:, None] * expert_value
    grad_gate = jnp.sum(upstream * expert_value, axis=1)
    grad_logits = (grad_gate[:, None] * gate_value[:, None] * (chosen - router_probs)).astype(bf16)
    grad_router = summed_rows(normed_mid, grad_logits)
    grad_mid = across(grad_logits, router_weight) + grad_mid_expert
    grad_middle_norm, grad_second_gain = rms_back(middle, second_scale, second_gain, grad_mid)
    grad_middle = upstream + grad_middle_norm
    middle_low = grad_middle.astype(bf16)
    grad_out_weight = summed_rows(gated, middle_low)
    grad_gated = across(middle_low, out_weight)
    grad_mixer = grad_gated * jax.nn.silu(gate_input)
    grad_gate_input = grad_gated * mixer_out * silu_slope(gate_input)
    grad_skip = jnp.sum(grad_mixer * conv_out, axis=0)

    expert_grads, out_low, grad_mixer = lax.optimization_barrier(
        (expert_grads, grad_out_weight.astype(bf16), grad_mixer)
    )
    expert_share = lax.psum_scatter(
        expert_grads.reshape(-1, model_width), "seq", scatter_dimension=0, tiled=True
    ).reshape(2, -1, model_width)
    out_share = total_over(out_low, seqs, experts)

    part, span, message = summarize(step_size, grad_mixer, selection, decay_log, True, rank + states)
    entry = exchange(message, log_rows, True)
    grad_step, grad_conv_scan, grad_maps, grad_decay_log = scan_backward(
        step_size, conv_out, grad_mixer, selection, decay_log, first, part, span, entry, rank
    )

    grad_step_raw = grad_step * jax.nn.sigmoid(step_raw)
    grad_step_bias = jnp.sum(grad_step_raw, axis=0)
    step_raw_low = grad_step_raw.astype(bf16)
    grad_step_weight = summed_rows(step_raw_low, step_low)
    grad_step_low = across(step_raw_low, step_weight)
    grad_selection = jnp.concatenate([grad_step_low, grad_maps[:, rank : rank + 2 * states]], axis=1).astype(bf16)
    grad_select_weight = summed_rows(conv_low, grad_selection)
    grad_conv_out = across(grad_selection, select_weight) + grad_conv_scan + skip_gain * grad_mixer
    grad_preact = grad_conv_out * silu_slope(preact)
    grad_conv_bias = jnp.sum(grad_preact, axis=0)
    grad_conv_weight = jnp.stack(
        [jnp.sum(grad_preact * padded[k * SEGS : k * SEGS + row_count], axis=0) for k in range(taps)], axis=1
    )
    heads = grad_preact[:reach].reshape(taps - 1, SEGS, inner)
    arrived = lax.ppermute(heads[:, 0], "seq", backward)
    back = jnp.concatenate([heads[:, 1:], arrived[:, None]], axis=1).reshape(reach, inner)
    trailing = jnp.concatenate([grad_preact, back], axis=0)
    grad_conv_input = jnp.zeros((), f32)
    for k in range(taps):
        shift = (taps - 1 - k) * SEGS
        grad_conv_input = grad_conv_input + conv_weight[k][None, :] * trailing[shift : shift + row_count]
    grad_projected = jnp.concatenate([grad_conv_input, grad_gate_input], axis=1).astype(bf16)
    grad_in_weight = summed_rows(grad_projected, normed_in)
    grad_normed = across(grad_projected, in_weight)
    grad_stream_norm, grad_first_gain = rms_back(stream, first_scale, first_gain, grad_normed)
    grad_tokens = grad_middle + grad_stream_norm

    devices = seqs * experts
    each, fewer = inner // devices, model_width // devices
    narrow = jnp.concatenate([grad_first_gain[:, None], grad_second_gain[:, None], grad_router], axis=1)
    narrow = jnp.pad(narrow.reshape(devices, fewer, -1), ((0, 0), (0, each - fewer), (0, 0))).reshape(inner, -1)
    columns = (
        grad_select_weight,
        grad_step_weight,
        grad_decay_log.T,
        grad_conv_weight,
        grad_conv_bias[:, None],
        grad_step_bias[:, None],
        grad_skip[:, None],
        narrow,
    )
    small = jnp.concatenate(columns, axis=1)
    small = jnp.pad(small, ((0, 0), (0, -small.shape[1] % LANES)))
    in_share = total_over(grad_in_weight, seqs, experts)
    small_share = total_over(small, seqs, experts)
    starts, pieces = 0, []
    for column in columns:
        pieces.append(small_share[:, starts : starts + column.shape[1]])
        starts += column.shape[1]
    narrow_share = pieces[7][:fewer]
    return (
        in_order(mixed.astype(bf16))[None],
        in_order(grad_tokens)[None],
        narrow_share[:, 0],
        in_share.T,
        pieces[3].T,
        pieces[4][:, 0],
        pieces[0],
        pieces[1].T,
        pieces[5][:, 0],
        pieces[2].T,
        pieces[6][:, 0],
        out_share,
        narrow_share[:, 1],
        narrow_share[:, 2:],
        expert_share[0].T.astype(f32)[None],
        expert_share[1].astype(f32)[None],
    )


def solution(mesh):
    return jax.shard_map(
        local,
        mesh=mesh,
        in_specs=(
            P("expert", "seq", None),
            P("expert", "seq", None),
            P("expert", "seq", None),
            P(),
            P(),
            P(),
            P(),
            P(),
            P(),
            P(),
            P(),
            P(),
            P(),
            P(),
            P(),
            P("expert", None, None),
            P("expert", None, None),
        ),
        out_specs=(
            P("expert", "seq", None),
            P("expert", "seq", None),
            P(("seq", "expert")),
            P(None, ("seq", "expert")),
            P(None, ("seq", "expert")),
            P(("seq", "expert")),
            P(("seq", "expert"), None),
            P(None, ("seq", "expert")),
            P(("seq", "expert")),
            P(None, ("seq", "expert")),
            P(("seq", "expert")),
            P(("seq", "expert"), None),
            P(("seq", "expert")),
            P(("seq", "expert"), None),
            P("expert", None, "seq"),
            P("expert", "seq", None),
        ),
        check_vma=False,
    )
```

```python
import functools
import math

import jax
import jax.numpy as jnp
from jax import lax
from jax.experimental import pallas as pl
from jax.experimental.pallas import tpu as pltpu
from jax.sharding import PartitionSpec as P

LANES = 128
SEGS = 8
LOG2E = math.log2(math.e)


def spread_ones(states):
    row = lax.broadcasted_iota(jnp.int32, (LANES, states * LANES), 0)
    lane = lax.broadcasted_iota(jnp.int32, (LANES, states * LANES), 1)
    return row, lane // LANES


def fill_maps(sel_ref, wide_ref, column, states):
    row, block = spread_ones(states)
    ones = jnp.where(row == block + column, 1.0, 0.0).astype(jnp.bfloat16)
    left, total = sel_ref[...], None
    for unused in range(3):
        part = left.astype(jnp.bfloat16)
        left = left - part.astype(jnp.float32)
        spread = jnp.dot(part, ones, preferred_element_type=jnp.float32)
        total = spread if total is None else total + spread
    wide_ref[...] = total


def gather_maps(sum_ref, column, states):
    row, block = spread_ones(states)
    ones = jnp.where(row == block + column, 1.0, 0.0).astype(jnp.bfloat16)
    left, total = sum_ref[...], None
    for unused in range(3):
        part = left.astype(jnp.bfloat16)
        left = left - part.astype(jnp.float32)
        summed = lax.dot_general(part, ones, (((1,), (1,)), ((), ())), preferred_element_type=jnp.float32)
        total = summed if total is None else total + summed
    return total


def at(n):
    return pl.ds(n * LANES, LANES)


def segment_prefix(value, span, rate, later):
    place = lax.broadcasted_iota(jnp.int32, (SEGS, LANES), 0)
    hop = 1
    while hop < SEGS:
        turn = SEGS - hop if later else hop
        has = (place < SEGS - hop) if later else (place >= hop)
        before = jnp.where(has, pltpu.roll(value, turn, 0), 0.0)
        value = value + jnp.exp2(rate * span) * before
        span = span + jnp.where(has, pltpu.roll(span, turn, 0), 0.0)
        hop *= 2
    return value


def span_prefix(span, later):
    place = lax.broadcasted_iota(jnp.int32, (SEGS, LANES), 0)
    hop = 1
    while hop < SEGS:
        turn = SEGS - hop if later else hop
        has = (place < SEGS - hop) if later else (place >= hop)
        span = span + jnp.where(has, pltpu.roll(span, turn, 0), 0.0)
        hop *= 2
    return span


def rates_of(log_ref, lanes, states):
    return [
        jnp.broadcast_to(-LOG2E * jnp.exp(log_ref[n : n + 1, lanes]), (SEGS, LANES))
        for n in range(states)
    ]


def summary_kernel(later, column, step_ref, other_ref, sel_ref, log_ref, part_ref, span_ref, msg_ref, wide):
    rows, width = step_ref.shape
    steps, states = rows // SEGS, log_ref.shape[0]
    fill_maps(sel_ref, wide, column, states)

    def block(eb, unused):
        lanes = pl.ds(pl.multiple_of(eb * LANES, LANES), LANES)
        rate = rates_of(log_ref, lanes, states)

        def advance(i, carry):
            span, memory = carry
            j = steps - 1 - i if later else i
            here = pl.ds(pl.multiple_of(j * SEGS, SEGS), SEGS)
            step = step_ref[here, lanes]
            other = other_ref[here, lanes]
            if not later:
                other = step * other
            new = []
            for n in range(states):
                decay = jnp.exp2(step * rate[n])
                fresh = wide[here, at(n)] * other
                if later:
                    new.append(decay * (memory[n] + fresh))
                else:
                    new.append(decay * memory[n] + fresh)
            return span + step, tuple(new)

        zero = jnp.zeros((SEGS, LANES), jnp.float32)
        span, memory = lax.fori_loop(0, steps, advance, (zero, (zero,) * states), unroll=8)
        total = span_prefix(span, later)
        span_ref[:, lanes] = total
        end = 0 if later else SEGS - 1
        for n in range(states):
            value = segment_prefix(memory[n], span, rate[n], later)
            part_ref[n, :, lanes] = value
            msg_ref[n, pl.ds(eb, 1), :] = value[end : end + 1]
            msg_ref[n, pl.ds(24 + eb, 1), :] = total[end : end + 1]
        return unused

    lax.fori_loop(0, width // LANES, block, 0)


def entering(part, span_total, rate, carried, later):
    place = lax.broadcasted_iota(jnp.int32, (SEGS, LANES), 0)
    ends = part + jnp.exp2(rate * span_total) * carried
    if later:
        return jnp.where(place == SEGS - 1, carried, pltpu.roll(ends, SEGS - 1, 0))
    return jnp.where(place == 0, carried, pltpu.roll(ends, 1, 0))


def forward_kernel(column, step_ref, conv_ref, sel_ref, log_ref, part_ref, span_ref, in_ref, y_ref, entry_ref, wide_in, wide_out):
    rows, width = step_ref.shape
    steps, states = rows // SEGS, log_ref.shape[0]
    fill_maps(sel_ref, wide_in, column, states)
    fill_maps(sel_ref, wide_out, column + states, states)

    def block(eb, unused):
        lanes = pl.ds(pl.multiple_of(eb * LANES, LANES), LANES)
        rate = rates_of(log_ref, lanes, states)
        first = []
        for n in range(states):
            carried = jnp.broadcast_to(in_ref[n, pl.ds(eb, 1), :], (SEGS, LANES))
            first.append(entering(part_ref[n, :, lanes], span_ref[:, lanes], rate[n], carried, False))
            entry_ref[n, :, lanes] = first[n]

        def advance(j, memory):
            here = pl.ds(pl.multiple_of(j * SEGS, SEGS), SEGS)
            step = step_ref[here, lanes]
            fresh = step * conv_ref[here, lanes]
            new, terms = [], []
            for n in range(states):
                value = jnp.exp2(step * rate[n]) * memory[n] + wide_in[here, at(n)] * fresh
                new.append(value)
                terms.append(wide_out[here, at(n)] * value)
            while len(terms) > 1:
                terms = [a + b for a, b in zip(terms[::2], terms[1::2])]
            y_ref[here, lanes] = terms[0]
            return tuple(new)

        lax.fori_loop(0, steps, advance, tuple(first), unroll=8)
        return unused

    lax.fori_loop(0, width // LANES, block, 0)


def backward_kernel(column, step_ref, conv_ref, grad_ref, sel_ref, log_ref, entry_ref, part_ref, span_ref, in_ref,
                    gstep_ref, gconv_ref, gmaps_ref, glog_ref, wide_in, wide_out, sum_in, sum_out, states_ref, decays_ref):
    rows, width = step_ref.shape
    steps, states = rows // SEGS, log_ref.shape[0]
    fill_maps(sel_ref, wide_in, column, states)
    fill_maps(sel_ref, wide_out, column + states, states)
    sum_in[...] = jnp.zeros_like(sum_in)
    sum_out[...] = jnp.zeros_like(sum_out)

    def block(eb, unused):
        lanes = pl.ds(pl.multiple_of(eb * LANES, LANES), LANES)
        rate = rates_of(log_ref, lanes, states)

        def advance(j, memory):
            here = pl.ds(pl.multiple_of(j * SEGS, SEGS), SEGS)
            step = step_ref[here, lanes]
            fresh = step * conv_ref[here, lanes]
            new = []
            for n in range(states):
                decay = jnp.exp2(step * rate[n])
                value = decay * memory[n] + wide_in[here, at(n)] * fresh
                decays_ref[j * states + n] = decay
                states_ref[(j + 1) * states + n] = value
                new.append(value)
            return tuple(new)

        first = []
        for n in range(states):
            first.append(entry_ref[n, :, lanes])
            states_ref[n] = first[n]
        lax.fori_loop(0, steps, advance, tuple(first), unroll=8)

        def retreat(i, carry):
            j = steps - 1 - i
            mu, slow = carry
            here = pl.ds(pl.multiple_of(j * SEGS, SEGS), SEGS)
            step = step_ref[here, lanes]
            conv = conv_ref[here, lanes]
            grad = grad_ref[here, lanes]
            fresh = step * conv
            new_mu, new_slow, by_in, by_rate = [], [], [], []
            for n in range(states):
                k = j * states + n
                lam = wide_out[here, at(n)] * grad + mu[n]
                sum_out[here, at(n)] += grad * states_ref[k + states]
                sum_in[here, at(n)] += lam * fresh
                by_in.append(lam * wide_in[here, at(n)])
                turned = lam * decays_ref[k]
                new_mu.append(turned)
                kept = turned * states_ref[k]
                by_rate.append(kept * rate[n])
                new_slow.append(slow[n] + kept * step)
            while len(by_in) > 1:
                by_in = [a + b for a, b in zip(by_in[::2], by_in[1::2])]
                by_rate = [a + b for a, b in zip(by_rate[::2], by_rate[1::2])]
            gstep_ref[here, lanes] = by_in[0] * conv + (1.0 / LOG2E) * by_rate[0]
            gconv_ref[here, lanes] = by_in[0] * step
            return tuple(new_mu), tuple(new_slow)

        last = []
        for n in range(states):
            carried = jnp.broadcast_to(in_ref[n, pl.ds(eb, 1), :], (SEGS, LANES))
            last.append(entering(part_ref[n, :, lanes], span_ref[:, lanes], rate[n], carried, True))
        zero = jnp.zeros((SEGS, LANES), jnp.float32)
        unused_mu, slow = lax.fori_loop(0, steps, retreat, (tuple(last), (zero,) * states), unroll=2)
        for n in range(states):
            glog_ref[n : n + 1, lanes] = (1.0 / LOG2E) * jnp.sum(slow[n] * rate[n], axis=0, keepdims=True)
        return unused

    lax.fori_loop(0, width // LANES, block, 0)

    gmaps_ref[...] = gather_maps(sum_in, column, states) + gather_maps(sum_out, column + states, states)


def exchange_kernel(later, size, msg_ref, log_ref, in_ref, taken, made, send_first, recv_first, send_second, recv_second):
    me = lax.axis_index("seq")
    barrier = pltpu.get_barrier_semaphore()
    for k in range(1, size):
        pl.semaphore_signal(
            barrier, inc=1, device_id={"seq": lax.rem(me + k, size)}, device_id_type=pl.DeviceIdType.MESH
        )
    pl.semaphore_wait(barrier, size - 1)

    def first(k):
        peer = lax.rem(me + k, size)
        return pltpu.make_async_remote_copy(
            src_ref=msg_ref.at[peer], dst_ref=taken.at[k], send_sem=send_first.at[k], recv_sem=recv_first.at[k],
            device_id={"seq": peer}, device_id_type=pl.DeviceIdType.MESH,
        )

    def second(k):
        peer = lax.rem(me + k, size)
        return pltpu.make_async_remote_copy(
            src_ref=made.at[peer], dst_ref=in_ref.at[me], send_sem=send_second.at[k], recv_sem=recv_second.at[k],
            device_id={"seq": peer}, device_id_type=pl.DeviceIdType.MESH,
        )

    outward = [first(k) for k in range(1, size)]
    for copy in outward:
        copy.start()
    taken[0] = msg_ref[me]
    rate = -LOG2E * jnp.exp(log_ref[me])
    for copy in outward:
        copy.wait()
    state = jnp.zeros(rate.shape, jnp.float32)
    for turn in range(size):
        d = size - 1 - turn if later else turn
        made[d] = state
        slot = lax.rem(me - d + size, size)
        state = jnp.exp2(rate * taken[slot, 24:48, :]) * state + taken[slot, 0:24, :]
    homeward = [second(k) for k in range(1, size)]
    for copy in homeward:
        copy.start()
    in_ref[me] = made[me]
    for copy in homeward:
        copy.wait()


WHOLE = pl.BlockSpec(memory_space=pltpu.VMEM)


def shaped(*dims, dtype=jnp.float32):
    return jax.ShapeDtypeStruct(dims, dtype)


def roomy(mebibytes, **more):
    return pltpu.CompilerParams(vmem_limit_bytes=mebibytes << 20, **more)


def summarize(step, other, selection, decay_log, later, column):
    rows, width = step.shape
    states, steps = decay_log.shape[0], rows // SEGS
    return pl.pallas_call(
        functools.partial(summary_kernel, later, column),
        out_shape=(shaped(states, SEGS, width), shaped(SEGS, width), shaped(states, 48, LANES)),
        in_specs=[WHOLE] * 4,
        out_specs=(WHOLE,) * 3,
        scratch_shapes=[pltpu.VMEM((rows, states * LANES), jnp.float32)],
        compiler_params=roomy(24),
        name="summary_later" if later else "summary_earlier",
    )(step, other, selection, decay_log)


def exchange(message, log_rows, later):
    states = message.shape[0]
    return pl.pallas_call(
        functools.partial(exchange_kernel, later, states),
        out_shape=shaped(states, 24, LANES),
        in_specs=[WHOLE] * 2,
        out_specs=WHOLE,
        scratch_shapes=[
            pltpu.VMEM((states, 48, LANES), jnp.float32),
            pltpu.VMEM((states, 24, LANES), jnp.float32),
        ]
        + [pltpu.SemaphoreType.DMA((states,))] * 4,
        compiler_params=roomy(16, collective_id=1 if later else 0, has_side_effects=True),
        name="exchange_later" if later else "exchange_earlier",
    )(message, log_rows)


def scan_forward(step, conv, selection, decay_log, part, span, entry, column):
    rows, width = step.shape
    states, steps = decay_log.shape[0], rows // SEGS
    wide = pltpu.VMEM((rows, states * LANES), jnp.float32)
    return pl.pallas_call(
        functools.partial(forward_kernel, column),
        out_shape=(shaped(rows, width), shaped(states, SEGS, width)),
        in_specs=[WHOLE] * 7,
        out_specs=(WHOLE,) * 2,
        scratch_shapes=[wide] * 2,
        compiler_params=roomy(28),
        name="scan_forward",
    )(step, conv, selection, decay_log, part, span, entry)


def scan_backward(step, conv, grad, selection, decay_log, first, part, span, entry, column):
    rows, width = step.shape
    states, steps = decay_log.shape[0], rows // SEGS
    wide = pltpu.VMEM((rows, states * LANES), jnp.float32)
    longer = pltpu.VMEM(((steps + 1) * states, SEGS, LANES), jnp.float32)
    return pl.pallas_call(
        functools.partial(backward_kernel, column),
        out_shape=(shaped(rows, width), shaped(rows, width), shaped(rows, LANES), shaped(states, width)),
        in_specs=[WHOLE] * 9,
        out_specs=(WHOLE,) * 4,
        scratch_shapes=[wide] * 4 + [longer, pltpu.VMEM((steps * states, SEGS, LANES), jnp.float32)],
        compiler_params=roomy(44),
        name="scan_backward",
    )(step, conv, grad, selection, decay_log, first, part, span, entry)


def segmented(block):
    rows = block.shape[0]
    return block.reshape(SEGS, rows // SEGS, -1).transpose(1, 0, 2).reshape(rows, -1)


def in_order(block):
    rows = block.shape[0]
    return block.reshape(rows // SEGS, SEGS, -1).transpose(1, 0, 2).reshape(rows, -1)


def rms_scale(stream):
    return lax.rsqrt(jnp.mean(stream * stream, axis=-1, keepdims=True) + 1e-05)


def rms_back(stream, scale, gain, grad):
    grown = grad * gain
    along = jnp.mean(stream * grown, axis=-1, keepdims=True)
    return scale * grown - stream * (scale * scale * scale * along), jnp.sum(grad * stream * scale, axis=0)


def silu_slope(value):
    gate = jax.nn.sigmoid(value)
    return gate * (1.0 + value * (1.0 - gate))


def product(left, right):
    return jnp.dot(left, right, preferred_element_type=jnp.float32)


def across(left, right):
    return jnp.einsum("tk,dk->td", left, right, preferred_element_type=jnp.float32)


def summed_rows(left, right):
    return jnp.einsum("tk,td->kd", left, right, preferred_element_type=jnp.float32)


CHUNK = 1024
GELU_OUT = math.sqrt(2.0 / math.pi)
GELU_IN = 0.044715


def transposed_dot(left, right):
    return lax.dot_general(left, right, (((1,), (1,)), ((), ())), preferred_element_type=jnp.float32)


def column_dot(left, right):
    return lax.dot_general(left, right, (((0,), (0,)), ((), ())), preferred_element_type=jnp.float32)


def three_parts(value):
    parts, left = [], value
    for unused in range(3):
        part = left.astype(jnp.bfloat16)
        left = left - part.astype(jnp.float32)
        parts.append(part)
    return parts


def expert_pull_kernel(up_ref, second_ref, pull_ref):
    pull_ref[...] = transposed_dot(up_ref[...], second_ref[...]).astype(jnp.bfloat16)


def expert_pull(upstream, second):
    rows, width = upstream.shape
    hidden = second.shape[0]
    return pl.pallas_call(
        expert_pull_kernel,
        grid=(hidden // CHUNK,),
        out_shape=shaped(rows, hidden, dtype=jnp.bfloat16),
        in_specs=[pl.BlockSpec((rows, width), lambda i: (0, 0)), pl.BlockSpec((CHUNK, width), lambda i: (i, 0))],
        out_specs=pl.BlockSpec((rows, CHUNK), lambda i: (0, i)),
        compiler_params=roomy(24),
        cost_estimate=pl.CostEstimate(flops=2 * rows * hidden * width, bytes_accessed=2 * (width + rows) * hidden, transcendentals=0),
        name="expert_pull",
    )(upstream, second)


def expert_kernel(got_ref, up_ref, pull_ref, first_ref, second_ref, active_ref, grad_ref, value_ref, sent_ref, value, sent):
    step, last = pl.program_id(0), pl.num_programs(0) - 1
    width = up_ref.shape[1]
    first = first_ref[...]
    pre = jnp.dot(got_ref[:, :width], first, preferred_element_type=jnp.float32)
    square = pre * pre
    bent = jnp.tanh(pre * (GELU_OUT + GELU_OUT * GELU_IN * square))
    share = 0.5 + 0.5 * bent
    active = (pre * share).astype(jnp.bfloat16)
    slope = share + pre * (0.5 - 0.5 * bent * bent) * (GELU_OUT + 3.0 * GELU_OUT * GELU_IN * square)
    grad = (slope * pull_ref[...].astype(jnp.float32)).astype(jnp.bfloat16)
    active_ref[...] = active
    grad_ref[...] = grad
    more_value = jnp.dot(active, second_ref[...], preferred_element_type=jnp.float32)
    more_sent = transposed_dot(grad, first)

    @pl.when(step == 0)
    def begin():
        value[...] = more_value
        sent[...] = more_sent

    @pl.when(step > 0)
    def go_on():
        value[...] += more_value
        sent[...] += more_sent

    @pl.when(step == last)
    def finish():
        low = value[...].astype(jnp.bfloat16)
        value_ref[...] = low
        sent_ref[:, :width] = sent[...].astype(jnp.bfloat16)
        along = jnp.sum(low.astype(jnp.float32) * up_ref[...].astype(jnp.float32), axis=1, keepdims=True)
        place = lax.broadcasted_iota(jnp.int32, (sent_ref.shape[0], LANES), 1)
        tail = jnp.zeros(place.shape, jnp.float32)
        for k, part in enumerate(three_parts(along)):
            tail = jnp.where(place == k, part.astype(jnp.float32), tail)
        sent_ref[:, width:] = tail.astype(jnp.bfloat16)


def expert_layer(received, upstream, pull, first, second):
    rows, width = upstream.shape
    hidden = second.shape[0]
    wide = received.shape[1]

    def fixed(cols):
        return pl.BlockSpec((rows, cols), lambda i: (0, 0))

    chunk = pl.BlockSpec((rows, CHUNK), lambda i: (0, i))
    return pl.pallas_call(
        expert_kernel,
        grid=(hidden // CHUNK,),
        out_shape=(
            shaped(rows, hidden, dtype=jnp.bfloat16),
            shaped(rows, hidden, dtype=jnp.bfloat16),
            shaped(rows, width, dtype=jnp.bfloat16),
            shaped(rows, wide, dtype=jnp.bfloat16),
        ),
        in_specs=[
            fixed(wide),
            fixed(width),
            chunk,
            pl.BlockSpec((width, CHUNK), lambda i: (0, i)),
            pl.BlockSpec((CHUNK, width), lambda i: (i, 0)),
        ],
        out_specs=(chunk, chunk, fixed(width), fixed(wide)),
        scratch_shapes=[pltpu.VMEM((rows, width), jnp.float32)] * 2,
        compiler_params=roomy(48),
        cost_estimate=pl.CostEstimate(flops=6 * rows * hidden * width, bytes_accessed=4 * hidden * (width + rows), transcendentals=rows * hidden),
        name="expert_layer",
    )(received, upstream, pull, first, second)


def expert_sums_kernel(hidden_ref, received_ref, active_ref, up_ref, out_ref, scaled_received, scaled_up):
    pair = out_ref.shape[0]
    half = out_ref.shape[2]
    width = up_ref.shape[1]

    @pl.when(pl.program_id(0) == 0)
    def scale():
        parts = received_ref[:, width:].astype(jnp.float32)
        gate = parts[:, 0:1] + parts[:, 1:2] + parts[:, 2:3]
        scaled_received[...] = (received_ref[:, :width].astype(jnp.float32) * gate).astype(jnp.bfloat16)
        scaled_up[...] = (up_ref[...].astype(jnp.float32) * gate).astype(jnp.bfloat16)

    for which, (left_ref, right_ref) in enumerate(((hidden_ref, scaled_received), (active_ref, scaled_up))):
        total = column_dot(left_ref[...], right_ref[...]).astype(jnp.bfloat16)
        for i in range(pair):
            out_ref[i, which] = total[i * half : (i + 1) * half]


def expert_sums(grad_hidden, received, activated, upstream, owners):
    rows, hidden = grad_hidden.shape
    width = upstream.shape[1]
    pair = 2
    chunk = pl.BlockSpec((rows, pair * hidden // owners), lambda i: (0, i))

    def fixed(cols):
        return pl.BlockSpec((rows, cols), lambda i: (0, 0))

    return pl.pallas_call(
        expert_sums_kernel,
        grid=(owners // pair,),
        out_shape=shaped(owners, 2, hidden // owners, width, dtype=jnp.bfloat16),
        in_specs=[chunk, fixed(received.shape[1]), chunk, fixed(width)],
        out_specs=pl.BlockSpec((pair, 2, hidden // owners, width), lambda i: (i, 0, 0, 0)),
        scratch_shapes=[pltpu.VMEM((rows, width), jnp.bfloat16)] * 2,
        compiler_params=roomy(32),
        cost_estimate=pl.CostEstimate(flops=4 * rows * hidden * width, bytes_accessed=4 * hidden * (width + rows), transcendentals=0),
        name="expert_sums",
    )(grad_hidden, received, activated, upstream)


ORDERS = ("xyz", "yzx", "zxy")
PIECE = 16


def shares_kernel(in_cols, token_ref, out_cols, middle_ref, small_ref, sum_ref, in_ref, out_ref, made, taken, half_a, half_b, half_c, one_a, one_b, one_c, sends, arrivals):
    seq, expert = lax.axis_index("seq"), lax.axis_index("expert")
    core = lax.rem(expert, 2)
    place = {"y": lax.div(seq, 4), "z": lax.rem(seq, 4), "x": lax.div(expert, 2)}
    third = token_ref.shape[1] // len(ORDERS)
    streams = [(L, q) for L in range(len(ORDERS)) for q in range(4)]

    def flip(i):
        return i + 1 - 2 * lax.rem(i, 2)

    def device(**moved):
        at = dict(place, **moved)
        return {"seq": at["y"] * 4 + at["z"], "expert": at["x"] * 2 + at.get("core", core)}

    partners = [device(core=1 - core)]
    for axis in "xyz":
        partners += [device(**{axis: flip(place[axis])}), device(**{axis: 3 - place[axis]})]
    barrier = pltpu.get_barrier_semaphore()
    for partner in partners:
        pl.semaphore_signal(barrier, inc=1, device_id=partner, device_id_type=pl.DeviceIdType.MESH)
    pl.semaphore_wait(barrier, len(partners))

    def send(source, target, partner, stream, number):
        k = streams.index(stream)
        copy = pltpu.make_async_remote_copy(
            src_ref=source, dst_ref=target, send_sem=sends.at[k, number], recv_sem=arrivals.at[k, number],
            device_id=partner, device_id_type=pl.DeviceIdType.MESH,
        )
        copy.start()
        return copy

    def add(target, source, unit):
        def step(i, unused):
            target[i] = target[i] + source[i]
            return unused

        lax.fori_loop(0, unit, step, 0, unroll=min(unit, 8))

    for source, target in ((in_cols, in_ref), (out_cols, out_ref)):

        def turn_over(k, unused, source=source, target=target):
            spot = pl.ds(pl.multiple_of(k * LANES, LANES), LANES)
            target[spot, :] = source[:, spot].T
            return unused

        lax.fori_loop(0, source.shape[1] // LANES, turn_over, 0)

    pending = {}
    for L, order in enumerate(ORDERS):
        lanes = pl.ds(L * third, third)
        for q in (6, 7):
            made[L, q] = jnp.zeros_like(made[L, q])

        def block(s, unused):
            y, z = lax.div(s, 4), lax.rem(s, 4)
            by_in = jnp.dot(
                in_ref[pl.ds(pl.multiple_of(s * 288, 16), 288), :], token_ref[:, lanes], preferred_element_type=jnp.float32
            ).astype(jnp.bfloat16)
            here = pl.ds(pl.multiple_of(s * 144, 16), 144)
            by_out = jnp.dot(out_ref[here, :], middle_ref[:, lanes], preferred_element_type=jnp.float32)
            left, right = small_ref[here, :LANES], small_ref[here, LANES:]
            for x in range(4):
                at = {"x": x, "y": y, "z": z}
                slot = (at[order[0]] * 4 + at[order[1]]) * 4 + at[order[2]]
                rows = by_in[72 * x : 72 * x + 72]
                more = by_out[36 * x : 36 * x + 36].astype(jnp.bfloat16)
                for q in range(4):
                    made[L, q, slot] = rows[16 * q : 16 * q + 16]
                made[L, 4, slot, 0:8] = rows[64:]
                made[L, 4, slot, 8:16] = more[:8]
                made[L, 5, slot] = more[8:24]
                made[L, 6, slot, 0:12] = more[24:]
                last = jnp.concatenate([left[36 * x : 36 * x + 36], right[36 * x : 36 * x + 36]], axis=0)
                for part in range(third // LANES):
                    k = 8 * (L * (third // LANES) + part)
                    made[L, 7, slot, 0:8, part * LANES : (part + 1) * LANES] = last[k : k + 8].astype(jnp.bfloat16)
            return unused

        lax.fori_loop(0, 16, block, 0, unroll=2)
        for q in range(4):
            pending[L, q] = [
                send(made.at[L, 4 * (1 - core) + q], taken.at[L, q], device(core=1 - core), (L, q), 0)
            ]

    halves, ones = (half_a, half_b, half_c), (one_a, one_b, one_c)
    holding = {}
    for L, q in streams:
        for copy in pending[L, q]:
            copy.wait()
        add(taken.at[L, q], made.at[L, 4 * core + q], 64)
        holding[L, q] = taken.at[L, q]
        pending[L, q] = start_halves(L, q, 0, holding[L, q], halves, place, flip, device, send)
    for turn in range(3):
        unit = 16 >> (2 * turn)
        for L, q in streams:
            axis = ORDERS[L][turn]
            i = place[axis]
            for copy in pending[L, q]:
                copy.wait()
            other = 3 - i if q < 2 else flip(i)
            got = halves[turn].at[L, q]
            add(got.at[0], holding[L, q].at[pl.ds(i * unit, unit)], unit)
            add(got.at[1], holding[L, q].at[pl.ds(other * unit, unit)], unit)
            partner = device(**{axis: other})
            pending[L, q] = [send(got.at[1], ones[turn].at[L, q], partner, (L, q), 3 + 3 * turn)]
        for L, q in streams:
            for copy in pending[L, q]:
                copy.wait()
            got = ones[turn].at[L, q]
            if turn < 2:
                add(got, halves[turn].at[L, q, 0], unit)
                holding[L, q] = got
                pending[L, q] = start_halves(L, q, turn + 1, got, halves, place, flip, device, send)
            else:
                whole = got[0].astype(jnp.float32) + halves[turn][L, q, 0, 0].astype(jnp.float32)
                sum_ref[4 * core + q, :, L * third : (L + 1) * third] = whole
    here = sum_ref.at[pl.ds(4 * core, 4)]
    send(here, here, device(core=1 - core), (0, 0), 10).wait()


def start_halves(L, q, turn, source, halves, place, flip, device, send):
    axis = ORDERS[L][turn]
    unit = 16 >> (2 * turn)
    i = place[axis]
    partner = flip(i) if q < 2 else 3 - i
    second = 3 - partner if q < 2 else flip(partner)
    target = halves[turn].at[L, q]
    return [
        send(source.at[pl.ds(partner * unit, unit)], target.at[0], device(**{axis: partner}), (L, q), 1 + 3 * turn),
        send(source.at[pl.ds(second * unit, unit)], target.at[1], device(**{axis: partner}), (L, q), 2 + 3 * turn),
    ]


def shares(in_cols, tokens, out_cols, middle, small):
    width = tokens.shape[1]
    third = width // len(ORDERS)

    def slots(*lead):
        return pltpu.VMEM((len(ORDERS),) + lead + (PIECE, third), jnp.bfloat16)

    return pl.pallas_call(
        shares_kernel,
        out_shape=shaped(8, PIECE, width),
        in_specs=[WHOLE] * 5,
        out_specs=WHOLE,
        scratch_shapes=[pltpu.VMEM(cols.shape[::-1], jnp.bfloat16) for cols in (in_cols, out_cols)]
        + [slots(8, 64), slots(4, 64)]
        + [slots(4, 2, 16 >> (2 * turn)) for turn in range(3)]
        + [slots(4, 16 >> (2 * turn)) for turn in range(3)]
        + [pltpu.SemaphoreType.DMA((12, 11))] * 2,
        compiler_params=roomy(60, collective_id=2, has_side_effects=True),
        name="shares",
    )(in_cols, tokens, out_cols, middle, small)


def local(
    tokens,
    expert_index,
    cotangent,
    first_gain,
    in_weight,
    conv_weight,
    conv_bias,
    select_weight,
    step_weight,
    step_bias,
    decay_log,
    skip_gain,
    out_weight,
    second_gain,
    router_weight,
    expert_first,
    expert_second,
):
    bf16, f32 = jnp.bfloat16, jnp.float32
    stream = segmented(tokens[0]).astype(f32)
    routes = segmented(expert_index[0])[:, 0]
    upstream = segmented(cotangent[0]).astype(f32)
    row_count, model_width = stream.shape
    inner = conv_bias.shape[0]
    rank = step_weight.shape[0]
    states = decay_log.shape[0]
    taps = conv_weight.shape[0]
    expert_count = router_weight.shape[1]
    capacity = 2 * row_count // expert_count
    seqs, experts = lax.axis_size("seq"), lax.axis_size("expert")
    reach = (taps - 1) * SEGS
    onward = [(i, i + 1) for i in range(seqs - 1)]
    backward = [(i + 1, i) for i in range(seqs - 1)]

    picks = (routes[:, None] == jnp.arange(expert_count, dtype=jnp.int32)[None, :]).astype(bf16)
    earlier = jnp.arange(row_count)[:, None] > jnp.arange(row_count)[None, :]
    ahead = product(earlier.astype(bf16), picks)
    chosen = picks.astype(f32)
    slot_index = routes * capacity + jnp.sum(ahead * chosen, axis=1).astype(jnp.int32)
    seats = jnp.arange(expert_count * capacity, dtype=jnp.int32)
    placing = (seats[:, None] == slot_index[None, :]).astype(bf16)

    def seated(rows):
        return product(placing, rows).astype(bf16)

    def swapped(rows):
        parts = rows.reshape(expert_count, capacity, -1)
        parts = lax.all_to_all(parts, "expert", split_axis=0, concat_axis=0, tiled=True)
        return parts.reshape(expert_count * capacity, -1)

    def unseated(rows):
        return jnp.einsum("st,sd->td", placing, rows, preferred_element_type=f32)

    upstream_there = swapped(seated(segmented(cotangent[0])))

    first_scale = rms_scale(stream)
    normed_in = (stream * first_scale * first_gain).astype(bf16)
    projected = product(normed_in, in_weight)
    conv_input = projected[:, :inner]
    gate_input = projected[:, inner:]

    ends = conv_input[row_count - reach :].reshape(taps - 1, SEGS, inner)
    arrived = lax.ppermute(ends[:, SEGS - 1], "seq", onward)
    front = jnp.concatenate([arrived[:, None], ends[:, : SEGS - 1]], axis=1).reshape(reach, inner)
    padded = jnp.concatenate([front, conv_input], axis=0)
    preact = conv_bias[None, :]
    for k in range(taps):
        preact = preact + conv_weight[k][None, :] * padded[k * SEGS : k * SEGS + row_count]
    conv_out = jax.nn.silu(preact)
    conv_low = conv_out.astype(bf16)
    selection = product(conv_low, jnp.pad(select_weight, ((0, 0), (0, LANES - select_weight.shape[1]))))
    step_low = selection[:, :rank].astype(bf16)
    step_raw = product(step_low, step_weight) + step_bias
    step_size = jax.nn.softplus(step_raw)

    log_rows = jnp.pad(decay_log.reshape(states, inner // LANES, LANES), ((0, 0), (0, 24 - inner // LANES), (0, 0)))
    part, span, message = summarize(step_size, conv_out, selection, decay_log, False, rank)
    entry = exchange(message, log_rows, False)
    entry, upstream_there = lax.optimization_barrier((entry, upstream_there))
    scanned, first = scan_forward(step_size, conv_out, selection, decay_log, part, span, entry, rank)

    mixer_out = scanned + skip_gain * conv_out
    gated = (mixer_out * jax.nn.silu(gate_input)).astype(bf16)
    middle = stream + product(gated, out_weight)
    second_scale = rms_scale(middle)
    normed_mid = (middle * second_scale * second_gain).astype(bf16)
    router_probs = jax.nn.softmax(product(normed_mid, router_weight), axis=-1)
    gate_value = jnp.sum(router_probs * chosen, axis=1)

    gate_parts = jnp.stack(three_parts(gate_value), axis=1)
    gate_parts = jnp.pad(gate_parts, ((0, 0), (0, LANES - gate_parts.shape[1])))
    leaving = seated(jnp.concatenate([normed_mid, gate_parts], axis=1))
    leaving, upstream_there = lax.optimization_barrier((leaving, upstream_there))
    received = swapped(leaving)
    pull = expert_pull(upstream_there, expert_second[0])
    activated, grad_hidden, value_there, grad_there = expert_layer(
        received, upstream_there, pull, expert_first[0], expert_second[0]
    )
    grad_home = unseated(swapped(grad_there))
    expert_grads = expert_sums(grad_hidden, received, activated, upstream_there, seqs)
    expert_grads, value_there = lax.optimization_barrier((expert_grads, value_there))
    value_home = swapped(value_there)

    grad_gate = jnp.sum(grad_home[:, model_width:], axis=1)
    grad_logits = (grad_gate[:, None] * gate_value[:, None] * (chosen - router_probs)).astype(bf16)
    grad_router = summed_rows(normed_mid, grad_logits)
    grad_mid = across(grad_logits, router_weight) + gate_value[:, None] * grad_home[:, :model_width]
    grad_middle_norm, grad_second_gain = rms_back(middle, second_scale, second_gain, grad_mid)
    grad_middle = upstream + grad_middle_norm
    middle_low = grad_middle.astype(bf16)
    grad_gated = across(middle_low, out_weight)
    grad_mixer = grad_gated * jax.nn.silu(gate_input)
    grad_gate_input = grad_gated * mixer_out * silu_slope(gate_input)
    grad_skip = jnp.sum(grad_mixer * conv_out, axis=0)

    expert_grads, grad_mixer = lax.optimization_barrier((expert_grads, grad_mixer))
    expert_share = lax.psum_scatter(
        expert_grads.reshape(-1, model_width), "seq", scatter_dimension=0, tiled=True
    ).reshape(2, -1, model_width)

    part, span, message = summarize(step_size, grad_mixer, selection, decay_log, True, rank + states)
    entry = exchange(message, log_rows, True)
    grad_step, grad_conv_scan, grad_maps, grad_decay_log = scan_backward(
        step_size, conv_out, grad_mixer, selection, decay_log, first, part, span, entry, rank
    )

    grad_step, value_home = lax.optimization_barrier((grad_step, value_home))
    mixed = middle + gate_value[:, None] * unseated(value_home)
    grad_step_raw = grad_step * jax.nn.sigmoid(step_raw)
    grad_step_bias = jnp.sum(grad_step_raw, axis=0)
    step_raw_low = grad_step_raw.astype(bf16)
    grad_step_weight = summed_rows(step_raw_low, step_low)
    grad_step_low = across(step_raw_low, step_weight)
    grad_selection = jnp.concatenate([grad_step_low, grad_maps[:, rank : rank + 2 * states]], axis=1).astype(bf16)
    grad_select_weight = summed_rows(conv_low, grad_selection)
    grad_conv_out = across(grad_selection, select_weight) + grad_conv_scan + skip_gain * grad_mixer
    grad_preact = grad_conv_out * silu_slope(preact)
    grad_conv_bias = jnp.sum(grad_preact, axis=0)
    grad_conv_weight = jnp.stack(
        [jnp.sum(grad_preact * padded[k * SEGS : k * SEGS + row_count], axis=0) for k in range(taps)], axis=1
    )
    heads = grad_preact[:reach].reshape(taps - 1, SEGS, inner)
    arrived = lax.ppermute(heads[:, 0], "seq", backward)
    back = jnp.concatenate([heads[:, 1:], arrived[:, None]], axis=1).reshape(reach, inner)
    trailing = jnp.concatenate([grad_preact, back], axis=0)
    grad_conv_input = jnp.zeros((), f32)
    for k in range(taps):
        shift = (taps - 1 - k) * SEGS
        grad_conv_input = grad_conv_input + conv_weight[k][None, :] * trailing[shift : shift + row_count]
    grad_projected = jnp.concatenate([grad_conv_input, grad_gate_input], axis=1).astype(bf16)
    grad_normed = across(grad_projected, in_weight)
    grad_stream_norm, grad_first_gain = rms_back(stream, first_scale, first_gain, grad_normed)
    grad_tokens = grad_middle + grad_stream_norm

    devices = seqs * experts
    each, fewer = inner // devices, model_width // devices
    narrow = jnp.concatenate([grad_first_gain[:, None], grad_second_gain[:, None], grad_router], axis=1)
    narrow = jnp.pad(narrow.reshape(devices, fewer, -1), ((0, 0), (0, each - fewer), (0, 0))).reshape(inner, -1)
    columns = (
        grad_select_weight,
        grad_step_weight,
        grad_decay_log.T,
        grad_conv_weight,
        grad_conv_bias[:, None],
        grad_step_bias[:, None],
        grad_skip[:, None],
        narrow,
    )
    small = jnp.concatenate(columns, axis=1)
    small = jnp.pad(small, ((0, 0), (0, -small.shape[1] % LANES)))
    in_cols, expert_share = lax.optimization_barrier((grad_projected, expert_share))
    sums = shares(in_cols, normed_in, gated, middle_low, small).reshape(-1, model_width)
    core = lax.axis_index("expert") % 2
    in_share = lax.dynamic_slice_in_dim(sums, 2 * each * core, 2 * each)
    out_share = lax.dynamic_slice_in_dim(sums, 4 * each + each * core, each)
    small_sum = sums[112:120].reshape(8, -1, LANES).transpose(1, 0, 2).reshape(-1, 2 * each, LANES)
    small_sum = small_sum.transpose(1, 0, 2).reshape(2 * each, -1)
    small_share = lax.dynamic_slice_in_dim(small_sum, each * core, each)
    starts, pieces = 0, []
    for column in columns:
        pieces.append(small_share[:, starts : starts + column.shape[1]])
        starts += column.shape[1]
    narrow_share = pieces[7][:fewer]
    return (
        in_order(mixed.astype(bf16))[None],
        in_order(grad_tokens)[None],
        narrow_share[:, 0],
        in_share.T,
        pieces[3].T,
        pieces[4][:, 0],
        pieces[0],
        pieces[1].T,
        pieces[5][:, 0],
        pieces[2].T,
        pieces[6][:, 0],
        out_share,
        narrow_share[:, 1],
        narrow_share[:, 2:],
        expert_share[0].T.astype(f32)[None],
        expert_share[1].astype(f32)[None],
    )


def solution(mesh):
    return jax.shard_map(
        local,
        mesh=mesh,
        in_specs=(
            P("expert", "seq", None),
            P("expert", "seq", None),
            P("expert", "seq", None),
            P(),
            P(),
            P(),
            P(),
            P(),
            P(),
            P(),
            P(),
            P(),
            P(),
            P(),
            P(),
            P("expert", None, None),
            P("expert", None, None),
        ),
        out_specs=(
            P("expert", "seq", None),
            P("expert", "seq", None),
            P(("seq", "expert")),
            P(None, ("seq", "expert")),
            P(None, ("seq", "expert")),
            P(("seq", "expert")),
            P(("seq", "expert"), None),
            P(None, ("seq", "expert")),
            P(("seq", "expert")),
            P(None, ("seq", "expert")),
            P(("seq", "expert")),
            P(("seq", "expert"), None),
            P(("seq", "expert")),
            P(("seq", "expert"), None),
            P("expert", None, "seq"),
            P("expert", "seq", None),
        ),
        check_vma=False,
    )
```

```python
import functools
import math

import jax
import jax.numpy as jnp
from jax import lax
from jax.experimental import pallas as pl
from jax.experimental.pallas import tpu as pltpu
from jax.sharding import PartitionSpec as P

LANES = 128
SEGS = 8
LOG2E = math.log2(math.e)
PARTS = 3
GRID = 4


def spread_ones(states):
    row = lax.broadcasted_iota(jnp.int32, (LANES, states * LANES), 0)
    lane = lax.broadcasted_iota(jnp.int32, (LANES, states * LANES), 1)
    return row, lane // LANES


def fill_maps(sel_ref, wide_ref, column):
    steps, states = wide_ref.shape[:2]
    row, block = spread_ones(states)
    ones = jnp.where(row == block + column, 1.0, 0.0).astype(jnp.bfloat16)
    left, total = sel_ref[...], None
    for unused in range(3):
        part = left.astype(jnp.bfloat16)
        left = left - part.astype(jnp.float32)
        spread = jnp.dot(part, ones, preferred_element_type=jnp.float32)
        total = spread if total is None else total + spread
    for n in range(states):
        wide_ref[:, n] = total[:, n * LANES : (n + 1) * LANES].reshape(steps, SEGS, LANES)


def gather_maps(sum_ref, column):
    steps, states = sum_ref.shape[:2]
    row, block = spread_ones(states)
    ones = jnp.where(row == block + column, 1.0, 0.0).astype(jnp.bfloat16)
    left = jnp.concatenate([sum_ref[:, n].reshape(steps * SEGS, LANES) for n in range(states)], axis=1)
    total = None
    for unused in range(3):
        part = left.astype(jnp.bfloat16)
        left = left - part.astype(jnp.float32)
        summed = transposed_dot(part, ones)
        total = summed if total is None else total + summed
    return total


def lanes_of(block):
    return pl.ds(pl.multiple_of(block * LANES, LANES), LANES)


def rows_of(j):
    return pl.ds(pl.multiple_of(j * SEGS, SEGS), SEGS)


def rates_of(log_ref, lanes):
    states = log_ref.shape[0]
    rate = -LOG2E * jnp.exp(log_ref[:, lanes])
    return jnp.stack([jnp.broadcast_to(rate[n : n + 1], (SEGS, LANES)) for n in range(states)])


def neighbour(value, hop, later, fill):
    axis = value.ndim - 2
    place = lax.broadcasted_iota(jnp.int32, value.shape, axis)
    if later:
        return jnp.where(place < SEGS - hop, pltpu.roll(value, SEGS - hop, axis), fill)
    return jnp.where(place >= hop, pltpu.roll(value, hop, axis), fill)


def summarize(later, part, step_ref, other_ref, wide, log_ref, part_ref, span_ref, message):
    steps, states = wide.shape[:2]
    blocks = step_ref.shape[1] // LANES // PARTS

    def block(i, unused):
        lanes = lanes_of(part * blocks + i)
        rate = rates_of(log_ref, lanes)

        def advance(turn, carry):
            span, memory = carry
            j = steps - 1 - turn if later else turn
            step = step_ref[rows_of(j), lanes]
            other = other_ref[rows_of(j), lanes]
            decay = jnp.exp2(step * rate)
            if later:
                memory = decay * (memory + wide[j] * other)
            else:
                memory = decay * memory + wide[j] * (step * other)
            return span + step, memory

        zero = jnp.zeros((SEGS, LANES), jnp.float32)
        span, memory = lax.fori_loop(0, steps, advance, (zero, jnp.zeros(rate.shape, jnp.float32)), unroll=8)
        hop = 1
        while hop < SEGS:
            memory = memory + jnp.exp2(rate * span) * neighbour(memory, hop, later, 0.0)
            span = span + neighbour(span, hop, later, 0.0)
            hop *= 2
        span_ref[:, lanes] = span
        part_ref[:, :, lanes] = memory
        end = 0 if later else SEGS - 1
        for n in range(states):
            message[n // GRID, n % GRID, pl.ds(i, 1), :] = memory[n, end : end + 1]
        for q in range(GRID):
            message[q, GRID, pl.ds(i, 1), :] = span[end : end + 1]
        return unused

    lax.fori_loop(0, blocks, block, 0)


def entering(later, part_ref, span_ref, rate, lanes, carried):
    ends = part_ref[:, :, lanes] + jnp.exp2(rate * span_ref[:, lanes]) * carried
    return neighbour(ends, 1, later, carried)


def carried_at(in_ref, part, i):
    states = GRID * GRID
    return jnp.stack(
        [jnp.broadcast_to(in_ref[n // GRID, n % GRID, pl.ds(i, 1), :], (SEGS, LANES)) for n in range(states)]
    )


def scan_part(part, step_ref, conv_ref, wide_in, wide_out, log_ref, part_ref, span_ref, in_ref, y_ref, entry_ref):
    steps = wide_in.shape[0]
    blocks = step_ref.shape[1] // LANES // PARTS

    def block(i, unused):
        lanes = lanes_of(part * blocks + i)
        rate = rates_of(log_ref, lanes)
        first = entering(False, part_ref, span_ref, rate, lanes, carried_at(in_ref, part, i))
        entry_ref[:, :, lanes] = first

        def advance(j, memory):
            step = step_ref[rows_of(j), lanes]
            memory = jnp.exp2(step * rate) * memory + wide_in[j] * (step * conv_ref[rows_of(j), lanes])
            y_ref[rows_of(j), lanes] = jnp.sum(wide_out[j] * memory, axis=0)
            return memory

        lax.fori_loop(0, steps, advance, first, unroll=8)
        return unused

    lax.fori_loop(0, blocks, block, 0)


def retreat_part(
    part, step_ref, conv_ref, grad_ref, raw_ref, wide_in, wide_out, log_ref, pull_ref, entry_ref, part_ref, span_ref, in_ref,
    low_ref, gconv_ref, glog_ref, gbias_ref, sum_in, sum_out, states_ref, decays_ref, raw_sum, raw_rows,
):
    steps = wide_in.shape[0]
    blocks = step_ref.shape[1] // LANES // PARTS

    def block(i, unused):
        lanes = lanes_of(part * blocks + i)
        rate = rates_of(log_ref, lanes)

        def advance(j, memory):
            step = step_ref[rows_of(j), lanes]
            decay = jnp.exp2(step * rate)
            memory = decay * memory + wide_in[j] * (step * conv_ref[rows_of(j), lanes])
            decays_ref[j] = decay
            states_ref[j + 1] = memory
            return memory

        first = entry_ref[:, :, lanes]
        states_ref[0] = first
        lax.fori_loop(0, steps, advance, first, unroll=8)

        def retreat(turn, carry):
            j = steps - 1 - turn
            mu, slow = carry
            step = step_ref[rows_of(j), lanes]
            conv = conv_ref[rows_of(j), lanes]
            grad = grad_ref[rows_of(j), lanes]
            lam = wide_out[j] * grad + mu
            sum_out[j] += grad * states_ref[j + 1]
            sum_in[j] += lam * (step * conv)
            by_in = jnp.sum(lam * wide_in[j], axis=0)
            mu = lam * decays_ref[j]
            kept = mu * states_ref[j]
            by_rate = jnp.sum(kept * rate, axis=0)
            grad_step = by_in * conv + (1.0 / LOG2E) * by_rate
            raw_rows[rows_of(j), :] = grad_step * jax.nn.sigmoid(raw_ref[rows_of(j), lanes])
            gconv_ref[rows_of(j), lanes] = by_in * step
            return mu, slow + kept * step

        last = entering(True, part_ref, span_ref, rate, lanes, carried_at(in_ref, part, i))
        unused_mu, slow = lax.fori_loop(0, steps, retreat, (last, jnp.zeros(rate.shape, jnp.float32)), unroll=4)
        glog_ref[:, lanes] = (1.0 / LOG2E) * jnp.sum(slow * rate, axis=1)
        raw_steps = raw_rows[...]
        gbias_ref[:, lanes] = jnp.sum(raw_steps, axis=0, keepdims=True)
        low = raw_steps.astype(jnp.bfloat16)
        low_ref[:, lanes] = low
        raw_sum[...] += transposed_dot(low, pull_ref[:, lanes])
        return unused

    lax.fori_loop(0, blocks, block, 0)


class Relay:
    def __init__(self, later, log_rows, message, got, row, rows_got, above, made, in_ref, sends, arrivals):
        self.later, self.log_rows, self.message, self.got = later, log_rows, message, got
        self.row, self.rows_got, self.above, self.made, self.in_ref = row, rows_got, above, made, in_ref
        self.sends, self.arrivals = sends, arrivals
        seq = lax.axis_index("seq")
        self.y, self.z = lax.div(seq, GRID), lax.rem(seq, GRID)
        self.flying = {}
        barrier = pltpu.get_barrier_semaphore()
        for k in range(1, GRID):
            for peer in (self.across(k), self.along(k)):
                pl.semaphore_signal(barrier, inc=1, device_id=peer, device_id_type=pl.DeviceIdType.MESH)

    def across(self, k):
        return {"seq": self.y * GRID + lax.rem(self.z + k, GRID)}

    def along(self, k):
        return {"seq": lax.rem(self.y + k, GRID) * GRID + self.z}

    def meet(self):
        pl.semaphore_wait(pltpu.get_barrier_semaphore(), 2 * (GRID - 1))

    def send(self, part, phase, k, source, target, peer):
        copy = pltpu.make_async_remote_copy(
            src_ref=source, dst_ref=target, send_sem=self.sends.at[part, phase, k], recv_sem=self.arrivals.at[part, phase, k],
            device_id=peer, device_id_type=pl.DeviceIdType.MESH,
        )
        copy.start()
        self.flying.setdefault((part, phase), []).append(copy)

    def land(self, part, phase):
        for copy in self.flying[part, phase]:
            copy.wait()

    def order(self):
        return range(GRID - 1, -1, -1) if self.later else range(GRID)

    def rate(self, part):
        return -LOG2E * jnp.exp(self.log_rows[part, self.z])

    def first(self, part):
        for k in range(1, GRID):
            peer = lax.rem(self.z + k, GRID)
            self.send(part, 0, k, self.message.at[part, peer], self.got.at[part, k], self.across(k))
        self.got[part, 0] = self.message[part, self.z]

    def second(self, part):
        self.land(part, 0)
        rate = self.rate(part)
        state, span = jnp.zeros(rate.shape, jnp.float32), jnp.zeros(rate.shape[1:], jnp.float32)
        for z in self.order():
            block = self.got[part, lax.rem(self.z - z + GRID, GRID)]
            state = jnp.exp2(rate * block[GRID]) * state + block[:GRID]
            span = span + block[GRID]
        self.row[part, :GRID] = state
        self.row[part, GRID] = span
        for k in range(1, GRID):
            self.send(part, 1, k, self.row.at[part], self.rows_got.at[part, k], self.along(k))
        self.rows_got[part, 0] = self.row[part]

    def third(self, part):
        self.land(part, 1)
        rate = self.rate(part)
        state = jnp.zeros(rate.shape, jnp.float32)
        for y in self.order():
            self.above[part, y] = state
            block = self.rows_got[part, lax.rem(self.y - y + GRID, GRID)]
            state = jnp.exp2(rate * block[GRID]) * state + block[:GRID]
        state = self.above[part, self.y]
        for z in self.order():
            self.made[part, z] = state
            block = self.got[part, lax.rem(self.z - z + GRID, GRID)]
            state = jnp.exp2(rate * block[GRID]) * state + block[:GRID]
        for k in range(1, GRID):
            peer = lax.rem(self.z + k, GRID)
            self.send(part, 2, k, self.made.at[part, peer], self.in_ref.at[part, self.z], self.across(k))
        self.in_ref[part, self.z] = self.made[part, self.z]

    def done(self, part):
        self.land(part, 2)


def staged(relay, summary, extra, scan):
    summary(0)
    relay.meet()
    relay.first(0)
    summary(1)
    relay.first(1)
    relay.second(0)
    summary(2)
    relay.first(2)
    relay.third(0)
    relay.second(1)
    extra()
    relay.second(2)
    relay.third(1)
    relay.done(0)
    scan(0)
    relay.third(2)
    relay.done(1)
    scan(1)
    relay.done(2)
    scan(2)


def forward_kernel(
    column, step_ref, conv_ref, sel_ref, log_ref, log_rows, y_ref, entry_ref, part_ref, span_ref, wide_in, wide_out, in_ref, *relayed
):
    states = log_ref.shape[0]
    relay = Relay(False, log_rows, *relayed[:6], in_ref, *relayed[6:])
    message = relayed[0]
    fill_maps(sel_ref, wide_in, column)

    def summary(part):
        summarize(False, part, step_ref, conv_ref, wide_in, log_ref, part_ref, span_ref, message.at[part])

    def scan(part):
        scan_part(part, step_ref, conv_ref, wide_in, wide_out, log_ref, part_ref, span_ref, in_ref.at[part], y_ref, entry_ref)

    staged(relay, summary, lambda: fill_maps(sel_ref, wide_out, column + states), scan)


def backward_kernel(
    column, step_ref, conv_ref, grad_ref, raw_ref, sel_ref, log_ref, log_rows, pull_ref, entry_ref,
    low_ref, gconv_ref, gsel_ref, glog_ref, gbias_ref,
    part_ref, span_ref, wide_in, wide_out, sum_in, sum_out, states_ref, decays_ref, raw_sum, raw_rows, in_ref, *relayed
):
    states = log_ref.shape[0]
    relay = Relay(True, log_rows, *relayed[:6], in_ref, *relayed[6:])
    message = relayed[0]
    fill_maps(sel_ref, wide_out, column + states)

    def summary(part):
        summarize(True, part, step_ref, grad_ref, wide_out, log_ref, part_ref, span_ref, message.at[part])

    def prepare():
        fill_maps(sel_ref, wide_in, column)
        sum_in[...] = jnp.zeros_like(sum_in)
        sum_out[...] = jnp.zeros_like(sum_out)
        raw_sum[...] = jnp.zeros_like(raw_sum)

    def scan(part):
        retreat_part(
            part, step_ref, conv_ref, grad_ref, raw_ref, wide_in, wide_out, log_ref, pull_ref, entry_ref, part_ref, span_ref,
            in_ref.at[part], low_ref, gconv_ref, glog_ref, gbias_ref, sum_in, sum_out, states_ref, decays_ref, raw_sum, raw_rows,
        )

    staged(relay, summary, prepare, scan)
    maps = gather_maps(sum_in, column) + gather_maps(sum_out, column + states)
    gsel_ref[...] = (raw_sum[...] + maps).astype(jnp.bfloat16)


WHOLE = pl.BlockSpec(memory_space=pltpu.VMEM)


def shaped(*dims, dtype=jnp.float32):
    return jax.ShapeDtypeStruct(dims, dtype)


def roomy(mebibytes, **more):
    return pltpu.CompilerParams(vmem_limit_bytes=mebibytes << 20, **more)


def wide_scratch(rows, states, extra=0):
    return pltpu.VMEM((rows // SEGS + extra, states, SEGS, LANES), jnp.float32)


def chain_scratch(states, width):
    return [pltpu.VMEM((states, SEGS, width), jnp.float32), pltpu.VMEM((SEGS, width), jnp.float32)]


def relay_scratch():
    def kept(*dims):
        return pltpu.VMEM((PARTS,) + dims + (SEGS, LANES), jnp.float32)

    return [
        kept(GRID, GRID),
        kept(GRID, GRID + 1),
        kept(GRID, GRID + 1),
        kept(GRID + 1),
        kept(GRID, GRID + 1),
        kept(GRID, GRID),
        kept(GRID, GRID),
        pltpu.SemaphoreType.DMA((PARTS, 3, GRID)),
        pltpu.SemaphoreType.DMA((PARTS, 3, GRID)),
    ]


def scan_forward(step, conv, selection, decay_log, log_rows, column):
    rows, width = step.shape
    states = decay_log.shape[0]
    return pl.pallas_call(
        functools.partial(forward_kernel, column),
        out_shape=(shaped(rows, width), shaped(states, SEGS, width)),
        in_specs=[WHOLE] * 5,
        out_specs=(WHOLE,) * 2,
        scratch_shapes=chain_scratch(states, width) + [wide_scratch(rows, states)] * 2 + relay_scratch(),
        compiler_params=roomy(32, collective_id=0, has_side_effects=True),
        name="scan_forward",
    )(step, conv, selection, decay_log, log_rows)


def scan_backward(step, conv, grad, raw, selection, decay_log, log_rows, pull, first, column):
    rows, width = step.shape
    states = decay_log.shape[0]
    narrow = pltpu.VMEM((rows, LANES), jnp.float32)
    return pl.pallas_call(
        functools.partial(backward_kernel, column),
        out_shape=(
            shaped(rows, width, dtype=jnp.bfloat16),
            shaped(rows, width),
            shaped(rows, LANES, dtype=jnp.bfloat16),
            shaped(states, width),
            shaped(1, width),
        ),
        in_specs=[WHOLE] * 9,
        out_specs=(WHOLE,) * 5,
        scratch_shapes=chain_scratch(states, width)
        + [wide_scratch(rows, states)] * 4
        + [wide_scratch(rows, states, 1), wide_scratch(rows, states)]
        + [narrow] * 2
        + relay_scratch(),
        compiler_params=roomy(46, collective_id=1, has_side_effects=True),
        name="scan_backward",
    )(step, conv, grad, raw, selection, decay_log, log_rows, pull, first)


def segmented(block):
    rows = block.shape[0]
    return block.reshape(SEGS, rows // SEGS, -1).transpose(1, 0, 2).reshape(rows, -1)


def in_order(block):
    rows = block.shape[0]
    return block.reshape(rows // SEGS, SEGS, -1).transpose(1, 0, 2).reshape(rows, -1)


def rms_scale(stream):
    return lax.rsqrt(jnp.mean(stream * stream, axis=-1, keepdims=True) + 1e-05)


def rms_back(stream, scale, gain, grad):
    grown = grad * gain
    along = jnp.mean(stream * grown, axis=-1, keepdims=True)
    return scale * grown - stream * (scale * scale * scale * along), jnp.sum(grad * stream * scale, axis=0)


def silu_slope(value):
    gate = jax.nn.sigmoid(value)
    return gate * (1.0 + value * (1.0 - gate))


def product(left, right):
    return jnp.dot(left, right, preferred_element_type=jnp.float32)


def across(left, right):
    return jnp.einsum("tk,dk->td", left, right, preferred_element_type=jnp.float32)


def summed_rows(left, right):
    return jnp.einsum("tk,td->kd", left, right, preferred_element_type=jnp.float32)


CHUNK = 1024
GELU_OUT = math.sqrt(2.0 / math.pi)
GELU_IN = 0.044715


def transposed_dot(left, right):
    return lax.dot_general(left, right, (((1,), (1,)), ((), ())), preferred_element_type=jnp.float32)


def column_dot(left, right):
    return lax.dot_general(left, right, (((0,), (0,)), ((), ())), preferred_element_type=jnp.float32)


def three_parts(value):
    parts, left = [], value
    for unused in range(3):
        part = left.astype(jnp.bfloat16)
        left = left - part.astype(jnp.float32)
        parts.append(part)
    return parts


def expert_pull_kernel(up_ref, second_ref, pull_ref):
    pull_ref[...] = transposed_dot(up_ref[...], second_ref[...]).astype(jnp.bfloat16)


def expert_pull(upstream, second):
    rows, width = upstream.shape
    hidden = second.shape[0]
    return pl.pallas_call(
        expert_pull_kernel,
        grid=(hidden // CHUNK,),
        out_shape=shaped(rows, hidden, dtype=jnp.bfloat16),
        in_specs=[pl.BlockSpec((rows, width), lambda i: (0, 0)), pl.BlockSpec((CHUNK, width), lambda i: (i, 0))],
        out_specs=pl.BlockSpec((rows, CHUNK), lambda i: (0, i)),
        compiler_params=roomy(60),
        cost_estimate=pl.CostEstimate(flops=2 * rows * hidden * width, bytes_accessed=2 * (width + rows) * hidden, transcendentals=0),
        name="expert_pull",
    )(upstream, second)


def expert_kernel(got_ref, up_ref, pull_ref, first_ref, second_ref, active_ref, grad_ref, value_ref, sent_ref, value, sent):
    step, last = pl.program_id(0), pl.num_programs(0) - 1
    width = up_ref.shape[1]
    first = first_ref[...]
    pre = jnp.dot(got_ref[:, :width], first, preferred_element_type=jnp.float32)
    square = pre * pre
    bent = jnp.tanh(pre * (GELU_OUT + GELU_OUT * GELU_IN * square))
    share = 0.5 + 0.5 * bent
    active = (pre * share).astype(jnp.bfloat16)
    slope = share + pre * (0.5 - 0.5 * bent * bent) * (GELU_OUT + 3.0 * GELU_OUT * GELU_IN * square)
    grad = (slope * pull_ref[...].astype(jnp.float32)).astype(jnp.bfloat16)
    active_ref[...] = active
    grad_ref[...] = grad
    more_value = jnp.dot(active, second_ref[...], preferred_element_type=jnp.float32)
    more_sent = transposed_dot(grad, first)

    @pl.when(step == 0)
    def begin():
        value[...] = more_value
        sent[...] = more_sent

    @pl.when(step > 0)
    def go_on():
        value[...] += more_value
        sent[...] += more_sent

    @pl.when(step == last)
    def finish():
        low = value[...].astype(jnp.bfloat16)
        value_ref[...] = low
        sent_ref[:, :width] = sent[...].astype(jnp.bfloat16)
        along = jnp.sum(low.astype(jnp.float32) * up_ref[...].astype(jnp.float32), axis=1, keepdims=True)
        place = lax.broadcasted_iota(jnp.int32, (sent_ref.shape[0], LANES), 1)
        tail = jnp.zeros(place.shape, jnp.float32)
        for k, part in enumerate(three_parts(along)):
            tail = jnp.where(place == k, part.astype(jnp.float32), tail)
        sent_ref[:, width:] = tail.astype(jnp.bfloat16)


def expert_layer(received, upstream, pull, first, second):
    rows, width = upstream.shape
    hidden = second.shape[0]
    wide = received.shape[1]

    def fixed(cols):
        return pl.BlockSpec((rows, cols), lambda i: (0, 0))

    chunk = pl.BlockSpec((rows, CHUNK), lambda i: (0, i))
    return pl.pallas_call(
        expert_kernel,
        grid=(hidden // CHUNK,),
        out_shape=(
            shaped(rows, hidden, dtype=jnp.bfloat16),
            shaped(rows, hidden, dtype=jnp.bfloat16),
            shaped(rows, width, dtype=jnp.bfloat16),
            shaped(rows, wide, dtype=jnp.bfloat16),
        ),
        in_specs=[
            fixed(wide),
            fixed(width),
            chunk,
            pl.BlockSpec((width, CHUNK), lambda i: (0, i)),
            pl.BlockSpec((CHUNK, width), lambda i: (i, 0)),
        ],
        out_specs=(chunk, chunk, fixed(width), fixed(wide)),
        scratch_shapes=[pltpu.VMEM((rows, width), jnp.float32)] * 2,
        compiler_params=roomy(60),
        cost_estimate=pl.CostEstimate(flops=6 * rows * hidden * width, bytes_accessed=4 * hidden * (width + rows), transcendentals=rows * hidden),
        name="expert_layer",
    )(received, upstream, pull, first, second)


def expert_sums_kernel(hidden_ref, received_ref, active_ref, up_ref, out_ref, scaled_received, scaled_up):
    pair = out_ref.shape[0]
    half = out_ref.shape[2]
    width = up_ref.shape[1]

    @pl.when(pl.program_id(0) == 0)
    def scale():
        parts = received_ref[:, width:].astype(jnp.float32)
        gate = parts[:, 0:1] + parts[:, 1:2] + parts[:, 2:3]
        scaled_received[...] = (received_ref[:, :width].astype(jnp.float32) * gate).astype(jnp.bfloat16)
        scaled_up[...] = (up_ref[...].astype(jnp.float32) * gate).astype(jnp.bfloat16)

    for which, (left_ref, right_ref) in enumerate(((hidden_ref, scaled_received), (active_ref, scaled_up))):
        total = column_dot(left_ref[...], right_ref[...]).astype(jnp.bfloat16)
        for i in range(pair):
            out_ref[i, which] = total[i * half : (i + 1) * half]


def expert_sums(grad_hidden, received, activated, upstream, owners):
    rows, hidden = grad_hidden.shape
    width = upstream.shape[1]
    pair = 2
    chunk = pl.BlockSpec((rows, pair * hidden // owners), lambda i: (0, i))

    def fixed(cols):
        return pl.BlockSpec((rows, cols), lambda i: (0, 0))

    return pl.pallas_call(
        expert_sums_kernel,
        grid=(owners // pair,),
        out_shape=shaped(owners, 2, hidden // owners, width, dtype=jnp.bfloat16),
        in_specs=[chunk, fixed(received.shape[1]), chunk, fixed(width)],
        out_specs=pl.BlockSpec((pair, 2, hidden // owners, width), lambda i: (i, 0, 0, 0)),
        scratch_shapes=[pltpu.VMEM((rows, width), jnp.bfloat16)] * 2,
        compiler_params=roomy(60),
        cost_estimate=pl.CostEstimate(flops=4 * rows * hidden * width, bytes_accessed=4 * hidden * (width + rows), transcendentals=0),
        name="expert_sums",
    )(grad_hidden, received, activated, upstream)


SELECTED = 104
BAND = 384


def conv_back_kernel(
    taps, gsel_ref, sel_ref, low_ref, gconv_ref, mixer_ref, conv_ref, pre_ref, padded_ref, weight_ref, skip_ref, glog_ref, gbias_ref,
    gpre_ref, left_ref, right_ref, rows_ref,
):
    rows = gconv_ref.shape[0]
    states = glog_ref.shape[0]
    gsel = gsel_ref[...]
    rank = SELECTED - 2 * states
    place = lax.broadcasted_iota(jnp.int32, sel_ref.shape, 1)
    step_low = jnp.where(place < rank, sel_ref[...], 0.0).astype(jnp.bfloat16)
    tall = lax.broadcasted_iota(jnp.int32, (rows_ref.shape[0], LANES), 0)
    wide = lax.broadcasted_iota(jnp.int32, (rows_ref.shape[0], LANES), 1)
    spots = jnp.where(wide == tall + SELECTED, 1.0, 0.0).astype(jnp.bfloat16)
    rows_ref[...] = jnp.zeros_like(rows_ref)
    rows_ref[:states, :] = glog_ref[...]
    for b in range(BAND // LANES):
        lanes = pl.ds(b * LANES, LANES)
        mixer = mixer_ref[:, lanes]
        conv = conv_ref[:, lanes]
        pre = pre_ref[:, lanes]
        grad = transposed_dot(gsel, weight_ref[pl.ds(b * LANES, LANES), :]) + gconv_ref[:, lanes] + skip_ref[:, lanes] * mixer
        grad = grad * silu_slope(pre)
        gpre_ref[:, lanes] = grad
        for k in range(taps):
            rows_ref[states + k : states + k + 1, lanes] = jnp.sum(grad * padded_ref[k * SEGS : k * SEGS + rows, lanes], axis=0, keepdims=True)
        rows_ref[states + taps : states + taps + 1, lanes] = jnp.sum(grad, axis=0, keepdims=True)
        rows_ref[states + taps + 1 : states + taps + 2, lanes] = gbias_ref[:, lanes]
        rows_ref[states + taps + 2 : states + taps + 3, lanes] = jnp.sum(mixer * conv, axis=0, keepdims=True)
        total = column_dot(conv.astype(jnp.bfloat16), gsel)
        for part in three_parts(rows_ref[:, lanes]):
            total = total + column_dot(part, spots)
        left_ref[pl.ds(b * LANES, LANES), :] = total
        right_ref[pl.ds(b * LANES, LANES), :] = column_dot(low_ref[:, lanes], step_low)


def conv_back(gsel, selection, low, grad_conv, grad_mixer, conv, preact, padded, weight, skip, grad_log, grad_bias, taps):
    rows, width = grad_conv.shape

    def band(height):
        return pl.BlockSpec((height, BAND), lambda i: (0, i))

    whole = pl.BlockSpec((rows, LANES), lambda i: (0, 0))
    down = pl.BlockSpec((BAND, LANES), lambda i: (i, 0))
    return pl.pallas_call(
        functools.partial(conv_back_kernel, taps),
        grid=(width // BAND,),
        out_shape=(shaped(rows, width), shaped(width, LANES), shaped(width, LANES)),
        in_specs=[whole, whole]
        + [band(rows)] * 5
        + [band(padded.shape[0]), down, band(1), band(grad_log.shape[0]), band(1)],
        out_specs=(band(rows), down, down),
        scratch_shapes=[pltpu.VMEM((24, BAND), jnp.float32)],
        compiler_params=roomy(60),
        name="conv_back",
    )(gsel, selection, low, grad_conv, grad_mixer, conv, preact, padded, weight, skip, grad_log, grad_bias)


CUT = 768


def token_back_kernel(taps, gpre_ref, next_ref, tap_ref, gate_ref, weight_ref, stream_ref, gain_ref, middle_ref, gconv_ref, token_ref, ggain_ref, total):
    step, last = pl.program_id(0), pl.num_programs(0) - 1
    half = pl.num_programs(0) // 2
    rows = gpre_ref.shape[0]

    def more(piece):
        summed = transposed_dot(piece, weight_ref[...])

        @pl.when(step == 0)
        def begin():
            total[...] = summed

        @pl.when(step > 0)
        def go_on():
            total[...] += summed

    @pl.when(step < half)
    def conv_part():
        place = lax.broadcasted_iota(jnp.int32, (SEGS, CUT), 0)
        grown = None
        for k in range(taps):
            late = taps - 1 - k
            shifted = gpre_ref[late * SEGS :, :]
            if late:
                wrapped = [
                    jnp.where(place == SEGS - 1, next_ref[j : j + 1, :], pltpu.roll(gpre_ref[j * SEGS : (j + 1) * SEGS, :], SEGS - 1, 0))
                    for j in range(late)
                ]
                shifted = jnp.concatenate([shifted] + wrapped, axis=0)
            term = tap_ref[k : k + 1, :] * shifted
            grown = term if grown is None else grown + term
        piece = grown.astype(jnp.bfloat16)
        gconv_ref[...] = piece
        more(piece)

    @pl.when(step >= half)
    def gate_part():
        more(gate_ref[...])

    @pl.when(step == last)
    def finish():
        stream = stream_ref[...].astype(jnp.float32)
        scale = rms_scale(stream)
        back, gain = rms_back(stream, scale, gain_ref[...], total[...])
        token_ref[...] = middle_ref[...] + back
        ggain_ref[...] = gain[None, :]


def token_back(grad_preact, following, taps, grad_gate, in_weight, stream, gain, grad_middle):
    rows, width = grad_preact.shape
    model = stream.shape[1]
    half = width // CUT

    def early(height):
        return pl.BlockSpec((height, CUT), lambda i: (0, jnp.minimum(i, half - 1)))

    fixed = pl.BlockSpec((rows, model), lambda i: (0, 0))
    row = pl.BlockSpec((1, model), lambda i: (0, 0))
    return pl.pallas_call(
        functools.partial(token_back_kernel, taps.shape[0]),
        grid=(2 * half,),
        out_shape=(shaped(rows, width, dtype=jnp.bfloat16), shaped(rows, model), shaped(1, model)),
        in_specs=[
            early(rows),
            early(following.shape[0]),
            early(taps.shape[0]),
            pl.BlockSpec((rows, CUT), lambda i: (0, jnp.maximum(i - half, 0))),
            pl.BlockSpec((model, CUT), lambda i: (0, i)),
            fixed,
            row,
            fixed,
        ],
        out_specs=(early(rows), fixed, row),
        scratch_shapes=[pltpu.VMEM((rows, model), jnp.float32)],
        compiler_params=roomy(60),
        name="token_back",
    )(grad_preact, following, taps, grad_gate, in_weight, stream, gain[None, :], grad_middle)


ORDERS = ("xyz", "yzx", "zxy")
PIECE = 16


def shares_kernel(
    conv_cols, gate_cols, token_ref, out_cols, middle_ref, left_ref, right_ref, narrow_ref, sum_ref, in_ref, out_ref, made, taken,
    half_a, half_b, half_c, one_a, one_b, one_c, sends, arrivals):
    seq, expert = lax.axis_index("seq"), lax.axis_index("expert")
    core = lax.rem(expert, 2)
    place = {"y": lax.div(seq, 4), "z": lax.rem(seq, 4), "x": lax.div(expert, 2)}
    third = token_ref.shape[1] // len(ORDERS)
    streams = [(L, q) for L in range(len(ORDERS)) for q in range(4)]

    def flip(i):
        return i + 1 - 2 * lax.rem(i, 2)

    def device(**moved):
        at = dict(place, **moved)
        return {"seq": at["y"] * 4 + at["z"], "expert": at["x"] * 2 + at.get("core", core)}

    partners = [device(core=1 - core)]
    for axis in "xyz":
        partners += [device(**{axis: flip(place[axis])}), device(**{axis: 3 - place[axis]})]
    barrier = pltpu.get_barrier_semaphore()
    for partner in partners:
        pl.semaphore_signal(barrier, inc=1, device_id=partner, device_id_type=pl.DeviceIdType.MESH)
    pl.semaphore_wait(barrier, len(partners))

    def send(source, target, partner, stream, number):
        k = streams.index(stream)
        copy = pltpu.make_async_remote_copy(
            src_ref=source, dst_ref=target, send_sem=sends.at[k, number], recv_sem=arrivals.at[k, number],
            device_id=partner, device_id_type=pl.DeviceIdType.MESH,
        )
        copy.start()
        return copy

    def add(target, source, unit):
        def step(i, unused):
            target[i] = target[i] + source[i]
            return unused

        lax.fori_loop(0, unit, step, 0, unroll=min(unit, 8))

    inner = out_cols.shape[1]
    for source, target, base in ((conv_cols, in_ref, 0), (gate_cols, in_ref, inner), (out_cols, out_ref, 0)):

        def turn_over(k, unused, source=source, target=target, base=base):
            spot = pl.ds(pl.multiple_of(k * LANES, LANES), LANES)
            target[pl.ds(pl.multiple_of(base + k * LANES, LANES), LANES), :] = source[:, spot].T
            return unused

        lax.fori_loop(0, source.shape[1] // LANES, turn_over, 0)

    pending = {}
    for L, order in enumerate(ORDERS):
        lanes = pl.ds(L * third, third)
        narrow = narrow_ref[:, lanes].astype(jnp.bfloat16)

        def block(s, unused):
            y, z = lax.div(s, 4), lax.rem(s, 4)
            by_in = jnp.dot(
                in_ref[pl.ds(pl.multiple_of(s * 288, 16), 288), :], token_ref[:, lanes], preferred_element_type=jnp.float32
            ).astype(jnp.bfloat16)
            here = pl.ds(pl.multiple_of(s * 144, 16), 144)
            by_out = jnp.dot(out_ref[here, :], middle_ref[:, lanes], preferred_element_type=jnp.float32)
            left, right = left_ref[here, :], right_ref[here, :]
            for x in range(4):
                at = {"x": x, "y": y, "z": z}
                slot = (at[order[0]] * 4 + at[order[1]]) * 4 + at[order[2]]
                rows = by_in[72 * x : 72 * x + 72]
                more = by_out[36 * x : 36 * x + 36].astype(jnp.bfloat16)
                for q in range(4):
                    made[L, q, slot] = rows[16 * q : 16 * q + 16]
                made[L, 4, slot, 0:8] = rows[64:]
                made[L, 4, slot, 8:16] = more[:8]
                made[L, 5, slot] = more[8:24]
                made[L, 6, slot, 0:12] = more[24:]
                made[L, 6, slot, 12:16] = narrow[8:12]
                made[L, 7, slot, 8:16] = narrow[0:8]
                last = jnp.concatenate([left[36 * x : 36 * x + 36], right[36 * x : 36 * x + 36]], axis=0)
                for part in range(third // LANES):
                    k = 8 * (L * (third // LANES) + part)
                    made[L, 7, slot, 0:8, part * LANES : (part + 1) * LANES] = last[k : k + 8].astype(jnp.bfloat16)
            return unused

        lax.fori_loop(0, 16, block, 0, unroll=2)
        for q in range(4):
            pending[L, q] = [
                send(made.at[L, 4 * (1 - core) + q], taken.at[L, q], device(core=1 - core), (L, q), 0)
            ]

    halves, ones = (half_a, half_b, half_c), (one_a, one_b, one_c)
    holding = {}
    for L, q in streams:
        for copy in pending[L, q]:
            copy.wait()
        add(taken.at[L, q], made.at[L, 4 * core + q], 64)
        holding[L, q] = taken.at[L, q]
        pending[L, q] = start_halves(L, q, 0, holding[L, q], halves, place, flip, device, send)
    for turn in range(3):
        unit = 16 >> (2 * turn)
        for L, q in streams:
            axis = ORDERS[L][turn]
            i = place[axis]
            for copy in pending[L, q]:
                copy.wait()
            other = 3 - i if q < 2 else flip(i)
            got = halves[turn].at[L, q]
            add(got.at[0], holding[L, q].at[pl.ds(i * unit, unit)], unit)
            add(got.at[1], holding[L, q].at[pl.ds(other * unit, unit)], unit)
            partner = device(**{axis: other})
            pending[L, q] = [send(got.at[1], ones[turn].at[L, q], partner, (L, q), 3 + 3 * turn)]
        for L, q in streams:
            for copy in pending[L, q]:
                copy.wait()
            got = ones[turn].at[L, q]
            if turn < 2:
                add(got, halves[turn].at[L, q, 0], unit)
                holding[L, q] = got
                pending[L, q] = start_halves(L, q, turn + 1, got, halves, place, flip, device, send)
            else:
                whole = got[0].astype(jnp.float32) + halves[turn][L, q, 0, 0].astype(jnp.float32)
                sum_ref[4 * core + q, :, L * third : (L + 1) * third] = whole
    here = sum_ref.at[pl.ds(4 * core, 4)]
    send(here, here, device(core=1 - core), (0, 0), 10).wait()


def start_halves(L, q, turn, source, halves, place, flip, device, send):
    axis = ORDERS[L][turn]
    unit = 16 >> (2 * turn)
    i = place[axis]
    partner = flip(i) if q < 2 else 3 - i
    second = 3 - partner if q < 2 else flip(partner)
    target = halves[turn].at[L, q]
    return [
        send(source.at[pl.ds(partner * unit, unit)], target.at[0], device(**{axis: partner}), (L, q), 1 + 3 * turn),
        send(source.at[pl.ds(second * unit, unit)], target.at[1], device(**{axis: partner}), (L, q), 2 + 3 * turn),
    ]


def shares(conv_cols, gate_cols, tokens, out_cols, middle, left, right, narrow):
    width = tokens.shape[1]
    rows, inner = out_cols.shape
    third = width // len(ORDERS)

    def slots(*lead):
        return pltpu.VMEM((len(ORDERS),) + lead + (PIECE, third), jnp.bfloat16)

    return pl.pallas_call(
        shares_kernel,
        out_shape=shaped(8, PIECE, width),
        in_specs=[WHOLE] * 8,
        out_specs=WHOLE,
        scratch_shapes=[pltpu.VMEM((2 * inner, rows), jnp.bfloat16), pltpu.VMEM((inner, rows), jnp.bfloat16)]
        + [slots(8, 64), slots(4, 64)]
        + [slots(4, 2, 16 >> (2 * turn)) for turn in range(3)]
        + [slots(4, 16 >> (2 * turn)) for turn in range(3)]
        + [pltpu.SemaphoreType.DMA((12, 11))] * 2,
        compiler_params=roomy(60, collective_id=2, has_side_effects=True),
        name="shares",
    )(conv_cols, gate_cols, tokens, out_cols, middle, left, right, narrow)


def local(
    tokens,
    expert_index,
    cotangent,
    first_gain,
    in_weight,
    conv_weight,
    conv_bias,
    select_weight,
    step_weight,
    step_bias,
    decay_log,
    skip_gain,
    out_weight,
    second_gain,
    router_weight,
    expert_first,
    expert_second,
):
    bf16, f32 = jnp.bfloat16, jnp.float32
    stream = segmented(tokens[0]).astype(f32)
    routes = segmented(expert_index[0])[:, 0]
    upstream = segmented(cotangent[0]).astype(f32)
    row_count, model_width = stream.shape
    inner = conv_bias.shape[0]
    rank = step_weight.shape[0]
    states = decay_log.shape[0]
    taps = conv_weight.shape[0]
    expert_count = router_weight.shape[1]
    capacity = 2 * row_count // expert_count
    seqs, experts = lax.axis_size("seq"), lax.axis_size("expert")
    reach = (taps - 1) * SEGS
    onward = [(i, i + 1) for i in range(seqs - 1)]
    backward = [(i + 1, i) for i in range(seqs - 1)]

    picks = (routes[:, None] == jnp.arange(expert_count, dtype=jnp.int32)[None, :]).astype(bf16)
    earlier = jnp.arange(row_count)[:, None] > jnp.arange(row_count)[None, :]
    ahead = product(earlier.astype(bf16), picks)
    chosen = picks.astype(f32)
    slot_index = routes * capacity + jnp.sum(ahead * chosen, axis=1).astype(jnp.int32)
    seats = jnp.arange(expert_count * capacity, dtype=jnp.int32)
    placing = (seats[:, None] == slot_index[None, :]).astype(bf16)

    def seated(rows):
        return product(placing, rows).astype(bf16)

    def swapped(rows):
        parts = rows.reshape(expert_count, capacity, -1)
        parts = lax.all_to_all(parts, "expert", split_axis=0, concat_axis=0, tiled=True)
        return parts.reshape(expert_count * capacity, -1)

    def unseated(rows):
        return jnp.einsum("st,sd->td", placing, rows, preferred_element_type=f32)

    upstream_there = swapped(seated(segmented(cotangent[0])))

    first_scale = rms_scale(stream)
    normed_in = (stream * first_scale * first_gain).astype(bf16)
    projected = product(normed_in, in_weight)
    conv_input = projected[:, :inner]
    gate_input = projected[:, inner:]

    ends = conv_input[row_count - reach :].reshape(taps - 1, SEGS, inner)
    arrived = lax.ppermute(ends[:, SEGS - 1], "seq", onward)
    front = jnp.concatenate([arrived[:, None], ends[:, : SEGS - 1]], axis=1).reshape(reach, inner)
    padded = jnp.concatenate([front, conv_input], axis=0)
    preact = conv_bias[None, :]
    for k in range(taps):
        preact = preact + conv_weight[k][None, :] * padded[k * SEGS : k * SEGS + row_count]
    conv_out = jax.nn.silu(preact)
    conv_low = conv_out.astype(bf16)
    select_wide = jnp.pad(select_weight, ((0, 0), (0, LANES - select_weight.shape[1])))
    selection = product(conv_low, select_wide)
    step_low = selection[:, :rank].astype(bf16)
    step_raw = product(step_low, step_weight) + step_bias
    step_size = jax.nn.softplus(step_raw)

    blocks = inner // LANES // PARTS
    log_rows = decay_log.reshape(GRID, GRID, PARTS, blocks, LANES).transpose(2, 0, 1, 3, 4)
    log_rows = jnp.pad(log_rows, ((0, 0), (0, 0), (0, 0), (0, SEGS - blocks), (0, 0)))
    step_size, upstream_there = lax.optimization_barrier((step_size, upstream_there))
    scanned, first = scan_forward(step_size, conv_out, selection, decay_log, log_rows, rank)

    mixer_out = scanned + skip_gain * conv_out
    gated = (mixer_out * jax.nn.silu(gate_input)).astype(bf16)
    middle = stream + product(gated, out_weight)
    second_scale = rms_scale(middle)
    normed_mid = (middle * second_scale * second_gain).astype(bf16)
    router_probs = jax.nn.softmax(product(normed_mid, router_weight), axis=-1)
    gate_value = jnp.sum(router_probs * chosen, axis=1)

    gate_parts = jnp.stack(three_parts(gate_value), axis=1)
    gate_parts = jnp.pad(gate_parts, ((0, 0), (0, LANES - gate_parts.shape[1])))
    leaving = seated(jnp.concatenate([normed_mid, gate_parts], axis=1))
    leaving, upstream_there = lax.optimization_barrier((leaving, upstream_there))
    received = swapped(leaving)
    pull = expert_pull(upstream_there, expert_second[0])
    activated, grad_hidden, value_there, grad_there = expert_layer(
        received, upstream_there, pull, expert_first[0], expert_second[0]
    )
    grad_home = unseated(swapped(grad_there))
    expert_grads = expert_sums(grad_hidden, received, activated, upstream_there, seqs)
    expert_grads, value_there = lax.optimization_barrier((expert_grads, value_there))
    value_home = swapped(value_there)

    grad_gate = jnp.sum(grad_home[:, model_width:], axis=1)
    grad_logits = (grad_gate[:, None] * gate_value[:, None] * (chosen - router_probs)).astype(bf16)
    grad_router = summed_rows(grad_logits, normed_mid)
    grad_mid = across(grad_logits, router_weight) + gate_value[:, None] * grad_home[:, :model_width]
    grad_middle_norm, grad_second_gain = rms_back(middle, second_scale, second_gain, grad_mid)
    grad_middle = upstream + grad_middle_norm
    middle_low = grad_middle.astype(bf16)
    grad_gated = across(middle_low, out_weight)
    grad_mixer = grad_gated * jax.nn.silu(gate_input)
    grad_gate_input = grad_gated * mixer_out * silu_slope(gate_input)

    expert_grads, grad_mixer = lax.optimization_barrier((expert_grads, grad_mixer))
    expert_share = lax.psum_scatter(
        expert_grads.reshape(-1, model_width), "seq", scatter_dimension=0, tiled=True
    ).reshape(2, -1, model_width)

    step_pull = jnp.pad(step_weight, ((0, LANES - rank), (0, 0)))
    step_raw_low, grad_conv_scan, grad_selection, grad_decay_log, grad_step_bias = scan_backward(
        step_size, conv_out, grad_mixer, step_raw, selection, decay_log, log_rows, step_pull, first, rank
    )
    grad_selection, value_home = lax.optimization_barrier((grad_selection, value_home))
    mixed = middle + gate_value[:, None] * unseated(value_home)
    grad_preact, left, right = conv_back(
        grad_selection,
        selection,
        step_raw_low,
        grad_conv_scan,
        grad_mixer,
        conv_out,
        preact,
        padded,
        select_wide,
        skip_gain[None, :],
        grad_decay_log,
        grad_step_bias,
        taps,
    )
    heads = grad_preact[:reach].reshape(taps - 1, SEGS, inner)
    following = lax.ppermute(heads[:, 0], "seq", backward)
    grad_conv_input, grad_tokens, grad_first_gain = token_back(
        grad_preact, following, conv_weight, grad_gate_input.astype(bf16), in_weight, stream, first_gain, grad_middle
    )

    devices = seqs * experts
    each, fewer = inner // devices, model_width // devices
    narrow = jnp.concatenate([grad_first_gain, grad_second_gain[None, :], grad_router, jnp.zeros((6, model_width), f32)])
    grad_conv_input, expert_share = lax.optimization_barrier((grad_conv_input, expert_share))
    sums = shares(grad_conv_input, grad_gate_input.astype(bf16), normed_in, gated, middle_low, left, right, narrow)
    sums = sums.reshape(-1, model_width)
    core = lax.axis_index("expert") % 2
    in_share = lax.dynamic_slice_in_dim(sums, 2 * each * core, 2 * each)
    out_share = lax.dynamic_slice_in_dim(sums, 4 * each + each * core, each)
    small = sums[112:120].reshape(8, -1, LANES).transpose(1, 0, 2).reshape(2, 2 * each, LANES)
    small = lax.dynamic_slice_in_dim(small, each * core, each, axis=1)
    rows_sum = small[0, :, rank + 2 * states :]
    owner = lax.axis_index("seq") * experts + lax.axis_index("expert")
    narrow_sum = jnp.concatenate([sums[120:128], sums[108:110]])
    narrow_sum = lax.dynamic_slice_in_dim(narrow_sum, owner * fewer, fewer, axis=1)
    return (
        in_order(mixed.astype(bf16))[None],
        in_order(grad_tokens)[None],
        narrow_sum[0],
        in_share.T,
        rows_sum[:, states : states + taps].T,
        rows_sum[:, states + taps],
        small[0, :, : rank + 2 * states],
        small[1, :, :rank].T,
        rows_sum[:, states + taps + 1],
        rows_sum[:, :states].T,
        rows_sum[:, states + taps + 2],
        out_share,
        narrow_sum[1],
        narrow_sum[2:].T,
        expert_share[0].T.astype(f32)[None],
        expert_share[1].astype(f32)[None],
    )


def solution(mesh):
    return jax.shard_map(
        local,
        mesh=mesh,
        in_specs=(
            P("expert", "seq", None),
            P("expert", "seq", None),
            P("expert", "seq", None),
            P(),
            P(),
            P(),
            P(),
            P(),
            P(),
            P(),
            P(),
            P(),
            P(),
            P(),
            P(),
            P("expert", None, None),
            P("expert", None, None),
        ),
        out_specs=(
            P("expert", "seq", None),
            P("expert", "seq", None),
            P(("seq", "expert")),
            P(None, ("seq", "expert")),
            P(None, ("seq", "expert")),
            P(("seq", "expert")),
            P(("seq", "expert"), None),
            P(None, ("seq", "expert")),
            P(("seq", "expert")),
            P(None, ("seq", "expert")),
            P(("seq", "expert")),
            P(("seq", "expert"), None),
            P(("seq", "expert")),
            P(("seq", "expert"), None),
            P("expert", None, "seq"),
            P("expert", "seq", None),
        ),
        check_vma=False,
    )
```

```python
import functools
import math

import jax
import jax.numpy as jnp
from jax import lax
from jax.experimental import pallas as pl
from jax.experimental.pallas import tpu as pltpu
from jax.sharding import PartitionSpec as P

LANES = 128
SEGS = 8
LOG2E = math.log2(math.e)
PARTS = 3
SELECTED = 104
EXPERTS = 8
CUT = 768
GRID = 4


def spread_ones(states):
    row = lax.broadcasted_iota(jnp.int32, (LANES, states * LANES), 0)
    lane = lax.broadcasted_iota(jnp.int32, (LANES, states * LANES), 1)
    return row, lane // LANES


def fill_maps(sel_ref, wide_ref, column):
    steps, states = wide_ref.shape[:2]
    row, block = spread_ones(states)
    ones = jnp.where(row == block + column, 1.0, 0.0).astype(jnp.bfloat16)
    left, total = sel_ref[...], None
    for unused in range(3):
        part = left.astype(jnp.bfloat16)
        left = left - part.astype(jnp.float32)
        spread = jnp.dot(part, ones, preferred_element_type=jnp.float32)
        total = spread if total is None else total + spread
    for n in range(states):
        wide_ref[:, n] = total[:, n * LANES : (n + 1) * LANES].reshape(steps, SEGS, LANES)


def gather_maps(sum_ref, column):
    steps, states = sum_ref.shape[:2]
    row, block = spread_ones(states)
    ones = jnp.where(row == block + column, 1.0, 0.0).astype(jnp.bfloat16)
    left = jnp.concatenate([sum_ref[:, n].reshape(steps * SEGS, LANES) for n in range(states)], axis=1)
    total = None
    for unused in range(3):
        part = left.astype(jnp.bfloat16)
        left = left - part.astype(jnp.float32)
        summed = transposed_dot(part, ones)
        total = summed if total is None else total + summed
    return total


def lanes_of(block):
    return pl.ds(pl.multiple_of(block * LANES, LANES), LANES)


def rows_of(j):
    return pl.ds(pl.multiple_of(j * SEGS, SEGS), SEGS)


def rates_of(log_ref, lanes):
    states = log_ref.shape[0]
    rate = -LOG2E * jnp.exp(log_ref[:, lanes])
    return jnp.stack([jnp.broadcast_to(rate[n : n + 1], (SEGS, LANES)) for n in range(states)])


def neighbour(value, hop, later, fill):
    axis = value.ndim - 2
    place = lax.broadcasted_iota(jnp.int32, value.shape, axis)
    if later:
        return jnp.where(place < SEGS - hop, pltpu.roll(value, SEGS - hop, axis), fill)
    return jnp.where(place >= hop, pltpu.roll(value, hop, axis), fill)


def summarize(later, part, step_ref, other_ref, wide, log_ref, part_ref, span_ref, message):
    steps, states = wide.shape[:2]
    blocks = step_ref.shape[1] // LANES // PARTS

    def block(i, unused):
        lanes = lanes_of(part * blocks + i)
        rate = rates_of(log_ref, lanes)

        def advance(turn, carry):
            span, memory = carry
            j = steps - 1 - turn if later else turn
            step = step_ref[rows_of(j), lanes]
            other = other_ref[rows_of(j), lanes]
            decay = jnp.exp2(step * rate)
            if later:
                memory = decay * (memory + wide[j] * other)
            else:
                memory = decay * memory + wide[j] * (step * other)
            return span + step, memory

        zero = jnp.zeros((SEGS, LANES), jnp.float32)
        span, memory = lax.fori_loop(0, steps, advance, (zero, jnp.zeros(rate.shape, jnp.float32)), unroll=8)
        hop = 1
        while hop < SEGS:
            memory = memory + jnp.exp2(rate * span) * neighbour(memory, hop, later, 0.0)
            span = span + neighbour(span, hop, later, 0.0)
            hop *= 2
        span_ref[:, lanes] = span
        part_ref[:, :, lanes] = memory
        end = 0 if later else SEGS - 1
        for n in range(states):
            message[n // GRID, n % GRID, pl.ds(i, 1), :] = memory[n, end : end + 1]
        for q in range(GRID):
            message[q, GRID, pl.ds(i, 1), :] = span[end : end + 1]
        return unused

    lax.fori_loop(0, blocks, block, 0)


def entering(later, part_ref, span_ref, rate, lanes, carried):
    ends = part_ref[:, :, lanes] + jnp.exp2(rate * span_ref[:, lanes]) * carried
    return neighbour(ends, 1, later, carried)


def carried_at(in_ref, part, i):
    states = GRID * GRID
    return jnp.stack(
        [jnp.broadcast_to(in_ref[n // GRID, n % GRID, pl.ds(i, 1), :], (SEGS, LANES)) for n in range(states)]
    )


def scan_part(part, step_ref, conv_ref, wide_in, wide_out, log_ref, part_ref, span_ref, in_ref, y_ref, entry_ref):
    steps = wide_in.shape[0]
    blocks = step_ref.shape[1] // LANES // PARTS

    def block(i, unused):
        lanes = lanes_of(part * blocks + i)
        rate = rates_of(log_ref, lanes)
        first = entering(False, part_ref, span_ref, rate, lanes, carried_at(in_ref, part, i))
        entry_ref[:, :, lanes] = first

        def advance(j, memory):
            step = step_ref[rows_of(j), lanes]
            memory = jnp.exp2(step * rate) * memory + wide_in[j] * (step * conv_ref[rows_of(j), lanes])
            y_ref[rows_of(j), lanes] = jnp.sum(wide_out[j] * memory, axis=0)
            return memory

        lax.fori_loop(0, steps, advance, first, unroll=8)
        return unused

    lax.fori_loop(0, blocks, block, 0)


def retreat_part(
    part, step_ref, conv_ref, grad_ref, raw_ref, wide_in, wide_out, log_ref, pull_ref, entry_ref, part_ref, span_ref, in_ref,
    low_ref, gconv_ref, glog_ref, gbias_ref, sum_in, sum_out, states_ref, decays_ref, raw_sum, raw_rows,
):
    steps = wide_in.shape[0]
    blocks = step_ref.shape[1] // LANES // PARTS

    def block(i, unused):
        lanes = lanes_of(part * blocks + i)
        rate = rates_of(log_ref, lanes)

        def advance(j, memory):
            step = step_ref[rows_of(j), lanes]
            decay = jnp.exp2(step * rate)
            memory = decay * memory + wide_in[j] * (step * conv_ref[rows_of(j), lanes])
            decays_ref[j] = decay
            states_ref[j + 1] = memory
            return memory

        first = entry_ref[:, :, lanes]
        states_ref[0] = first
        lax.fori_loop(0, steps, advance, first, unroll=8)

        def retreat(turn, carry):
            j = steps - 1 - turn
            mu, slow = carry
            step = step_ref[rows_of(j), lanes]
            conv = conv_ref[rows_of(j), lanes]
            grad = grad_ref[rows_of(j), lanes]
            lam = wide_out[j] * grad + mu
            sum_out[j] += grad * states_ref[j + 1]
            sum_in[j] += lam * (step * conv)
            by_in = jnp.sum(lam * wide_in[j], axis=0)
            mu = lam * decays_ref[j]
            kept = mu * states_ref[j]
            by_rate = jnp.sum(kept * rate, axis=0)
            grad_step = by_in * conv + (1.0 / LOG2E) * by_rate
            raw_rows[rows_of(j), :] = grad_step * jax.nn.sigmoid(raw_ref[rows_of(j), lanes])
            gconv_ref[rows_of(j), lanes] = by_in * step
            return mu, slow + kept * step

        last = entering(True, part_ref, span_ref, rate, lanes, carried_at(in_ref, part, i))
        unused_mu, slow = lax.fori_loop(0, steps, retreat, (last, jnp.zeros(rate.shape, jnp.float32)), unroll=4)
        glog_ref[:, lanes] = (1.0 / LOG2E) * jnp.sum(slow * rate, axis=1)
        raw_steps = raw_rows[...]
        gbias_ref[:, lanes] = jnp.sum(raw_steps, axis=0, keepdims=True)
        low = raw_steps.astype(jnp.bfloat16)
        low_ref[:, lanes] = low
        raw_sum[...] += transposed_dot(low, pull_ref[:, lanes])
        return unused

    lax.fori_loop(0, blocks, block, 0)


class Relay:
    def __init__(self, later, log_rows, in_ref, message, got, row, rows_got, above, made, sends, arrivals, chained=False):
        self.later, self.log_rows, self.message, self.got = later, log_rows, message, got
        self.row, self.rows_got, self.above, self.made, self.in_ref = row, rows_got, above, made, in_ref
        self.sends, self.arrivals = sends, arrivals
        seq = lax.axis_index("seq")
        self.y, self.z = lax.div(seq, GRID), lax.rem(seq, GRID)
        self.flying = {}
        barrier = pltpu.get_barrier_semaphore()
        peers = [self.across(k) for k in range(1, GRID)] + [self.along(k) for k in range(1, GRID)]
        if chained:
            peers += [self.onward(1), self.onward(-1)]
        for peer in peers:
            pl.semaphore_signal(barrier, inc=1, device_id=peer, device_id_type=pl.DeviceIdType.MESH)
        self.peers = len(peers)

    def onward(self, k):
        size = GRID * GRID
        return {"seq": lax.rem(self.y * GRID + self.z + k + size, size)}

    def across(self, k):
        return {"seq": self.y * GRID + lax.rem(self.z + k, GRID)}

    def along(self, k):
        return {"seq": lax.rem(self.y + k, GRID) * GRID + self.z}

    def meet(self):
        pl.semaphore_wait(pltpu.get_barrier_semaphore(), self.peers)

    def send(self, part, phase, k, source, target, peer):
        copy = pltpu.make_async_remote_copy(
            src_ref=source, dst_ref=target, send_sem=self.sends.at[part, phase, k], recv_sem=self.arrivals.at[part, phase, k],
            device_id=peer, device_id_type=pl.DeviceIdType.MESH,
        )
        copy.start()
        self.flying.setdefault((part, phase), []).append(copy)

    def land(self, part, phase):
        for copy in self.flying[part, phase]:
            copy.wait()

    def order(self):
        return range(GRID - 1, -1, -1) if self.later else range(GRID)

    def rate(self, part):
        return -LOG2E * jnp.exp(self.log_rows[part, self.z])

    def first(self, part):
        for k in range(1, GRID):
            peer = lax.rem(self.z + k, GRID)
            self.send(part, 0, k, self.message.at[part, peer], self.got.at[part, k], self.across(k))
        self.got[part, 0] = self.message[part, self.z]

    def second(self, part):
        self.land(part, 0)
        rate = self.rate(part)
        state, span = jnp.zeros(rate.shape, jnp.float32), jnp.zeros(rate.shape[1:], jnp.float32)
        for z in self.order():
            block = self.got[part, lax.rem(self.z - z + GRID, GRID)]
            state = jnp.exp2(rate * block[GRID]) * state + block[:GRID]
            span = span + block[GRID]
        self.row[part, :GRID] = state
        self.row[part, GRID] = span
        for k in range(1, GRID):
            self.send(part, 1, k, self.row.at[part], self.rows_got.at[part, k], self.along(k))
        self.rows_got[part, 0] = self.row[part]

    def third(self, part):
        self.land(part, 1)
        rate = self.rate(part)
        state = jnp.zeros(rate.shape, jnp.float32)
        for y in self.order():
            self.above[part, y] = state
            block = self.rows_got[part, lax.rem(self.y - y + GRID, GRID)]
            state = jnp.exp2(rate * block[GRID]) * state + block[:GRID]
        state = self.above[part, self.y]
        for z in self.order():
            self.made[part, z] = state
            block = self.got[part, lax.rem(self.z - z + GRID, GRID)]
            state = jnp.exp2(rate * block[GRID]) * state + block[:GRID]
        for k in range(1, GRID):
            peer = lax.rem(self.z + k, GRID)
            self.send(part, 2, k, self.made.at[part, peer], self.in_ref.at[part, self.z], self.across(k))
        self.in_ref[part, self.z] = self.made[part, self.z]

    def done(self, part):
        self.land(part, 2)


def staged(relay, summary, extra, scan):
    summary(0)
    relay.first(0)
    summary(1)
    relay.first(1)
    relay.second(0)
    summary(2)
    relay.first(2)
    relay.third(0)
    relay.second(1)
    extra()
    relay.second(2)
    relay.third(1)
    relay.done(0)
    scan(0)
    relay.third(2)
    relay.done(1)
    scan(1)
    relay.done(2)
    scan(2)


def mixer_kernel(
    token_ref, gain_ref, in_hbm, tap_ref, tap_bias_ref, select_ref, step_weight_ref, step_bias_ref, log_ref, log_rows, skip_ref,
    out_hbm, second_gain_ref, router_ref, slot_ref, route_ref,
    normed_out, gate_out, padded_out, pre_out, conv_out, raw_out, step_out, sel_out, entry_out, mixer_out, gated_out,
    middle_out, normed_mid_out, probs_out, chosen_out, leaving_out,
    normed, in_ref, out_ref, padded, gate, pre, conv, raw, step, sel, entry, mixer, gated, middle, normed_mid, probs, chosen, leaving,
    tail, tail_got, part_ref, span_ref, wide_in, wide_out, loads, saves, passing, relay_in, *relayed
):
    rows, width = step.shape
    taps, states = tap_ref.shape[0], log_ref.shape[0]
    reach = (taps - 1) * SEGS
    rank = SELECTED - 2 * states
    pieces = in_ref.shape[0]
    cut = in_ref.shape[2]
    blocks = width // LANES

    loading = [pltpu.make_async_copy(in_hbm.at[:, pl.ds(k * cut, cut)], in_ref.at[k], loads.at[k]) for k in range(pieces)]
    loading.append(pltpu.make_async_copy(out_hbm, out_ref, loads.at[pieces]))
    for copy in loading:
        copy.start()
    saving = []

    def save(source, target):
        copy = pltpu.make_async_copy(source, target, saves.at[len(saving)])
        copy.start()
        saving.append(copy)

    relay = Relay(False, log_rows, relay_in, *relayed, chained=True)

    stream = token_ref[...].astype(jnp.float32)
    normed[...] = (stream * rms_scale(stream) * gain_ref[...]).astype(jnp.bfloat16)
    save(normed, normed_out)
    for k in range(pieces // 2):
        loading[k].wait()
        padded[reach:, k * cut : (k + 1) * cut] = jnp.dot(normed[...], in_ref[k], preferred_element_type=jnp.float32)
    tail[...] = jnp.zeros_like(tail)
    for k in range(taps - 1):
        row = reach + rows - (taps - 1 - k) * SEGS + SEGS - 1
        tail[k : k + 1, :] = padded[row : row + 1, :]
    relay.meet()
    handing = pltpu.make_async_remote_copy(
        src_ref=tail, dst_ref=tail_got, send_sem=passing.at[0], recv_sem=passing.at[1],
        device_id=relay.onward(1), device_id_type=pl.DeviceIdType.MESH,
    )
    handing.start()
    for k in range(pieces // 2, pieces):
        loading[k].wait()
        spot = slice((k - pieces // 2) * cut, (k - pieces // 2 + 1) * cut)
        gate[:, spot] = jnp.dot(normed[...], in_ref[k], preferred_element_type=jnp.float32)
    save(gate, gate_out)
    handing.wait()
    started = jnp.where(lax.axis_index("seq") > 0, 1.0, 0.0)
    for k in range(taps - 1):
        row = rows + k * SEGS
        segment = lax.broadcasted_iota(jnp.int32, (SEGS, width), 0)
        before = pltpu.roll(padded[row : row + SEGS, :], 1, 0)
        padded[k * SEGS : (k + 1) * SEGS, :] = jnp.where(segment == 0, started * tail_got[k : k + 1, :], before)
    save(padded, padded_out)

    sel[...] = jnp.zeros_like(sel)

    def convolve(b, unused):
        lanes = lanes_of(b)
        value = tap_bias_ref[:, lanes]
        for k in range(taps):
            value = value + tap_ref[k : k + 1, lanes] * padded[k * SEGS : k * SEGS + rows, lanes]
        pre[:, lanes] = value
        value = value * jax.nn.sigmoid(value)
        conv[:, lanes] = value
        sel[...] += jnp.dot(value.astype(jnp.bfloat16), select_ref[lanes, :], preferred_element_type=jnp.float32)
        return unused

    lax.fori_loop(0, blocks, convolve, 0)
    save(pre, pre_out)
    save(conv, conv_out)
    save(sel, sel_out)
    step_low = sel[...].astype(jnp.bfloat16)

    def size(b, unused):
        lanes = lanes_of(b)
        value = jnp.dot(step_low, step_weight_ref[:, lanes], preferred_element_type=jnp.float32) + step_bias_ref[:, lanes]
        raw[:, lanes] = value
        step[:, lanes] = jnp.maximum(value, 0.0) + jnp.log1p(jnp.exp(-jnp.abs(value)))
        return unused

    lax.fori_loop(0, blocks, size, 0)
    save(raw, raw_out)
    save(step, step_out)
    fill_maps(sel, wide_in, rank)

    def summary(part):
        summarize(False, part, step, conv, wide_in, log_ref, part_ref, span_ref, relay.message.at[part])

    def scan(part):
        scan_part(part, step, conv, wide_in, wide_out, log_ref, part_ref, span_ref, relay_in.at[part], mixer, entry)

    staged(relay, summary, lambda: fill_maps(sel, wide_out, rank + states), scan)
    save(entry, entry_out)

    def blend(b, unused):
        lanes = lanes_of(b)
        value = mixer[:, lanes] + skip_ref[:, lanes] * conv[:, lanes]
        mixer[:, lanes] = value
        opening = gate[:, lanes]
        gated[:, lanes] = (value * (opening * jax.nn.sigmoid(opening))).astype(jnp.bfloat16)
        return unused

    lax.fori_loop(0, blocks, blend, 0)
    save(mixer, mixer_out)
    save(gated, gated_out)
    loading[pieces].wait()
    value = token_ref[...].astype(jnp.float32) + jnp.dot(gated[...], out_ref[...], preferred_element_type=jnp.float32)
    middle[...] = value
    save(middle, middle_out)
    normed_mid[...] = (value * rms_scale(value) * second_gain_ref[...]).astype(jnp.bfloat16)
    save(normed_mid, normed_mid_out)
    logits = jnp.dot(normed_mid[...], router_ref[...], preferred_element_type=jnp.float32)
    place = lax.broadcasted_iota(jnp.int32, (rows, LANES), 1)
    logits = jnp.where(place < EXPERTS, logits, -1e30)
    grown = jnp.exp(logits - jnp.max(logits, axis=1, keepdims=True))
    grown = jnp.where(place < EXPERTS, grown, 0.0)
    probs[...] = grown / jnp.sum(grown, axis=1, keepdims=True)
    save(probs, probs_out)
    gate_value = jnp.sum(jnp.where(place == route_ref[...], probs[...], 0.0), axis=1, keepdims=True)
    chosen[...] = jnp.broadcast_to(gate_value, (rows, LANES))
    save(chosen, chosen_out)
    parts = jnp.zeros((rows, LANES), jnp.float32)
    for k, piece in enumerate(three_parts(gate_value)):
        parts = jnp.where(place == k, piece.astype(jnp.float32), parts)
    seats = leaving.shape[0]
    seating = jnp.where(lax.broadcasted_iota(jnp.int32, (seats, rows), 0) == slot_ref[...], 1.0, 0.0).astype(jnp.bfloat16)
    model = token_ref.shape[1]
    leaving[:, :model] = jnp.dot(seating, normed_mid[...], preferred_element_type=jnp.float32).astype(jnp.bfloat16)
    leaving[:, model:] = jnp.dot(seating, parts.astype(jnp.bfloat16), preferred_element_type=jnp.float32).astype(jnp.bfloat16)
    save(leaving, leaving_out)
    for copy in saving:
        copy.wait()


def backward_kernel(
    column, step_ref, conv_ref, grad_ref, raw_ref, sel_ref, log_ref, log_rows, pull_ref, entry_ref,
    low_ref, gconv_ref, gsel_ref, glog_ref, gbias_ref,
    part_ref, span_ref, wide_in, wide_out, sum_in, sum_out, states_ref, decays_ref, raw_sum, raw_rows, in_ref, *relayed
):
    states = log_ref.shape[0]
    relay = Relay(True, log_rows, in_ref, *relayed)
    relay.meet()
    message = relayed[0]
    fill_maps(sel_ref, wide_out, column + states)

    def summary(part):
        summarize(True, part, step_ref, grad_ref, wide_out, log_ref, part_ref, span_ref, message.at[part])

    def prepare():
        fill_maps(sel_ref, wide_in, column)
        sum_in[...] = jnp.zeros_like(sum_in)
        sum_out[...] = jnp.zeros_like(sum_out)
        raw_sum[...] = jnp.zeros_like(raw_sum)

    def scan(part):
        retreat_part(
            part, step_ref, conv_ref, grad_ref, raw_ref, wide_in, wide_out, log_ref, pull_ref, entry_ref, part_ref, span_ref,
            in_ref.at[part], low_ref, gconv_ref, glog_ref, gbias_ref, sum_in, sum_out, states_ref, decays_ref, raw_sum, raw_rows,
        )

    staged(relay, summary, prepare, scan)
    maps = gather_maps(sum_in, column) + gather_maps(sum_out, column + states)
    gsel_ref[...] = (raw_sum[...] + maps).astype(jnp.bfloat16)


WHOLE = pl.BlockSpec(memory_space=pltpu.VMEM)


def shaped(*dims, dtype=jnp.float32):
    return jax.ShapeDtypeStruct(dims, dtype)


def roomy(mebibytes, **more):
    return pltpu.CompilerParams(vmem_limit_bytes=mebibytes << 20, **more)


def busy(elements):
    return pl.CostEstimate(flops=4096 * elements, bytes_accessed=16 * elements, transcendentals=4 * elements)


def wide_scratch(rows, states, extra=0):
    return pltpu.VMEM((rows // SEGS + extra, states, SEGS, LANES), jnp.float32)


def chain_scratch(states, width):
    return [pltpu.VMEM((states, SEGS, width), jnp.float32), pltpu.VMEM((SEGS, width), jnp.float32)]


def relay_scratch():
    def kept(*dims):
        return pltpu.VMEM((PARTS,) + dims + (SEGS, LANES), jnp.float32)

    return [
        kept(GRID, GRID),
        kept(GRID, GRID + 1),
        kept(GRID, GRID + 1),
        kept(GRID + 1),
        kept(GRID, GRID + 1),
        kept(GRID, GRID),
        kept(GRID, GRID),
        pltpu.SemaphoreType.DMA((PARTS, 3, GRID)),
        pltpu.SemaphoreType.DMA((PARTS, 3, GRID)),
    ]


def mixer(tokens, gain, in_weight, taps, tap_bias, select, step_weight, step_bias, decay_log, log_rows, skip, out_weight, second_gain, router, slots, routes, seats):
    rows, model = tokens.shape
    states, width = decay_log.shape
    reach = (taps.shape[0] - 1) * SEGS
    bf16, f32 = jnp.bfloat16, jnp.float32
    anywhere = pl.BlockSpec(memory_space=pl.ANY)
    results = [
        ((rows, model), bf16),
        ((rows, width), f32),
        ((rows + reach, width), f32),
        ((rows, width), f32),
        ((rows, width), f32),
        ((rows, width), f32),
        ((rows, width), f32),
        ((rows, LANES), f32),
        ((states, SEGS, width), f32),
        ((rows, width), f32),
        ((rows, width), bf16),
        ((rows, model), f32),
        ((rows, model), bf16),
        ((rows, LANES), f32),
        ((rows, LANES), f32),
        ((seats, model + LANES), bf16),
    ]
    kept = [pltpu.VMEM(dims, dtype) for dims, dtype in results]
    weights = [pltpu.VMEM((2 * width // CUT, model, CUT), bf16), pltpu.VMEM(out_weight.shape, bf16)]
    relayed = relay_scratch()
    return pl.pallas_call(
        mixer_kernel,
        out_shape=tuple(shaped(*dims, dtype=dtype) for dims, dtype in results),
        in_specs=[WHOLE] * 2 + [anywhere] + [WHOLE] * 8 + [anywhere] + [WHOLE] * 4,
        out_specs=(anywhere,) * len(results),
        scratch_shapes=kept[:1]
        + weights
        + [kept[2], kept[1]]
        + kept[3:]
        + [pltpu.VMEM((SEGS, width), f32)] * 2
        + chain_scratch(states, width)
        + [wide_scratch(rows, states)] * 2
        + [
            pltpu.SemaphoreType.DMA((2 * width // CUT + 1,)),
            pltpu.SemaphoreType.DMA((len(results),)),
            pltpu.SemaphoreType.DMA((2,)),
        ]
        + relayed,
        compiler_params=roomy(60, collective_id=0, has_side_effects=True),
        cost_estimate=busy(rows * states * width),
        name="mixer",
    )(tokens, gain, in_weight, taps, tap_bias, select, step_weight, step_bias, decay_log, log_rows, skip, out_weight, second_gain, router, slots, routes)


def scan_backward(step, conv, grad, raw, selection, decay_log, log_rows, pull, first, column):
    rows, width = step.shape
    states = decay_log.shape[0]
    narrow = pltpu.VMEM((rows, LANES), jnp.float32)
    return pl.pallas_call(
        functools.partial(backward_kernel, column),
        out_shape=(
            shaped(rows, width, dtype=jnp.bfloat16),
            shaped(rows, width),
            shaped(rows, LANES, dtype=jnp.bfloat16),
            shaped(states, width),
            shaped(1, width),
        ),
        in_specs=[WHOLE] * 9,
        out_specs=(WHOLE,) * 5,
        scratch_shapes=chain_scratch(states, width)
        + [wide_scratch(rows, states)] * 4
        + [wide_scratch(rows, states, 1), wide_scratch(rows, states)]
        + [narrow] * 2
        + relay_scratch(),
        compiler_params=roomy(46, collective_id=1, has_side_effects=True),
        cost_estimate=busy(rows * states * width),
        name="scan_backward",
    )(step, conv, grad, raw, selection, decay_log, log_rows, pull, first)


def segmented(block):
    rows = block.shape[0]
    return block.reshape(SEGS, rows // SEGS, -1).transpose(1, 0, 2).reshape(rows, -1)


def in_order(block):
    rows = block.shape[0]
    return block.reshape(rows // SEGS, SEGS, -1).transpose(1, 0, 2).reshape(rows, -1)


def rms_scale(stream):
    return lax.rsqrt(jnp.mean(stream * stream, axis=-1, keepdims=True) + 1e-05)


def rms_back(stream, scale, gain, grad):
    grown = grad * gain
    along = jnp.mean(stream * grown, axis=-1, keepdims=True)
    return scale * grown - stream * (scale * scale * scale * along), jnp.sum(grad * stream * scale, axis=0)


def silu_slope(value):
    gate = jax.nn.sigmoid(value)
    return gate * (1.0 + value * (1.0 - gate))


def product(left, right):
    return jnp.dot(left, right, preferred_element_type=jnp.float32)


def across(left, right):
    return jnp.einsum("tk,dk->td", left, right, preferred_element_type=jnp.float32)


def summed_rows(left, right):
    return jnp.einsum("tk,td->kd", left, right, preferred_element_type=jnp.float32)


CHUNK = 1024
GELU_OUT = math.sqrt(2.0 / math.pi)
GELU_IN = 0.044715


def transposed_dot(left, right):
    return lax.dot_general(left, right, (((1,), (1,)), ((), ())), preferred_element_type=jnp.float32)


def column_dot(left, right):
    return lax.dot_general(left, right, (((0,), (0,)), ((), ())), preferred_element_type=jnp.float32)


def three_parts(value):
    parts, left = [], value
    for unused in range(3):
        part = left.astype(jnp.bfloat16)
        left = left - part.astype(jnp.float32)
        parts.append(part)
    return parts


def expert_pull_kernel(up_ref, second_ref, pull_ref):
    pull_ref[...] = transposed_dot(up_ref[...], second_ref[...]).astype(jnp.bfloat16)


def expert_pull(upstream, second):
    rows, width = upstream.shape
    hidden = second.shape[0]
    return pl.pallas_call(
        expert_pull_kernel,
        grid=(hidden // CHUNK,),
        out_shape=shaped(rows, hidden, dtype=jnp.bfloat16),
        in_specs=[pl.BlockSpec((rows, width), lambda i: (0, 0)), pl.BlockSpec((CHUNK, width), lambda i: (i, 0))],
        out_specs=pl.BlockSpec((rows, CHUNK), lambda i: (0, i)),
        compiler_params=roomy(60),
        cost_estimate=pl.CostEstimate(flops=2 * rows * hidden * width, bytes_accessed=2 * (width + rows) * hidden, transcendentals=0),
        name="expert_pull",
    )(upstream, second)


def expert_kernel(got_ref, up_ref, pull_ref, first_ref, second_ref, active_ref, grad_ref, value_ref, sent_ref, value, sent):
    step, last = pl.program_id(0), pl.num_programs(0) - 1
    width = up_ref.shape[1]
    first = first_ref[...]
    pre = jnp.dot(got_ref[:, :width], first, preferred_element_type=jnp.float32)
    square = pre * pre
    bent = jnp.tanh(pre * (GELU_OUT + GELU_OUT * GELU_IN * square))
    share = 0.5 + 0.5 * bent
    active = (pre * share).astype(jnp.bfloat16)
    slope = share + pre * (0.5 - 0.5 * bent * bent) * (GELU_OUT + 3.0 * GELU_OUT * GELU_IN * square)
    grad = (slope * pull_ref[...].astype(jnp.float32)).astype(jnp.bfloat16)
    active_ref[...] = active
    grad_ref[...] = grad
    more_value = jnp.dot(active, second_ref[...], preferred_element_type=jnp.float32)
    more_sent = transposed_dot(grad, first)

    @pl.when(step == 0)
    def begin():
        value[...] = more_value
        sent[...] = more_sent

    @pl.when(step > 0)
    def go_on():
        value[...] += more_value
        sent[...] += more_sent

    @pl.when(step == last)
    def finish():
        low = value[...].astype(jnp.bfloat16)
        value_ref[...] = low
        sent_ref[:, :width] = sent[...].astype(jnp.bfloat16)
        along = jnp.sum(low.astype(jnp.float32) * up_ref[...].astype(jnp.float32), axis=1, keepdims=True)
        place = lax.broadcasted_iota(jnp.int32, (sent_ref.shape[0], LANES), 1)
        tail = jnp.zeros(place.shape, jnp.float32)
        for k, part in enumerate(three_parts(along)):
            tail = jnp.where(place == k, part.astype(jnp.float32), tail)
        sent_ref[:, width:] = tail.astype(jnp.bfloat16)


def expert_layer(received, upstream, pull, first, second):
    rows, width = upstream.shape
    hidden = second.shape[0]
    wide = received.shape[1]

    def fixed(cols):
        return pl.BlockSpec((rows, cols), lambda i: (0, 0))

    chunk = pl.BlockSpec((rows, CHUNK), lambda i: (0, i))
    return pl.pallas_call(
        expert_kernel,
        grid=(hidden // CHUNK,),
        out_shape=(
            shaped(rows, hidden, dtype=jnp.bfloat16),
            shaped(rows, hidden, dtype=jnp.bfloat16),
            shaped(rows, width, dtype=jnp.bfloat16),
            shaped(rows, wide, dtype=jnp.bfloat16),
        ),
        in_specs=[
            fixed(wide),
            fixed(width),
            chunk,
            pl.BlockSpec((width, CHUNK), lambda i: (0, i)),
            pl.BlockSpec((CHUNK, width), lambda i: (i, 0)),
        ],
        out_specs=(chunk, chunk, fixed(width), fixed(wide)),
        scratch_shapes=[pltpu.VMEM((rows, width), jnp.float32)] * 2,
        compiler_params=roomy(60),
        cost_estimate=pl.CostEstimate(flops=6 * rows * hidden * width, bytes_accessed=4 * hidden * (width + rows), transcendentals=rows * hidden),
        name="expert_layer",
    )(received, upstream, pull, first, second)


def expert_sums_kernel(hidden_ref, received_ref, active_ref, up_ref, out_ref, scaled_received, scaled_up):
    pair = out_ref.shape[0]
    half = out_ref.shape[2]
    width = up_ref.shape[1]

    @pl.when(pl.program_id(0) == 0)
    def scale():
        parts = received_ref[:, width:].astype(jnp.float32)
        gate = parts[:, 0:1] + parts[:, 1:2] + parts[:, 2:3]
        scaled_received[...] = (received_ref[:, :width].astype(jnp.float32) * gate).astype(jnp.bfloat16)
        scaled_up[...] = (up_ref[...].astype(jnp.float32) * gate).astype(jnp.bfloat16)

    for which, (left_ref, right_ref) in enumerate(((hidden_ref, scaled_received), (active_ref, scaled_up))):
        total = column_dot(left_ref[...], right_ref[...]).astype(jnp.bfloat16)
        for i in range(pair):
            out_ref[i, which] = total[i * half : (i + 1) * half]


def expert_sums(grad_hidden, received, activated, upstream, owners):
    rows, hidden = grad_hidden.shape
    width = upstream.shape[1]
    pair = 2
    chunk = pl.BlockSpec((rows, pair * hidden // owners), lambda i: (0, i))

    def fixed(cols):
        return pl.BlockSpec((rows, cols), lambda i: (0, 0))

    return pl.pallas_call(
        expert_sums_kernel,
        grid=(owners // pair,),
        out_shape=shaped(owners, 2, hidden // owners, width, dtype=jnp.bfloat16),
        in_specs=[chunk, fixed(received.shape[1]), chunk, fixed(width)],
        out_specs=pl.BlockSpec((pair, 2, hidden // owners, width), lambda i: (i, 0, 0, 0)),
        scratch_shapes=[pltpu.VMEM((rows, width), jnp.bfloat16)] * 2,
        compiler_params=roomy(60),
        cost_estimate=pl.CostEstimate(flops=4 * rows * hidden * width, bytes_accessed=4 * hidden * (width + rows), transcendentals=0),
        name="expert_sums",
    )(grad_hidden, received, activated, upstream)


BAND = 384


def conv_back_kernel(
    taps, gsel_ref, sel_ref, low_ref, gconv_ref, mixer_ref, conv_ref, pre_ref, padded_ref, weight_ref, skip_ref, glog_ref, gbias_ref,
    gpre_ref, left_ref, right_ref, rows_ref,
):
    rows = gconv_ref.shape[0]
    states = glog_ref.shape[0]
    gsel = gsel_ref[...]
    rank = SELECTED - 2 * states
    place = lax.broadcasted_iota(jnp.int32, sel_ref.shape, 1)
    step_low = jnp.where(place < rank, sel_ref[...], 0.0).astype(jnp.bfloat16)
    tall = lax.broadcasted_iota(jnp.int32, (rows_ref.shape[0], LANES), 0)
    wide = lax.broadcasted_iota(jnp.int32, (rows_ref.shape[0], LANES), 1)
    spots = jnp.where(wide == tall + SELECTED, 1.0, 0.0).astype(jnp.bfloat16)
    rows_ref[...] = jnp.zeros_like(rows_ref)
    rows_ref[:states, :] = glog_ref[...]
    for b in range(BAND // LANES):
        lanes = pl.ds(b * LANES, LANES)
        mixer = mixer_ref[:, lanes]
        conv = conv_ref[:, lanes]
        pre = pre_ref[:, lanes]
        grad = transposed_dot(gsel, weight_ref[pl.ds(b * LANES, LANES), :]) + gconv_ref[:, lanes] + skip_ref[:, lanes] * mixer
        grad = grad * silu_slope(pre)
        gpre_ref[:, lanes] = grad
        for k in range(taps):
            rows_ref[states + k : states + k + 1, lanes] = jnp.sum(grad * padded_ref[k * SEGS : k * SEGS + rows, lanes], axis=0, keepdims=True)
        rows_ref[states + taps : states + taps + 1, lanes] = jnp.sum(grad, axis=0, keepdims=True)
        rows_ref[states + taps + 1 : states + taps + 2, lanes] = gbias_ref[:, lanes]
        rows_ref[states + taps + 2 : states + taps + 3, lanes] = jnp.sum(mixer * conv, axis=0, keepdims=True)
        total = column_dot(conv.astype(jnp.bfloat16), gsel)
        for part in three_parts(rows_ref[:, lanes]):
            total = total + column_dot(part, spots)
        left_ref[pl.ds(b * LANES, LANES), :] = total
        right_ref[pl.ds(b * LANES, LANES), :] = column_dot(low_ref[:, lanes], step_low)


def conv_back(gsel, selection, low, grad_conv, grad_mixer, conv, preact, padded, weight, skip, grad_log, grad_bias, taps):
    rows, width = grad_conv.shape

    def band(height):
        return pl.BlockSpec((height, BAND), lambda i: (0, i))

    whole = pl.BlockSpec((rows, LANES), lambda i: (0, 0))
    down = pl.BlockSpec((BAND, LANES), lambda i: (i, 0))
    return pl.pallas_call(
        functools.partial(conv_back_kernel, taps),
        grid=(width // BAND,),
        out_shape=(shaped(rows, width), shaped(width, LANES), shaped(width, LANES)),
        in_specs=[whole, whole]
        + [band(rows)] * 5
        + [band(padded.shape[0]), down, band(1), band(grad_log.shape[0]), band(1)],
        out_specs=(band(rows), down, down),
        scratch_shapes=[pltpu.VMEM((24, BAND), jnp.float32)],
        compiler_params=roomy(60),
        name="conv_back",
    )(gsel, selection, low, grad_conv, grad_mixer, conv, preact, padded, weight, skip, grad_log, grad_bias)


def token_back_kernel(taps, gpre_ref, next_ref, tap_ref, gate_ref, weight_ref, stream_ref, gain_ref, middle_ref, gconv_ref, token_ref, ggain_ref, total):
    step, last = pl.program_id(0), pl.num_programs(0) - 1
    half = pl.num_programs(0) // 2
    rows = gpre_ref.shape[0]

    def more(piece):
        summed = transposed_dot(piece, weight_ref[...])

        @pl.when(step == 0)
        def begin():
            total[...] = summed

        @pl.when(step > 0)
        def go_on():
            total[...] += summed

    @pl.when(step < half)
    def conv_part():
        place = lax.broadcasted_iota(jnp.int32, (SEGS, CUT), 0)
        grown = None
        for k in range(taps):
            late = taps - 1 - k
            shifted = gpre_ref[late * SEGS :, :]
            if late:
                wrapped = [
                    jnp.where(place == SEGS - 1, next_ref[j : j + 1, :], pltpu.roll(gpre_ref[j * SEGS : (j + 1) * SEGS, :], SEGS - 1, 0))
                    for j in range(late)
                ]
                shifted = jnp.concatenate([shifted] + wrapped, axis=0)
            term = tap_ref[k : k + 1, :] * shifted
            grown = term if grown is None else grown + term
        piece = grown.astype(jnp.bfloat16)
        gconv_ref[...] = piece
        more(piece)

    @pl.when(step >= half)
    def gate_part():
        more(gate_ref[...])

    @pl.when(step == last)
    def finish():
        stream = stream_ref[...].astype(jnp.float32)
        scale = rms_scale(stream)
        back, gain = rms_back(stream, scale, gain_ref[...], total[...])
        token_ref[...] = middle_ref[...] + back
        ggain_ref[...] = gain[None, :]


def token_back(grad_preact, following, taps, grad_gate, in_weight, stream, gain, grad_middle):
    rows, width = grad_preact.shape
    model = stream.shape[1]
    half = width // CUT

    def early(height):
        return pl.BlockSpec((height, CUT), lambda i: (0, jnp.minimum(i, half - 1)))

    fixed = pl.BlockSpec((rows, model), lambda i: (0, 0))
    row = pl.BlockSpec((1, model), lambda i: (0, 0))
    return pl.pallas_call(
        functools.partial(token_back_kernel, taps.shape[0]),
        grid=(2 * half,),
        out_shape=(shaped(rows, width, dtype=jnp.bfloat16), shaped(rows, model), shaped(1, model)),
        in_specs=[
            early(rows),
            early(following.shape[0]),
            early(taps.shape[0]),
            pl.BlockSpec((rows, CUT), lambda i: (0, jnp.maximum(i - half, 0))),
            pl.BlockSpec((model, CUT), lambda i: (0, i)),
            fixed,
            row,
            fixed,
        ],
        out_specs=(early(rows), fixed, row),
        scratch_shapes=[pltpu.VMEM((rows, model), jnp.float32)],
        compiler_params=roomy(60),
        name="token_back",
    )(grad_preact, following, taps, grad_gate, in_weight, stream, gain[None, :], grad_middle)


ORDERS = ("xyz", "yzx", "zxy")
PIECE = 16


def shares_kernel(
    conv_cols, gate_cols, token_ref, out_cols, middle_ref, left_ref, right_ref, narrow_ref, sum_ref, in_ref, out_ref, made, taken,
    half_a, half_b, half_c, one_a, one_b, one_c, sends, arrivals):
    seq, expert = lax.axis_index("seq"), lax.axis_index("expert")
    core = lax.rem(expert, 2)
    place = {"y": lax.div(seq, 4), "z": lax.rem(seq, 4), "x": lax.div(expert, 2)}
    third = token_ref.shape[1] // len(ORDERS)
    streams = [(L, q) for L in range(len(ORDERS)) for q in range(4)]

    def flip(i):
        return i + 1 - 2 * lax.rem(i, 2)

    def device(**moved):
        at = dict(place, **moved)
        return {"seq": at["y"] * 4 + at["z"], "expert": at["x"] * 2 + at.get("core", core)}

    partners = [device(core=1 - core)]
    for axis in "xyz":
        partners += [device(**{axis: flip(place[axis])}), device(**{axis: 3 - place[axis]})]
    barrier = pltpu.get_barrier_semaphore()
    for partner in partners:
        pl.semaphore_signal(barrier, inc=1, device_id=partner, device_id_type=pl.DeviceIdType.MESH)
    pl.semaphore_wait(barrier, len(partners))

    def send(source, target, partner, stream, number):
        k = streams.index(stream)
        copy = pltpu.make_async_remote_copy(
            src_ref=source, dst_ref=target, send_sem=sends.at[k, number], recv_sem=arrivals.at[k, number],
            device_id=partner, device_id_type=pl.DeviceIdType.MESH,
        )
        copy.start()
        return copy

    def add(target, source, unit):
        def step(i, unused):
            target[i] = target[i] + source[i]
            return unused

        lax.fori_loop(0, unit, step, 0, unroll=min(unit, 8))

    inner = out_cols.shape[1]
    for source, target, base in ((conv_cols, in_ref, 0), (gate_cols, in_ref, inner), (out_cols, out_ref, 0)):

        def turn_over(k, unused, source=source, target=target, base=base):
            spot = pl.ds(pl.multiple_of(k * LANES, LANES), LANES)
            target[pl.ds(pl.multiple_of(base + k * LANES, LANES), LANES), :] = source[:, spot].T
            return unused

        lax.fori_loop(0, source.shape[1] // LANES, turn_over, 0)

    pending = {}
    for L, order in enumerate(ORDERS):
        lanes = pl.ds(L * third, third)
        narrow = narrow_ref[:, lanes].astype(jnp.bfloat16)

        def block(s, unused):
            y, z = lax.div(s, 4), lax.rem(s, 4)
            by_in = jnp.dot(
                in_ref[pl.ds(pl.multiple_of(s * 288, 16), 288), :], token_ref[:, lanes], preferred_element_type=jnp.float32
            ).astype(jnp.bfloat16)
            here = pl.ds(pl.multiple_of(s * 144, 16), 144)
            by_out = jnp.dot(out_ref[here, :], middle_ref[:, lanes], preferred_element_type=jnp.float32)
            left, right = left_ref[here, :], right_ref[here, :]
            for x in range(4):
                at = {"x": x, "y": y, "z": z}
                slot = (at[order[0]] * 4 + at[order[1]]) * 4 + at[order[2]]
                rows = by_in[72 * x : 72 * x + 72]
                more = by_out[36 * x : 36 * x + 36].astype(jnp.bfloat16)
                for q in range(4):
                    made[L, q, slot] = rows[16 * q : 16 * q + 16]
                made[L, 4, slot, 0:8] = rows[64:]
                made[L, 4, slot, 8:16] = more[:8]
                made[L, 5, slot] = more[8:24]
                made[L, 6, slot, 0:12] = more[24:]
                made[L, 6, slot, 12:16] = narrow[8:12]
                made[L, 7, slot, 8:16] = narrow[0:8]
                last = jnp.concatenate([left[36 * x : 36 * x + 36], right[36 * x : 36 * x + 36]], axis=0)
                for part in range(third // LANES):
                    k = 8 * (L * (third // LANES) + part)
                    made[L, 7, slot, 0:8, part * LANES : (part + 1) * LANES] = last[k : k + 8].astype(jnp.bfloat16)
            return unused

        lax.fori_loop(0, 16, block, 0, unroll=2)
        for q in range(4):
            pending[L, q] = [
                send(made.at[L, 4 * (1 - core) + q], taken.at[L, q], device(core=1 - core), (L, q), 0)
            ]

    halves, ones = (half_a, half_b, half_c), (one_a, one_b, one_c)
    holding = {}
    for L, q in streams:
        for copy in pending[L, q]:
            copy.wait()
        add(taken.at[L, q], made.at[L, 4 * core + q], 64)
        holding[L, q] = taken.at[L, q]
        pending[L, q] = start_halves(L, q, 0, holding[L, q], halves, place, flip, device, send)
    for turn in range(3):
        unit = 16 >> (2 * turn)
        for L, q in streams:
            axis = ORDERS[L][turn]
            i = place[axis]
            for copy in pending[L, q]:
                copy.wait()
            other = 3 - i if q < 2 else flip(i)
            got = halves[turn].at[L, q]
            add(got.at[0], holding[L, q].at[pl.ds(i * unit, unit)], unit)
            add(got.at[1], holding[L, q].at[pl.ds(other * unit, unit)], unit)
            partner = device(**{axis: other})
            pending[L, q] = [send(got.at[1], ones[turn].at[L, q], partner, (L, q), 3 + 3 * turn)]
        for L, q in streams:
            for copy in pending[L, q]:
                copy.wait()
            got = ones[turn].at[L, q]
            if turn < 2:
                add(got, halves[turn].at[L, q, 0], unit)
                holding[L, q] = got
                pending[L, q] = start_halves(L, q, turn + 1, got, halves, place, flip, device, send)
            else:
                whole = got[0].astype(jnp.float32) + halves[turn][L, q, 0, 0].astype(jnp.float32)
                sum_ref[4 * core + q, :, L * third : (L + 1) * third] = whole
    here = sum_ref.at[pl.ds(4 * core, 4)]
    send(here, here, device(core=1 - core), (0, 0), 10).wait()


def start_halves(L, q, turn, source, halves, place, flip, device, send):
    axis = ORDERS[L][turn]
    unit = 16 >> (2 * turn)
    i = place[axis]
    partner = flip(i) if q < 2 else 3 - i
    second = 3 - partner if q < 2 else flip(partner)
    target = halves[turn].at[L, q]
    return [
        send(source.at[pl.ds(partner * unit, unit)], target.at[0], device(**{axis: partner}), (L, q), 1 + 3 * turn),
        send(source.at[pl.ds(second * unit, unit)], target.at[1], device(**{axis: partner}), (L, q), 2 + 3 * turn),
    ]


def shares(conv_cols, gate_cols, tokens, out_cols, middle, left, right, narrow):
    width = tokens.shape[1]
    rows, inner = out_cols.shape
    third = width // len(ORDERS)

    def slots(*lead):
        return pltpu.VMEM((len(ORDERS),) + lead + (PIECE, third), jnp.bfloat16)

    return pl.pallas_call(
        shares_kernel,
        out_shape=shaped(8, PIECE, width),
        in_specs=[WHOLE] * 8,
        out_specs=WHOLE,
        scratch_shapes=[pltpu.VMEM((2 * inner, rows), jnp.bfloat16), pltpu.VMEM((inner, rows), jnp.bfloat16)]
        + [slots(8, 64), slots(4, 64)]
        + [slots(4, 2, 16 >> (2 * turn)) for turn in range(3)]
        + [slots(4, 16 >> (2 * turn)) for turn in range(3)]
        + [pltpu.SemaphoreType.DMA((12, 11))] * 2,
        compiler_params=roomy(60, collective_id=2, has_side_effects=True),
        name="shares",
    )(conv_cols, gate_cols, tokens, out_cols, middle, left, right, narrow)


def local(
    tokens,
    expert_index,
    cotangent,
    first_gain,
    in_weight,
    conv_weight,
    conv_bias,
    select_weight,
    step_weight,
    step_bias,
    decay_log,
    skip_gain,
    out_weight,
    second_gain,
    router_weight,
    expert_first,
    expert_second,
):
    bf16, f32 = jnp.bfloat16, jnp.float32
    stream = segmented(tokens[0])
    routes = segmented(expert_index[0])[:, 0]
    upstream = segmented(cotangent[0]).astype(f32)
    row_count, model_width = stream.shape
    seat_count = 2 * row_count
    inner = conv_bias.shape[0]
    rank = step_weight.shape[0]
    states = decay_log.shape[0]
    taps = conv_weight.shape[0]
    expert_count = router_weight.shape[1]
    capacity = 2 * row_count // expert_count
    seqs, experts = lax.axis_size("seq"), lax.axis_size("expert")
    reach = (taps - 1) * SEGS
    backward = [(i + 1, i) for i in range(seqs - 1)]

    picks = (routes[:, None] == jnp.arange(expert_count, dtype=jnp.int32)[None, :]).astype(bf16)
    earlier = jnp.arange(row_count)[:, None] > jnp.arange(row_count)[None, :]
    ahead = product(earlier.astype(bf16), picks)
    chosen = picks.astype(f32)
    slot_index = routes * capacity + jnp.sum(ahead * chosen, axis=1).astype(jnp.int32)
    seats = jnp.arange(expert_count * capacity, dtype=jnp.int32)
    placing = (seats[:, None] == slot_index[None, :]).astype(bf16)

    def seated(rows):
        return product(placing, rows).astype(bf16)

    def swapped(rows):
        parts = rows.reshape(expert_count, capacity, -1)
        parts = lax.all_to_all(parts, "expert", split_axis=0, concat_axis=0, tiled=True)
        return parts.reshape(expert_count * capacity, -1)

    def unseated(rows):
        return jnp.einsum("st,sd->td", placing, rows, preferred_element_type=f32)

    upstream_there = swapped(seated(segmented(cotangent[0])))

    select_wide = jnp.pad(select_weight, ((0, 0), (0, LANES - select_weight.shape[1])))
    step_wide = jnp.pad(step_weight, ((0, LANES - rank), (0, 0)))
    router_wide = jnp.pad(router_weight, ((0, 0), (0, LANES - expert_count)))
    blocks = inner // LANES // PARTS
    log_rows = decay_log.reshape(GRID, GRID, PARTS, blocks, LANES).transpose(2, 0, 1, 3, 4)
    log_rows = jnp.pad(log_rows, ((0, 0), (0, 0), (0, 0), (0, SEGS - blocks), (0, 0)))
    (
        normed_in, gate_input, padded, preact, conv_out, step_raw, step_size, selection, first, mixer_out, gated,
        middle, normed_mid, router_probs, gate_wide, leaving,
    ) = mixer(
        stream, first_gain[None, :], in_weight, conv_weight, conv_bias[None, :], select_wide, step_wide, step_bias[None, :], decay_log,
        log_rows, skip_gain[None, :], out_weight, second_gain[None, :], router_wide, slot_index[None, :], routes[:, None], seat_count,
    )
    router_probs = router_probs[:, :expert_count]
    gate_value = gate_wide[:, 0]
    second_scale = rms_scale(middle)
    leaving, upstream_there = lax.optimization_barrier((leaving, upstream_there))
    received = swapped(leaving)
    pull = expert_pull(upstream_there, expert_second[0])
    activated, grad_hidden, value_there, grad_there = expert_layer(
        received, upstream_there, pull, expert_first[0], expert_second[0]
    )
    grad_home = unseated(swapped(grad_there))
    expert_grads = expert_sums(grad_hidden, received, activated, upstream_there, seqs)
    expert_grads, value_there = lax.optimization_barrier((expert_grads, value_there))
    value_home = swapped(value_there)

    grad_gate = jnp.sum(grad_home[:, model_width:], axis=1)
    grad_logits = (grad_gate[:, None] * gate_value[:, None] * (chosen - router_probs)).astype(bf16)
    grad_router = summed_rows(grad_logits, normed_mid)
    grad_mid = across(grad_logits, router_weight) + gate_value[:, None] * grad_home[:, :model_width]
    grad_middle_norm, grad_second_gain = rms_back(middle, second_scale, second_gain, grad_mid)
    grad_middle = upstream + grad_middle_norm
    middle_low = grad_middle.astype(bf16)
    grad_gated = across(middle_low, out_weight)
    grad_mixer = grad_gated * jax.nn.silu(gate_input)
    grad_gate_input = grad_gated * mixer_out * silu_slope(gate_input)

    expert_grads, grad_mixer = lax.optimization_barrier((expert_grads, grad_mixer))
    expert_share = lax.psum_scatter(
        expert_grads.reshape(-1, model_width), "seq", scatter_dimension=0, tiled=True
    ).reshape(2, -1, model_width)

    step_raw_low, grad_conv_scan, grad_selection, grad_decay_log, grad_step_bias = scan_backward(
        step_size, conv_out, grad_mixer, step_raw, selection, decay_log, log_rows, step_wide, first, rank
    )
    grad_selection, value_home = lax.optimization_barrier((grad_selection, value_home))
    mixed = middle + gate_value[:, None] * unseated(value_home)
    grad_preact, left, right = conv_back(
        grad_selection,
        selection,
        step_raw_low,
        grad_conv_scan,
        grad_mixer,
        conv_out,
        preact,
        padded,
        select_wide,
        skip_gain[None, :],
        grad_decay_log,
        grad_step_bias,
        taps,
    )
    heads = grad_preact[:reach].reshape(taps - 1, SEGS, inner)
    following = lax.ppermute(heads[:, 0], "seq", backward)
    grad_conv_input, grad_tokens, grad_first_gain = token_back(
        grad_preact, following, conv_weight, grad_gate_input.astype(bf16), in_weight, stream, first_gain, grad_middle
    )

    devices = seqs * experts
    each, fewer = inner // devices, model_width // devices
    narrow = jnp.concatenate([grad_first_gain, grad_second_gain[None, :], grad_router, jnp.zeros((6, model_width), f32)])
    grad_conv_input, expert_share = lax.optimization_barrier((grad_conv_input, expert_share))
    sums = shares(grad_conv_input, grad_gate_input.astype(bf16), normed_in, gated, middle_low, left, right, narrow)
    sums = sums.reshape(-1, model_width)
    core = lax.axis_index("expert") % 2
    in_share = lax.dynamic_slice_in_dim(sums, 2 * each * core, 2 * each)
    out_share = lax.dynamic_slice_in_dim(sums, 4 * each + each * core, each)
    small = sums[112:120].reshape(8, -1, LANES).transpose(1, 0, 2).reshape(2, 2 * each, LANES)
    small = lax.dynamic_slice_in_dim(small, each * core, each, axis=1)
    rows_sum = small[0, :, rank + 2 * states :]
    owner = lax.axis_index("seq") * experts + lax.axis_index("expert")
    narrow_sum = jnp.concatenate([sums[120:128], sums[108:110]])
    narrow_sum = lax.dynamic_slice_in_dim(narrow_sum, owner * fewer, fewer, axis=1)
    return (
        in_order(mixed.astype(bf16))[None],
        in_order(grad_tokens)[None],
        narrow_sum[0],
        in_share.T,
        rows_sum[:, states : states + taps].T,
        rows_sum[:, states + taps],
        small[0, :, : rank + 2 * states],
        small[1, :, :rank].T,
        rows_sum[:, states + taps + 1],
        rows_sum[:, :states].T,
        rows_sum[:, states + taps + 2],
        out_share,
        narrow_sum[1],
        narrow_sum[2:].T,
        expert_share[0].T.astype(f32)[None],
        expert_share[1].astype(f32)[None],
    )


def solution(mesh):
    return jax.shard_map(
        local,
        mesh=mesh,
        in_specs=(
            P("expert", "seq", None),
            P("expert", "seq", None),
            P("expert", "seq", None),
            P(),
            P(),
            P(),
            P(),
            P(),
            P(),
            P(),
            P(),
            P(),
            P(),
            P(),
            P(),
            P("expert", None, None),
            P("expert", None, None),
        ),
        out_specs=(
            P("expert", "seq", None),
            P("expert", "seq", None),
            P(("seq", "expert")),
            P(None, ("seq", "expert")),
            P(None, ("seq", "expert")),
            P(("seq", "expert")),
            P(("seq", "expert"), None),
            P(None, ("seq", "expert")),
            P(("seq", "expert")),
            P(None, ("seq", "expert")),
            P(("seq", "expert")),
            P(("seq", "expert"), None),
            P(("seq", "expert")),
            P(("seq", "expert"), None),
            P("expert", None, "seq"),
            P("expert", "seq", None),
        ),
        check_vma=False,
    )
```

```python
import functools
import math

import jax
import jax.numpy as jnp
from jax import lax
from jax.experimental import pallas as pl
from jax.experimental.pallas import tpu as pltpu
from jax.sharding import PartitionSpec as P

LANES = 128
SEGS = 8
LOG2E = math.log2(math.e)
PARTS = 3
SELECTED = 104
EXPERTS = 8
CAPACITY = 64
CUT = 768
GRID = 4


def spread_ones(states):
    row = lax.broadcasted_iota(jnp.int32, (LANES, states * LANES), 0)
    lane = lax.broadcasted_iota(jnp.int32, (LANES, states * LANES), 1)
    return row, lane // LANES


def fill_maps(sel_ref, wide_ref, column):
    steps, states = wide_ref.shape[:2]
    row, block = spread_ones(states)
    ones = jnp.where(row == block + column, 1.0, 0.0).astype(jnp.bfloat16)
    left, total = sel_ref[...], None
    for unused in range(3):
        part = left.astype(jnp.bfloat16)
        left = left - part.astype(jnp.float32)
        spread = jnp.dot(part, ones, preferred_element_type=jnp.float32)
        total = spread if total is None else total + spread
    for n in range(states):
        wide_ref[:, n] = total[:, n * LANES : (n + 1) * LANES].reshape(steps, SEGS, LANES)


def gather_maps(sum_ref, column):
    steps, states = sum_ref.shape[:2]
    row, block = spread_ones(states)
    ones = jnp.where(row == block + column, 1.0, 0.0).astype(jnp.bfloat16)
    left = jnp.concatenate([sum_ref[:, n].reshape(steps * SEGS, LANES) for n in range(states)], axis=1)
    total = None
    for unused in range(3):
        part = left.astype(jnp.bfloat16)
        left = left - part.astype(jnp.float32)
        summed = transposed_dot(part, ones)
        total = summed if total is None else total + summed
    return total


def lanes_of(block):
    return pl.ds(pl.multiple_of(block * LANES, LANES), LANES)


def rows_of(j):
    return pl.ds(pl.multiple_of(j * SEGS, SEGS), SEGS)


def rates_of(log_ref, lanes):
    states = log_ref.shape[0]
    rate = -LOG2E * jnp.exp(log_ref[:, lanes])
    return jnp.stack([jnp.broadcast_to(rate[n : n + 1], (SEGS, LANES)) for n in range(states)])


def neighbour(value, hop, later, fill):
    axis = value.ndim - 2
    place = lax.broadcasted_iota(jnp.int32, value.shape, axis)
    if later:
        return jnp.where(place < SEGS - hop, pltpu.roll(value, SEGS - hop, axis), fill)
    return jnp.where(place >= hop, pltpu.roll(value, hop, axis), fill)


def summarize(later, part, step_ref, other_ref, wide, log_ref, part_ref, span_ref, message):
    steps, states = wide.shape[:2]
    blocks = step_ref.shape[1] // LANES // PARTS

    def block(i, unused):
        lanes = lanes_of(part * blocks + i)
        rate = rates_of(log_ref, lanes)

        def advance(turn, carry):
            span, memory = carry
            j = steps - 1 - turn if later else turn
            step = step_ref[rows_of(j), lanes]
            other = other_ref[rows_of(j), lanes]
            decay = jnp.exp2(step * rate)
            if later:
                memory = decay * (memory + wide[j] * other)
            else:
                memory = decay * memory + wide[j] * (step * other)
            return span + step, memory

        zero = jnp.zeros((SEGS, LANES), jnp.float32)
        span, memory = lax.fori_loop(0, steps, advance, (zero, jnp.zeros(rate.shape, jnp.float32)), unroll=8)
        hop = 1
        while hop < SEGS:
            memory = memory + jnp.exp2(rate * span) * neighbour(memory, hop, later, 0.0)
            span = span + neighbour(span, hop, later, 0.0)
            hop *= 2
        span_ref[:, lanes] = span
        part_ref[:, :, lanes] = memory
        end = 0 if later else SEGS - 1
        for n in range(states):
            message[n // GRID, n % GRID, pl.ds(i, 1), :] = memory[n, end : end + 1]
        for q in range(GRID):
            message[q, GRID, pl.ds(i, 1), :] = span[end : end + 1]
        return unused

    lax.fori_loop(0, blocks, block, 0)


def entering(later, part_ref, span_ref, rate, lanes, carried):
    ends = part_ref[:, :, lanes] + jnp.exp2(rate * span_ref[:, lanes]) * carried
    return neighbour(ends, 1, later, carried)


def carried_at(in_ref, part, i):
    states = GRID * GRID
    return jnp.stack(
        [jnp.broadcast_to(in_ref[n // GRID, n % GRID, pl.ds(i, 1), :], (SEGS, LANES)) for n in range(states)]
    )


def scan_part(part, step_ref, conv_ref, wide_in, wide_out, log_ref, part_ref, span_ref, in_ref, y_ref, entry_ref):
    steps = wide_in.shape[0]
    blocks = step_ref.shape[1] // LANES // PARTS

    def block(i, unused):
        lanes = lanes_of(part * blocks + i)
        rate = rates_of(log_ref, lanes)
        first = entering(False, part_ref, span_ref, rate, lanes, carried_at(in_ref, part, i))
        entry_ref[:, :, lanes] = first

        def advance(j, memory):
            step = step_ref[rows_of(j), lanes]
            memory = jnp.exp2(step * rate) * memory + wide_in[j] * (step * conv_ref[rows_of(j), lanes])
            y_ref[rows_of(j), lanes] = jnp.sum(wide_out[j] * memory, axis=0)
            return memory

        lax.fori_loop(0, steps, advance, first, unroll=8)
        return unused

    lax.fori_loop(0, blocks, block, 0)


def retreat_part(
    part, step_ref, conv_ref, grad_ref, raw_ref, wide_in, wide_out, log_ref, pull_ref, entry_ref, part_ref, span_ref, in_ref,
    low_ref, gconv_ref, glog_ref, gbias_ref, sum_in, sum_out, states_ref, decays_ref, raw_sum, raw_rows,
):
    steps = wide_in.shape[0]
    blocks = step_ref.shape[1] // LANES // PARTS

    def block(i, unused):
        lanes = lanes_of(part * blocks + i)
        rate = rates_of(log_ref, lanes)

        def advance(j, memory):
            step = step_ref[rows_of(j), lanes]
            decay = jnp.exp2(step * rate)
            memory = decay * memory + wide_in[j] * (step * conv_ref[rows_of(j), lanes])
            decays_ref[j] = decay
            states_ref[j + 1] = memory
            return memory

        first = entry_ref[:, :, lanes]
        states_ref[0] = first
        lax.fori_loop(0, steps, advance, first, unroll=8)

        def retreat(turn, carry):
            j = steps - 1 - turn
            mu, slow = carry
            step = step_ref[rows_of(j), lanes]
            conv = conv_ref[rows_of(j), lanes]
            grad = grad_ref[rows_of(j), lanes]
            lam = wide_out[j] * grad + mu
            sum_out[j] += grad * states_ref[j + 1]
            sum_in[j] += lam * (step * conv)
            by_in = jnp.sum(lam * wide_in[j], axis=0)
            mu = lam * decays_ref[j]
            kept = mu * states_ref[j]
            by_rate = jnp.sum(kept * rate, axis=0)
            grad_step = by_in * conv + (1.0 / LOG2E) * by_rate
            raw_rows[rows_of(j), :] = grad_step * jax.nn.sigmoid(raw_ref[rows_of(j), lanes])
            gconv_ref[rows_of(j), lanes] = by_in * step
            return mu, slow + kept * step

        last = entering(True, part_ref, span_ref, rate, lanes, carried_at(in_ref, part, i))
        unused_mu, slow = lax.fori_loop(0, steps, retreat, (last, jnp.zeros(rate.shape, jnp.float32)), unroll=4)
        glog_ref[:, lanes] = (1.0 / LOG2E) * jnp.sum(slow * rate, axis=1)
        raw_steps = raw_rows[...]
        gbias_ref[:, lanes] = jnp.sum(raw_steps, axis=0, keepdims=True)
        low = raw_steps.astype(jnp.bfloat16)
        low_ref[:, lanes] = low
        raw_sum[:, : pull_ref.shape[0]] += transposed_dot(low, pull_ref[:, lanes])
        return unused

    lax.fori_loop(0, blocks, block, 0)


class Relay:
    def __init__(self, later, log_ref, log_rows, in_ref, message, got, row, rows_got, above, made, sends, arrivals, chained=False):
        self.later, self.log_rows, self.message, self.got = later, log_rows, message, got
        self.row, self.rows_got, self.above, self.made, self.in_ref = row, rows_got, above, made, in_ref
        self.sends, self.arrivals = sends, arrivals
        seq = lax.axis_index("seq")
        self.y, self.z = lax.div(seq, GRID), lax.rem(seq, GRID)
        blocks = log_ref.shape[1] // LANES // PARTS
        log_rows[...] = jnp.zeros_like(log_rows)
        for part in range(PARTS):
            for b in range(blocks):
                lanes = pl.ds((part * blocks + b) * LANES, LANES)
                for n in range(GRID * GRID):
                    log_rows[part, n // GRID, n % GRID, b : b + 1, :] = log_ref[n : n + 1, lanes]
        self.flying = {}
        barrier = pltpu.get_barrier_semaphore()
        peers = [self.across(k) for k in range(1, GRID)] + [self.along(k) for k in range(1, GRID)]
        if chained:
            peers += [self.onward(1), self.onward(-1)]
        for peer in peers:
            pl.semaphore_signal(barrier, inc=1, device_id=peer, device_id_type=pl.DeviceIdType.MESH)
        self.peers = len(peers)

    def onward(self, k):
        size = GRID * GRID
        return {"seq": lax.rem(self.y * GRID + self.z + k + size, size)}

    def across(self, k):
        return {"seq": self.y * GRID + lax.rem(self.z + k, GRID)}

    def along(self, k):
        return {"seq": lax.rem(self.y + k, GRID) * GRID + self.z}

    def meet(self):
        pl.semaphore_wait(pltpu.get_barrier_semaphore(), self.peers)

    def send(self, part, phase, k, source, target, peer):
        copy = pltpu.make_async_remote_copy(
            src_ref=source, dst_ref=target, send_sem=self.sends.at[part, phase, k], recv_sem=self.arrivals.at[part, phase, k],
            device_id=peer, device_id_type=pl.DeviceIdType.MESH,
        )
        copy.start()
        self.flying.setdefault((part, phase), []).append(copy)

    def land(self, part, phase):
        for copy in self.flying[part, phase]:
            copy.wait()

    def order(self):
        return range(GRID - 1, -1, -1) if self.later else range(GRID)

    def rate(self, part):
        return -LOG2E * jnp.exp(self.log_rows[part, self.z])

    def first(self, part):
        for k in range(1, GRID):
            peer = lax.rem(self.z + k, GRID)
            self.send(part, 0, k, self.message.at[part, peer], self.got.at[part, k], self.across(k))
        self.got[part, 0] = self.message[part, self.z]

    def second(self, part):
        self.land(part, 0)
        rate = self.rate(part)
        state, span = jnp.zeros(rate.shape, jnp.float32), jnp.zeros(rate.shape[1:], jnp.float32)
        for z in self.order():
            block = self.got[part, lax.rem(self.z - z + GRID, GRID)]
            state = jnp.exp2(rate * block[GRID]) * state + block[:GRID]
            span = span + block[GRID]
        self.row[part, :GRID] = state
        self.row[part, GRID] = span
        for k in range(1, GRID):
            self.send(part, 1, k, self.row.at[part], self.rows_got.at[part, k], self.along(k))
        self.rows_got[part, 0] = self.row[part]

    def third(self, part):
        self.land(part, 1)
        rate = self.rate(part)
        state = jnp.zeros(rate.shape, jnp.float32)
        for y in self.order():
            self.above[part, y] = state
            block = self.rows_got[part, lax.rem(self.y - y + GRID, GRID)]
            state = jnp.exp2(rate * block[GRID]) * state + block[:GRID]
        state = self.above[part, self.y]
        for z in self.order():
            self.made[part, z] = state
            block = self.got[part, lax.rem(self.z - z + GRID, GRID)]
            state = jnp.exp2(rate * block[GRID]) * state + block[:GRID]
        for k in range(1, GRID):
            peer = lax.rem(self.z + k, GRID)
            self.send(part, 2, k, self.made.at[part, peer], self.in_ref.at[part, self.z], self.across(k))
        self.in_ref[part, self.z] = self.made[part, self.z]

    def done(self, part):
        self.land(part, 2)


def staged(relay, summary, extra, scan):
    summary(0)
    relay.first(0)
    summary(1)
    relay.first(1)
    relay.second(0)
    summary(2)
    relay.first(2)
    relay.third(0)
    relay.second(1)
    extra()
    relay.second(2)
    relay.third(1)
    relay.done(0)
    scan(0)
    relay.third(2)
    relay.done(1)
    scan(1)
    relay.done(2)
    scan(2)


def named_experts(slot_ref, rows):
    slot = slot_ref[...]
    first = lax.broadcasted_iota(jnp.int32, (rows, EXPERTS), 1) * CAPACITY
    return jnp.where((slot >= first) & (slot < first + CAPACITY), 1.0, 0.0)


def seated_rows(slot_ref, rows, seats):
    return jnp.where(lax.broadcasted_iota(jnp.int32, (rows, seats), 1) == slot_ref[...], 1.0, 0.0).astype(jnp.bfloat16)


def mixer_kernel(
    token_ref, row_ref, in_hbm, tap_ref, select_ref, step_weight_ref, log_ref, out_hbm, router_ref, slot_ref,
    normed_out, gate_out, padded_out, pre_out, conv_out, raw_out, step_out, sel_out, entry_out, mixer_out, gated_out,
    middle_out, normed_mid_out, probs_out, chosen_out, leaving_out,
    normed, in_ref, out_ref, padded, gate, pre, conv, raw, step, sel, entry, mixer, gated, middle, normed_mid, probs, chosen, leaving,
    tail, tail_got, part_ref, span_ref, wide_in, wide_out, loads, saves, passing, log_rows, relay_in, *relayed
):
    rows, width = step.shape
    model = token_ref.shape[1]
    tap_bias_ref, step_bias_ref, skip_ref = (row_ref.at[k : k + 1] for k in range(3))
    gain_ref, second_gain_ref = row_ref.at[3:4, :model], row_ref.at[3:4, model:]
    taps, states = tap_ref.shape[0], log_ref.shape[0]
    reach = (taps - 1) * SEGS
    rank = SELECTED - 2 * states
    pieces = in_ref.shape[0]
    cut = in_ref.shape[2]
    blocks = width // LANES

    loading = [pltpu.make_async_copy(in_hbm.at[:, pl.ds(k * cut, cut)], in_ref.at[k], loads.at[k]) for k in range(pieces)]
    loading.append(pltpu.make_async_copy(out_hbm, out_ref, loads.at[pieces]))
    for copy in loading:
        copy.start()
    saving = []

    def save(source, target):
        copy = pltpu.make_async_copy(source, target, saves.at[len(saving)])
        copy.start()
        saving.append(copy)

    relay = Relay(False, log_ref, log_rows, relay_in, *relayed, chained=True)

    stream = token_ref[...].astype(jnp.float32)
    normed[...] = (stream * rms_scale(stream) * gain_ref[...]).astype(jnp.bfloat16)
    save(normed, normed_out)
    for k in range(pieces // 2):
        loading[k].wait()
        padded[reach:, k * cut : (k + 1) * cut] = jnp.dot(normed[...], in_ref[k], preferred_element_type=jnp.float32)
    tail[...] = jnp.zeros_like(tail)
    for k in range(taps - 1):
        row = reach + rows - (taps - 1 - k) * SEGS + SEGS - 1
        tail[k : k + 1, :] = padded[row : row + 1, :]
    relay.meet()
    handing = pltpu.make_async_remote_copy(
        src_ref=tail, dst_ref=tail_got, send_sem=passing.at[0], recv_sem=passing.at[1],
        device_id=relay.onward(1), device_id_type=pl.DeviceIdType.MESH,
    )
    handing.start()
    for k in range(pieces // 2, pieces):
        loading[k].wait()
        spot = slice((k - pieces // 2) * cut, (k - pieces // 2 + 1) * cut)
        gate[:, spot] = jnp.dot(normed[...], in_ref[k], preferred_element_type=jnp.float32)
    save(gate, gate_out)
    handing.wait()
    started = jnp.where(lax.axis_index("seq") > 0, 1.0, 0.0)
    for k in range(taps - 1):
        row = rows + k * SEGS
        segment = lax.broadcasted_iota(jnp.int32, (SEGS, width), 0)
        before = pltpu.roll(padded[row : row + SEGS, :], 1, 0)
        padded[k * SEGS : (k + 1) * SEGS, :] = jnp.where(segment == 0, started * tail_got[k : k + 1, :], before)
    save(padded, padded_out)

    sel[...] = jnp.zeros_like(sel)

    def convolve(b, unused):
        lanes = lanes_of(b)
        value = tap_bias_ref[:, lanes]
        for k in range(taps):
            value = value + tap_ref[k : k + 1, lanes] * padded[k * SEGS : k * SEGS + rows, lanes]
        pre[:, lanes] = value
        value = value * jax.nn.sigmoid(value)
        conv[:, lanes] = value
        sel[:, :SELECTED] += jnp.dot(value.astype(jnp.bfloat16), select_ref[lanes, :], preferred_element_type=jnp.float32)
        return unused

    lax.fori_loop(0, blocks, convolve, 0)
    save(pre, pre_out)
    save(conv, conv_out)
    save(sel, sel_out)
    step_low = sel[:, :rank].astype(jnp.bfloat16)

    def size(b, unused):
        lanes = lanes_of(b)
        value = jnp.dot(step_low, step_weight_ref[:, lanes], preferred_element_type=jnp.float32) + step_bias_ref[:, lanes]
        raw[:, lanes] = value
        step[:, lanes] = jnp.maximum(value, 0.0) + jnp.log1p(jnp.exp(-jnp.abs(value)))
        return unused

    lax.fori_loop(0, blocks, size, 0)
    save(raw, raw_out)
    save(step, step_out)
    fill_maps(sel, wide_in, rank)

    def summary(part):
        summarize(False, part, step, conv, wide_in, log_ref, part_ref, span_ref, relay.message.at[part])

    def scan(part):
        scan_part(part, step, conv, wide_in, wide_out, log_ref, part_ref, span_ref, relay_in.at[part], mixer, entry)

    staged(relay, summary, lambda: fill_maps(sel, wide_out, rank + states), scan)
    save(entry, entry_out)

    def blend(b, unused):
        lanes = lanes_of(b)
        value = mixer[:, lanes] + skip_ref[:, lanes] * conv[:, lanes]
        mixer[:, lanes] = value
        opening = gate[:, lanes]
        gated[:, lanes] = (value * (opening * jax.nn.sigmoid(opening))).astype(jnp.bfloat16)
        return unused

    lax.fori_loop(0, blocks, blend, 0)
    save(mixer, mixer_out)
    save(gated, gated_out)
    loading[pieces].wait()
    value = token_ref[...].astype(jnp.float32) + jnp.dot(gated[...], out_ref[...], preferred_element_type=jnp.float32)
    middle[...] = value
    save(middle, middle_out)
    normed_mid[...] = (value * rms_scale(value) * second_gain_ref[...]).astype(jnp.bfloat16)
    save(normed_mid, normed_mid_out)
    logits = jnp.dot(normed_mid[...], router_ref[...], preferred_element_type=jnp.float32)
    grown = jnp.exp(logits - jnp.max(logits, axis=1, keepdims=True))
    probs[...] = grown / jnp.sum(grown, axis=1, keepdims=True)
    save(probs, probs_out)
    gate_value = jnp.sum(named_experts(slot_ref, rows) * probs[...], axis=1, keepdims=True)
    chosen[...] = jnp.broadcast_to(gate_value, (rows, LANES))
    save(chosen, chosen_out)
    place = lax.broadcasted_iota(jnp.int32, (rows, LANES), 1)
    parts = jnp.zeros((rows, LANES), jnp.float32)
    for k, piece in enumerate(three_parts(gate_value)):
        parts = jnp.where(place == k, piece.astype(jnp.float32), parts)
    seating = seated_rows(slot_ref, rows, leaving.shape[0])
    leaving[:, :model] = column_dot(seating, normed_mid[...]).astype(jnp.bfloat16)
    leaving[:, model:] = column_dot(seating, parts.astype(jnp.bfloat16)).astype(jnp.bfloat16)
    save(leaving, leaving_out)
    for copy in saving:
        copy.wait()


def mixer_back_kernel(
    back_hbm, slot_ref, probs_ref, chosen_ref, normed_ref, router_ref, middle_ref, up_ref, out_hbm, gate_hbm,
    mixer_hbm, conv_hbm, step_hbm, raw_hbm, sel_ref, pre_hbm, padded_hbm, entry_hbm, log_ref, step_weight_ref, select_ref,
    tap_ref, packed_ref, in_hbm, token_ref,
    low_out, gate_out, conv_out, left_out, right_out, narrow_out, token_out,
    back, out_ref, gate, mixer, conv, step, raw, padded, entry, in_ref,
    middle_low, grad_gate, grad_conv, left, right, narrow, grad_middle, mixed, low, gsel, glog, gbias, total, tail, tail_got, row_ref,
    part_ref, span_ref, wide_in, wide_out, sum_in, sum_out, states_ref, decays_ref, raw_sum, raw_rows,
    loads, saves, passing, log_rows, relay_in, *relayed
):
    rows, width = step.shape
    model = up_ref.shape[1]
    skip_ref, gain_ref, second_gain_ref = packed_ref.at[2:3], packed_ref.at[3:4, :model], packed_ref.at[3:4, model:]
    taps, states = tap_ref.shape[0], log_ref.shape[0]
    rank = SELECTED - 2 * states
    held, cut = in_ref.shape[0], in_ref.shape[2]
    blocks = width // LANES
    saving, numbers = [], iter(range(64))

    def load(source, target):
        copy = pltpu.make_async_copy(source, target, loads.at[next(numbers)])
        copy.start()
        return copy

    def save(source, target):
        copy = pltpu.make_async_copy(source, target, saves.at[len(saving)])
        copy.start()
        saving.append(copy)

    def weight(k):
        return load(in_hbm.at[:, pl.ds(k * cut, cut)], in_ref.at[k % held])

    early = [load(back_hbm, back), load(out_hbm, out_ref), load(gate_hbm, gate), load(mixer_hbm, mixer)]
    scanning = [load(step_hbm, step), load(conv_hbm, conv), load(raw_hbm, raw), load(entry_hbm, entry)]
    padding = load(padded_hbm, padded)
    weights = {k: weight(k) for k in range(held, 2 * held)}
    relay = Relay(True, log_ref, log_rows, relay_in, *relayed, chained=True)

    early[0].wait()
    seating = seated_rows(slot_ref, rows, back.shape[0])
    chosen = chosen_ref[:, 0:1]
    along = jnp.sum(jnp.dot(seating, back[:, model:], preferred_element_type=jnp.float32), axis=1, keepdims=True)
    place = lax.broadcasted_iota(jnp.int32, (rows, LANES), 1)
    logits = (along * chosen * (named_experts(slot_ref, rows) - probs_ref[...])).astype(jnp.bfloat16)
    grad = transposed_dot(logits, router_ref[...]) + chosen * jnp.dot(seating, back[:, :model], preferred_element_type=jnp.float32)
    narrow[...] = jnp.zeros_like(narrow)
    narrow[2 : 2 + EXPERTS, :] = column_dot(logits, normed_ref[...])
    value = middle_ref[...]
    returned, gained = rms_back(value, rms_scale(value), second_gain_ref[...], grad)
    narrow[1:2, :] = gained[None, :]
    value = up_ref[...].astype(jnp.float32) + returned
    grad_middle[...] = value
    middle_low[...] = value.astype(jnp.bfloat16)
    save(middle_low, low_out)
    for copy in early[1:]:
        copy.wait()

    def open_gate(b, unused):
        lanes = lanes_of(b)
        grown = transposed_dot(middle_low[...], out_ref[lanes, :])
        opening = gate[:, lanes]
        mixed[:, lanes] = grown * (opening * jax.nn.sigmoid(opening))
        grad_gate[:, lanes] = (grown * mixer[:, lanes] * silu_slope(opening)).astype(jnp.bfloat16)
        return unused

    lax.fori_loop(0, blocks, open_gate, 0)
    save(grad_gate, gate_out)
    pre, gconv = gate, mixer
    activating = load(pre_hbm, pre)
    for copy in scanning:
        copy.wait()

    fill_maps(sel_ref, wide_out, rank + states)

    def summary(part):
        summarize(True, part, step, mixed, wide_out, log_ref, part_ref, span_ref, relay.message.at[part])

    def prepare():
        fill_maps(sel_ref, wide_in, rank)
        sum_in[...] = jnp.zeros_like(sum_in)
        sum_out[...] = jnp.zeros_like(sum_out)
        raw_sum[...] = jnp.zeros_like(raw_sum)

    def scan(part):
        retreat_part(
            part, step, conv, mixed, raw, wide_in, wide_out, log_ref, step_weight_ref, entry, part_ref, span_ref,
            relay_in.at[part], low, gconv, glog, gbias, sum_in, sum_out, states_ref, decays_ref, raw_sum, raw_rows,
        )

    relay.meet()
    staged(relay, summary, prepare, scan)
    maps = gather_maps(sum_in, rank) + gather_maps(sum_out, rank + states)
    gsel[...] = (raw_sum[...] + maps).astype(jnp.bfloat16)

    activating.wait()
    padding.wait()
    step_low = jnp.where(place < rank, sel_ref[...], 0.0).astype(jnp.bfloat16)
    tall = lax.broadcasted_iota(jnp.int32, (row_ref.shape[0], LANES), 0)
    spots = jnp.where(lax.broadcasted_iota(jnp.int32, tall.shape, 1) == tall + SELECTED, 1.0, 0.0).astype(jnp.bfloat16)
    row_ref[...] = jnp.zeros_like(row_ref)

    def convolve_back(b, unused):
        lanes = lanes_of(b)
        around, kept = mixed[:, lanes], conv[:, lanes]
        grown = transposed_dot(gsel[:, :SELECTED], select_ref[lanes, :]) + gconv[:, lanes] + skip_ref[:, lanes] * around
        grown = grown * silu_slope(pre[:, lanes])
        gconv[:, lanes] = grown
        row_ref[:states, :] = glog[:, lanes]
        for k in range(taps):
            row_ref[states + k : states + k + 1, :] = jnp.sum(
                grown * padded[k * SEGS : k * SEGS + rows, lanes], axis=0, keepdims=True
            )
        row_ref[states + taps : states + taps + 1, :] = jnp.sum(grown, axis=0, keepdims=True)
        row_ref[states + taps + 1 : states + taps + 2, :] = gbias[:, lanes]
        row_ref[states + taps + 2 : states + taps + 3, :] = jnp.sum(around * kept, axis=0, keepdims=True)
        summed = column_dot(kept.astype(jnp.bfloat16), gsel[...])
        for piece in three_parts(row_ref[...]):
            summed = summed + column_dot(piece, spots)
        left[lanes, :] = summed
        right[lanes, :] = column_dot(low[:, lanes], step_low)
        return unused

    lax.fori_loop(0, blocks, convolve_back, 0)
    save(left, left_out)
    save(right, right_out)

    tail[...] = jnp.zeros_like(tail)
    for k in range(taps - 1):
        tail[k : k + 1, :] = gconv[k * SEGS : k * SEGS + 1, :]
    handing = pltpu.make_async_remote_copy(
        src_ref=tail, dst_ref=tail_got, send_sem=passing.at[0], recv_sem=passing.at[1],
        device_id=relay.onward(-1), device_id_type=pl.DeviceIdType.MESH,
    )
    handing.start()
    for k in range(held):
        weights[held + k].wait()
        summed = transposed_dot(grad_gate[:, k * cut : (k + 1) * cut], in_ref[k])
        total[...] = summed if k == 0 else total[...] + summed
        weights[k] = weight(k)
    handing.wait()
    goes_on = jnp.where(lax.axis_index("seq") < GRID * GRID - 1, 1.0, 0.0)
    segment = lax.broadcasted_iota(jnp.int32, (SEGS, cut), 0)
    for k in range(held):
        spot = slice(k * cut, (k + 1) * cut)
        grown = None
        for t in range(taps):
            late = taps - 1 - t
            shifted = gconv[late * SEGS :, spot]
            if late:
                wrapped = [
                    jnp.where(
                        segment == SEGS - 1,
                        goes_on * tail_got[j : j + 1, spot],
                        pltpu.roll(gconv[j * SEGS : (j + 1) * SEGS, spot], SEGS - 1, 0),
                    )
                    for j in range(late)
                ]
                shifted = jnp.concatenate([shifted] + wrapped, axis=0)
            term = tap_ref[t : t + 1, spot] * shifted
            grown = term if grown is None else grown + term
        grad_conv[:, spot] = grown.astype(jnp.bfloat16)
        weights[k].wait()
        total[...] += transposed_dot(grad_conv[:, spot], in_ref[k])
    save(grad_conv, conv_out)
    stream = token_ref[...].astype(jnp.float32)
    returned, gained = rms_back(stream, rms_scale(stream), gain_ref[...], total[...])
    narrow[0:1, :] = gained[None, :]
    total[...] = grad_middle[...] + returned
    save(narrow, narrow_out)
    save(total, token_out)
    for copy in saving:
        copy.wait()


WHOLE = pl.BlockSpec(memory_space=pltpu.VMEM)


def shaped(*dims, dtype=jnp.float32):
    return jax.ShapeDtypeStruct(dims, dtype)


def roomy(mebibytes, **more):
    return pltpu.CompilerParams(vmem_limit_bytes=mebibytes << 20, **more)


def busy(elements):
    return pl.CostEstimate(flops=4096 * elements, bytes_accessed=16 * elements, transcendentals=4 * elements)


def wide_scratch(rows, states, extra=0):
    return pltpu.VMEM((rows // SEGS + extra, states, SEGS, LANES), jnp.float32)


def chain_scratch(states, width):
    return [pltpu.VMEM((states, SEGS, width), jnp.float32), pltpu.VMEM((SEGS, width), jnp.float32)]


def relay_scratch():
    def kept(*dims):
        return pltpu.VMEM((PARTS,) + dims + (SEGS, LANES), jnp.float32)

    return [
        kept(GRID, GRID),
        kept(GRID, GRID),
        kept(GRID, GRID + 1),
        kept(GRID, GRID + 1),
        kept(GRID + 1),
        kept(GRID, GRID + 1),
        kept(GRID, GRID),
        kept(GRID, GRID),
        pltpu.SemaphoreType.DMA((PARTS, 3, GRID)),
        pltpu.SemaphoreType.DMA((PARTS, 3, GRID)),
    ]


def mixer(tokens, packed, in_weight, taps, select, step_weight, decay_log, out_weight, router, slots, seats):
    rows, model = tokens.shape
    states, width = decay_log.shape
    reach = (taps.shape[0] - 1) * SEGS
    bf16, f32 = jnp.bfloat16, jnp.float32
    anywhere = pl.BlockSpec(memory_space=pl.ANY)
    results = [
        ((rows, model), bf16),
        ((rows, width), f32),
        ((rows + reach, width), f32),
        ((rows, width), f32),
        ((rows, width), f32),
        ((rows, width), f32),
        ((rows, width), f32),
        ((rows, LANES), f32),
        ((states, SEGS, width), f32),
        ((rows, width), f32),
        ((rows, width), bf16),
        ((rows, model), f32),
        ((rows, model), bf16),
        ((rows, EXPERTS), f32),
        ((rows, LANES), f32),
        ((seats, model + LANES), bf16),
    ]
    kept = [pltpu.VMEM(dims, dtype) for dims, dtype in results]
    weights = [pltpu.VMEM((2 * width // CUT, model, CUT), bf16), pltpu.VMEM(out_weight.shape, bf16)]
    relayed = relay_scratch()
    return pl.pallas_call(
        mixer_kernel,
        out_shape=tuple(shaped(*dims, dtype=dtype) for dims, dtype in results),
        in_specs=[WHOLE] * 2 + [anywhere] + [WHOLE] * 4 + [anywhere] + [WHOLE] * 2,
        out_specs=(anywhere,) * len(results),
        scratch_shapes=kept[:1]
        + weights
        + [kept[2], kept[1]]
        + kept[3:]
        + [pltpu.VMEM((SEGS, width), f32)] * 2
        + chain_scratch(states, width)
        + [wide_scratch(rows, states)] * 2
        + [
            pltpu.SemaphoreType.DMA((2 * width // CUT + 1,)),
            pltpu.SemaphoreType.DMA((len(results),)),
            pltpu.SemaphoreType.DMA((2,)),
        ]
        + relayed,
        compiler_params=roomy(60, collective_id=0, has_side_effects=True),
        cost_estimate=busy(rows * states * width),
        name="mixer",
    )(tokens, packed, in_weight, taps, select, step_weight, decay_log, out_weight, router, slots)


def mixer_back(
    back, slots, probs, chosen, normed, router, middle, up, out_weight, gate, mixed, conv, step, raw, selection, pre, padded, entry,
    decay_log, step_weight, select, taps, packed, in_weight, tokens,
):
    rows, width = step.shape
    model = tokens.shape[1]
    states = decay_log.shape[0]
    bf16, f32 = jnp.bfloat16, jnp.float32
    anywhere = pl.BlockSpec(memory_space=pl.ANY)
    held = width // CUT
    tall = ((rows, width), f32)
    results = [
        ((rows, model), bf16),
        ((rows, width), bf16),
        ((rows, width), bf16),
        ((width, LANES), f32),
        ((width, LANES), f32),
        ((16, model), f32),
        ((rows, model), f32),
    ]
    streamed = (0, 8, 9, 10, 11, 12, 13, 15, 16, 17, 23)
    kept = (
        [(back.shape, bf16), (out_weight.shape, bf16)]
        + [tall] * 5
        + [(padded.shape, f32), (entry.shape, f32), ((held, model, CUT), bf16)]
        + results[:6]
        + [((rows, model), f32), tall, ((rows, width), bf16), ((rows, LANES), bf16), ((states, width), f32), ((1, width), f32)]
        + [((rows, model), f32), ((SEGS, width), f32), ((SEGS, width), f32), ((24, LANES), f32)]
    )
    return pl.pallas_call(
        mixer_back_kernel,
        out_shape=tuple(shaped(*dims, dtype=dtype) for dims, dtype in results),
        in_specs=[anywhere if k in streamed else WHOLE for k in range(25)],
        out_specs=(anywhere,) * len(results),
        scratch_shapes=[pltpu.VMEM(dims, dtype) for dims, dtype in kept]
        + chain_scratch(states, width)
        + [wide_scratch(rows, states)] * 4
        + [wide_scratch(rows, states, 1), wide_scratch(rows, states)]
        + [pltpu.VMEM((rows, LANES), f32)] * 2
        + [pltpu.SemaphoreType.DMA((10 + 2 * held,)), pltpu.SemaphoreType.DMA((len(results),)), pltpu.SemaphoreType.DMA((2,))]
        + relay_scratch(),
        compiler_params=roomy(62, collective_id=1, has_side_effects=True),
        cost_estimate=busy(rows * states * width),
        name="mixer_back",
    )(
        back, slots, probs, chosen, normed, router, middle, up, out_weight, gate, mixed, conv, step, raw, selection, pre, padded, entry,
        decay_log, step_weight, select, taps, packed, in_weight, tokens,
    )


def segmented(block):
    rows = block.shape[0]
    return block.reshape(SEGS, rows // SEGS, -1).transpose(1, 0, 2).reshape(rows, -1)


def in_order(block):
    rows = block.shape[0]
    return block.reshape(rows // SEGS, SEGS, -1).transpose(1, 0, 2).reshape(rows, -1)


def rms_scale(stream):
    return lax.rsqrt(jnp.mean(stream * stream, axis=-1, keepdims=True) + 1e-05)


def rms_back(stream, scale, gain, grad):
    grown = grad * gain
    along = jnp.mean(stream * grown, axis=-1, keepdims=True)
    return scale * grown - stream * (scale * scale * scale * along), jnp.sum(grad * stream * scale, axis=0)


def silu_slope(value):
    gate = jax.nn.sigmoid(value)
    return gate * (1.0 + value * (1.0 - gate))


def product(left, right):
    return jnp.dot(left, right, preferred_element_type=jnp.float32)


def across(left, right):
    return jnp.einsum("tk,dk->td", left, right, preferred_element_type=jnp.float32)


def summed_rows(left, right):
    return jnp.einsum("tk,td->kd", left, right, preferred_element_type=jnp.float32)


CHUNK = 1024
GELU_OUT = math.sqrt(2.0 / math.pi)
GELU_IN = 0.044715


def transposed_dot(left, right):
    return lax.dot_general(left, right, (((1,), (1,)), ((), ())), preferred_element_type=jnp.float32)


def column_dot(left, right):
    return lax.dot_general(left, right, (((0,), (0,)), ((), ())), preferred_element_type=jnp.float32)


def three_parts(value):
    parts, left = [], value
    for unused in range(3):
        part = left.astype(jnp.bfloat16)
        left = left - part.astype(jnp.float32)
        parts.append(part)
    return parts


def expert_pull_kernel(up_ref, second_ref, pull_ref):
    pull_ref[...] = transposed_dot(up_ref[...], second_ref[...]).astype(jnp.bfloat16)


def expert_pull(upstream, second):
    rows, width = upstream.shape
    hidden = second.shape[0]
    return pl.pallas_call(
        expert_pull_kernel,
        grid=(hidden // CHUNK,),
        out_shape=shaped(rows, hidden, dtype=jnp.bfloat16),
        in_specs=[pl.BlockSpec((rows, width), lambda i: (0, 0)), pl.BlockSpec((CHUNK, width), lambda i: (i, 0))],
        out_specs=pl.BlockSpec((rows, CHUNK), lambda i: (0, i)),
        compiler_params=roomy(60),
        cost_estimate=pl.CostEstimate(flops=2 * rows * hidden * width, bytes_accessed=2 * (width + rows) * hidden, transcendentals=0),
        name="expert_pull",
    )(upstream, second)


def expert_kernel(got_ref, up_ref, pull_ref, first_ref, second_ref, active_ref, grad_ref, value_ref, sent_ref, value, sent):
    step, last = pl.program_id(0), pl.num_programs(0) - 1
    width = up_ref.shape[1]
    first = first_ref[...]
    pre = jnp.dot(got_ref[:, :width], first, preferred_element_type=jnp.float32)
    square = pre * pre
    bent = jnp.tanh(pre * (GELU_OUT + GELU_OUT * GELU_IN * square))
    share = 0.5 + 0.5 * bent
    active = (pre * share).astype(jnp.bfloat16)
    slope = share + pre * (0.5 - 0.5 * bent * bent) * (GELU_OUT + 3.0 * GELU_OUT * GELU_IN * square)
    grad = (slope * pull_ref[...].astype(jnp.float32)).astype(jnp.bfloat16)
    active_ref[...] = active
    grad_ref[...] = grad
    more_value = jnp.dot(active, second_ref[...], preferred_element_type=jnp.float32)
    more_sent = transposed_dot(grad, first)

    @pl.when(step == 0)
    def begin():
        value[...] = more_value
        sent[...] = more_sent

    @pl.when(step > 0)
    def go_on():
        value[...] += more_value
        sent[...] += more_sent

    @pl.when(step == last)
    def finish():
        low = value[...].astype(jnp.bfloat16)
        value_ref[...] = low
        sent_ref[:, :width] = sent[...].astype(jnp.bfloat16)
        along = jnp.sum(low.astype(jnp.float32) * up_ref[...].astype(jnp.float32), axis=1, keepdims=True)
        place = lax.broadcasted_iota(jnp.int32, (sent_ref.shape[0], LANES), 1)
        tail = jnp.zeros(place.shape, jnp.float32)
        for k, part in enumerate(three_parts(along)):
            tail = jnp.where(place == k, part.astype(jnp.float32), tail)
        sent_ref[:, width:] = tail.astype(jnp.bfloat16)


def expert_layer(received, upstream, pull, first, second):
    rows, width = upstream.shape
    hidden = second.shape[0]
    wide = received.shape[1]

    def fixed(cols):
        return pl.BlockSpec((rows, cols), lambda i: (0, 0))

    chunk = pl.BlockSpec((rows, CHUNK), lambda i: (0, i))
    return pl.pallas_call(
        expert_kernel,
        grid=(hidden // CHUNK,),
        out_shape=(
            shaped(rows, hidden, dtype=jnp.bfloat16),
            shaped(rows, hidden, dtype=jnp.bfloat16),
            shaped(rows, width, dtype=jnp.bfloat16),
            shaped(rows, wide, dtype=jnp.bfloat16),
        ),
        in_specs=[
            fixed(wide),
            fixed(width),
            chunk,
            pl.BlockSpec((width, CHUNK), lambda i: (0, i)),
            pl.BlockSpec((CHUNK, width), lambda i: (i, 0)),
        ],
        out_specs=(chunk, chunk, fixed(width), fixed(wide)),
        scratch_shapes=[pltpu.VMEM((rows, width), jnp.float32)] * 2,
        compiler_params=roomy(60),
        cost_estimate=pl.CostEstimate(flops=6 * rows * hidden * width, bytes_accessed=4 * hidden * (width + rows), transcendentals=rows * hidden),
        name="expert_layer",
    )(received, upstream, pull, first, second)


def expert_sums_kernel(hidden_ref, received_ref, active_ref, up_ref, out_ref, scaled_received, scaled_up):
    pair = out_ref.shape[0]
    half = out_ref.shape[2]
    width = up_ref.shape[1]

    @pl.when(pl.program_id(0) == 0)
    def scale():
        parts = received_ref[:, width:].astype(jnp.float32)
        gate = parts[:, 0:1] + parts[:, 1:2] + parts[:, 2:3]
        scaled_received[...] = (received_ref[:, :width].astype(jnp.float32) * gate).astype(jnp.bfloat16)
        scaled_up[...] = (up_ref[...].astype(jnp.float32) * gate).astype(jnp.bfloat16)

    for which, (left_ref, right_ref) in enumerate(((hidden_ref, scaled_received), (active_ref, scaled_up))):
        total = column_dot(left_ref[...], right_ref[...]).astype(jnp.bfloat16)
        for i in range(pair):
            out_ref[i, which] = total[i * half : (i + 1) * half]


def expert_sums(grad_hidden, received, activated, upstream, owners):
    rows, hidden = grad_hidden.shape
    width = upstream.shape[1]
    pair = 2
    chunk = pl.BlockSpec((rows, pair * hidden // owners), lambda i: (0, i))

    def fixed(cols):
        return pl.BlockSpec((rows, cols), lambda i: (0, 0))

    return pl.pallas_call(
        expert_sums_kernel,
        grid=(owners // pair,),
        out_shape=shaped(owners, 2, hidden // owners, width, dtype=jnp.bfloat16),
        in_specs=[chunk, fixed(received.shape[1]), chunk, fixed(width)],
        out_specs=pl.BlockSpec((pair, 2, hidden // owners, width), lambda i: (i, 0, 0, 0)),
        scratch_shapes=[pltpu.VMEM((rows, width), jnp.bfloat16)] * 2,
        compiler_params=roomy(60),
        cost_estimate=pl.CostEstimate(flops=4 * rows * hidden * width, bytes_accessed=4 * hidden * (width + rows), transcendentals=0),
        name="expert_sums",
    )(grad_hidden, received, activated, upstream)


ORDERS = ("xyz", "yzx", "zxy")
PIECE = 16


def shares_kernel(
    conv_cols, gate_cols, token_ref, out_cols, middle_ref, left_ref, right_ref, narrow_ref, sum_ref, in_ref, out_ref, made, taken,
    half_a, half_b, half_c, one_a, one_b, one_c, sends, arrivals):
    seq, expert = lax.axis_index("seq"), lax.axis_index("expert")
    core = lax.rem(expert, 2)
    place = {"y": lax.div(seq, 4), "z": lax.rem(seq, 4), "x": lax.div(expert, 2)}
    third = token_ref.shape[1] // len(ORDERS)
    streams = [(L, q) for L in range(len(ORDERS)) for q in range(4)]

    def flip(i):
        return i + 1 - 2 * lax.rem(i, 2)

    def device(**moved):
        at = dict(place, **moved)
        return {"seq": at["y"] * 4 + at["z"], "expert": at["x"] * 2 + at.get("core", core)}

    partners = [device(core=1 - core)]
    for axis in "xyz":
        partners += [device(**{axis: flip(place[axis])}), device(**{axis: 3 - place[axis]})]
    barrier = pltpu.get_barrier_semaphore()
    for partner in partners:
        pl.semaphore_signal(barrier, inc=1, device_id=partner, device_id_type=pl.DeviceIdType.MESH)
    pl.semaphore_wait(barrier, len(partners))

    def send(source, target, partner, stream, number):
        k = streams.index(stream)
        copy = pltpu.make_async_remote_copy(
            src_ref=source, dst_ref=target, send_sem=sends.at[k, number], recv_sem=arrivals.at[k, number],
            device_id=partner, device_id_type=pl.DeviceIdType.MESH,
        )
        copy.start()
        return copy

    def add(target, source, unit):
        def step(i, unused):
            target[i] = target[i] + source[i]
            return unused

        lax.fori_loop(0, unit, step, 0, unroll=min(unit, 8))

    inner = out_cols.shape[1]
    for source, target, base in ((conv_cols, in_ref, 0), (gate_cols, in_ref, inner), (out_cols, out_ref, 0)):

        def turn_over(k, unused, source=source, target=target, base=base):
            spot = pl.ds(pl.multiple_of(k * LANES, LANES), LANES)
            target[pl.ds(pl.multiple_of(base + k * LANES, LANES), LANES), :] = source[:, spot].T
            return unused

        lax.fori_loop(0, source.shape[1] // LANES, turn_over, 0)

    pending = {}
    for L, order in enumerate(ORDERS):
        lanes = pl.ds(L * third, third)
        narrow = narrow_ref[:, lanes].astype(jnp.bfloat16)

        def block(s, unused):
            y, z = lax.div(s, 4), lax.rem(s, 4)
            by_in = jnp.dot(
                in_ref[pl.ds(pl.multiple_of(s * 288, 16), 288), :], token_ref[:, lanes], preferred_element_type=jnp.float32
            ).astype(jnp.bfloat16)
            here = pl.ds(pl.multiple_of(s * 144, 16), 144)
            by_out = jnp.dot(out_ref[here, :], middle_ref[:, lanes], preferred_element_type=jnp.float32)
            left, right = left_ref[here, :], right_ref[here, :]
            for x in range(4):
                at = {"x": x, "y": y, "z": z}
                slot = (at[order[0]] * 4 + at[order[1]]) * 4 + at[order[2]]
                rows = by_in[72 * x : 72 * x + 72]
                more = by_out[36 * x : 36 * x + 36].astype(jnp.bfloat16)
                for q in range(4):
                    made[L, q, slot] = rows[16 * q : 16 * q + 16]
                made[L, 4, slot, 0:8] = rows[64:]
                made[L, 4, slot, 8:16] = more[:8]
                made[L, 5, slot] = more[8:24]
                made[L, 6, slot, 0:12] = more[24:]
                made[L, 6, slot, 12:16] = narrow[8:12]
                made[L, 7, slot, 8:16] = narrow[0:8]
                last = jnp.concatenate([left[36 * x : 36 * x + 36], right[36 * x : 36 * x + 36]], axis=0)
                for part in range(third // LANES):
                    k = 8 * (L * (third // LANES) + part)
                    made[L, 7, slot, 0:8, part * LANES : (part + 1) * LANES] = last[k : k + 8].astype(jnp.bfloat16)
            return unused

        lax.fori_loop(0, 16, block, 0, unroll=2)
        for q in range(4):
            pending[L, q] = [
                send(made.at[L, 4 * (1 - core) + q], taken.at[L, q], device(core=1 - core), (L, q), 0)
            ]

    halves, ones = (half_a, half_b, half_c), (one_a, one_b, one_c)
    holding = {}
    for L, q in streams:
        for copy in pending[L, q]:
            copy.wait()
        add(taken.at[L, q], made.at[L, 4 * core + q], 64)
        holding[L, q] = taken.at[L, q]
        pending[L, q] = start_halves(L, q, 0, holding[L, q], halves, place, flip, device, send)
    for turn in range(3):
        unit = 16 >> (2 * turn)
        for L, q in streams:
            axis = ORDERS[L][turn]
            i = place[axis]
            for copy in pending[L, q]:
                copy.wait()
            other = 3 - i if q < 2 else flip(i)
            got = halves[turn].at[L, q]
            add(got.at[0], holding[L, q].at[pl.ds(i * unit, unit)], unit)
            add(got.at[1], holding[L, q].at[pl.ds(other * unit, unit)], unit)
            partner = device(**{axis: other})
            pending[L, q] = [send(got.at[1], ones[turn].at[L, q], partner, (L, q), 3 + 3 * turn)]
        for L, q in streams:
            for copy in pending[L, q]:
                copy.wait()
            got = ones[turn].at[L, q]
            if turn < 2:
                add(got, halves[turn].at[L, q, 0], unit)
                holding[L, q] = got
                pending[L, q] = start_halves(L, q, turn + 1, got, halves, place, flip, device, send)
            else:
                whole = got[0].astype(jnp.float32) + halves[turn][L, q, 0, 0].astype(jnp.float32)
                sum_ref[4 * core + q, :, L * third : (L + 1) * third] = whole
    here = sum_ref.at[pl.ds(4 * core, 4)]
    send(here, here, device(core=1 - core), (0, 0), 10).wait()


def start_halves(L, q, turn, source, halves, place, flip, device, send):
    axis = ORDERS[L][turn]
    unit = 16 >> (2 * turn)
    i = place[axis]
    partner = flip(i) if q < 2 else 3 - i
    second = 3 - partner if q < 2 else flip(partner)
    target = halves[turn].at[L, q]
    return [
        send(source.at[pl.ds(partner * unit, unit)], target.at[0], device(**{axis: partner}), (L, q), 1 + 3 * turn),
        send(source.at[pl.ds(second * unit, unit)], target.at[1], device(**{axis: partner}), (L, q), 2 + 3 * turn),
    ]


def shares(conv_cols, gate_cols, tokens, out_cols, middle, left, right, narrow):
    width = tokens.shape[1]
    rows, inner = out_cols.shape
    third = width // len(ORDERS)

    def slots(*lead):
        return pltpu.VMEM((len(ORDERS),) + lead + (PIECE, third), jnp.bfloat16)

    return pl.pallas_call(
        shares_kernel,
        out_shape=shaped(8, PIECE, width),
        in_specs=[WHOLE] * 8,
        out_specs=WHOLE,
        scratch_shapes=[pltpu.VMEM((2 * inner, rows), jnp.bfloat16), pltpu.VMEM((inner, rows), jnp.bfloat16)]
        + [slots(8, 64), slots(4, 64)]
        + [slots(4, 2, 16 >> (2 * turn)) for turn in range(3)]
        + [slots(4, 16 >> (2 * turn)) for turn in range(3)]
        + [pltpu.SemaphoreType.DMA((12, 11))] * 2,
        compiler_params=roomy(60, collective_id=2, has_side_effects=True),
        name="shares",
    )(conv_cols, gate_cols, tokens, out_cols, middle, left, right, narrow)


def local(
    tokens,
    expert_index,
    cotangent,
    first_gain,
    in_weight,
    conv_weight,
    conv_bias,
    select_weight,
    step_weight,
    step_bias,
    decay_log,
    skip_gain,
    out_weight,
    second_gain,
    router_weight,
    expert_first,
    expert_second,
):
    bf16, f32 = jnp.bfloat16, jnp.float32
    stream = segmented(tokens[0])
    routes = segmented(expert_index[0])[:, 0]
    upstream = segmented(cotangent[0])
    row_count, model_width = stream.shape
    seat_count = 2 * row_count
    inner = conv_bias.shape[0]
    rank = step_weight.shape[0]
    states = decay_log.shape[0]
    taps = conv_weight.shape[0]
    expert_count = router_weight.shape[1]
    capacity = 2 * row_count // expert_count
    seqs, experts = lax.axis_size("seq"), lax.axis_size("expert")
    reach = (taps - 1) * SEGS

    picks = (routes[:, None] == jnp.arange(expert_count, dtype=jnp.int32)[None, :]).astype(bf16)
    earlier = jnp.arange(row_count)[:, None] > jnp.arange(row_count)[None, :]
    ahead = product(earlier.astype(bf16), picks)
    chosen = picks.astype(f32)
    slot_index = routes * capacity + jnp.sum(ahead * chosen, axis=1).astype(jnp.int32)
    seats = jnp.arange(expert_count * capacity, dtype=jnp.int32)
    placing = (seats[:, None] == slot_index[None, :]).astype(bf16)

    def seated(rows):
        return product(placing, rows).astype(bf16)

    def swapped(rows):
        parts = rows.reshape(expert_count, capacity, -1)
        parts = lax.all_to_all(parts, "expert", split_axis=0, concat_axis=0, tiled=True)
        return parts.reshape(expert_count * capacity, -1)

    def unseated(rows):
        return jnp.einsum("st,sd->td", placing, rows, preferred_element_type=f32)

    upstream_there = swapped(seated(upstream))

    packed = jnp.concatenate([conv_bias, step_bias, skip_gain, first_gain, second_gain]).reshape(4, inner)
    slot_column = slot_index[:, None]
    (
        normed_in, gate_input, padded, preact, conv_out, step_raw, step_size, selection, first, mixer_out, gated,
        middle, normed_mid, router_probs, gate_wide, leaving,
    ) = mixer(
        stream, packed, in_weight, conv_weight, select_weight, step_weight, decay_log, out_weight, router_weight, slot_column, seat_count
    )
    leaving, upstream_there = lax.optimization_barrier((leaving, upstream_there))
    received = swapped(leaving)
    pull = expert_pull(upstream_there, expert_second[0])
    activated, grad_hidden, value_there, grad_there = expert_layer(
        received, upstream_there, pull, expert_first[0], expert_second[0]
    )
    back = swapped(grad_there)
    expert_grads = expert_sums(grad_hidden, received, activated, upstream_there, seqs)
    expert_grads, value_there, back = lax.optimization_barrier((expert_grads, value_there, back))
    value_home = swapped(value_there)
    expert_share = lax.psum_scatter(
        expert_grads.reshape(-1, model_width), "seq", scatter_dimension=0, tiled=True
    ).reshape(2, -1, model_width)
    middle_low, grad_gate_input, grad_conv_input, left, right, narrow, grad_tokens = mixer_back(
        back, slot_column, router_probs, gate_wide, normed_mid, router_weight, middle, upstream, out_weight, gate_input, mixer_out, conv_out,
        step_size, step_raw, selection, preact, padded, first, decay_log, step_weight, select_weight, conv_weight, packed, in_weight, stream,
    )
    middle_low, value_home = lax.optimization_barrier((middle_low, value_home))
    mixed = middle + gate_wide[:, 0:1] * unseated(value_home)

    devices = seqs * experts
    each, fewer = inner // devices, model_width // devices
    grad_conv_input, expert_share = lax.optimization_barrier((grad_conv_input, expert_share))
    sums = shares(grad_conv_input, grad_gate_input, normed_in, gated, middle_low, left, right, narrow)
    sums = sums.reshape(-1, model_width)
    core = lax.axis_index("expert") % 2
    in_share = lax.dynamic_slice_in_dim(sums, 2 * each * core, 2 * each)
    out_share = lax.dynamic_slice_in_dim(sums, 4 * each + each * core, each)
    small = sums[112:120].reshape(8, -1, LANES).transpose(1, 0, 2).reshape(2, 2 * each, LANES)
    small = lax.dynamic_slice_in_dim(small, each * core, each, axis=1)
    rows_sum = small[0, :, rank + 2 * states :]
    owner = lax.axis_index("seq") * experts + lax.axis_index("expert")
    narrow_sum = jnp.concatenate([sums[120:128], sums[108:110]])
    narrow_sum = lax.dynamic_slice_in_dim(narrow_sum, owner * fewer, fewer, axis=1)
    return (
        in_order(mixed.astype(bf16))[None],
        in_order(grad_tokens)[None],
        narrow_sum[0],
        in_share.T,
        rows_sum[:, states : states + taps].T,
        rows_sum[:, states + taps],
        small[0, :, : rank + 2 * states],
        small[1, :, :rank].T,
        rows_sum[:, states + taps + 1],
        rows_sum[:, :states].T,
        rows_sum[:, states + taps + 2],
        out_share,
        narrow_sum[1],
        narrow_sum[2:].T,
        expert_share[0].T.astype(f32)[None],
        expert_share[1].astype(f32)[None],
    )


def solution(mesh):
    return jax.shard_map(
        local,
        mesh=mesh,
        in_specs=(
            P("expert", "seq", None),
            P("expert", "seq", None),
            P("expert", "seq", None),
            P(),
            P(),
            P(),
            P(),
            P(),
            P(),
            P(),
            P(),
            P(),
            P(),
            P(),
            P(),
            P("expert", None, None),
            P("expert", None, None),
        ),
        out_specs=(
            P("expert", "seq", None),
            P("expert", "seq", None),
            P(("seq", "expert")),
            P(None, ("seq", "expert")),
            P(None, ("seq", "expert")),
            P(("seq", "expert")),
            P(("seq", "expert"), None),
            P(None, ("seq", "expert")),
            P(("seq", "expert")),
            P(None, ("seq", "expert")),
            P(("seq", "expert")),
            P(("seq", "expert"), None),
            P(("seq", "expert")),
            P(("seq", "expert"), None),
            P("expert", None, "seq"),
            P("expert", "seq", None),
        ),
        check_vma=False,
    )
```

```python
import functools
import math

import jax
import jax.numpy as jnp
from jax import lax
from jax.experimental import pallas as pl
from jax.experimental.pallas import tpu as pltpu
from jax.sharding import PartitionSpec as P

LANES = 128
SEGS = 8
LOG2E = math.log2(math.e)
PARTS = 3
SELECTED = 104
EXPERTS = 8
CAPACITY = 64
CUT = 768
GRID = 4


def spread_ones(states):
    row = lax.broadcasted_iota(jnp.int32, (LANES, states * LANES), 0)
    lane = lax.broadcasted_iota(jnp.int32, (LANES, states * LANES), 1)
    return row, lane // LANES


def fill_maps(sel_ref, wide_ref, column):
    steps, states = wide_ref.shape[:2]
    row, block = spread_ones(states)
    ones = jnp.where(row == block + column, 1.0, 0.0).astype(jnp.bfloat16)
    left, total = sel_ref[...], None
    for unused in range(3):
        part = left.astype(jnp.bfloat16)
        left = left - part.astype(jnp.float32)
        spread = jnp.dot(part, ones, preferred_element_type=jnp.float32)
        total = spread if total is None else total + spread
    for n in range(states):
        wide_ref[:, n] = total[:, n * LANES : (n + 1) * LANES].reshape(steps, SEGS, LANES)


def gather_maps(sum_ref, column):
    steps, states = sum_ref.shape[:2]
    row, block = spread_ones(states)
    ones = jnp.where(row == block + column, 1.0, 0.0).astype(jnp.bfloat16)
    left = jnp.concatenate([sum_ref[:, n].reshape(steps * SEGS, LANES) for n in range(states)], axis=1)
    total = None
    for unused in range(3):
        part = left.astype(jnp.bfloat16)
        left = left - part.astype(jnp.float32)
        summed = transposed_dot(part, ones)
        total = summed if total is None else total + summed
    return total


def lanes_of(block):
    return pl.ds(pl.multiple_of(block * LANES, LANES), LANES)


def rows_of(j):
    return pl.ds(pl.multiple_of(j * SEGS, SEGS), SEGS)


def rates_of(log_ref, lanes):
    states = log_ref.shape[0]
    rate = -LOG2E * jnp.exp(log_ref[:, lanes])
    return jnp.stack([jnp.broadcast_to(rate[n : n + 1], (SEGS, LANES)) for n in range(states)])


def neighbour(value, hop, later, fill):
    axis = value.ndim - 2
    place = lax.broadcasted_iota(jnp.int32, value.shape, axis)
    if later:
        return jnp.where(place < SEGS - hop, pltpu.roll(value, SEGS - hop, axis), fill)
    return jnp.where(place >= hop, pltpu.roll(value, hop, axis), fill)


def summarize(later, part, step_ref, other_ref, wide, log_ref, part_ref, span_ref, message):
    steps, states = wide.shape[:2]
    blocks = step_ref.shape[1] // LANES // PARTS

    def block(i, unused):
        lanes = lanes_of(part * blocks + i)
        rate = rates_of(log_ref, lanes)

        def advance(turn, carry):
            span, memory = carry
            j = steps - 1 - turn if later else turn
            step = step_ref[rows_of(j), lanes]
            other = other_ref[rows_of(j), lanes]
            decay = jnp.exp2(step * rate)
            if later:
                memory = decay * (memory + wide[j] * other)
            else:
                memory = decay * memory + wide[j] * (step * other)
            return span + step, memory

        zero = jnp.zeros((SEGS, LANES), jnp.float32)
        span, memory = lax.fori_loop(0, steps, advance, (zero, jnp.zeros(rate.shape, jnp.float32)), unroll=8)
        hop = 1
        while hop < SEGS:
            memory = memory + jnp.exp2(rate * span) * neighbour(memory, hop, later, 0.0)
            span = span + neighbour(span, hop, later, 0.0)
            hop *= 2
        span_ref[:, lanes] = span
        part_ref[:, :, lanes] = memory
        end = 0 if later else SEGS - 1
        for n in range(states):
            message[n // GRID, n % GRID, pl.ds(i, 1), :] = memory[n, end : end + 1]
        for q in range(GRID):
            message[q, GRID, pl.ds(i, 1), :] = span[end : end + 1]
        return unused

    lax.fori_loop(0, blocks, block, 0)


def entering(later, part_ref, span_ref, rate, lanes, carried):
    ends = part_ref[:, :, lanes] + jnp.exp2(rate * span_ref[:, lanes]) * carried
    return neighbour(ends, 1, later, carried)


def carried_at(in_ref, part, i):
    states = GRID * GRID
    return jnp.stack(
        [jnp.broadcast_to(in_ref[n // GRID, n % GRID, pl.ds(i, 1), :], (SEGS, LANES)) for n in range(states)]
    )


def scan_part(part, step_ref, conv_ref, wide_in, wide_out, log_ref, part_ref, span_ref, in_ref, y_ref, entry_ref):
    steps = wide_in.shape[0]
    blocks = step_ref.shape[1] // LANES // PARTS

    def block(i, unused):
        lanes = lanes_of(part * blocks + i)
        rate = rates_of(log_ref, lanes)
        first = entering(False, part_ref, span_ref, rate, lanes, carried_at(in_ref, part, i))
        entry_ref[:, :, lanes] = first

        def advance(j, memory):
            step = step_ref[rows_of(j), lanes]
            memory = jnp.exp2(step * rate) * memory + wide_in[j] * (step * conv_ref[rows_of(j), lanes])
            y_ref[rows_of(j), lanes] = jnp.sum(wide_out[j] * memory, axis=0)
            return memory

        lax.fori_loop(0, steps, advance, first, unroll=8)
        return unused

    lax.fori_loop(0, blocks, block, 0)


def retreat_part(
    part, step_ref, conv_ref, grad_ref, raw_ref, wide_in, wide_out, log_ref, pull_ref, entry_ref, part_ref, span_ref, in_ref,
    low_ref, gconv_ref, glog_ref, gbias_ref, sum_in, sum_out, states_ref, decays_ref, raw_sum, raw_rows,
):
    steps = wide_in.shape[0]
    blocks = step_ref.shape[1] // LANES // PARTS

    def block(i, unused):
        lanes = lanes_of(part * blocks + i)
        rate = rates_of(log_ref, lanes)

        def advance(j, memory):
            step = step_ref[rows_of(j), lanes]
            decay = jnp.exp2(step * rate)
            memory = decay * memory + wide_in[j] * (step * conv_ref[rows_of(j), lanes])
            decays_ref[j] = decay
            states_ref[j + 1] = memory
            return memory

        first = entry_ref[:, :, lanes]
        states_ref[0] = first
        lax.fori_loop(0, steps, advance, first, unroll=8)

        def retreat(turn, carry):
            j = steps - 1 - turn
            mu, slow = carry
            step = step_ref[rows_of(j), lanes]
            conv = conv_ref[rows_of(j), lanes]
            grad = grad_ref[rows_of(j), lanes]
            lam = wide_out[j] * grad + mu
            sum_out[j] += grad * states_ref[j + 1]
            sum_in[j] += lam * (step * conv)
            by_in = jnp.sum(lam * wide_in[j], axis=0)
            mu = lam * decays_ref[j]
            kept = mu * states_ref[j]
            by_rate = jnp.sum(kept * rate, axis=0)
            grad_step = by_in * conv + (1.0 / LOG2E) * by_rate
            raw_rows[rows_of(j), :] = grad_step * jax.nn.sigmoid(raw_ref[rows_of(j), lanes])
            gconv_ref[rows_of(j), lanes] = by_in * step
            return mu, slow + kept * step

        last = entering(True, part_ref, span_ref, rate, lanes, carried_at(in_ref, part, i))
        unused_mu, slow = lax.fori_loop(0, steps, retreat, (last, jnp.zeros(rate.shape, jnp.float32)), unroll=4)
        glog_ref[:, lanes] = (1.0 / LOG2E) * jnp.sum(slow * rate, axis=1)
        raw_steps = raw_rows[...]
        gbias_ref[:, lanes] = jnp.sum(raw_steps, axis=0, keepdims=True)
        low = raw_steps.astype(jnp.bfloat16)
        low_ref[:, lanes] = low
        raw_sum[:, : pull_ref.shape[0]] += transposed_dot(low, pull_ref[:, lanes])
        return unused

    lax.fori_loop(0, blocks, block, 0)


def expert_peers():
    me = lax.axis_index("expert")
    return [lax.rem(me + k, EXPERTS) for k in range(1, EXPERTS)]


def seats_of(device):
    return pl.ds(pl.multiple_of(device * CAPACITY, CAPACITY), CAPACITY)


def trade(source, target, send_sems, recv_sems):
    me = lax.axis_index("expert")
    copies = [
        pltpu.make_async_remote_copy(
            src_ref=source.at[seats_of(peer)], dst_ref=target.at[seats_of(me)], send_sem=send_sems.at[k], recv_sem=recv_sems.at[k],
            device_id={"expert": peer}, device_id_type=pl.DeviceIdType.MESH,
        )
        for k, peer in enumerate(expert_peers())
    ]
    copies.append(pltpu.make_async_copy(source.at[seats_of(me)], target.at[seats_of(me)], send_sems.at[EXPERTS - 1]))
    for copy in copies:
        copy.start()
    return copies


class Relay:
    def __init__(self, later, log_ref, log_rows, in_ref, message, got, row, rows_got, above, made, sends, arrivals, others=()):
        self.later, self.log_rows, self.message, self.got = later, log_rows, message, got
        self.row, self.rows_got, self.above, self.made, self.in_ref = row, rows_got, above, made, in_ref
        self.sends, self.arrivals = sends, arrivals
        seq = lax.axis_index("seq")
        self.y, self.z = lax.div(seq, GRID), lax.rem(seq, GRID)
        blocks = log_ref.shape[1] // LANES // PARTS
        log_rows[...] = jnp.zeros_like(log_rows)
        for part in range(PARTS):
            for b in range(blocks):
                lanes = pl.ds((part * blocks + b) * LANES, LANES)
                for n in range(GRID * GRID):
                    log_rows[part, n // GRID, n % GRID, b : b + 1, :] = log_ref[n : n + 1, lanes]
        self.flying = {}
        barrier = pltpu.get_barrier_semaphore()
        peers = [self.across(k) for k in range(1, GRID)] + [self.along(k) for k in range(1, GRID)]
        peers += [self.onward(1), self.onward(-1)] + list(others)
        for peer in peers:
            pl.semaphore_signal(barrier, inc=1, device_id=peer, device_id_type=pl.DeviceIdType.MESH)
        self.peers = len(peers)

    def onward(self, k):
        size = GRID * GRID
        return {"seq": lax.rem(self.y * GRID + self.z + k + size, size)}

    def across(self, k):
        return {"seq": self.y * GRID + lax.rem(self.z + k, GRID)}

    def along(self, k):
        return {"seq": lax.rem(self.y + k, GRID) * GRID + self.z}

    def meet(self):
        pl.semaphore_wait(pltpu.get_barrier_semaphore(), self.peers)

    def send(self, part, phase, k, source, target, peer):
        copy = pltpu.make_async_remote_copy(
            src_ref=source, dst_ref=target, send_sem=self.sends.at[part, phase, k], recv_sem=self.arrivals.at[part, phase, k],
            device_id=peer, device_id_type=pl.DeviceIdType.MESH,
        )
        copy.start()
        self.flying.setdefault((part, phase), []).append(copy)

    def land(self, part, phase):
        for copy in self.flying[part, phase]:
            copy.wait()

    def order(self):
        return range(GRID - 1, -1, -1) if self.later else range(GRID)

    def rate(self, part):
        return -LOG2E * jnp.exp(self.log_rows[part, self.z])

    def first(self, part):
        for k in range(1, GRID):
            peer = lax.rem(self.z + k, GRID)
            self.send(part, 0, k, self.message.at[part, peer], self.got.at[part, k], self.across(k))
        self.got[part, 0] = self.message[part, self.z]

    def second(self, part):
        self.land(part, 0)
        rate = self.rate(part)
        state, span = jnp.zeros(rate.shape, jnp.float32), jnp.zeros(rate.shape[1:], jnp.float32)
        for z in self.order():
            block = self.got[part, lax.rem(self.z - z + GRID, GRID)]
            state = jnp.exp2(rate * block[GRID]) * state + block[:GRID]
            span = span + block[GRID]
        self.row[part, :GRID] = state
        self.row[part, GRID] = span
        for k in range(1, GRID):
            self.send(part, 1, k, self.row.at[part], self.rows_got.at[part, k], self.along(k))
        self.rows_got[part, 0] = self.row[part]

    def third(self, part):
        self.land(part, 1)
        rate = self.rate(part)
        state = jnp.zeros(rate.shape, jnp.float32)
        for y in self.order():
            self.above[part, y] = state
            block = self.rows_got[part, lax.rem(self.y - y + GRID, GRID)]
            state = jnp.exp2(rate * block[GRID]) * state + block[:GRID]
        state = self.above[part, self.y]
        for z in self.order():
            self.made[part, z] = state
            block = self.got[part, lax.rem(self.z - z + GRID, GRID)]
            state = jnp.exp2(rate * block[GRID]) * state + block[:GRID]
        for k in range(1, GRID):
            peer = lax.rem(self.z + k, GRID)
            self.send(part, 2, k, self.made.at[part, peer], self.in_ref.at[part, self.z], self.across(k))
        self.in_ref[part, self.z] = self.made[part, self.z]

    def done(self, part):
        self.land(part, 2)


def staged(relay, summary, extra, scan):
    summary(0)
    relay.first(0)
    summary(1)
    relay.first(1)
    relay.second(0)
    summary(2)
    relay.first(2)
    relay.third(0)
    relay.second(1)
    extra()
    relay.second(2)
    relay.third(1)
    relay.done(0)
    scan(0)
    relay.third(2)
    relay.done(1)
    scan(1)
    relay.done(2)
    scan(2)


def named_experts(slots, rows):
    first = (lax.broadcasted_iota(jnp.int32, (rows, EXPERTS), 1) * CAPACITY).astype(jnp.float32)
    return jnp.where((slots >= first) & (slots < first + CAPACITY), 1.0, 0.0)


def seated_rows(slots, rows, seats):
    seat = lax.broadcasted_iota(jnp.int32, (rows, seats), 1).astype(jnp.float32)
    return jnp.where(seat == slots, 1.0, 0.0).astype(jnp.bfloat16)


def slots_of(routes, rows):
    expert = lax.broadcasted_iota(jnp.int32, (rows, EXPERTS), 1)
    named = jnp.where(expert == routes, 1.0, 0.0)
    later = lax.broadcasted_iota(jnp.int32, (rows, rows), 0) > lax.broadcasted_iota(jnp.int32, (rows, rows), 1)
    ahead = jnp.dot(jnp.where(later, 1.0, 0.0).astype(jnp.bfloat16), named.astype(jnp.bfloat16), preferred_element_type=jnp.float32)
    return jnp.sum(named * (ahead + (expert * CAPACITY).astype(jnp.float32)), axis=1, keepdims=True)


def mixer_kernel(
    token_ref, up_ref, row_ref, in_hbm, tap_ref, select_ref, step_weight_ref, log_ref, out_hbm, router_ref, route_ref,
    normed_out, gate_out, padded_out, pre_out, conv_out, raw_out, step_out, sel_out, entry_out, mixer_out, gated_out,
    middle_out, normed_mid_out, probs_out, chosen_out, leaving_out, slot_out, up_out,
    normed, in_ref, out_ref, padded, gate, pre, conv, raw, step, sel, entry, mixer, gated, middle, normed_mid, probs, chosen, leaving, slots, up_seated,
    tail, tail_got, part_ref, span_ref, wide_in, wide_out, loads, saves, passing, goes, comes, log_rows, relay_in, *relayed
):
    rows, width = step.shape
    model = token_ref.shape[1]
    tap_bias_ref, step_bias_ref, skip_ref = (row_ref.at[k : k + 1] for k in range(3))
    gain_ref, second_gain_ref = row_ref.at[3:4, :model], row_ref.at[3:4, model:]
    taps, states = tap_ref.shape[0], log_ref.shape[0]
    reach = (taps - 1) * SEGS
    rank = SELECTED - 2 * states
    pieces = in_ref.shape[0]
    cut = in_ref.shape[2]
    blocks = width // LANES

    loading = [pltpu.make_async_copy(in_hbm.at[:, pl.ds(k * cut, cut)], in_ref.at[k], loads.at[k]) for k in range(pieces)]
    loading.append(pltpu.make_async_copy(out_hbm, out_ref, loads.at[pieces]))
    for copy in loading:
        copy.start()
    saving = []

    def save(source, target):
        copy = pltpu.make_async_copy(source, target, saves.at[len(saving)])
        copy.start()
        saving.append(copy)

    relay = Relay(False, log_ref, log_rows, relay_in, *relayed, others=[{"expert": peer} for peer in expert_peers()])

    stream = token_ref[...].astype(jnp.float32)
    normed[...] = (stream * rms_scale(stream) * gain_ref[...]).astype(jnp.bfloat16)
    save(normed, normed_out)
    for k in range(pieces // 2):
        loading[k].wait()
        padded[reach:, k * cut : (k + 1) * cut] = jnp.dot(normed[...], in_ref[k], preferred_element_type=jnp.float32)
    tail[...] = jnp.zeros_like(tail)
    for k in range(taps - 1):
        row = reach + rows - (taps - 1 - k) * SEGS + SEGS - 1
        tail[k : k + 1, :] = padded[row : row + 1, :]
    slot = slots_of(route_ref[...], rows)
    slots[...] = jnp.broadcast_to(slot, slots.shape)
    save(slots, slot_out)
    seating = seated_rows(slot, rows, leaving.shape[0])
    up_seated[...] = column_dot(seating, up_ref[...]).astype(jnp.bfloat16)
    relay.meet()
    handing = pltpu.make_async_remote_copy(
        src_ref=tail, dst_ref=tail_got, send_sem=passing.at[0], recv_sem=passing.at[1],
        device_id=relay.onward(1), device_id_type=pl.DeviceIdType.MESH,
    )
    handing.start()
    trading = trade(up_seated, up_out, goes, comes)
    for k in range(pieces // 2, pieces):
        loading[k].wait()
        spot = slice((k - pieces // 2) * cut, (k - pieces // 2 + 1) * cut)
        gate[:, spot] = jnp.dot(normed[...], in_ref[k], preferred_element_type=jnp.float32)
    save(gate, gate_out)
    handing.wait()
    started = jnp.where(lax.axis_index("seq") > 0, 1.0, 0.0)
    for k in range(taps - 1):
        row = rows + k * SEGS
        segment = lax.broadcasted_iota(jnp.int32, (SEGS, width), 0)
        before = pltpu.roll(padded[row : row + SEGS, :], 1, 0)
        padded[k * SEGS : (k + 1) * SEGS, :] = jnp.where(segment == 0, started * tail_got[k : k + 1, :], before)
    save(padded, padded_out)

    sel[...] = jnp.zeros_like(sel)

    def convolve(b, unused):
        lanes = lanes_of(b)
        value = tap_bias_ref[:, lanes]
        for k in range(taps):
            value = value + tap_ref[k : k + 1, lanes] * padded[k * SEGS : k * SEGS + rows, lanes]
        pre[:, lanes] = value
        value = value * jax.nn.sigmoid(value)
        conv[:, lanes] = value
        sel[:, :SELECTED] += jnp.dot(value.astype(jnp.bfloat16), select_ref[lanes, :], preferred_element_type=jnp.float32)
        return unused

    lax.fori_loop(0, blocks, convolve, 0)
    save(pre, pre_out)
    save(conv, conv_out)
    save(sel, sel_out)
    step_low = sel[:, :rank].astype(jnp.bfloat16)

    def size(b, unused):
        lanes = lanes_of(b)
        value = jnp.dot(step_low, step_weight_ref[:, lanes], preferred_element_type=jnp.float32) + step_bias_ref[:, lanes]
        raw[:, lanes] = value
        step[:, lanes] = jnp.maximum(value, 0.0) + jnp.log1p(jnp.exp(-jnp.abs(value)))
        return unused

    lax.fori_loop(0, blocks, size, 0)
    save(raw, raw_out)
    save(step, step_out)
    fill_maps(sel, wide_in, rank)

    def summary(part):
        summarize(False, part, step, conv, wide_in, log_ref, part_ref, span_ref, relay.message.at[part])

    def scan(part):
        scan_part(part, step, conv, wide_in, wide_out, log_ref, part_ref, span_ref, relay_in.at[part], mixer, entry)

    staged(relay, summary, lambda: fill_maps(sel, wide_out, rank + states), scan)
    save(entry, entry_out)

    def blend(b, unused):
        lanes = lanes_of(b)
        value = mixer[:, lanes] + skip_ref[:, lanes] * conv[:, lanes]
        mixer[:, lanes] = value
        opening = gate[:, lanes]
        gated[:, lanes] = (value * (opening * jax.nn.sigmoid(opening))).astype(jnp.bfloat16)
        return unused

    lax.fori_loop(0, blocks, blend, 0)
    save(mixer, mixer_out)
    save(gated, gated_out)
    loading[pieces].wait()
    value = token_ref[...].astype(jnp.float32) + jnp.dot(gated[...], out_ref[...], preferred_element_type=jnp.float32)
    middle[...] = value
    save(middle, middle_out)
    normed_mid[...] = (value * rms_scale(value) * second_gain_ref[...]).astype(jnp.bfloat16)
    save(normed_mid, normed_mid_out)
    logits = jnp.dot(normed_mid[...], router_ref[...], preferred_element_type=jnp.float32)
    grown = jnp.exp(logits - jnp.max(logits, axis=1, keepdims=True))
    probs[...] = grown / jnp.sum(grown, axis=1, keepdims=True)
    save(probs, probs_out)
    gate_value = jnp.sum(named_experts(slots[:, 0:1], rows) * probs[...], axis=1, keepdims=True)
    chosen[...] = jnp.broadcast_to(gate_value, (rows, LANES))
    save(chosen, chosen_out)
    place = lax.broadcasted_iota(jnp.int32, (rows, LANES), 1)
    parts = jnp.zeros((rows, LANES), jnp.float32)
    for k, piece in enumerate(three_parts(gate_value)):
        parts = jnp.where(place == k, piece.astype(jnp.float32), parts)
    seating = seated_rows(slots[:, 0:1], rows, leaving.shape[0])
    leaving[:, :model] = column_dot(seating, normed_mid[...]).astype(jnp.bfloat16)
    leaving[:, model:] = column_dot(seating, parts.astype(jnp.bfloat16)).astype(jnp.bfloat16)
    save(leaving, leaving_out)
    for copy in saving + trading:
        copy.wait()


def mixer_back_kernel(
    back_hbm, slot_ref, probs_ref, chosen_ref, normed_ref, router_ref, middle_ref, up_ref, out_hbm, gate_hbm,
    mixer_hbm, conv_hbm, step_hbm, raw_hbm, sel_ref, pre_hbm, padded_hbm, entry_hbm, log_ref, step_weight_ref, select_ref,
    tap_ref, packed_ref, in_hbm, token_ref, value_hbm,
    low_out, gate_out, conv_out, left_out, right_out, narrow_out, token_out, value_out,
    back, out_ref, gate, mixer, conv, step, raw, padded, entry, in_ref,
    middle_low, grad_gate, grad_conv, left, right, narrow, grad_middle, mixed, low, gsel, glog, gbias, total, tail, tail_got, row_ref,
    part_ref, span_ref, wide_in, wide_out, sum_in, sum_out, states_ref, decays_ref, raw_sum, raw_rows,
    loads, saves, passing, goes, comes, log_rows, relay_in, *relayed
):
    rows, width = step.shape
    model = up_ref.shape[1]
    skip_ref, gain_ref, second_gain_ref = packed_ref.at[2:3], packed_ref.at[3:4, :model], packed_ref.at[3:4, model:]
    taps, states = tap_ref.shape[0], log_ref.shape[0]
    rank = SELECTED - 2 * states
    held, cut = in_ref.shape[0], in_ref.shape[2]
    blocks = width // LANES
    saving, numbers = [], iter(range(64))

    def load(source, target):
        copy = pltpu.make_async_copy(source, target, loads.at[next(numbers)])
        copy.start()
        return copy

    def save(source, target):
        copy = pltpu.make_async_copy(source, target, saves.at[len(saving)])
        copy.start()
        saving.append(copy)

    def weight(k):
        return load(in_hbm.at[:, pl.ds(k * cut, cut)], in_ref.at[k % held])

    early = [load(back_hbm, back), load(out_hbm, out_ref), load(gate_hbm, gate), load(mixer_hbm, mixer)]
    scanning = [load(step_hbm, step), load(conv_hbm, conv), load(raw_hbm, raw), load(entry_hbm, entry)]
    padding = load(padded_hbm, padded)
    weights = {k: weight(k) for k in range(held, 2 * held)}
    relay = Relay(True, log_ref, log_rows, relay_in, *relayed, others=[{"expert": peer} for peer in expert_peers()])

    early[0].wait()
    slots = slot_ref[:, 0:1]
    seating = seated_rows(slots, rows, back.shape[0])
    chosen = chosen_ref[:, 0:1]
    along = jnp.sum(jnp.dot(seating, back[:, model:], preferred_element_type=jnp.float32), axis=1, keepdims=True)
    place = lax.broadcasted_iota(jnp.int32, (rows, LANES), 1)
    logits = (along * chosen * (named_experts(slots, rows) - probs_ref[...])).astype(jnp.bfloat16)
    grad = transposed_dot(logits, router_ref[...]) + chosen * jnp.dot(seating, back[:, :model], preferred_element_type=jnp.float32)
    narrow[...] = jnp.zeros_like(narrow)
    narrow[2 : 2 + EXPERTS, :] = column_dot(logits, normed_ref[...])
    value = middle_ref[...]
    returned, gained = rms_back(value, rms_scale(value), second_gain_ref[...], grad)
    narrow[1:2, :] = gained[None, :]
    value = up_ref[...].astype(jnp.float32) + returned
    grad_middle[...] = value
    middle_low[...] = value.astype(jnp.bfloat16)
    save(middle_low, low_out)
    for copy in early[1:]:
        copy.wait()

    def open_gate(b, unused):
        lanes = lanes_of(b)
        grown = transposed_dot(middle_low[...], out_ref[lanes, :])
        opening = gate[:, lanes]
        mixed[:, lanes] = grown * (opening * jax.nn.sigmoid(opening))
        grad_gate[:, lanes] = (grown * mixer[:, lanes] * silu_slope(opening)).astype(jnp.bfloat16)
        return unused

    lax.fori_loop(0, blocks, open_gate, 0)
    save(grad_gate, gate_out)
    pre, gconv = gate, mixer
    activating = load(pre_hbm, pre)
    for copy in scanning:
        copy.wait()

    fill_maps(sel_ref, wide_out, rank + states)

    def summary(part):
        summarize(True, part, step, mixed, wide_out, log_ref, part_ref, span_ref, relay.message.at[part])

    def prepare():
        fill_maps(sel_ref, wide_in, rank)
        sum_in[...] = jnp.zeros_like(sum_in)
        sum_out[...] = jnp.zeros_like(sum_out)
        raw_sum[...] = jnp.zeros_like(raw_sum)

    def scan(part):
        retreat_part(
            part, step, conv, mixed, raw, wide_in, wide_out, log_ref, step_weight_ref, entry, part_ref, span_ref,
            relay_in.at[part], low, gconv, glog, gbias, sum_in, sum_out, states_ref, decays_ref, raw_sum, raw_rows,
        )

    relay.meet()
    trading = trade(value_hbm, value_out, goes, comes)
    staged(relay, summary, prepare, scan)
    maps = gather_maps(sum_in, rank) + gather_maps(sum_out, rank + states)
    gsel[...] = (raw_sum[...] + maps).astype(jnp.bfloat16)

    activating.wait()
    padding.wait()
    step_low = jnp.where(place < rank, sel_ref[...], 0.0).astype(jnp.bfloat16)
    tall = lax.broadcasted_iota(jnp.int32, (row_ref.shape[0], LANES), 0)
    spots = jnp.where(lax.broadcasted_iota(jnp.int32, tall.shape, 1) == tall + SELECTED, 1.0, 0.0).astype(jnp.bfloat16)
    row_ref[...] = jnp.zeros_like(row_ref)

    def convolve_back(b, unused):
        lanes = lanes_of(b)
        around, kept = mixed[:, lanes], conv[:, lanes]
        grown = transposed_dot(gsel[:, :SELECTED], select_ref[lanes, :]) + gconv[:, lanes] + skip_ref[:, lanes] * around
        grown = grown * silu_slope(pre[:, lanes])
        gconv[:, lanes] = grown
        row_ref[:states, :] = glog[:, lanes]
        for k in range(taps):
            row_ref[states + k : states + k + 1, :] = jnp.sum(
                grown * padded[k * SEGS : k * SEGS + rows, lanes], axis=0, keepdims=True
            )
        row_ref[states + taps : states + taps + 1, :] = jnp.sum(grown, axis=0, keepdims=True)
        row_ref[states + taps + 1 : states + taps + 2, :] = gbias[:, lanes]
        row_ref[states + taps + 2 : states + taps + 3, :] = jnp.sum(around * kept, axis=0, keepdims=True)
        summed = column_dot(kept.astype(jnp.bfloat16), gsel[...])
        for piece in three_parts(row_ref[...]):
            summed = summed + column_dot(piece, spots)
        left[lanes, :] = summed
        right[lanes, :] = column_dot(low[:, lanes], step_low)
        return unused

    lax.fori_loop(0, blocks, convolve_back, 0)
    save(left, left_out)
    save(right, right_out)

    tail[...] = jnp.zeros_like(tail)
    for k in range(taps - 1):
        tail[k : k + 1, :] = gconv[k * SEGS : k * SEGS + 1, :]
    handing = pltpu.make_async_remote_copy(
        src_ref=tail, dst_ref=tail_got, send_sem=passing.at[0], recv_sem=passing.at[1],
        device_id=relay.onward(-1), device_id_type=pl.DeviceIdType.MESH,
    )
    handing.start()
    for k in range(held):
        weights[held + k].wait()
        summed = transposed_dot(grad_gate[:, k * cut : (k + 1) * cut], in_ref[k])
        total[...] = summed if k == 0 else total[...] + summed
        weights[k] = weight(k)
    handing.wait()
    goes_on = jnp.where(lax.axis_index("seq") < GRID * GRID - 1, 1.0, 0.0)
    segment = lax.broadcasted_iota(jnp.int32, (SEGS, cut), 0)
    for k in range(held):
        spot = slice(k * cut, (k + 1) * cut)
        grown = None
        for t in range(taps):
            late = taps - 1 - t
            shifted = gconv[late * SEGS :, spot]
            if late:
                wrapped = [
                    jnp.where(
                        segment == SEGS - 1,
                        goes_on * tail_got[j : j + 1, spot],
                        pltpu.roll(gconv[j * SEGS : (j + 1) * SEGS, spot], SEGS - 1, 0),
                    )
                    for j in range(late)
                ]
                shifted = jnp.concatenate([shifted] + wrapped, axis=0)
            term = tap_ref[t : t + 1, spot] * shifted
            grown = term if grown is None else grown + term
        grad_conv[:, spot] = grown.astype(jnp.bfloat16)
        weights[k].wait()
        total[...] += transposed_dot(grad_conv[:, spot], in_ref[k])
    save(grad_conv, conv_out)
    stream = token_ref[...].astype(jnp.float32)
    returned, gained = rms_back(stream, rms_scale(stream), gain_ref[...], total[...])
    narrow[0:1, :] = gained[None, :]
    total[...] = grad_middle[...] + returned
    save(narrow, narrow_out)
    save(total, token_out)
    for copy in saving + trading:
        copy.wait()


WHOLE = pl.BlockSpec(memory_space=pltpu.VMEM)


def shaped(*dims, dtype=jnp.float32):
    return jax.ShapeDtypeStruct(dims, dtype)


def roomy(mebibytes, **more):
    return pltpu.CompilerParams(vmem_limit_bytes=mebibytes << 20, **more)


def busy(elements):
    return pl.CostEstimate(flops=4096 * elements, bytes_accessed=16 * elements, transcendentals=4 * elements)


def wide_scratch(rows, states, extra=0):
    return pltpu.VMEM((rows // SEGS + extra, states, SEGS, LANES), jnp.float32)


def chain_scratch(states, width):
    return [pltpu.VMEM((states, SEGS, width), jnp.float32), pltpu.VMEM((SEGS, width), jnp.float32)]


def relay_scratch():
    def kept(*dims):
        return pltpu.VMEM((PARTS,) + dims + (SEGS, LANES), jnp.float32)

    return [
        kept(GRID, GRID),
        kept(GRID, GRID),
        kept(GRID, GRID + 1),
        kept(GRID, GRID + 1),
        kept(GRID + 1),
        kept(GRID, GRID + 1),
        kept(GRID, GRID),
        kept(GRID, GRID),
        pltpu.SemaphoreType.DMA((PARTS, 3, GRID)),
        pltpu.SemaphoreType.DMA((PARTS, 3, GRID)),
    ]


def mixer(tokens, upstream, packed, in_weight, taps, select, step_weight, decay_log, out_weight, router, routes, seats):
    rows, model = tokens.shape
    states, width = decay_log.shape
    reach = (taps.shape[0] - 1) * SEGS
    bf16, f32 = jnp.bfloat16, jnp.float32
    anywhere = pl.BlockSpec(memory_space=pl.ANY)
    results = [
        ((rows, model), bf16),
        ((rows, width), f32),
        ((rows + reach, width), f32),
        ((rows, width), f32),
        ((rows, width), f32),
        ((rows, width), f32),
        ((rows, width), f32),
        ((rows, LANES), f32),
        ((states, SEGS, width), f32),
        ((rows, width), f32),
        ((rows, width), bf16),
        ((rows, model), f32),
        ((rows, model), bf16),
        ((rows, EXPERTS), f32),
        ((rows, LANES), f32),
        ((seats, model + LANES), bf16),
        ((rows, LANES), f32),
        ((seats, model), bf16),
    ]
    kept = [pltpu.VMEM(dims, dtype) for dims, dtype in results]
    weights = [pltpu.VMEM((2 * width // CUT, model, CUT), bf16), pltpu.VMEM(out_weight.shape, bf16)]
    relayed = relay_scratch()
    return pl.pallas_call(
        mixer_kernel,
        out_shape=tuple(shaped(*dims, dtype=dtype) for dims, dtype in results),
        in_specs=[WHOLE] * 3 + [anywhere] + [WHOLE] * 4 + [anywhere] + [WHOLE] * 2,
        out_specs=(anywhere,) * len(results),
        scratch_shapes=kept[:1]
        + weights
        + [kept[2], kept[1]]
        + kept[3:]
        + [pltpu.VMEM((SEGS, width), f32)] * 2
        + chain_scratch(states, width)
        + [wide_scratch(rows, states)] * 2
        + [
            pltpu.SemaphoreType.DMA((2 * width // CUT + 1,)),
            pltpu.SemaphoreType.DMA((len(results),)),
            pltpu.SemaphoreType.DMA((2,)),
            pltpu.SemaphoreType.DMA((EXPERTS,)),
            pltpu.SemaphoreType.DMA((EXPERTS,)),
        ]
        + relayed,
        compiler_params=roomy(60, collective_id=0, has_side_effects=True),
        cost_estimate=busy(rows * states * width),
        name="mixer",
    )(tokens, upstream, packed, in_weight, taps, select, step_weight, decay_log, out_weight, router, routes)


def mixer_back(
    back, slots, probs, chosen, normed, router, middle, up, out_weight, gate, mixed, conv, step, raw, selection, pre, padded, entry,
    decay_log, step_weight, select, taps, packed, in_weight, tokens, value,
):
    rows, width = step.shape
    model = tokens.shape[1]
    states = decay_log.shape[0]
    bf16, f32 = jnp.bfloat16, jnp.float32
    anywhere = pl.BlockSpec(memory_space=pl.ANY)
    held = width // CUT
    tall = ((rows, width), f32)
    results = [
        ((rows, model), bf16),
        ((rows, width), bf16),
        ((rows, width), bf16),
        ((width, LANES), f32),
        ((width, LANES), f32),
        ((16, model), f32),
        ((rows, model), f32),
        (value.shape, bf16),
    ]
    streamed = (0, 8, 9, 10, 11, 12, 13, 15, 16, 17, 23, 25)
    kept = (
        [(back.shape, bf16), (out_weight.shape, bf16)]
        + [tall] * 5
        + [(padded.shape, f32), (entry.shape, f32), ((held, model, CUT), bf16)]
        + results[:6]
        + [((rows, model), f32), tall, ((rows, width), bf16), ((rows, LANES), bf16), ((states, width), f32), ((1, width), f32)]
        + [((rows, model), f32), ((SEGS, width), f32), ((SEGS, width), f32), ((24, LANES), f32)]
    )
    return pl.pallas_call(
        mixer_back_kernel,
        out_shape=tuple(shaped(*dims, dtype=dtype) for dims, dtype in results),
        in_specs=[anywhere if k in streamed else WHOLE for k in range(26)],
        out_specs=(anywhere,) * len(results),
        scratch_shapes=[pltpu.VMEM(dims, dtype) for dims, dtype in kept]
        + chain_scratch(states, width)
        + [wide_scratch(rows, states)] * 4
        + [wide_scratch(rows, states, 1), wide_scratch(rows, states)]
        + [pltpu.VMEM((rows, LANES), f32)] * 2
        + [pltpu.SemaphoreType.DMA((10 + 2 * held,)), pltpu.SemaphoreType.DMA((len(results),)), pltpu.SemaphoreType.DMA((2,))]
        + [pltpu.SemaphoreType.DMA((EXPERTS,))] * 2
        + relay_scratch(),
        compiler_params=roomy(62, collective_id=1, has_side_effects=True),
        cost_estimate=busy(rows * states * width),
        name="mixer_back",
    )(
        back, slots, probs, chosen, normed, router, middle, up, out_weight, gate, mixed, conv, step, raw, selection, pre, padded, entry,
        decay_log, step_weight, select, taps, packed, in_weight, tokens, value,
    )


def segmented(block):
    rows = block.shape[0]
    return block.reshape(SEGS, rows // SEGS, -1).transpose(1, 0, 2).reshape(rows, -1)


def in_order(block):
    rows = block.shape[0]
    return block.reshape(rows // SEGS, SEGS, -1).transpose(1, 0, 2).reshape(rows, -1)


def rms_scale(stream):
    return lax.rsqrt(jnp.mean(stream * stream, axis=-1, keepdims=True) + 1e-05)


def rms_back(stream, scale, gain, grad):
    grown = grad * gain
    along = jnp.mean(stream * grown, axis=-1, keepdims=True)
    return scale * grown - stream * (scale * scale * scale * along), jnp.sum(grad * stream * scale, axis=0)


def silu_slope(value):
    gate = jax.nn.sigmoid(value)
    return gate * (1.0 + value * (1.0 - gate))


def product(left, right):
    return jnp.dot(left, right, preferred_element_type=jnp.float32)


def across(left, right):
    return jnp.einsum("tk,dk->td", left, right, preferred_element_type=jnp.float32)


def summed_rows(left, right):
    return jnp.einsum("tk,td->kd", left, right, preferred_element_type=jnp.float32)


CHUNK = 512
GELU_OUT = math.sqrt(2.0 / math.pi)
GELU_IN = 0.044715


def transposed_dot(left, right):
    return lax.dot_general(left, right, (((1,), (1,)), ((), ())), preferred_element_type=jnp.float32)


def column_dot(left, right):
    return lax.dot_general(left, right, (((0,), (0,)), ((), ())), preferred_element_type=jnp.float32)


def three_parts(value):
    parts, left = [], value
    for unused in range(3):
        part = left.astype(jnp.bfloat16)
        left = left - part.astype(jnp.float32)
        parts.append(part)
    return parts


def experts_kernel(
    leaving_hbm, up_ref, first_hbm, second_hbm, back_out, value_out, sums_out,
    received, first, second, pull, active, grad, value, sent, back, scaled_received, scaled_up, staged_sums,
    loads, saves, goes, comes, returns, arrives,
):
    rows, width = up_ref.shape
    hidden = second.shape[0]
    barrier = pltpu.get_barrier_semaphore()
    for peer in expert_peers():
        pl.semaphore_signal(barrier, inc=1, device_id={"expert": peer}, device_id_type=pl.DeviceIdType.MESH)
    loading = [
        pltpu.make_async_copy(second_hbm, second, loads.at[0]),
        pltpu.make_async_copy(first_hbm, first, loads.at[1]),
    ]
    for copy in loading:
        copy.start()
    pl.semaphore_wait(barrier, EXPERTS - 1)
    arriving = trade(leaving_hbm, received, goes, comes)
    loading[0].wait()

    def pulled(i, unused):
        cols = pl.ds(pl.multiple_of(i * CHUNK, CHUNK), CHUNK)
        pull[:, cols] = transposed_dot(up_ref[...], second[cols, :]).astype(jnp.bfloat16)
        return unused

    lax.fori_loop(0, hidden // CHUNK, pulled, 0)
    loading[1].wait()
    for copy in arriving:
        copy.wait()

    def layer(i, unused):
        cols = pl.ds(pl.multiple_of(i * CHUNK, CHUNK), CHUNK)
        pre = jnp.dot(received[:, :width], first[:, cols], preferred_element_type=jnp.float32)
        square = pre * pre
        bent = jnp.tanh(pre * (GELU_OUT + GELU_OUT * GELU_IN * square))
        share = 0.5 + 0.5 * bent
        slope = share + pre * (0.5 - 0.5 * bent * bent) * (GELU_OUT + 3.0 * GELU_OUT * GELU_IN * square)
        active[:, cols] = (pre * share).astype(jnp.bfloat16)
        grad[:, cols] = (slope * pull[:, cols].astype(jnp.float32)).astype(jnp.bfloat16)
        return unused

    lax.fori_loop(0, hidden // CHUNK, layer, 0)
    value[...] = jnp.dot(active[...], second[...], preferred_element_type=jnp.float32).astype(jnp.bfloat16)
    saving = [pltpu.make_async_copy(value, value_out, saves.at[0])]
    saving[0].start()
    sent[:, :width] = transposed_dot(grad[...], first[...]).astype(jnp.bfloat16)
    along = jnp.sum(value[...].astype(jnp.float32) * up_ref[...].astype(jnp.float32), axis=1, keepdims=True)
    place = lax.broadcasted_iota(jnp.int32, (rows, LANES), 1)
    tail = jnp.zeros(place.shape, jnp.float32)
    for k, part in enumerate(three_parts(along)):
        tail = jnp.where(place == k, part.astype(jnp.float32), tail)
    sent[:, width:] = tail.astype(jnp.bfloat16)
    returning = trade(sent, back, returns, arrives)

    parts = received[:, width:].astype(jnp.float32)
    gate = parts[:, 0:1] + parts[:, 1:2] + parts[:, 2:3]
    scaled_received[...] = (received[:, :width].astype(jnp.float32) * gate).astype(jnp.bfloat16)
    scaled_up[...] = (up_ref[...].astype(jnp.float32) * gate).astype(jnp.bfloat16)
    half = sums_out.shape[2]
    pairs = hidden // half // 2

    def stored(i, slot):
        return pltpu.make_async_copy(staged_sums.at[slot], sums_out.at[pl.ds(2 * i, 2)], saves.at[1 + slot])

    def sums(i, unused):
        slot = lax.rem(i, 2)
        cols = pl.ds(pl.multiple_of(i * 2 * half, 2 * half), 2 * half)

        @pl.when(i >= 2)
        def free():
            stored(i - 2, slot).wait()

        for which, (left, right) in enumerate(((grad, scaled_received), (active, scaled_up))):
            total = column_dot(left[:, cols], right[...]).astype(jnp.bfloat16)
            for k in range(2):
                staged_sums[slot, k, which] = total[k * half : (k + 1) * half]
        stored(i, slot).start()
        return unused

    lax.fori_loop(0, pairs, sums, 0)
    for i in (pairs - 2, pairs - 1):
        stored(i, i % 2).wait()
    for copy in returning:
        copy.wait()
    last = pltpu.make_async_copy(back, back_out, saves.at[3])
    last.start()
    last.wait()
    saving[0].wait()


def expert_pass(leaving, upstream, first, second, owners):
    rows, width = upstream.shape
    hidden = second.shape[0]
    wide = leaving.shape[1]
    bf16 = jnp.bfloat16
    half = hidden // owners
    anywhere = pl.BlockSpec(memory_space=pl.ANY)

    def kept(*dims):
        return pltpu.VMEM(dims, bf16)

    return pl.pallas_call(
        experts_kernel,
        out_shape=(
            shaped(rows, wide, dtype=bf16),
            shaped(rows, width, dtype=bf16),
            shaped(owners, 2, half, width, dtype=bf16),
        ),
        in_specs=[anywhere, WHOLE, anywhere, anywhere],
        out_specs=(anywhere,) * 3,
        scratch_shapes=[
            kept(rows, wide),
            kept(width, hidden),
            kept(hidden, width),
            kept(rows, hidden),
            kept(rows, hidden),
            kept(rows, hidden),
            kept(rows, width),
            kept(rows, wide),
            kept(rows, wide),
            kept(rows, width),
            kept(rows, width),
            kept(2, 2, 2, half, width),
            pltpu.SemaphoreType.DMA((2,)),
            pltpu.SemaphoreType.DMA((4,)),
        ]
        + [pltpu.SemaphoreType.DMA((EXPERTS,))] * 4,
        compiler_params=roomy(60, collective_id=3, has_side_effects=True),
        cost_estimate=pl.CostEstimate(flops=12 * rows * hidden * width, bytes_accessed=8 * hidden * width, transcendentals=rows * hidden),
        name="experts",
    )(leaving, upstream, first, second)


ORDERS = ("xyz", "yzx", "zxy")
PIECE = 16


def shares_kernel(
    conv_cols, gate_cols, token_ref, out_cols, middle_ref, left_ref, right_ref, narrow_ref,
    in_out, out_out, left_out, right_out, narrow_out, sum_ref, in_ref, out_ref, made, taken,
    half_a, half_b, half_c, one_a, one_b, one_c, sends, arrivals):
    seq, expert = lax.axis_index("seq"), lax.axis_index("expert")
    core = lax.rem(expert, 2)
    place = {"y": lax.div(seq, 4), "z": lax.rem(seq, 4), "x": lax.div(expert, 2)}
    third = token_ref.shape[1] // len(ORDERS)
    streams = [(L, q) for L in range(len(ORDERS)) for q in range(4)]

    def flip(i):
        return i + 1 - 2 * lax.rem(i, 2)

    def device(**moved):
        at = dict(place, **moved)
        return {"seq": at["y"] * 4 + at["z"], "expert": at["x"] * 2 + at.get("core", core)}

    partners = [device(core=1 - core)]
    for axis in "xyz":
        partners += [device(**{axis: flip(place[axis])}), device(**{axis: 3 - place[axis]})]
    barrier = pltpu.get_barrier_semaphore()
    for partner in partners:
        pl.semaphore_signal(barrier, inc=1, device_id=partner, device_id_type=pl.DeviceIdType.MESH)
    pl.semaphore_wait(barrier, len(partners))

    def send(source, target, partner, stream, number):
        k = streams.index(stream)
        copy = pltpu.make_async_remote_copy(
            src_ref=source, dst_ref=target, send_sem=sends.at[k, number], recv_sem=arrivals.at[k, number],
            device_id=partner, device_id_type=pl.DeviceIdType.MESH,
        )
        copy.start()
        return copy

    def add(target, source, unit):
        def step(i, unused):
            target[i] = target[i] + source[i]
            return unused

        lax.fori_loop(0, unit, step, 0, unroll=min(unit, 8))

    inner = out_cols.shape[1]
    for source, target, base in ((conv_cols, in_ref, 0), (gate_cols, in_ref, inner), (out_cols, out_ref, 0)):

        def turn_over(k, unused, source=source, target=target, base=base):
            spot = pl.ds(pl.multiple_of(k * LANES, LANES), LANES)
            target[pl.ds(pl.multiple_of(base + k * LANES, LANES), LANES), :] = source[:, spot].T
            return unused

        lax.fori_loop(0, source.shape[1] // LANES, turn_over, 0)

    halves, ones = (half_a, half_b, half_c), (one_a, one_b, one_c)
    pending, holding = {}, {}

    def set_out(L):
        for q in range(4):
            for copy in pending[L, q]:
                copy.wait()
            add(taken.at[L, q], made.at[L, 4 * core + q], 64)
            holding[L, q] = taken.at[L, q]
            pending[L, q] = start_halves(L, q, 0, holding[L, q], halves, place, flip, device, send)

    for L, order in enumerate(ORDERS):
        lanes = pl.ds(L * third, third)
        narrow = narrow_ref[:, lanes].astype(jnp.bfloat16)

        def block(s, unused):
            y, z = lax.div(s, 4), lax.rem(s, 4)
            by_in = jnp.dot(
                in_ref[pl.ds(pl.multiple_of(s * 288, 16), 288), :], token_ref[:, lanes], preferred_element_type=jnp.float32
            ).astype(jnp.bfloat16)
            here = pl.ds(pl.multiple_of(s * 144, 16), 144)
            by_out = jnp.dot(out_ref[here, :], middle_ref[:, lanes], preferred_element_type=jnp.float32)
            left, right = left_ref[here, :], right_ref[here, :]
            for x in range(4):
                at = {"x": x, "y": y, "z": z}
                slot = (at[order[0]] * 4 + at[order[1]]) * 4 + at[order[2]]
                rows = by_in[72 * x : 72 * x + 72]
                more = by_out[36 * x : 36 * x + 36].astype(jnp.bfloat16)
                for q in range(4):
                    made[L, q, slot] = rows[16 * q : 16 * q + 16]
                made[L, 4, slot, 0:8] = rows[64:]
                made[L, 4, slot, 8:16] = more[:8]
                made[L, 5, slot] = more[8:24]
                made[L, 6, slot, 0:12] = more[24:]
                made[L, 6, slot, 12:16] = narrow[8:12]
                made[L, 7, slot, 8:16] = narrow[0:8]
                last = jnp.concatenate([left[36 * x : 36 * x + 36], right[36 * x : 36 * x + 36]], axis=0)
                for part in range(third // LANES):
                    k = 8 * (L * (third // LANES) + part)
                    made[L, 7, slot, 0:8, part * LANES : (part + 1) * LANES] = last[k : k + 8].astype(jnp.bfloat16)
            return unused

        lax.fori_loop(0, 16, block, 0, unroll=2)
        for q in range(4):
            pending[L, q] = [
                send(made.at[L, 4 * (1 - core) + q], taken.at[L, q], device(core=1 - core), (L, q), 0)
            ]

        if L:
            set_out(L - 1)
    set_out(len(ORDERS) - 1)
    for turn in range(3):
        unit = 16 >> (2 * turn)
        for L, q in streams:
            axis = ORDERS[L][turn]
            i = place[axis]
            for copy in pending[L, q]:
                copy.wait()
            other = 3 - i if q < 2 else flip(i)
            got = halves[turn].at[L, q]
            add(got.at[0], holding[L, q].at[pl.ds(i * unit, unit)], unit)
            add(got.at[1], holding[L, q].at[pl.ds(other * unit, unit)], unit)
            partner = device(**{axis: other})
            pending[L, q] = [send(got.at[1], ones[turn].at[L, q], partner, (L, q), 3 + 3 * turn)]
        for L, q in streams:
            for copy in pending[L, q]:
                copy.wait()
            got = ones[turn].at[L, q]
            if turn < 2:
                add(got, halves[turn].at[L, q, 0], unit)
                holding[L, q] = got
                pending[L, q] = start_halves(L, q, turn + 1, got, halves, place, flip, device, send)
            else:
                whole = got[0].astype(jnp.float32) + halves[turn][L, q, 0, 0].astype(jnp.float32)
                sum_ref[4 * core + q, :, L * third : (L + 1) * third] = whole
    here = sum_ref.at[pl.ds(4 * core, 4)]
    send(here, here, device(core=1 - core), (0, 0), 10).wait()
    whole = jnp.concatenate([sum_ref[q] for q in range(8)], axis=0)
    last = jnp.concatenate([whole[112:120, k * LANES : (k + 1) * LANES] for k in range(whole.shape[1] // LANES)], axis=0)
    narrow_out[...] = jnp.concatenate([whole[120:128], whole[108:112], whole[108:112]], axis=0)
    for c in range(2):

        @pl.when(core == c)
        def pick(c=c):
            in_out[...] = whole[36 * c : 36 * c + 36]
            out_out[...] = whole[72 + 18 * c : 90 + 18 * c]
            left_out[...] = last[18 * c : 18 * c + 18]
            right_out[...] = last[36 + 18 * c : 54 + 18 * c]


def start_halves(L, q, turn, source, halves, place, flip, device, send):
    axis = ORDERS[L][turn]
    unit = 16 >> (2 * turn)
    i = place[axis]
    partner = flip(i) if q < 2 else 3 - i
    second = 3 - partner if q < 2 else flip(partner)
    target = halves[turn].at[L, q]
    return [
        send(source.at[pl.ds(partner * unit, unit)], target.at[0], device(**{axis: partner}), (L, q), 1 + 3 * turn),
        send(source.at[pl.ds(second * unit, unit)], target.at[1], device(**{axis: partner}), (L, q), 2 + 3 * turn),
    ]


def shares(conv_cols, gate_cols, tokens, out_cols, middle, left, right, narrow):
    width = tokens.shape[1]
    rows, inner = out_cols.shape
    third = width // len(ORDERS)

    def slots(*lead):
        return pltpu.VMEM((len(ORDERS),) + lead + (PIECE, third), jnp.bfloat16)

    return pl.pallas_call(
        shares_kernel,
        out_shape=(shaped(36, width), shaped(18, width), shaped(18, LANES), shaped(18, LANES), shaped(16, width)),
        in_specs=[WHOLE] * 8,
        out_specs=(WHOLE,) * 5,
        scratch_shapes=[pltpu.VMEM((8, PIECE, width), jnp.float32)]
        + [pltpu.VMEM((2 * inner, rows), jnp.bfloat16), pltpu.VMEM((inner, rows), jnp.bfloat16)]
        + [slots(8, 64), slots(4, 64)]
        + [slots(4, 2, 16 >> (2 * turn)) for turn in range(3)]
        + [slots(4, 16 >> (2 * turn)) for turn in range(3)]
        + [pltpu.SemaphoreType.DMA((12, 11))] * 2,
        compiler_params=roomy(60, collective_id=2, has_side_effects=True),
        name="shares",
    )(conv_cols, gate_cols, tokens, out_cols, middle, left, right, narrow)


def local(
    tokens,
    expert_index,
    cotangent,
    first_gain,
    in_weight,
    conv_weight,
    conv_bias,
    select_weight,
    step_weight,
    step_bias,
    decay_log,
    skip_gain,
    out_weight,
    second_gain,
    router_weight,
    expert_first,
    expert_second,
):
    bf16, f32 = jnp.bfloat16, jnp.float32
    stream = segmented(tokens[0])
    routes = segmented(expert_index[0])
    upstream = segmented(cotangent[0])
    row_count, model_width = stream.shape
    seat_count = 2 * row_count
    inner = conv_bias.shape[0]
    rank = step_weight.shape[0]
    states = decay_log.shape[0]
    taps = conv_weight.shape[0]
    seqs, experts = lax.axis_size("seq"), lax.axis_size("expert")
    packed = jnp.concatenate([conv_bias, step_bias, skip_gain, first_gain, second_gain]).reshape(4, inner)
    (
        normed_in, gate_input, padded, preact, conv_out, step_raw, step_size, selection, first, mixer_out, gated,
        middle, normed_mid, router_probs, gate_wide, leaving, slots, upstream_there,
    ) = mixer(
        stream, upstream, packed, in_weight, conv_weight, select_weight, step_weight, decay_log, out_weight, router_weight, routes, seat_count
    )
    back, value_there, expert_grads = expert_pass(leaving, upstream_there, expert_first[0], expert_second[0], seqs)
    expert_share = lax.psum_scatter(
        expert_grads.reshape(-1, model_width), "seq", scatter_dimension=0, tiled=True
    ).reshape(2, -1, model_width)
    middle_low, grad_gate_input, grad_conv_input, left, right, narrow, grad_tokens, value_home = mixer_back(
        back, slots, router_probs, gate_wide, normed_mid, router_weight, middle, upstream, out_weight, gate_input, mixer_out, conv_out,
        step_size, step_raw, selection, preact, padded, first, decay_log, step_weight, select_weight, conv_weight, packed, in_weight, stream, value_there,
    )
    placing = (slots[:, 0:1] == jnp.arange(seat_count, dtype=f32)[None, :]).astype(bf16)
    mixed = middle + gate_wide[:, 0:1] * product(placing, value_home)

    devices = seqs * experts
    each, fewer = inner // devices, model_width // devices
    in_share, out_share, left, right, narrow = shares(
        grad_conv_input, grad_gate_input, normed_in, gated, middle_low, left, right, narrow
    )
    rows_sum = left[:, rank + 2 * states :]
    owner = lax.axis_index("seq") * experts + lax.axis_index("expert")
    narrow_sum = lax.dynamic_slice_in_dim(narrow, owner * fewer, fewer, axis=1)
    return (
        in_order(mixed.astype(bf16))[None],
        in_order(grad_tokens)[None],
        narrow_sum[0],
        in_share.T,
        rows_sum[:, states : states + taps].T,
        rows_sum[:, states + taps],
        left[:, : rank + 2 * states],
        right[:, :rank].T,
        rows_sum[:, states + taps + 1],
        rows_sum[:, :states].T,
        rows_sum[:, states + taps + 2],
        out_share,
        narrow_sum[1],
        narrow_sum[2:10].T,
        expert_share[0].T.astype(f32)[None],
        expert_share[1].astype(f32)[None],
    )


def solution(mesh):
    return jax.shard_map(
        local,
        mesh=mesh,
        in_specs=(
            P("expert", "seq", None),
            P("expert", "seq", None),
            P("expert", "seq", None),
            P(),
            P(),
            P(),
            P(),
            P(),
            P(),
            P(),
            P(),
            P(),
            P(),
            P(),
            P(),
            P("expert", None, None),
            P("expert", None, None),
        ),
        out_specs=(
            P("expert", "seq", None),
            P("expert", "seq", None),
            P(("seq", "expert")),
            P(None, ("seq", "expert")),
            P(None, ("seq", "expert")),
            P(("seq", "expert")),
            P(("seq", "expert"), None),
            P(None, ("seq", "expert")),
            P(("seq", "expert")),
            P(None, ("seq", "expert")),
            P(("seq", "expert")),
            P(("seq", "expert"), None),
            P(("seq", "expert")),
            P(("seq", "expert"), None),
            P("expert", None, "seq"),
            P("expert", "seq", None),
        ),
        check_vma=False,
    )
```

```python
import functools
import math

import jax
import jax.numpy as jnp
from jax import lax
from jax.experimental import pallas as pl
from jax.experimental.pallas import tpu as pltpu
from jax.sharding import PartitionSpec as P

LANES = 128
SEGS = 8
LOG2E = math.log2(math.e)
PARTS = 3
SELECTED = 104
EXPERTS = 8
CAPACITY = 64
CUT = 768
GRID = 4


def spread_ones(states):
    row = lax.broadcasted_iota(jnp.int32, (LANES, states * LANES), 0)
    lane = lax.broadcasted_iota(jnp.int32, (LANES, states * LANES), 1)
    return row, lane // LANES


def fill_maps(sel_ref, wide_ref, column):
    steps, states = wide_ref.shape[:2]
    row, block = spread_ones(states)
    ones = jnp.where(row == block + column, 1.0, 0.0).astype(jnp.bfloat16)
    left, total = sel_ref[...], None
    for unused in range(3):
        part = left.astype(jnp.bfloat16)
        left = left - part.astype(jnp.float32)
        spread = jnp.dot(part, ones, preferred_element_type=jnp.float32)
        total = spread if total is None else total + spread
    for n in range(states):
        wide_ref[:, n] = total[:, n * LANES : (n + 1) * LANES].reshape(steps, SEGS, LANES)


def gather_maps(sum_ref, column):
    steps, states = sum_ref.shape[:2]
    row, block = spread_ones(states)
    ones = jnp.where(row == block + column, 1.0, 0.0).astype(jnp.bfloat16)
    left = jnp.concatenate([sum_ref[:, n].reshape(steps * SEGS, LANES) for n in range(states)], axis=1)
    total = None
    for unused in range(3):
        part = left.astype(jnp.bfloat16)
        left = left - part.astype(jnp.float32)
        summed = transposed_dot(part, ones)
        total = summed if total is None else total + summed
    return total


def lanes_of(block):
    return pl.ds(pl.multiple_of(block * LANES, LANES), LANES)


def rows_of(j):
    return pl.ds(pl.multiple_of(j * SEGS, SEGS), SEGS)


def rates_of(log_ref, lanes):
    states = log_ref.shape[0]
    rate = -LOG2E * jnp.exp(log_ref[:, lanes])
    return jnp.stack([jnp.broadcast_to(rate[n : n + 1], (SEGS, LANES)) for n in range(states)])


def neighbour(value, hop, later, fill):
    axis = value.ndim - 2
    place = lax.broadcasted_iota(jnp.int32, value.shape, axis)
    if later:
        return jnp.where(place < SEGS - hop, pltpu.roll(value, SEGS - hop, axis), fill)
    return jnp.where(place >= hop, pltpu.roll(value, hop, axis), fill)


def summarize(later, part, step_ref, other_ref, wide, log_ref, part_ref, span_ref, message):
    steps, states = wide.shape[:2]
    blocks = step_ref.shape[1] // LANES // PARTS

    def block(i, unused):
        lanes = lanes_of(part * blocks + i)
        rate = rates_of(log_ref, lanes)

        def advance(turn, carry):
            span, memory = carry
            j = steps - 1 - turn if later else turn
            step = step_ref[rows_of(j), lanes]
            other = other_ref[rows_of(j), lanes]
            decay = jnp.exp2(step * rate)
            if later:
                memory = decay * (memory + wide[j] * other)
            else:
                memory = decay * memory + wide[j] * (step * other)
            return span + step, memory

        zero = jnp.zeros((SEGS, LANES), jnp.float32)
        span, memory = lax.fori_loop(0, steps, advance, (zero, jnp.zeros(rate.shape, jnp.float32)), unroll=8)
        hop = 1
        while hop < SEGS:
            memory = memory + jnp.exp2(rate * span) * neighbour(memory, hop, later, 0.0)
            span = span + neighbour(span, hop, later, 0.0)
            hop *= 2
        span_ref[:, lanes] = span
        part_ref[:, :, lanes] = memory
        end = 0 if later else SEGS - 1
        for n in range(states):
            message[n // GRID, n % GRID, pl.ds(i, 1), :] = memory[n, end : end + 1]
        for q in range(GRID):
            message[q, GRID, pl.ds(i, 1), :] = span[end : end + 1]
        return unused

    lax.fori_loop(0, blocks, block, 0)


def entering(later, part_ref, span_ref, rate, lanes, carried):
    ends = part_ref[:, :, lanes] + jnp.exp2(rate * span_ref[:, lanes]) * carried
    return neighbour(ends, 1, later, carried)


def carried_at(in_ref, part, i):
    states = GRID * GRID
    return jnp.stack(
        [jnp.broadcast_to(in_ref[n // GRID, n % GRID, pl.ds(i, 1), :], (SEGS, LANES)) for n in range(states)]
    )


def scan_part(part, step_ref, conv_ref, wide_in, wide_out, log_ref, part_ref, span_ref, in_ref, y_ref, entry_ref):
    steps = wide_in.shape[0]
    blocks = step_ref.shape[1] // LANES // PARTS

    def block(i, unused):
        lanes = lanes_of(part * blocks + i)
        rate = rates_of(log_ref, lanes)
        first = entering(False, part_ref, span_ref, rate, lanes, carried_at(in_ref, part, i))
        entry_ref[:, :, lanes] = first

        def advance(j, memory):
            step = step_ref[rows_of(j), lanes]
            memory = jnp.exp2(step * rate) * memory + wide_in[j] * (step * conv_ref[rows_of(j), lanes])
            y_ref[rows_of(j), lanes] = jnp.sum(wide_out[j] * memory, axis=0)
            return memory

        lax.fori_loop(0, steps, advance, first, unroll=8)
        return unused

    lax.fori_loop(0, blocks, block, 0)


def retreat_part(
    part, step_ref, conv_ref, grad_ref, raw_ref, wide_in, wide_out, log_ref, pull_ref, entry_ref, part_ref, span_ref, in_ref,
    low_ref, gconv_ref, glog_ref, gbias_ref, sum_in, sum_out, states_ref, decays_ref, raw_sum, raw_rows,
):
    steps = wide_in.shape[0]
    blocks = step_ref.shape[1] // LANES // PARTS

    def block(i, unused):
        lanes = lanes_of(part * blocks + i)
        rate = rates_of(log_ref, lanes)

        def advance(j, memory):
            step = step_ref[rows_of(j), lanes]
            decay = jnp.exp2(step * rate)
            memory = decay * memory + wide_in[j] * (step * conv_ref[rows_of(j), lanes])
            decays_ref[j] = decay
            states_ref[j + 1] = memory
            return memory

        first = entry_ref[:, :, lanes]
        states_ref[0] = first
        lax.fori_loop(0, steps, advance, first, unroll=8)

        def retreat(turn, carry):
            j = steps - 1 - turn
            mu, slow = carry
            step = step_ref[rows_of(j), lanes]
            conv = conv_ref[rows_of(j), lanes]
            grad = grad_ref[rows_of(j), lanes]
            lam = wide_out[j] * grad + mu
            sum_out[j] += grad * states_ref[j + 1]
            sum_in[j] += lam * (step * conv)
            by_in = jnp.sum(lam * wide_in[j], axis=0)
            mu = lam * decays_ref[j]
            kept = mu * states_ref[j]
            by_rate = jnp.sum(kept * rate, axis=0)
            grad_step = by_in * conv + (1.0 / LOG2E) * by_rate
            raw_rows[rows_of(j), :] = grad_step * jax.nn.sigmoid(raw_ref[rows_of(j), lanes])
            gconv_ref[rows_of(j), lanes] = by_in * step
            return mu, slow + kept * step

        last = entering(True, part_ref, span_ref, rate, lanes, carried_at(in_ref, part, i))
        unused_mu, slow = lax.fori_loop(0, steps, retreat, (last, jnp.zeros(rate.shape, jnp.float32)), unroll=4)
        glog_ref[:, lanes] = (1.0 / LOG2E) * jnp.sum(slow * rate, axis=1)
        raw_steps = raw_rows[...]
        gbias_ref[:, lanes] = jnp.sum(raw_steps, axis=0, keepdims=True)
        low = raw_steps.astype(jnp.bfloat16)
        low_ref[:, lanes] = low
        raw_sum[:, : pull_ref.shape[0]] += transposed_dot(low, pull_ref[:, lanes])
        return unused

    lax.fori_loop(0, blocks, block, 0)


def expert_peers():
    me = lax.axis_index("expert")
    return [lax.rem(me + k, EXPERTS) for k in range(1, EXPERTS)]


def seats_of(device):
    return pl.ds(pl.multiple_of(device * CAPACITY, CAPACITY), CAPACITY)


def trade(source, target, send_sems, recv_sems):
    me = lax.axis_index("expert")
    copies = [
        pltpu.make_async_remote_copy(
            src_ref=source.at[seats_of(peer)], dst_ref=target.at[seats_of(me)], send_sem=send_sems.at[k], recv_sem=recv_sems.at[k],
            device_id={"expert": peer}, device_id_type=pl.DeviceIdType.MESH,
        )
        for k, peer in enumerate(expert_peers())
    ]
    copies.append(pltpu.make_async_copy(source.at[seats_of(me)], target.at[seats_of(me)], send_sems.at[EXPERTS - 1]))
    for copy in copies:
        copy.start()
    return copies


class Relay:
    def __init__(self, later, log_ref, log_rows, in_ref, message, got, row, rows_got, above, made, sends, arrivals, others=()):
        self.later, self.log_rows, self.message, self.got = later, log_rows, message, got
        self.row, self.rows_got, self.above, self.made, self.in_ref = row, rows_got, above, made, in_ref
        self.sends, self.arrivals = sends, arrivals
        seq = lax.axis_index("seq")
        self.y, self.z = lax.div(seq, GRID), lax.rem(seq, GRID)
        blocks = log_ref.shape[1] // LANES // PARTS
        log_rows[...] = jnp.zeros_like(log_rows)
        for part in range(PARTS):
            for b in range(blocks):
                lanes = pl.ds((part * blocks + b) * LANES, LANES)
                for n in range(GRID * GRID):
                    log_rows[part, n // GRID, n % GRID, b : b + 1, :] = log_ref[n : n + 1, lanes]
        self.flying = {}
        barrier = pltpu.get_barrier_semaphore()
        peers = [self.across(k) for k in range(1, GRID)] + [self.along(k) for k in range(1, GRID)]
        peers += [self.onward(1), self.onward(-1)] + list(others)
        for peer in peers:
            pl.semaphore_signal(barrier, inc=1, device_id=peer, device_id_type=pl.DeviceIdType.MESH)
        self.peers = len(peers)

    def onward(self, k):
        size = GRID * GRID
        return {"seq": lax.rem(self.y * GRID + self.z + k + size, size)}

    def across(self, k):
        return {"seq": self.y * GRID + lax.rem(self.z + k, GRID)}

    def along(self, k):
        return {"seq": lax.rem(self.y + k, GRID) * GRID + self.z}

    def meet(self):
        pl.semaphore_wait(pltpu.get_barrier_semaphore(), self.peers)

    def send(self, part, phase, k, source, target, peer):
        copy = pltpu.make_async_remote_copy(
            src_ref=source, dst_ref=target, send_sem=self.sends.at[part, phase, k], recv_sem=self.arrivals.at[part, phase, k],
            device_id=peer, device_id_type=pl.DeviceIdType.MESH,
        )
        copy.start()
        self.flying.setdefault((part, phase), []).append(copy)

    def land(self, part, phase):
        for copy in self.flying[part, phase]:
            copy.wait()

    def order(self):
        return range(GRID - 1, -1, -1) if self.later else range(GRID)

    def rate(self, part):
        return -LOG2E * jnp.exp(self.log_rows[part, self.z])

    def first(self, part):
        for k in range(1, GRID):
            peer = lax.rem(self.z + k, GRID)
            self.send(part, 0, k, self.message.at[part, peer], self.got.at[part, k], self.across(k))
        self.got[part, 0] = self.message[part, self.z]

    def second(self, part):
        self.land(part, 0)
        rate = self.rate(part)
        state, span = jnp.zeros(rate.shape, jnp.float32), jnp.zeros(rate.shape[1:], jnp.float32)
        for z in self.order():
            block = self.got[part, lax.rem(self.z - z + GRID, GRID)]
            state = jnp.exp2(rate * block[GRID]) * state + block[:GRID]
            span = span + block[GRID]
        self.row[part, :GRID] = state
        self.row[part, GRID] = span
        for k in range(1, GRID):
            self.send(part, 1, k, self.row.at[part], self.rows_got.at[part, k], self.along(k))
        self.rows_got[part, 0] = self.row[part]

    def third(self, part):
        self.land(part, 1)
        rate = self.rate(part)
        state = jnp.zeros(rate.shape, jnp.float32)
        for y in self.order():
            self.above[part, y] = state
            block = self.rows_got[part, lax.rem(self.y - y + GRID, GRID)]
            state = jnp.exp2(rate * block[GRID]) * state + block[:GRID]
        state = self.above[part, self.y]
        for z in self.order():
            self.made[part, z] = state
            block = self.got[part, lax.rem(self.z - z + GRID, GRID)]
            state = jnp.exp2(rate * block[GRID]) * state + block[:GRID]
        for k in range(1, GRID):
            peer = lax.rem(self.z + k, GRID)
            self.send(part, 2, k, self.made.at[part, peer], self.in_ref.at[part, self.z], self.across(k))
        self.in_ref[part, self.z] = self.made[part, self.z]

    def done(self, part):
        self.land(part, 2)


def staged(relay, summary, extra, scan):
    summary(0)
    relay.first(0)
    summary(1)
    relay.first(1)
    relay.second(0)
    summary(2)
    relay.first(2)
    relay.third(0)
    relay.second(1)
    extra()
    relay.second(2)
    relay.third(1)
    relay.done(0)
    scan(0)
    relay.third(2)
    relay.done(1)
    scan(1)
    relay.done(2)
    scan(2)


def named_experts(slots, rows):
    first = (lax.broadcasted_iota(jnp.int32, (rows, EXPERTS), 1) * CAPACITY).astype(jnp.float32)
    return jnp.where((slots >= first) & (slots < first + CAPACITY), 1.0, 0.0)


def seated_rows(slots, rows, seats):
    seat = lax.broadcasted_iota(jnp.int32, (rows, seats), 1).astype(jnp.float32)
    return jnp.where(seat == slots, 1.0, 0.0).astype(jnp.bfloat16)


def order_ones(rows, back):
    row, token = lax.broadcasted_iota(jnp.int32, (rows, rows), 0), lax.broadcasted_iota(jnp.int32, (rows, rows), 1)
    if back:
        row, token = token, row
    same = token == lax.rem(row, SEGS) * (rows // SEGS) + lax.div(row, SEGS)
    return jnp.where(same, 1.0, 0.0).astype(jnp.bfloat16)


def slots_of(routes, rows):
    expert = lax.broadcasted_iota(jnp.int32, (rows, EXPERTS), 1)
    named = jnp.where(lax.broadcasted_iota(jnp.int32, (EXPERTS, rows), 0) == routes, 1.0, 0.0).astype(jnp.bfloat16)
    named = transposed_dot(order_ones(rows, False), named)
    later = lax.broadcasted_iota(jnp.int32, (rows, rows), 0) > lax.broadcasted_iota(jnp.int32, (rows, rows), 1)
    ahead = jnp.dot(jnp.where(later, 1.0, 0.0).astype(jnp.bfloat16), named.astype(jnp.bfloat16), preferred_element_type=jnp.float32)
    return jnp.sum(named * (ahead + (expert * CAPACITY).astype(jnp.float32)), axis=1, keepdims=True)


def mixer_kernel(
    token_in, up_in, tap_bias_in, step_bias_in, skip_in, gain_in, second_gain_in, in_hbm, tap_ref, select_ref, step_weight_ref, log_ref, out_hbm, router_ref, route_ref,
    normed_out, gate_out, padded_out, pre_out, conv_out, raw_out, step_out, sel_out, entry_out, mixer_out, gated_out,
    middle_out, normed_mid_out, probs_out, chosen_out, leaving_out, slot_out, up_out, token_out, up_order_out, row_out,
    normed, in_ref, out_ref, padded, gate, pre, conv, raw, step, sel, entry, mixer, gated, middle, normed_mid, probs, chosen, leaving, slots, up_seated, token_ref, up_ref, row_ref,
    tail, tail_got, part_ref, span_ref, wide_in, wide_out, loads, saves, passing, goes, comes, log_rows, relay_in, *relayed
):
    rows, width = step.shape
    model = token_ref.shape[1]
    tap_bias_ref, step_bias_ref, skip_ref = (row_ref.at[k : k + 1] for k in range(3))
    gain_ref, second_gain_ref = row_ref.at[3:4, :model], row_ref.at[3:4, model:]
    taps, states = tap_ref.shape[0], log_ref.shape[0]
    reach = (taps - 1) * SEGS
    rank = SELECTED - 2 * states
    pieces = in_ref.shape[0]
    cut = in_ref.shape[2]
    blocks = width // LANES

    loading = [pltpu.make_async_copy(in_hbm.at[:, pl.ds(k * cut, cut)], in_ref.at[k], loads.at[k]) for k in range(pieces)]
    loading.append(pltpu.make_async_copy(out_hbm, out_ref, loads.at[pieces]))
    for copy in loading:
        copy.start()
    saving = []

    def save(source, target):
        copy = pltpu.make_async_copy(source, target, saves.at[len(saving)])
        copy.start()
        saving.append(copy)

    relay = Relay(False, log_ref, log_rows, relay_in, *relayed, others=[{"expert": peer} for peer in expert_peers()])

    for k, vector in enumerate((tap_bias_in, step_bias_in, skip_in)):
        row_ref[k : k + 1, :] = vector[...][None, :]
    row_ref[3:4, :model] = gain_in[...][None, :]
    row_ref[3:4, model:] = second_gain_in[...][None, :]
    row_ref[4:, :] = jnp.zeros_like(row_ref[4:, :])
    save(row_ref, row_out)
    ordering = order_ones(rows, False)
    stream = jnp.dot(ordering, token_in[...], preferred_element_type=jnp.float32)
    token_ref[...] = stream.astype(jnp.bfloat16)
    save(token_ref, token_out)
    normed[...] = (stream * rms_scale(stream) * gain_ref[...]).astype(jnp.bfloat16)
    save(normed, normed_out)
    for k in range(pieces // 2):
        loading[k].wait()
        padded[reach:, k * cut : (k + 1) * cut] = jnp.dot(normed[...], in_ref[k], preferred_element_type=jnp.float32)
    tail[...] = jnp.zeros_like(tail)
    for k in range(taps - 1):
        row = reach + rows - (taps - 1 - k) * SEGS + SEGS - 1
        tail[k : k + 1, :] = padded[row : row + 1, :]
    slot = slots_of(route_ref[...], rows)
    slots[...] = jnp.broadcast_to(slot, slots.shape)
    save(slots, slot_out)
    seating = seated_rows(slot, rows, leaving.shape[0])
    up_ref[...] = jnp.dot(ordering, up_in[...], preferred_element_type=jnp.float32).astype(jnp.bfloat16)
    save(up_ref, up_order_out)
    up_seated[...] = column_dot(seating, up_ref[...]).astype(jnp.bfloat16)
    relay.meet()
    handing = pltpu.make_async_remote_copy(
        src_ref=tail, dst_ref=tail_got, send_sem=passing.at[0], recv_sem=passing.at[1],
        device_id=relay.onward(1), device_id_type=pl.DeviceIdType.MESH,
    )
    handing.start()
    trading = trade(up_seated, up_out, goes, comes)
    for k in range(pieces // 2, pieces):
        loading[k].wait()
        spot = slice((k - pieces // 2) * cut, (k - pieces // 2 + 1) * cut)
        gate[:, spot] = jnp.dot(normed[...], in_ref[k], preferred_element_type=jnp.float32)
    save(gate, gate_out)
    handing.wait()
    started = jnp.where(lax.axis_index("seq") > 0, 1.0, 0.0)
    for k in range(taps - 1):
        row = rows + k * SEGS
        segment = lax.broadcasted_iota(jnp.int32, (SEGS, width), 0)
        before = pltpu.roll(padded[row : row + SEGS, :], 1, 0)
        padded[k * SEGS : (k + 1) * SEGS, :] = jnp.where(segment == 0, started * tail_got[k : k + 1, :], before)
    save(padded, padded_out)

    sel[...] = jnp.zeros_like(sel)

    def convolve(b, unused):
        lanes = lanes_of(b)
        value = tap_bias_ref[:, lanes]
        for k in range(taps):
            value = value + tap_ref[k : k + 1, lanes] * padded[k * SEGS : k * SEGS + rows, lanes]
        pre[:, lanes] = value
        value = value * jax.nn.sigmoid(value)
        conv[:, lanes] = value
        sel[:, :SELECTED] += transposed_dot(value.astype(jnp.bfloat16), select_ref[:, lanes])
        return unused

    lax.fori_loop(0, blocks, convolve, 0)
    save(pre, pre_out)
    save(conv, conv_out)
    save(sel, sel_out)
    step_low = sel[:, :rank].astype(jnp.bfloat16)

    def size(b, unused):
        lanes = lanes_of(b)
        value = jnp.dot(step_low, step_weight_ref[:, lanes], preferred_element_type=jnp.float32) + step_bias_ref[:, lanes]
        raw[:, lanes] = value
        step[:, lanes] = jnp.maximum(value, 0.0) + jnp.log1p(jnp.exp(-jnp.abs(value)))
        return unused

    lax.fori_loop(0, blocks, size, 0)
    save(raw, raw_out)
    save(step, step_out)
    fill_maps(sel, wide_in, rank)

    def summary(part):
        summarize(False, part, step, conv, wide_in, log_ref, part_ref, span_ref, relay.message.at[part])

    def scan(part):
        scan_part(part, step, conv, wide_in, wide_out, log_ref, part_ref, span_ref, relay_in.at[part], mixer, entry)

    staged(relay, summary, lambda: fill_maps(sel, wide_out, rank + states), scan)
    save(entry, entry_out)

    def blend(b, unused):
        lanes = lanes_of(b)
        value = mixer[:, lanes] + skip_ref[:, lanes] * conv[:, lanes]
        mixer[:, lanes] = value
        opening = gate[:, lanes]
        gated[:, lanes] = (value * (opening * jax.nn.sigmoid(opening))).astype(jnp.bfloat16)
        return unused

    lax.fori_loop(0, blocks, blend, 0)
    save(mixer, mixer_out)
    save(gated, gated_out)
    loading[pieces].wait()
    value = token_ref[...].astype(jnp.float32) + jnp.dot(gated[...], out_ref[...], preferred_element_type=jnp.float32)
    middle[...] = value
    save(middle, middle_out)
    normed_mid[...] = (value * rms_scale(value) * second_gain_ref[...]).astype(jnp.bfloat16)
    save(normed_mid, normed_mid_out)
    logits = transposed_dot(normed_mid[...], router_ref[...])
    grown = jnp.exp(logits - jnp.max(logits, axis=1, keepdims=True))
    probs[...] = grown / jnp.sum(grown, axis=1, keepdims=True)
    save(probs, probs_out)
    gate_value = jnp.sum(named_experts(slots[:, 0:1], rows) * probs[...], axis=1, keepdims=True)
    chosen[...] = jnp.broadcast_to(gate_value, (rows, LANES))
    save(chosen, chosen_out)
    place = lax.broadcasted_iota(jnp.int32, (rows, LANES), 1)
    parts = jnp.zeros((rows, LANES), jnp.float32)
    for k, piece in enumerate(three_parts(gate_value)):
        parts = jnp.where(place == k, piece.astype(jnp.float32), parts)
    seating = seated_rows(slots[:, 0:1], rows, leaving.shape[0])
    leaving[:, :model] = column_dot(seating, normed_mid[...]).astype(jnp.bfloat16)
    leaving[:, model:] = column_dot(seating, parts.astype(jnp.bfloat16)).astype(jnp.bfloat16)
    save(leaving, leaving_out)
    for copy in saving + trading:
        copy.wait()


def mixer_back_kernel(
    back_hbm, slot_ref, probs_ref, chosen_ref, normed_ref, router_ref, middle_ref, up_ref, out_hbm, gate_hbm,
    mixer_hbm, conv_hbm, step_hbm, raw_hbm, sel_ref, pre_hbm, padded_hbm, entry_hbm, log_ref, step_weight_ref, select_ref,
    tap_ref, packed_ref, in_hbm, token_ref, value_hbm,
    low_out, gate_out, conv_out, left_out, right_out, narrow_out, token_out, value_out,
    back, out_ref, gate, mixer, conv, step, raw, padded, entry, in_ref,
    middle_low, grad_gate, grad_conv, left, right, narrow, grad_middle, mixed, low, gsel, glog, gbias, total, tail, tail_got, row_ref,
    part_ref, span_ref, wide_in, wide_out, sum_in, sum_out, states_ref, decays_ref, raw_sum, raw_rows,
    loads, saves, passing, goes, comes, log_rows, relay_in, *relayed
):
    rows, width = step.shape
    model = up_ref.shape[1]
    skip_ref, gain_ref, second_gain_ref = packed_ref.at[2:3], packed_ref.at[3:4, :model], packed_ref.at[3:4, model:]
    taps, states = tap_ref.shape[0], log_ref.shape[0]
    rank = SELECTED - 2 * states
    held, cut = in_ref.shape[0], in_ref.shape[2]
    blocks = width // LANES
    saving, numbers = [], iter(range(64))

    def load(source, target):
        copy = pltpu.make_async_copy(source, target, loads.at[next(numbers)])
        copy.start()
        return copy

    def save(source, target):
        copy = pltpu.make_async_copy(source, target, saves.at[len(saving)])
        copy.start()
        saving.append(copy)

    def weight(k):
        return load(in_hbm.at[:, pl.ds(k * cut, cut)], in_ref.at[k % held])

    early = [load(back_hbm, back), load(out_hbm, out_ref), load(gate_hbm, gate), load(mixer_hbm, mixer)]
    scanning = [load(step_hbm, step), load(conv_hbm, conv), load(raw_hbm, raw), load(entry_hbm, entry)]
    padding = load(padded_hbm, padded)
    weights = {k: weight(k) for k in range(held, 2 * held)}
    relay = Relay(True, log_ref, log_rows, relay_in, *relayed, others=[{"expert": peer} for peer in expert_peers()])

    early[0].wait()
    slots = slot_ref[:, 0:1]
    seating = seated_rows(slots, rows, back.shape[0])
    chosen = chosen_ref[:, 0:1]
    along = jnp.sum(jnp.dot(seating, back[:, model:], preferred_element_type=jnp.float32), axis=1, keepdims=True)
    place = lax.broadcasted_iota(jnp.int32, (rows, LANES), 1)
    logits = (along * chosen * (named_experts(slots, rows) - probs_ref[...])).astype(jnp.bfloat16)
    grad = jnp.dot(logits, router_ref[...], preferred_element_type=jnp.float32) + chosen * jnp.dot(seating, back[:, :model], preferred_element_type=jnp.float32)
    narrow[...] = jnp.zeros_like(narrow)
    narrow[:EXPERTS, :] = column_dot(logits, normed_ref[...])
    value = middle_ref[...]
    returned, gained = rms_back(value, rms_scale(value), second_gain_ref[...], grad)
    narrow[EXPERTS + 1 : EXPERTS + 2, :] = gained[None, :]
    value = up_ref[...].astype(jnp.float32) + returned
    grad_middle[...] = value
    middle_low[...] = value.astype(jnp.bfloat16)
    save(middle_low, low_out)
    for copy in early[1:]:
        copy.wait()

    def open_gate(b, unused):
        lanes = lanes_of(b)
        grown = transposed_dot(middle_low[...], out_ref[lanes, :])
        opening = gate[:, lanes]
        mixed[:, lanes] = grown * (opening * jax.nn.sigmoid(opening))
        grad_gate[:, lanes] = (grown * mixer[:, lanes] * silu_slope(opening)).astype(jnp.bfloat16)
        return unused

    lax.fori_loop(0, blocks, open_gate, 0)
    save(grad_gate, gate_out)
    pre, gconv = gate, mixer
    activating = load(pre_hbm, pre)
    for copy in scanning:
        copy.wait()

    fill_maps(sel_ref, wide_out, rank + states)

    def summary(part):
        summarize(True, part, step, mixed, wide_out, log_ref, part_ref, span_ref, relay.message.at[part])

    def prepare():
        fill_maps(sel_ref, wide_in, rank)
        sum_in[...] = jnp.zeros_like(sum_in)
        sum_out[...] = jnp.zeros_like(sum_out)
        raw_sum[...] = jnp.zeros_like(raw_sum)

    def scan(part):
        retreat_part(
            part, step, conv, mixed, raw, wide_in, wide_out, log_ref, step_weight_ref, entry, part_ref, span_ref,
            relay_in.at[part], low, gconv, glog, gbias, sum_in, sum_out, states_ref, decays_ref, raw_sum, raw_rows,
        )

    relay.meet()
    trading = trade(value_hbm, value_out, goes, comes)
    staged(relay, summary, prepare, scan)
    maps = gather_maps(sum_in, rank) + gather_maps(sum_out, rank + states)
    gsel[...] = (raw_sum[...] + maps).astype(jnp.bfloat16)

    activating.wait()
    padding.wait()
    step_low = jnp.where(place < rank, sel_ref[...], 0.0).astype(jnp.bfloat16)
    tall = lax.broadcasted_iota(jnp.int32, (row_ref.shape[0], LANES), 0)
    spots = jnp.where(lax.broadcasted_iota(jnp.int32, tall.shape, 1) == tall + SELECTED, 1.0, 0.0).astype(jnp.bfloat16)
    row_ref[...] = jnp.zeros_like(row_ref)

    def convolve_back(b, unused):
        lanes = lanes_of(b)
        around, kept = mixed[:, lanes], conv[:, lanes]
        grown = jnp.dot(gsel[:, :SELECTED], select_ref[:, lanes], preferred_element_type=jnp.float32) + gconv[:, lanes] + skip_ref[:, lanes] * around
        grown = grown * silu_slope(pre[:, lanes])
        gconv[:, lanes] = grown
        row_ref[:states, :] = glog[:, lanes]
        for k in range(taps):
            row_ref[states + k : states + k + 1, :] = jnp.sum(
                grown * padded[k * SEGS : k * SEGS + rows, lanes], axis=0, keepdims=True
            )
        row_ref[states + taps : states + taps + 1, :] = jnp.sum(grown, axis=0, keepdims=True)
        row_ref[states + taps + 1 : states + taps + 2, :] = gbias[:, lanes]
        row_ref[states + taps + 2 : states + taps + 3, :] = jnp.sum(around * kept, axis=0, keepdims=True)
        summed = column_dot(kept.astype(jnp.bfloat16), gsel[...])
        for piece in three_parts(row_ref[...]):
            summed = summed + column_dot(piece, spots)
        left[lanes, :] = summed
        right[lanes, :] = column_dot(low[:, lanes], step_low)
        return unused

    lax.fori_loop(0, blocks, convolve_back, 0)
    save(left, left_out)
    save(right, right_out)

    tail[...] = jnp.zeros_like(tail)
    for k in range(taps - 1):
        tail[k : k + 1, :] = gconv[k * SEGS : k * SEGS + 1, :]
    handing = pltpu.make_async_remote_copy(
        src_ref=tail, dst_ref=tail_got, send_sem=passing.at[0], recv_sem=passing.at[1],
        device_id=relay.onward(-1), device_id_type=pl.DeviceIdType.MESH,
    )
    handing.start()
    for k in range(held):
        weights[held + k].wait()
        summed = transposed_dot(grad_gate[:, k * cut : (k + 1) * cut], in_ref[k])
        total[...] = summed if k == 0 else total[...] + summed
        weights[k] = weight(k)
    handing.wait()
    goes_on = jnp.where(lax.axis_index("seq") < GRID * GRID - 1, 1.0, 0.0)
    segment = lax.broadcasted_iota(jnp.int32, (SEGS, cut), 0)
    for k in range(held):
        spot = slice(k * cut, (k + 1) * cut)
        grown = None
        for t in range(taps):
            late = taps - 1 - t
            shifted = gconv[late * SEGS :, spot]
            if late:
                wrapped = [
                    jnp.where(
                        segment == SEGS - 1,
                        goes_on * tail_got[j : j + 1, spot],
                        pltpu.roll(gconv[j * SEGS : (j + 1) * SEGS, spot], SEGS - 1, 0),
                    )
                    for j in range(late)
                ]
                shifted = jnp.concatenate([shifted] + wrapped, axis=0)
            term = tap_ref[t : t + 1, spot] * shifted
            grown = term if grown is None else grown + term
        grad_conv[:, spot] = grown.astype(jnp.bfloat16)
        weights[k].wait()
        total[...] += transposed_dot(grad_conv[:, spot], in_ref[k])
    save(grad_conv, conv_out)
    stream = token_ref[...].astype(jnp.float32)
    returned, gained = rms_back(stream, rms_scale(stream), gain_ref[...], total[...])
    narrow[EXPERTS : EXPERTS + 1, :] = gained[None, :]
    save(narrow, narrow_out)
    value = grad_middle[...] + returned
    ordering = order_ones(rows, True)
    total[...] = sum(jnp.dot(ordering, part, preferred_element_type=jnp.float32) for part in three_parts(value))
    save(total, token_out)
    for copy in saving + trading:
        copy.wait()


WHOLE = pl.BlockSpec(memory_space=pltpu.VMEM)


def shaped(*dims, dtype=jnp.float32):
    return jax.ShapeDtypeStruct(dims, dtype)


def roomy(mebibytes, **more):
    return pltpu.CompilerParams(vmem_limit_bytes=mebibytes << 20, **more)


def busy(elements):
    return pl.CostEstimate(flops=4096 * elements, bytes_accessed=16 * elements, transcendentals=4 * elements)


def wide_scratch(rows, states, extra=0):
    return pltpu.VMEM((rows // SEGS + extra, states, SEGS, LANES), jnp.float32)


def chain_scratch(states, width):
    return [pltpu.VMEM((states, SEGS, width), jnp.float32), pltpu.VMEM((SEGS, width), jnp.float32)]


def relay_scratch():
    def kept(*dims):
        return pltpu.VMEM((PARTS,) + dims + (SEGS, LANES), jnp.float32)

    return [
        kept(GRID, GRID),
        kept(GRID, GRID),
        kept(GRID, GRID + 1),
        kept(GRID, GRID + 1),
        kept(GRID + 1),
        kept(GRID, GRID + 1),
        kept(GRID, GRID),
        kept(GRID, GRID),
        pltpu.SemaphoreType.DMA((PARTS, 3, GRID)),
        pltpu.SemaphoreType.DMA((PARTS, 3, GRID)),
    ]


def mixer(tokens, upstream, tap_bias, step_bias, skip, gain, second_gain, in_weight, taps, select, step_weight, decay_log, out_weight, router, routes, seats):
    rows, model = tokens.shape
    states, width = decay_log.shape
    reach = (taps.shape[0] - 1) * SEGS
    bf16, f32 = jnp.bfloat16, jnp.float32
    anywhere = pl.BlockSpec(memory_space=pl.ANY)
    results = [
        ((rows, model), bf16),
        ((rows, width), f32),
        ((rows + reach, width), f32),
        ((rows, width), f32),
        ((rows, width), f32),
        ((rows, width), f32),
        ((rows, width), f32),
        ((rows, LANES), f32),
        ((states, SEGS, width), f32),
        ((rows, width), f32),
        ((rows, width), bf16),
        ((rows, model), f32),
        ((rows, model), bf16),
        ((rows, EXPERTS), f32),
        ((rows, LANES), f32),
        ((seats, model + LANES), bf16),
        ((rows, LANES), f32),
        ((seats, model), bf16),
        ((rows, model), bf16),
        ((rows, model), bf16),
        ((SEGS, width), f32),
    ]
    kept = [pltpu.VMEM(dims, dtype) for dims, dtype in results]
    weights = [pltpu.VMEM((2 * width // CUT, model, CUT), bf16), pltpu.VMEM(out_weight.shape, bf16)]
    relayed = relay_scratch()
    return pl.pallas_call(
        mixer_kernel,
        out_shape=tuple(shaped(*dims, dtype=dtype) for dims, dtype in results),
        in_specs=[WHOLE] * 7 + [anywhere] + [WHOLE] * 4 + [anywhere] + [WHOLE] * 2,
        out_specs=(anywhere,) * len(results),
        scratch_shapes=kept[:1]
        + weights
        + [kept[2], kept[1]]
        + kept[3:]
        + [pltpu.VMEM((SEGS, width), f32)] * 2
        + chain_scratch(states, width)
        + [wide_scratch(rows, states)] * 2
        + [
            pltpu.SemaphoreType.DMA((2 * width // CUT + 1,)),
            pltpu.SemaphoreType.DMA((len(results),)),
            pltpu.SemaphoreType.DMA((2,)),
            pltpu.SemaphoreType.DMA((EXPERTS,)),
            pltpu.SemaphoreType.DMA((EXPERTS,)),
        ]
        + relayed,
        compiler_params=roomy(60, collective_id=0, has_side_effects=True),
        cost_estimate=busy(rows * states * width),
        name="mixer",
    )(tokens, upstream, tap_bias, step_bias, skip, gain, second_gain, in_weight, taps, select, step_weight, decay_log, out_weight, router, routes)


def mixer_back(
    back, slots, probs, chosen, normed, router, middle, up, out_weight, gate, mixed, conv, step, raw, selection, pre, padded, entry,
    decay_log, step_weight, select, taps, packed, in_weight, tokens, value,
):
    rows, width = step.shape
    model = tokens.shape[1]
    states = decay_log.shape[0]
    bf16, f32 = jnp.bfloat16, jnp.float32
    anywhere = pl.BlockSpec(memory_space=pl.ANY)
    held = width // CUT
    tall = ((rows, width), f32)
    results = [
        ((rows, model), bf16),
        ((rows, width), bf16),
        ((rows, width), bf16),
        ((width, LANES), f32),
        ((width, LANES), f32),
        ((16, model), f32),
        ((rows, model), f32),
        (value.shape, bf16),
    ]
    streamed = (0, 8, 9, 10, 11, 12, 13, 15, 16, 17, 23, 25)
    kept = (
        [(back.shape, bf16), (out_weight.shape, bf16)]
        + [tall] * 5
        + [(padded.shape, f32), (entry.shape, f32), ((held, model, CUT), bf16)]
        + results[:6]
        + [((rows, model), f32), tall, ((rows, width), bf16), ((rows, LANES), bf16), ((states, width), f32), ((1, width), f32)]
        + [((rows, model), f32), ((SEGS, width), f32), ((SEGS, width), f32), ((24, LANES), f32)]
    )
    return pl.pallas_call(
        mixer_back_kernel,
        out_shape=tuple(shaped(*dims, dtype=dtype) for dims, dtype in results),
        in_specs=[anywhere if k in streamed else WHOLE for k in range(26)],
        out_specs=(anywhere,) * len(results),
        scratch_shapes=[pltpu.VMEM(dims, dtype) for dims, dtype in kept]
        + chain_scratch(states, width)
        + [wide_scratch(rows, states)] * 4
        + [wide_scratch(rows, states, 1), wide_scratch(rows, states)]
        + [pltpu.VMEM((rows, LANES), f32)] * 2
        + [pltpu.SemaphoreType.DMA((10 + 2 * held,)), pltpu.SemaphoreType.DMA((len(results),)), pltpu.SemaphoreType.DMA((2,))]
        + [pltpu.SemaphoreType.DMA((EXPERTS,))] * 2
        + relay_scratch(),
        compiler_params=roomy(62, collective_id=1, has_side_effects=True),
        cost_estimate=busy(rows * states * width),
        name="mixer_back",
    )(
        back, slots, probs, chosen, normed, router, middle, up, out_weight, gate, mixed, conv, step, raw, selection, pre, padded, entry,
        decay_log, step_weight, select, taps, packed, in_weight, tokens, value,
    )


def segmented(block):
    rows = block.shape[0]
    return block.reshape(SEGS, rows // SEGS, -1).transpose(1, 0, 2).reshape(rows, -1)


def in_order(block):
    rows = block.shape[0]
    return block.reshape(rows // SEGS, SEGS, -1).transpose(1, 0, 2).reshape(rows, -1)


def rms_scale(stream):
    return lax.rsqrt(jnp.mean(stream * stream, axis=-1, keepdims=True) + 1e-05)


def rms_back(stream, scale, gain, grad):
    grown = grad * gain
    along = jnp.mean(stream * grown, axis=-1, keepdims=True)
    return scale * grown - stream * (scale * scale * scale * along), jnp.sum(grad * stream * scale, axis=0)


def silu_slope(value):
    gate = jax.nn.sigmoid(value)
    return gate * (1.0 + value * (1.0 - gate))


def product(left, right):
    return jnp.dot(left, right, preferred_element_type=jnp.float32)


def across(left, right):
    return jnp.einsum("tk,dk->td", left, right, preferred_element_type=jnp.float32)


def summed_rows(left, right):
    return jnp.einsum("tk,td->kd", left, right, preferred_element_type=jnp.float32)


CHUNK = 512
GELU_OUT = math.sqrt(2.0 / math.pi)
GELU_IN = 0.044715


def transposed_dot(left, right):
    return lax.dot_general(left, right, (((1,), (1,)), ((), ())), preferred_element_type=jnp.float32)


def column_dot(left, right):
    return lax.dot_general(left, right, (((0,), (0,)), ((), ())), preferred_element_type=jnp.float32)


def three_parts(value):
    parts, left = [], value
    for unused in range(3):
        part = left.astype(jnp.bfloat16)
        left = left - part.astype(jnp.float32)
        parts.append(part)
    return parts


def experts_kernel(
    leaving_hbm, up_ref, first_hbm, second_hbm, back_out, value_out, sums_out,
    received, first, second, pull, active, grad, value, sent, back, scaled_received, scaled_up, staged_sums,
    loads, saves, goes, comes, returns, arrives,
):
    rows, width = up_ref.shape
    hidden = second.shape[0]
    barrier = pltpu.get_barrier_semaphore()
    for peer in expert_peers():
        pl.semaphore_signal(barrier, inc=1, device_id={"expert": peer}, device_id_type=pl.DeviceIdType.MESH)
    loading = [
        pltpu.make_async_copy(second_hbm, second, loads.at[0]),
        pltpu.make_async_copy(first_hbm, first, loads.at[1]),
    ]
    for copy in loading:
        copy.start()
    pl.semaphore_wait(barrier, EXPERTS - 1)
    arriving = trade(leaving_hbm, received, goes, comes)
    loading[0].wait()

    def pulled(i, unused):
        cols = pl.ds(pl.multiple_of(i * CHUNK, CHUNK), CHUNK)
        pull[:, cols] = transposed_dot(up_ref[...], second[cols, :]).astype(jnp.bfloat16)
        return unused

    lax.fori_loop(0, hidden // CHUNK, pulled, 0)
    loading[1].wait()
    for copy in arriving:
        copy.wait()

    def layer(i, unused):
        cols = pl.ds(pl.multiple_of(i * CHUNK, CHUNK), CHUNK)
        pre = jnp.dot(received[:, :width], first[:, cols], preferred_element_type=jnp.float32)
        square = pre * pre
        bent = jnp.tanh(pre * (GELU_OUT + GELU_OUT * GELU_IN * square))
        share = 0.5 + 0.5 * bent
        slope = share + pre * (0.5 - 0.5 * bent * bent) * (GELU_OUT + 3.0 * GELU_OUT * GELU_IN * square)
        active[:, cols] = (pre * share).astype(jnp.bfloat16)
        grad[:, cols] = (slope * pull[:, cols].astype(jnp.float32)).astype(jnp.bfloat16)
        return unused

    lax.fori_loop(0, hidden // CHUNK, layer, 0)
    value[...] = jnp.dot(active[...], second[...], preferred_element_type=jnp.float32).astype(jnp.bfloat16)
    saving = [pltpu.make_async_copy(value, value_out, saves.at[0])]
    saving[0].start()
    sent[:, :width] = transposed_dot(grad[...], first[...]).astype(jnp.bfloat16)
    along = jnp.sum(value[...].astype(jnp.float32) * up_ref[...].astype(jnp.float32), axis=1, keepdims=True)
    place = lax.broadcasted_iota(jnp.int32, (rows, LANES), 1)
    tail = jnp.zeros(place.shape, jnp.float32)
    for k, part in enumerate(three_parts(along)):
        tail = jnp.where(place == k, part.astype(jnp.float32), tail)
    sent[:, width:] = tail.astype(jnp.bfloat16)
    returning = trade(sent, back, returns, arrives)

    parts = received[:, width:].astype(jnp.float32)
    gate = parts[:, 0:1] + parts[:, 1:2] + parts[:, 2:3]
    scaled_received[...] = (received[:, :width].astype(jnp.float32) * gate).astype(jnp.bfloat16)
    scaled_up[...] = (up_ref[...].astype(jnp.float32) * gate).astype(jnp.bfloat16)
    half = sums_out.shape[2]
    pairs = hidden // half // 2

    def stored(i, slot):
        return pltpu.make_async_copy(staged_sums.at[slot], sums_out.at[pl.ds(2 * i, 2)], saves.at[1 + slot])

    def sums(i, unused):
        slot = lax.rem(i, 2)
        cols = pl.ds(pl.multiple_of(i * 2 * half, 2 * half), 2 * half)

        @pl.when(i >= 2)
        def free():
            stored(i - 2, slot).wait()

        for which, (left, right) in enumerate(((grad, scaled_received), (active, scaled_up))):
            total = column_dot(left[:, cols], right[...]).astype(jnp.bfloat16)
            for k in range(2):
                staged_sums[slot, k, which] = total[k * half : (k + 1) * half]
        stored(i, slot).start()
        return unused

    lax.fori_loop(0, pairs, sums, 0)
    for i in (pairs - 2, pairs - 1):
        stored(i, i % 2).wait()
    for copy in returning:
        copy.wait()
    last = pltpu.make_async_copy(back, back_out, saves.at[3])
    last.start()
    last.wait()
    saving[0].wait()


def expert_pass(leaving, upstream, first, second, owners):
    rows, width = upstream.shape
    hidden = second.shape[0]
    wide = leaving.shape[1]
    bf16 = jnp.bfloat16
    half = hidden // owners
    anywhere = pl.BlockSpec(memory_space=pl.ANY)

    def kept(*dims):
        return pltpu.VMEM(dims, bf16)

    return pl.pallas_call(
        experts_kernel,
        out_shape=(
            shaped(rows, wide, dtype=bf16),
            shaped(rows, width, dtype=bf16),
            shaped(owners, 2, half, width, dtype=bf16),
        ),
        in_specs=[anywhere, WHOLE, anywhere, anywhere],
        out_specs=(anywhere,) * 3,
        scratch_shapes=[
            kept(rows, wide),
            kept(width, hidden),
            kept(hidden, width),
            kept(rows, hidden),
            kept(rows, hidden),
            kept(rows, hidden),
            kept(rows, width),
            kept(rows, wide),
            kept(rows, wide),
            kept(rows, width),
            kept(rows, width),
            kept(2, 2, 2, half, width),
            pltpu.SemaphoreType.DMA((2,)),
            pltpu.SemaphoreType.DMA((4,)),
        ]
        + [pltpu.SemaphoreType.DMA((EXPERTS,))] * 4,
        compiler_params=roomy(60, collective_id=3, has_side_effects=True),
        cost_estimate=pl.CostEstimate(flops=12 * rows * hidden * width, bytes_accessed=8 * hidden * width, transcendentals=rows * hidden),
        name="experts",
    )(leaving, upstream, first, second)


ORDERS = ("xyz", "yzx", "zxy")
PIECE = 16


def shares_kernel(
    conv_cols, gate_cols, token_ref, out_cols, middle_ref, left_ref, right_ref, narrow_ref,
    in_out, out_out, left_out, right_out, narrow_out, sum_ref, in_ref, out_ref, made, taken,
    half_a, half_b, half_c, one_a, one_b, one_c, sends, arrivals):
    seq, expert = lax.axis_index("seq"), lax.axis_index("expert")
    core = lax.rem(expert, 2)
    place = {"y": lax.div(seq, 4), "z": lax.rem(seq, 4), "x": lax.div(expert, 2)}
    third = token_ref.shape[1] // len(ORDERS)
    streams = [(L, q) for L in range(len(ORDERS)) for q in range(4)]

    def flip(i):
        return i + 1 - 2 * lax.rem(i, 2)

    def device(**moved):
        at = dict(place, **moved)
        return {"seq": at["y"] * 4 + at["z"], "expert": at["x"] * 2 + at.get("core", core)}

    partners = [device(core=1 - core)]
    for axis in "xyz":
        partners += [device(**{axis: flip(place[axis])}), device(**{axis: 3 - place[axis]})]
    barrier = pltpu.get_barrier_semaphore()
    for partner in partners:
        pl.semaphore_signal(barrier, inc=1, device_id=partner, device_id_type=pl.DeviceIdType.MESH)
    pl.semaphore_wait(barrier, len(partners))

    def send(source, target, partner, stream, number):
        k = streams.index(stream)
        copy = pltpu.make_async_remote_copy(
            src_ref=source, dst_ref=target, send_sem=sends.at[k, number], recv_sem=arrivals.at[k, number],
            device_id=partner, device_id_type=pl.DeviceIdType.MESH,
        )
        copy.start()
        return copy

    def add(target, source, unit):
        def step(i, unused):
            target[i] = target[i] + source[i]
            return unused

        lax.fori_loop(0, unit, step, 0, unroll=min(unit, 8))

    inner = out_cols.shape[1]
    for source, target, base in ((conv_cols, in_ref, 0), (gate_cols, in_ref, inner), (out_cols, out_ref, 0)):

        def turn_over(k, unused, source=source, target=target, base=base):
            spot = pl.ds(pl.multiple_of(k * LANES, LANES), LANES)
            target[pl.ds(pl.multiple_of(base + k * LANES, LANES), LANES), :] = source[:, spot].T
            return unused

        lax.fori_loop(0, source.shape[1] // LANES, turn_over, 0)

    halves, ones = (half_a, half_b, half_c), (one_a, one_b, one_c)
    pending, holding = {}, {}

    def set_out(L):
        for q in range(4):
            for copy in pending[L, q]:
                copy.wait()
            add(taken.at[L, q], made.at[L, 4 * core + q], 64)
            holding[L, q] = taken.at[L, q]
            pending[L, q] = start_halves(L, q, 0, holding[L, q], halves, place, flip, device, send)

    for L, order in enumerate(ORDERS):
        lanes = pl.ds(L * third, third)
        narrow = narrow_ref[:, lanes].astype(jnp.bfloat16)

        def block(s, unused):
            y, z = lax.div(s, 4), lax.rem(s, 4)
            by_in = jnp.dot(
                in_ref[pl.ds(pl.multiple_of(s * 288, 16), 288), :], token_ref[:, lanes], preferred_element_type=jnp.float32
            ).astype(jnp.bfloat16)
            here = pl.ds(pl.multiple_of(s * 144, 16), 144)
            by_out = jnp.dot(out_ref[here, :], middle_ref[:, lanes], preferred_element_type=jnp.float32)
            left, right = left_ref[here, :], right_ref[here, :]
            for x in range(4):
                at = {"x": x, "y": y, "z": z}
                slot = (at[order[0]] * 4 + at[order[1]]) * 4 + at[order[2]]
                rows = by_in[72 * x : 72 * x + 72]
                more = by_out[36 * x : 36 * x + 36].astype(jnp.bfloat16)
                for q in range(4):
                    made[L, q, slot] = rows[16 * q : 16 * q + 16]
                made[L, 4, slot, 0:8] = rows[64:]
                made[L, 4, slot, 8:16] = more[:8]
                made[L, 5, slot] = more[8:24]
                made[L, 6, slot, 0:12] = more[24:]
                made[L, 6, slot, 12:16] = narrow[8:12]
                made[L, 7, slot, 8:16] = narrow[0:8]
                last = jnp.concatenate([left[36 * x : 36 * x + 36], right[36 * x : 36 * x + 36]], axis=0)
                for part in range(third // LANES):
                    k = 8 * (L * (third // LANES) + part)
                    made[L, 7, slot, 0:8, part * LANES : (part + 1) * LANES] = last[k : k + 8].astype(jnp.bfloat16)
            return unused

        lax.fori_loop(0, 16, block, 0, unroll=2)
        for q in range(4):
            pending[L, q] = [
                send(made.at[L, 4 * (1 - core) + q], taken.at[L, q], device(core=1 - core), (L, q), 0)
            ]

        if L:
            set_out(L - 1)
    set_out(len(ORDERS) - 1)
    for turn in range(3):
        unit = 16 >> (2 * turn)
        for L, q in streams:
            axis = ORDERS[L][turn]
            i = place[axis]
            for copy in pending[L, q]:
                copy.wait()
            other = 3 - i if q < 2 else flip(i)
            got = halves[turn].at[L, q]
            add(got.at[0], holding[L, q].at[pl.ds(i * unit, unit)], unit)
            add(got.at[1], holding[L, q].at[pl.ds(other * unit, unit)], unit)
            partner = device(**{axis: other})
            pending[L, q] = [send(got.at[1], ones[turn].at[L, q], partner, (L, q), 3 + 3 * turn)]
        for L, q in streams:
            for copy in pending[L, q]:
                copy.wait()
            got = ones[turn].at[L, q]
            if turn < 2:
                add(got, halves[turn].at[L, q, 0], unit)
                holding[L, q] = got
                pending[L, q] = start_halves(L, q, turn + 1, got, halves, place, flip, device, send)
            else:
                whole = got[0].astype(jnp.float32) + halves[turn][L, q, 0, 0].astype(jnp.float32)
                sum_ref[4 * core + q, :, L * third : (L + 1) * third] = whole
    here = sum_ref.at[pl.ds(4 * core, 4)]
    send(here, here, device(core=1 - core), (0, 0), 10).wait()
    whole = jnp.concatenate([sum_ref[q] for q in range(8)], axis=0)
    last = [whole[112:120, k * LANES : (k + 1) * LANES] for k in range(whole.shape[1] // LANES)]
    last = jnp.concatenate(last + [jnp.zeros((8, LANES), jnp.float32)], axis=0)
    narrow_out[...] = jnp.concatenate([whole[120:128], whole[108:112], whole[108:112]], axis=0)
    for c in range(2):

        @pl.when(core == c)
        def pick(c=c):
            in_out[...] = whole[36 * c : 36 * c + 40]
            out_out[...] = whole[72 + 18 * c : 90 + 18 * c]
            left_out[...] = last[18 * c : 18 * c + 24]
            right_out[...] = last[36 + 18 * c : 60 + 18 * c]


def start_halves(L, q, turn, source, halves, place, flip, device, send):
    axis = ORDERS[L][turn]
    unit = 16 >> (2 * turn)
    i = place[axis]
    partner = flip(i) if q < 2 else 3 - i
    second = 3 - partner if q < 2 else flip(partner)
    target = halves[turn].at[L, q]
    return [
        send(source.at[pl.ds(partner * unit, unit)], target.at[0], device(**{axis: partner}), (L, q), 1 + 3 * turn),
        send(source.at[pl.ds(second * unit, unit)], target.at[1], device(**{axis: partner}), (L, q), 2 + 3 * turn),
    ]


def shares(conv_cols, gate_cols, tokens, out_cols, middle, left, right, narrow):
    width = tokens.shape[1]
    rows, inner = out_cols.shape
    third = width // len(ORDERS)

    def slots(*lead):
        return pltpu.VMEM((len(ORDERS),) + lead + (PIECE, third), jnp.bfloat16)

    return pl.pallas_call(
        shares_kernel,
        out_shape=(shaped(40, width), shaped(18, width), shaped(24, LANES), shaped(24, LANES), shaped(16, width)),
        in_specs=[WHOLE] * 8,
        out_specs=(WHOLE,) * 5,
        scratch_shapes=[pltpu.VMEM((8, PIECE, width), jnp.float32)]
        + [pltpu.VMEM((2 * inner, rows), jnp.bfloat16), pltpu.VMEM((inner, rows), jnp.bfloat16)]
        + [slots(8, 64), slots(4, 64)]
        + [slots(4, 2, 16 >> (2 * turn)) for turn in range(3)]
        + [slots(4, 16 >> (2 * turn)) for turn in range(3)]
        + [pltpu.SemaphoreType.DMA((12, 11))] * 2,
        compiler_params=roomy(60, collective_id=2, has_side_effects=True),
        name="shares",
    )(conv_cols, gate_cols, tokens, out_cols, middle, left, right, narrow)


def finish_kernel(
    in_ref, left_ref, right_ref, narrow_ref, expert_ref,
    in_out, tap_out, tap_bias_out, select_out, step_out, step_bias_out, decay_out, skip_out, gain_out, second_out, router_out,
    expert_first_out, expert_second_out,
):
    def turned(value):
        size = value.shape[0]
        same = lax.broadcasted_iota(jnp.int32, (size, size), 0) == lax.broadcasted_iota(jnp.int32, (size, size), 1)
        ones = jnp.where(same, 1.0, 0.0).astype(jnp.bfloat16)
        return sum(column_dot(part, ones) for part in three_parts(value))

    each, taps, states = tap_out.shape[1], tap_out.shape[0], decay_out.shape[0]
    in_out[...] = in_ref[: in_out.shape[0], :]
    select_out[...] = left_ref[:each, : select_out.shape[1]]
    sums = turned(left_ref[...])[SELECTED:, :each]
    decay_out[...] = sums[:states]
    tap_out[...] = sums[states : states + taps]
    tap_bias_out[...] = sums[states + taps : states + taps + 1]
    step_bias_out[...] = sums[states + taps + 1 : states + taps + 2]
    skip_out[...] = sums[states + taps + 2 : states + taps + 3]
    step_out[...] = right_ref[:each, : step_out.shape[1]]
    fewer = router_out.shape[1]
    owner = lax.axis_index("seq") * EXPERTS + lax.axis_index("expert")
    shape = (narrow_ref.shape[1], LANES)
    mine = lax.broadcasted_iota(jnp.int32, shape, 0) == lax.broadcasted_iota(jnp.int32, shape, 1) + owner * fewer
    ones = jnp.where(mine, 1.0, 0.0).astype(jnp.bfloat16)
    parts = three_parts(narrow_ref[...])
    picked = sum(jnp.dot(part, ones, preferred_element_type=jnp.float32) for part in parts)
    gain_out[...] = picked[EXPERTS : EXPERTS + 1, :fewer]
    second_out[...] = picked[EXPERTS + 1 : EXPERTS + 2, :fewer]
    router_out[...] = picked[:EXPERTS, :fewer]
    expert_first_out[...] = expert_ref[0].astype(jnp.float32)
    expert_second_out[...] = expert_ref[1].astype(jnp.float32)


def finish(in_share, left, right, narrow, expert_share, devices, taps, states, rank, inner):
    model = in_share.shape[1]
    each, fewer, hidden = inner // devices, model // devices, expert_share.shape[1]
    dims = (
        (2 * each, model), (taps, each), (1, each), (each, rank + 2 * states), (each, rank), (1, each), (states, each), (1, each),
        (1, fewer), (1, fewer), (EXPERTS, fewer), (hidden, model), (hidden, model),
    )
    return pl.pallas_call(
        finish_kernel,
        out_shape=tuple(shaped(*size) for size in dims),
        in_specs=[WHOLE] * 5,
        out_specs=(WHOLE,) * len(dims),
        compiler_params=roomy(32),
        name="finish",
    )(in_share, left, right, narrow, expert_share)


def local(
    tokens,
    expert_index,
    cotangent,
    first_gain,
    in_weight,
    conv_weight,
    conv_bias,
    select_weight,
    step_weight,
    step_bias,
    decay_log,
    skip_gain,
    out_weight,
    second_gain,
    router_weight,
    expert_first,
    expert_second,
):
    bf16, f32 = jnp.bfloat16, jnp.float32
    row_count, model_width = tokens.shape[1:]
    seat_count = 2 * row_count
    inner = conv_bias.shape[0]
    rank = step_weight.shape[0]
    states = decay_log.shape[0]
    taps = conv_weight.shape[0]
    seqs, experts = lax.axis_size("seq"), lax.axis_size("expert")
    (
        normed_in, gate_input, padded, preact, conv_out, step_raw, step_size, selection, first, mixer_out, gated,
        middle, normed_mid, router_probs, gate_wide, leaving, slots, upstream_there, stream, upstream, packed,
    ) = mixer(
        tokens[0], cotangent[0], conv_bias, step_bias, skip_gain, first_gain, second_gain, in_weight, conv_weight, select_weight.T, step_weight, decay_log, out_weight, router_weight.T, expert_index[:, :, 0], seat_count
    )
    back, value_there, expert_grads = expert_pass(leaving, upstream_there, expert_first[0], expert_second[0], seqs)
    expert_share = lax.psum_scatter(
        expert_grads.reshape(-1, model_width), "seq", scatter_dimension=0, tiled=True
    ).reshape(2, -1, model_width)
    middle_low, grad_gate_input, grad_conv_input, left, right, narrow, grad_tokens, value_home = mixer_back(
        back, slots, router_probs, gate_wide, normed_mid, router_weight.T, middle, upstream, out_weight, gate_input, mixer_out, conv_out,
        step_size, step_raw, selection, preact, padded, first, decay_log, step_weight, select_weight.T, conv_weight, packed, in_weight, stream, value_there,
    )
    placing = (slots[:, 0:1] == jnp.arange(seat_count, dtype=f32)[None, :]).astype(bf16)
    mixed = middle + gate_wide[:, 0:1] * product(placing, value_home)

    devices = seqs * experts
    each, fewer = inner // devices, model_width // devices
    in_share, out_share, left, right, narrow = shares(
        grad_conv_input, grad_gate_input, normed_in, gated, middle_low, left, right, narrow
    )
    in_grad, tap_grad, tap_bias_grad, select_grad, step_grad, step_bias_grad, decay_grad, skip_grad, gain_grad, second_grad, router_grad, first_grad, second_hidden = finish(
        in_share, left, right, narrow, expert_share, devices, taps, states, rank, inner
    )
    return (
        in_order(mixed.astype(bf16))[None],
        grad_tokens[None],
        gain_grad[0],
        in_grad.T,
        tap_grad,
        tap_bias_grad[0],
        select_grad,
        step_grad.T,
        step_bias_grad[0],
        decay_grad,
        skip_grad[0],
        out_share,
        second_grad[0],
        router_grad.T,
        first_grad.T[None],
        second_hidden[None],
    )


def solution(mesh):
    return jax.shard_map(
        local,
        mesh=mesh,
        in_specs=(
            P("expert", "seq", None),
            P("expert", "seq", None),
            P("expert", "seq", None),
            P(),
            P(),
            P(),
            P(),
            P(),
            P(),
            P(),
            P(),
            P(),
            P(),
            P(),
            P(),
            P("expert", None, None),
            P("expert", None, None),
        ),
        out_specs=(
            P("expert", "seq", None),
            P("expert", "seq", None),
            P(("seq", "expert")),
            P(None, ("seq", "expert")),
            P(None, ("seq", "expert")),
            P(("seq", "expert")),
            P(("seq", "expert"), None),
            P(None, ("seq", "expert")),
            P(("seq", "expert")),
            P(None, ("seq", "expert")),
            P(("seq", "expert")),
            P(("seq", "expert"), None),
            P(("seq", "expert")),
            P(("seq", "expert"), None),
            P("expert", None, "seq"),
            P("expert", "seq", None),
        ),
        check_vma=False,
    )
```

```python
import functools
import math

import jax
import jax.numpy as jnp
from jax import lax
from jax.experimental import pallas as pl
from jax.experimental.pallas import tpu as pltpu
from jax.sharding import PartitionSpec as P

LANES = 128
SEGS = 8
LOG2E = math.log2(math.e)
PARTS = 3
SELECTED = 104
EXPERTS = 8
CAPACITY = 64
CUT = 768
GRID = 4


def spread_ones(states):
    row = lax.broadcasted_iota(jnp.int32, (LANES, states * LANES), 0)
    lane = lax.broadcasted_iota(jnp.int32, (LANES, states * LANES), 1)
    return row, lane // LANES


def fill_maps(sel_ref, wide_ref, column):
    steps, states = wide_ref.shape[:2]
    row, block = spread_ones(states)
    ones = jnp.where(row == block + column, 1.0, 0.0).astype(jnp.bfloat16)
    left, total = sel_ref[...], None
    for unused in range(3):
        part = left.astype(jnp.bfloat16)
        left = left - part.astype(jnp.float32)
        spread = jnp.dot(part, ones, preferred_element_type=jnp.float32)
        total = spread if total is None else total + spread
    for n in range(states):
        wide_ref[:, n] = total[:, n * LANES : (n + 1) * LANES].reshape(steps, SEGS, LANES)


def gather_maps(sum_ref, column):
    steps, states = sum_ref.shape[:2]
    row, block = spread_ones(states)
    ones = jnp.where(row == block + column, 1.0, 0.0).astype(jnp.bfloat16)
    left = jnp.concatenate([sum_ref[:, n].reshape(steps * SEGS, LANES) for n in range(states)], axis=1)
    total = None
    for unused in range(3):
        part = left.astype(jnp.bfloat16)
        left = left - part.astype(jnp.float32)
        summed = transposed_dot(part, ones)
        total = summed if total is None else total + summed
    return total


def lanes_of(block):
    return pl.ds(pl.multiple_of(block * LANES, LANES), LANES)


def rows_of(j):
    return pl.ds(pl.multiple_of(j * SEGS, SEGS), SEGS)


def rates_of(log_ref, lanes):
    states = log_ref.shape[0]
    rate = -LOG2E * jnp.exp(log_ref[:, lanes])
    return jnp.stack([jnp.broadcast_to(rate[n : n + 1], (SEGS, LANES)) for n in range(states)])


def neighbour(value, hop, later, fill):
    axis = value.ndim - 2
    place = lax.broadcasted_iota(jnp.int32, value.shape, axis)
    if later:
        return jnp.where(place < SEGS - hop, pltpu.roll(value, SEGS - hop, axis), fill)
    return jnp.where(place >= hop, pltpu.roll(value, hop, axis), fill)


def summarize(later, part, step_ref, other_ref, wide, log_ref, part_ref, span_ref, message):
    steps, states = wide.shape[:2]
    blocks = step_ref.shape[1] // LANES // PARTS

    def block(i, unused):
        lanes = lanes_of(part * blocks + i)
        rate = rates_of(log_ref, lanes)

        def advance(turn, carry):
            span, memory = carry
            j = steps - 1 - turn if later else turn
            step = step_ref[rows_of(j), lanes]
            other = other_ref[rows_of(j), lanes]
            decay = jnp.exp2(step * rate)
            if later:
                memory = decay * (memory + wide[j] * other)
            else:
                memory = decay * memory + wide[j] * (step * other)
            return span + step, memory

        zero = jnp.zeros((SEGS, LANES), jnp.float32)
        span, memory = lax.fori_loop(0, steps, advance, (zero, jnp.zeros(rate.shape, jnp.float32)), unroll=16)
        hop = 1
        while hop < SEGS:
            memory = memory + jnp.exp2(rate * span) * neighbour(memory, hop, later, 0.0)
            span = span + neighbour(span, hop, later, 0.0)
            hop *= 2
        span_ref[:, lanes] = span
        part_ref[:, :, lanes] = memory
        end = 0 if later else SEGS - 1
        for n in range(states):
            message[n // GRID, n % GRID, pl.ds(i, 1), :] = memory[n, end : end + 1]
        for q in range(GRID):
            message[q, GRID, pl.ds(i, 1), :] = span[end : end + 1]
        return unused

    lax.fori_loop(0, blocks, block, 0)


def entering(later, part_ref, span_ref, rate, lanes, carried):
    ends = part_ref[:, :, lanes] + jnp.exp2(rate * span_ref[:, lanes]) * carried
    return neighbour(ends, 1, later, carried)


def carried_at(in_ref, part, i):
    states = GRID * GRID
    return jnp.stack(
        [jnp.broadcast_to(in_ref[n // GRID, n % GRID, pl.ds(i, 1), :], (SEGS, LANES)) for n in range(states)]
    )


def scan_part(part, step_ref, conv_ref, wide_in, wide_out, log_ref, part_ref, span_ref, in_ref, y_ref, entry_ref):
    steps = wide_in.shape[0]
    blocks = step_ref.shape[1] // LANES // PARTS

    def block(i, unused):
        lanes = lanes_of(part * blocks + i)
        rate = rates_of(log_ref, lanes)
        first = entering(False, part_ref, span_ref, rate, lanes, carried_at(in_ref, part, i))
        entry_ref[:, :, lanes] = first

        def advance(j, memory):
            step = step_ref[rows_of(j), lanes]
            memory = jnp.exp2(step * rate) * memory + wide_in[j] * (step * conv_ref[rows_of(j), lanes])
            y_ref[rows_of(j), lanes] = jnp.sum(wide_out[j] * memory, axis=0)
            return memory

        lax.fori_loop(0, steps, advance, first, unroll=16)
        return unused

    lax.fori_loop(0, blocks, block, 0)


def retreat_part(
    part, step_ref, conv_ref, grad_ref, raw_ref, wide_in, wide_out, log_ref, pull_ref, entry_ref, part_ref, span_ref, in_ref,
    low_ref, gconv_ref, glog_ref, gbias_ref, sum_in, sum_out, states_ref, decays_ref, raw_sum, raw_rows,
):
    steps = wide_in.shape[0]
    blocks = step_ref.shape[1] // LANES // PARTS

    def block(i, unused):
        lanes = lanes_of(part * blocks + i)
        rate = rates_of(log_ref, lanes)

        def advance(j, memory):
            step = step_ref[rows_of(j), lanes]
            decay = jnp.exp2(step * rate)
            memory = decay * memory + wide_in[j] * (step * conv_ref[rows_of(j), lanes])
            decays_ref[j] = decay
            states_ref[j + 1] = memory
            return memory

        first = entry_ref[:, :, lanes]
        states_ref[0] = first
        lax.fori_loop(0, steps, advance, first, unroll=8)

        def retreat(turn, carry):
            j = steps - 1 - turn
            mu, slow = carry
            step = step_ref[rows_of(j), lanes]
            conv = conv_ref[rows_of(j), lanes]
            grad = grad_ref[rows_of(j), lanes]
            lam = wide_out[j] * grad + mu
            sum_out[j] += grad * states_ref[j + 1]
            sum_in[j] += lam * (step * conv)
            by_in = jnp.sum(lam * wide_in[j], axis=0)
            mu = lam * decays_ref[j]
            kept = mu * states_ref[j]
            by_rate = jnp.sum(kept * rate, axis=0)
            grad_step = by_in * conv + (1.0 / LOG2E) * by_rate
            raw_rows[rows_of(j), :] = grad_step * jax.nn.sigmoid(raw_ref[rows_of(j), lanes])
            gconv_ref[rows_of(j), lanes] = by_in * step
            return mu, slow + kept * step

        last = entering(True, part_ref, span_ref, rate, lanes, carried_at(in_ref, part, i))
        unused_mu, slow = lax.fori_loop(0, steps, retreat, (last, jnp.zeros(rate.shape, jnp.float32)), unroll=8)
        glog_ref[:, lanes] = (1.0 / LOG2E) * jnp.sum(slow * rate, axis=1)
        raw_steps = raw_rows[...]
        gbias_ref[:, lanes] = jnp.sum(raw_steps, axis=0, keepdims=True)
        low = raw_steps.astype(jnp.bfloat16)
        low_ref[:, lanes] = low
        raw_sum[:, : pull_ref.shape[0]] += transposed_dot(low, pull_ref[:, lanes])
        return unused

    lax.fori_loop(0, blocks, block, 0)


def expert_peers():
    me = lax.axis_index("expert")
    return [lax.rem(me + k, EXPERTS) for k in range(1, EXPERTS)]


def seats_of(device):
    return pl.ds(pl.multiple_of(device * CAPACITY, CAPACITY), CAPACITY)


def trade(source, target, send_sems, recv_sems):
    me = lax.axis_index("expert")
    copies = [
        pltpu.make_async_remote_copy(
            src_ref=source.at[seats_of(peer)], dst_ref=target.at[seats_of(me)], send_sem=send_sems.at[k], recv_sem=recv_sems.at[k],
            device_id={"expert": peer}, device_id_type=pl.DeviceIdType.MESH,
        )
        for k, peer in enumerate(expert_peers())
    ]
    copies.append(pltpu.make_async_copy(source.at[seats_of(me)], target.at[seats_of(me)], send_sems.at[EXPERTS - 1]))
    for copy in copies:
        copy.start()
    return copies


class Relay:
    def __init__(self, later, log_ref, log_rows, in_ref, message, got, row, rows_got, above, made, sends, arrivals, others=()):
        self.later, self.log_rows, self.message, self.got = later, log_rows, message, got
        self.row, self.rows_got, self.above, self.made, self.in_ref = row, rows_got, above, made, in_ref
        self.sends, self.arrivals = sends, arrivals
        seq = lax.axis_index("seq")
        self.y, self.z = lax.div(seq, GRID), lax.rem(seq, GRID)
        blocks = log_ref.shape[1] // LANES // PARTS
        log_rows[...] = jnp.zeros_like(log_rows)
        for part in range(PARTS):
            for b in range(blocks):
                lanes = pl.ds((part * blocks + b) * LANES, LANES)
                for n in range(GRID * GRID):
                    log_rows[part, n // GRID, n % GRID, b : b + 1, :] = log_ref[n : n + 1, lanes]
        self.flying = {}
        barrier = pltpu.get_barrier_semaphore()
        peers = [self.across(k) for k in range(1, GRID)] + [self.along(k) for k in range(1, GRID)]
        peers += [self.onward(1), self.onward(-1)] + list(others)
        for peer in peers:
            pl.semaphore_signal(barrier, inc=1, device_id=peer, device_id_type=pl.DeviceIdType.MESH)
        self.peers = len(peers)

    def onward(self, k):
        size = GRID * GRID
        return {"seq": lax.rem(self.y * GRID + self.z + k + size, size)}

    def across(self, k):
        return {"seq": self.y * GRID + lax.rem(self.z + k, GRID)}

    def along(self, k):
        return {"seq": lax.rem(self.y + k, GRID) * GRID + self.z}

    def meet(self):
        pl.semaphore_wait(pltpu.get_barrier_semaphore(), self.peers)

    def send(self, part, phase, k, source, target, peer):
        copy = pltpu.make_async_remote_copy(
            src_ref=source, dst_ref=target, send_sem=self.sends.at[part, phase, k], recv_sem=self.arrivals.at[part, phase, k],
            device_id=peer, device_id_type=pl.DeviceIdType.MESH,
        )
        copy.start()
        self.flying.setdefault((part, phase), []).append(copy)

    def land(self, part, phase):
        for copy in self.flying[part, phase]:
            copy.wait()

    def order(self):
        return range(GRID - 1, -1, -1) if self.later else range(GRID)

    def rate(self, part):
        return -LOG2E * jnp.exp(self.log_rows[part, self.z])

    def first(self, part):
        for k in range(1, GRID):
            peer = lax.rem(self.z + k, GRID)
            self.send(part, 0, k, self.message.at[part, peer], self.got.at[part, k], self.across(k))
        self.got[part, 0] = self.message[part, self.z]

    def second(self, part):
        self.land(part, 0)
        rate = self.rate(part)
        state, span = jnp.zeros(rate.shape, jnp.float32), jnp.zeros(rate.shape[1:], jnp.float32)
        for z in self.order():
            block = self.got[part, lax.rem(self.z - z + GRID, GRID)]
            state = jnp.exp2(rate * block[GRID]) * state + block[:GRID]
            span = span + block[GRID]
        self.row[part, :GRID] = state
        self.row[part, GRID] = span
        for k in range(1, GRID):
            self.send(part, 1, k, self.row.at[part], self.rows_got.at[part, k], self.along(k))
        self.rows_got[part, 0] = self.row[part]

    def third(self, part):
        self.land(part, 1)
        rate = self.rate(part)
        state = jnp.zeros(rate.shape, jnp.float32)
        for y in self.order():
            self.above[part, y] = state
            block = self.rows_got[part, lax.rem(self.y - y + GRID, GRID)]
            state = jnp.exp2(rate * block[GRID]) * state + block[:GRID]
        state = self.above[part, self.y]
        for z in self.order():
            self.made[part, z] = state
            block = self.got[part, lax.rem(self.z - z + GRID, GRID)]
            state = jnp.exp2(rate * block[GRID]) * state + block[:GRID]
        for k in range(1, GRID):
            peer = lax.rem(self.z + k, GRID)
            self.send(part, 2, k, self.made.at[part, peer], self.in_ref.at[part, self.z], self.across(k))
        self.in_ref[part, self.z] = self.made[part, self.z]

    def done(self, part):
        self.land(part, 2)


def staged(relay, summary, extra, scan):
    summary(0)
    relay.first(0)
    summary(1)
    relay.first(1)
    relay.second(0)
    summary(2)
    relay.first(2)
    relay.third(0)
    relay.second(1)
    extra()
    relay.second(2)
    relay.third(1)
    relay.done(0)
    scan(0)
    relay.third(2)
    relay.done(1)
    scan(1)
    relay.done(2)
    scan(2)


def named_experts(slots, rows):
    first = (lax.broadcasted_iota(jnp.int32, (rows, EXPERTS), 1) * CAPACITY).astype(jnp.float32)
    return jnp.where((slots >= first) & (slots < first + CAPACITY), 1.0, 0.0)


def seated_rows(slots, rows, seats):
    seat = lax.broadcasted_iota(jnp.int32, (rows, seats), 1).astype(jnp.float32)
    return jnp.where(seat == slots, 1.0, 0.0).astype(jnp.bfloat16)


def order_ones(rows, back):
    row, token = lax.broadcasted_iota(jnp.int32, (rows, rows), 0), lax.broadcasted_iota(jnp.int32, (rows, rows), 1)
    if back:
        row, token = token, row
    same = token == lax.rem(row, SEGS) * (rows // SEGS) + lax.div(row, SEGS)
    return jnp.where(same, 1.0, 0.0).astype(jnp.bfloat16)


def slots_of(routes, rows):
    expert = lax.broadcasted_iota(jnp.int32, (rows, EXPERTS), 1)
    named = jnp.where(lax.broadcasted_iota(jnp.int32, (EXPERTS, rows), 0) == routes, 1.0, 0.0).astype(jnp.bfloat16)
    named = transposed_dot(order_ones(rows, False), named)
    later = lax.broadcasted_iota(jnp.int32, (rows, rows), 0) > lax.broadcasted_iota(jnp.int32, (rows, rows), 1)
    ahead = jnp.dot(jnp.where(later, 1.0, 0.0).astype(jnp.bfloat16), named.astype(jnp.bfloat16), preferred_element_type=jnp.float32)
    return jnp.sum(named * (ahead + (expert * CAPACITY).astype(jnp.float32)), axis=1, keepdims=True)


def mixer_kernel(
    token_in, up_in, tap_bias_in, step_bias_in, skip_in, gain_in, second_gain_in, in_hbm, tap_ref, select_ref, step_weight_ref, log_ref, out_hbm, router_ref, route_ref,
    normed_out, gate_out, padded_out, pre_out, conv_out, raw_out, step_out, sel_out, entry_out, mixer_out, gated_out,
    middle_out, normed_mid_out, probs_out, chosen_out, leaving_out, slot_out, up_out, token_out, up_order_out, row_out,
    normed, in_ref, out_ref, padded, gate, pre, conv, raw, step, sel, entry, mixer, gated, middle, normed_mid, probs, chosen, leaving, slots, up_seated, token_ref, up_ref, row_ref,
    tail, tail_got, part_ref, span_ref, wide_in, wide_out, loads, saves, passing, goes, comes, log_rows, relay_in, *relayed
):
    rows, width = step.shape
    model = token_ref.shape[1]
    tap_bias_ref, step_bias_ref, skip_ref = (row_ref.at[k : k + 1] for k in range(3))
    gain_ref, second_gain_ref = row_ref.at[3:4, :model], row_ref.at[3:4, model:]
    taps, states = tap_ref.shape[0], log_ref.shape[0]
    reach = (taps - 1) * SEGS
    rank = SELECTED - 2 * states
    pieces = in_ref.shape[0]
    cut = in_ref.shape[2]
    blocks = width // LANES

    loading = [pltpu.make_async_copy(in_hbm.at[:, pl.ds(k * cut, cut)], in_ref.at[k], loads.at[k]) for k in range(pieces)]
    loading.append(pltpu.make_async_copy(out_hbm, out_ref, loads.at[pieces]))
    for copy in loading:
        copy.start()
    saving = []

    def save(source, target):
        copy = pltpu.make_async_copy(source, target, saves.at[len(saving)])
        copy.start()
        saving.append(copy)

    relay = Relay(False, log_ref, log_rows, relay_in, *relayed, others=[{"expert": peer} for peer in expert_peers()])

    for k, vector in enumerate((tap_bias_in, step_bias_in, skip_in)):
        row_ref[k : k + 1, :] = vector[...][None, :]
    row_ref[3:4, :model] = gain_in[...][None, :]
    row_ref[3:4, model:] = second_gain_in[...][None, :]
    row_ref[4:, :] = jnp.zeros_like(row_ref[4:, :])
    save(row_ref, row_out)
    ordering = order_ones(rows, False)
    stream = jnp.dot(ordering, token_in[...], preferred_element_type=jnp.float32)
    token_ref[...] = stream.astype(jnp.bfloat16)
    save(token_ref, token_out)
    normed[...] = (stream * rms_scale(stream) * gain_ref[...]).astype(jnp.bfloat16)
    save(normed, normed_out)
    for k in range(pieces // 2):
        loading[k].wait()
        padded[reach:, k * cut : (k + 1) * cut] = jnp.dot(normed[...], in_ref[k], preferred_element_type=jnp.float32)
    tail[...] = jnp.zeros_like(tail)
    for k in range(taps - 1):
        row = reach + rows - (taps - 1 - k) * SEGS + SEGS - 1
        tail[k : k + 1, :] = padded[row : row + 1, :]
    slot = slots_of(route_ref[...], rows)
    slots[...] = jnp.broadcast_to(slot, slots.shape)
    save(slots, slot_out)
    seating = seated_rows(slot, rows, leaving.shape[0])
    up_ref[...] = jnp.dot(ordering, up_in[...], preferred_element_type=jnp.float32).astype(jnp.bfloat16)
    save(up_ref, up_order_out)
    up_seated[...] = column_dot(seating, up_ref[...]).astype(jnp.bfloat16)
    relay.meet()
    handing = pltpu.make_async_remote_copy(
        src_ref=tail, dst_ref=tail_got, send_sem=passing.at[0], recv_sem=passing.at[1],
        device_id=relay.onward(1), device_id_type=pl.DeviceIdType.MESH,
    )
    handing.start()
    trading = trade(up_seated, up_out, goes, comes)
    for k in range(pieces // 2, pieces):
        loading[k].wait()
        spot = slice((k - pieces // 2) * cut, (k - pieces // 2 + 1) * cut)
        gate[:, spot] = jnp.dot(normed[...], in_ref[k], preferred_element_type=jnp.float32)
    save(gate, gate_out)
    handing.wait()
    started = jnp.where(lax.axis_index("seq") > 0, 1.0, 0.0)
    for k in range(taps - 1):
        row = rows + k * SEGS
        segment = lax.broadcasted_iota(jnp.int32, (SEGS, width), 0)
        before = pltpu.roll(padded[row : row + SEGS, :], 1, 0)
        padded[k * SEGS : (k + 1) * SEGS, :] = jnp.where(segment == 0, started * tail_got[k : k + 1, :], before)
    save(padded, padded_out)

    sel[...] = jnp.zeros_like(sel)

    def convolve(b, unused):
        lanes = lanes_of(b)
        value = tap_bias_ref[:, lanes]
        for k in range(taps):
            value = value + tap_ref[k : k + 1, lanes] * padded[k * SEGS : k * SEGS + rows, lanes]
        pre[:, lanes] = value
        value = value * jax.nn.sigmoid(value)
        conv[:, lanes] = value
        sel[:, :SELECTED] += transposed_dot(value.astype(jnp.bfloat16), select_ref[:, lanes])
        return unused

    lax.fori_loop(0, blocks, convolve, 0)
    save(pre, pre_out)
    save(conv, conv_out)
    save(sel, sel_out)
    step_low = sel[:, :rank].astype(jnp.bfloat16)

    def size(b, unused):
        lanes = lanes_of(b)
        value = jnp.dot(step_low, step_weight_ref[:, lanes], preferred_element_type=jnp.float32) + step_bias_ref[:, lanes]
        raw[:, lanes] = value
        step[:, lanes] = jnp.maximum(value, 0.0) + jnp.log1p(jnp.exp(-jnp.abs(value)))
        return unused

    lax.fori_loop(0, blocks, size, 0)
    save(raw, raw_out)
    save(step, step_out)
    fill_maps(sel, wide_in, rank)

    def summary(part):
        summarize(False, part, step, conv, wide_in, log_ref, part_ref, span_ref, relay.message.at[part])

    def scan(part):
        scan_part(part, step, conv, wide_in, wide_out, log_ref, part_ref, span_ref, relay_in.at[part], mixer, entry)

    staged(relay, summary, lambda: fill_maps(sel, wide_out, rank + states), scan)
    save(entry, entry_out)

    def blend(b, unused):
        lanes = lanes_of(b)
        value = mixer[:, lanes] + skip_ref[:, lanes] * conv[:, lanes]
        mixer[:, lanes] = value
        opening = gate[:, lanes]
        gated[:, lanes] = (value * (opening * jax.nn.sigmoid(opening))).astype(jnp.bfloat16)
        return unused

    lax.fori_loop(0, blocks, blend, 0)
    save(mixer, mixer_out)
    save(gated, gated_out)
    loading[pieces].wait()
    value = token_ref[...].astype(jnp.float32) + jnp.dot(gated[...], out_ref[...], preferred_element_type=jnp.float32)
    middle[...] = value
    save(middle, middle_out)
    normed_mid[...] = (value * rms_scale(value) * second_gain_ref[...]).astype(jnp.bfloat16)
    save(normed_mid, normed_mid_out)
    logits = transposed_dot(normed_mid[...], router_ref[...])
    grown = jnp.exp(logits - jnp.max(logits, axis=1, keepdims=True))
    probs[...] = grown / jnp.sum(grown, axis=1, keepdims=True)
    save(probs, probs_out)
    gate_value = jnp.sum(named_experts(slots[:, 0:1], rows) * probs[...], axis=1, keepdims=True)
    chosen[...] = jnp.broadcast_to(gate_value, (rows, LANES))
    save(chosen, chosen_out)
    place = lax.broadcasted_iota(jnp.int32, (rows, LANES), 1)
    parts = jnp.zeros((rows, LANES), jnp.float32)
    for k, piece in enumerate(three_parts(gate_value)):
        parts = jnp.where(place == k, piece.astype(jnp.float32), parts)
    seating = seated_rows(slots[:, 0:1], rows, leaving.shape[0])
    leaving[:, :model] = column_dot(seating, normed_mid[...]).astype(jnp.bfloat16)
    leaving[:, model:] = column_dot(seating, parts.astype(jnp.bfloat16)).astype(jnp.bfloat16)
    save(leaving, leaving_out)
    for copy in saving + trading:
        copy.wait()


def mixer_back_kernel(
    back_hbm, slot_ref, probs_ref, chosen_ref, normed_ref, router_ref, middle_ref, up_ref, out_hbm, gate_hbm,
    mixer_hbm, conv_hbm, step_hbm, raw_hbm, sel_ref, pre_hbm, padded_hbm, entry_hbm, log_ref, step_weight_ref, select_ref,
    tap_ref, packed_ref, in_hbm, token_ref, value_hbm,
    low_out, gate_out, conv_out, left_out, right_out, narrow_out, token_out, value_out,
    back, out_ref, gate, mixer, conv, step, raw, padded, entry, in_ref,
    middle_low, grad_gate, grad_conv, left, right, narrow, grad_middle, mixed, low, gsel, glog, gbias, total, tail, tail_got, row_ref,
    part_ref, span_ref, wide_in, wide_out, sum_in, sum_out, states_ref, decays_ref, raw_sum, raw_rows,
    loads, saves, passing, goes, comes, log_rows, relay_in, *relayed
):
    rows, width = step.shape
    model = up_ref.shape[1]
    skip_ref, gain_ref, second_gain_ref = packed_ref.at[2:3], packed_ref.at[3:4, :model], packed_ref.at[3:4, model:]
    taps, states = tap_ref.shape[0], log_ref.shape[0]
    rank = SELECTED - 2 * states
    held, cut = in_ref.shape[0], in_ref.shape[2]
    blocks = width // LANES
    saving, numbers = [], iter(range(64))

    def load(source, target):
        copy = pltpu.make_async_copy(source, target, loads.at[next(numbers)])
        copy.start()
        return copy

    def save(source, target):
        copy = pltpu.make_async_copy(source, target, saves.at[len(saving)])
        copy.start()
        saving.append(copy)

    def weight(k):
        return load(in_hbm.at[:, pl.ds(k * cut, cut)], in_ref.at[k % held])

    early = [load(back_hbm, back), load(out_hbm, out_ref), load(gate_hbm, gate), load(mixer_hbm, mixer)]
    scanning = [load(step_hbm, step), load(conv_hbm, conv), load(raw_hbm, raw), load(entry_hbm, entry)]
    padding = load(padded_hbm, padded)
    weights = {k: weight(k) for k in range(held, 2 * held)}
    relay = Relay(True, log_ref, log_rows, relay_in, *relayed, others=[{"expert": peer} for peer in expert_peers()])

    early[0].wait()
    slots = slot_ref[:, 0:1]
    seating = seated_rows(slots, rows, back.shape[0])
    chosen = chosen_ref[:, 0:1]
    along = jnp.sum(jnp.dot(seating, back[:, model:], preferred_element_type=jnp.float32), axis=1, keepdims=True)
    place = lax.broadcasted_iota(jnp.int32, (rows, LANES), 1)
    logits = (along * chosen * (named_experts(slots, rows) - probs_ref[...])).astype(jnp.bfloat16)
    grad = jnp.dot(logits, router_ref[...], preferred_element_type=jnp.float32) + chosen * jnp.dot(seating, back[:, :model], preferred_element_type=jnp.float32)
    narrow[...] = jnp.zeros_like(narrow)
    narrow[:EXPERTS, :] = column_dot(logits, normed_ref[...])
    value = middle_ref[...]
    returned, gained = rms_back(value, rms_scale(value), second_gain_ref[...], grad)
    narrow[EXPERTS + 1 : EXPERTS + 2, :] = gained[None, :]
    value = up_ref[...].astype(jnp.float32) + returned
    grad_middle[...] = value
    middle_low[...] = value.astype(jnp.bfloat16)
    save(middle_low, low_out)
    for copy in early[1:]:
        copy.wait()

    def open_gate(b, unused):
        lanes = lanes_of(b)
        grown = transposed_dot(middle_low[...], out_ref[lanes, :])
        opening = gate[:, lanes]
        mixed[:, lanes] = grown * (opening * jax.nn.sigmoid(opening))
        grad_gate[:, lanes] = (grown * mixer[:, lanes] * silu_slope(opening)).astype(jnp.bfloat16)
        return unused

    lax.fori_loop(0, blocks, open_gate, 0)
    save(grad_gate, gate_out)
    pre, gconv = gate, mixer
    activating = load(pre_hbm, pre)
    for copy in scanning:
        copy.wait()

    fill_maps(sel_ref, wide_out, rank + states)

    def summary(part):
        summarize(True, part, step, mixed, wide_out, log_ref, part_ref, span_ref, relay.message.at[part])

    def prepare():
        fill_maps(sel_ref, wide_in, rank)
        sum_in[...] = jnp.zeros_like(sum_in)
        sum_out[...] = jnp.zeros_like(sum_out)
        raw_sum[...] = jnp.zeros_like(raw_sum)

    def scan(part):
        retreat_part(
            part, step, conv, mixed, raw, wide_in, wide_out, log_ref, step_weight_ref, entry, part_ref, span_ref,
            relay_in.at[part], low, gconv, glog, gbias, sum_in, sum_out, states_ref, decays_ref, raw_sum, raw_rows,
        )

    relay.meet()
    trading = trade(value_hbm, value_out, goes, comes)
    staged(relay, summary, prepare, scan)
    maps = gather_maps(sum_in, rank) + gather_maps(sum_out, rank + states)
    gsel[...] = (raw_sum[...] + maps).astype(jnp.bfloat16)

    activating.wait()
    padding.wait()
    step_low = jnp.where(place < rank, sel_ref[...], 0.0).astype(jnp.bfloat16)
    tall = lax.broadcasted_iota(jnp.int32, (row_ref.shape[0], LANES), 0)
    spots = jnp.where(lax.broadcasted_iota(jnp.int32, tall.shape, 1) == tall + SELECTED, 1.0, 0.0).astype(jnp.bfloat16)
    row_ref[...] = jnp.zeros_like(row_ref)

    def convolve_back(b, unused):
        lanes = lanes_of(b)
        around, kept = mixed[:, lanes], conv[:, lanes]
        grown = jnp.dot(gsel[:, :SELECTED], select_ref[:, lanes], preferred_element_type=jnp.float32) + gconv[:, lanes] + skip_ref[:, lanes] * around
        grown = grown * silu_slope(pre[:, lanes])
        gconv[:, lanes] = grown
        row_ref[:states, :] = glog[:, lanes]
        for k in range(taps):
            row_ref[states + k : states + k + 1, :] = jnp.sum(
                grown * padded[k * SEGS : k * SEGS + rows, lanes], axis=0, keepdims=True
            )
        row_ref[states + taps : states + taps + 1, :] = jnp.sum(grown, axis=0, keepdims=True)
        row_ref[states + taps + 1 : states + taps + 2, :] = gbias[:, lanes]
        row_ref[states + taps + 2 : states + taps + 3, :] = jnp.sum(around * kept, axis=0, keepdims=True)
        summed = column_dot(kept.astype(jnp.bfloat16), gsel[...])
        for piece in three_parts(row_ref[...]):
            summed = summed + column_dot(piece, spots)
        left[lanes, :] = summed
        right[lanes, :] = column_dot(low[:, lanes], step_low)
        return unused

    lax.fori_loop(0, blocks, convolve_back, 0)
    save(left, left_out)
    save(right, right_out)

    tail[...] = jnp.zeros_like(tail)
    for k in range(taps - 1):
        tail[k : k + 1, :] = gconv[k * SEGS : k * SEGS + 1, :]
    handing = pltpu.make_async_remote_copy(
        src_ref=tail, dst_ref=tail_got, send_sem=passing.at[0], recv_sem=passing.at[1],
        device_id=relay.onward(-1), device_id_type=pl.DeviceIdType.MESH,
    )
    handing.start()
    for k in range(held):
        weights[held + k].wait()
        summed = transposed_dot(grad_gate[:, k * cut : (k + 1) * cut], in_ref[k])
        total[...] = summed if k == 0 else total[...] + summed
        weights[k] = weight(k)
    handing.wait()
    goes_on = jnp.where(lax.axis_index("seq") < GRID * GRID - 1, 1.0, 0.0)
    segment = lax.broadcasted_iota(jnp.int32, (SEGS, cut), 0)
    for k in range(held):
        spot = slice(k * cut, (k + 1) * cut)
        grown = None
        for t in range(taps):
            late = taps - 1 - t
            shifted = gconv[late * SEGS :, spot]
            if late:
                wrapped = [
                    jnp.where(
                        segment == SEGS - 1,
                        goes_on * tail_got[j : j + 1, spot],
                        pltpu.roll(gconv[j * SEGS : (j + 1) * SEGS, spot], SEGS - 1, 0),
                    )
                    for j in range(late)
                ]
                shifted = jnp.concatenate([shifted] + wrapped, axis=0)
            term = tap_ref[t : t + 1, spot] * shifted
            grown = term if grown is None else grown + term
        grad_conv[:, spot] = grown.astype(jnp.bfloat16)
        weights[k].wait()
        total[...] += transposed_dot(grad_conv[:, spot], in_ref[k])
    save(grad_conv, conv_out)
    stream = token_ref[...].astype(jnp.float32)
    returned, gained = rms_back(stream, rms_scale(stream), gain_ref[...], total[...])
    narrow[EXPERTS : EXPERTS + 1, :] = gained[None, :]
    save(narrow, narrow_out)
    value = grad_middle[...] + returned
    ordering = order_ones(rows, True)
    total[...] = sum(jnp.dot(ordering, part, preferred_element_type=jnp.float32) for part in three_parts(value))
    save(total, token_out)
    for copy in saving + trading:
        copy.wait()


WHOLE = pl.BlockSpec(memory_space=pltpu.VMEM)


def shaped(*dims, dtype=jnp.float32):
    return jax.ShapeDtypeStruct(dims, dtype)


def roomy(mebibytes, **more):
    return pltpu.CompilerParams(vmem_limit_bytes=mebibytes << 20, **more)


def busy(elements):
    return pl.CostEstimate(flops=4096 * elements, bytes_accessed=16 * elements, transcendentals=4 * elements)


def wide_scratch(rows, states, extra=0):
    return pltpu.VMEM((rows // SEGS + extra, states, SEGS, LANES), jnp.float32)


def chain_scratch(states, width):
    return [pltpu.VMEM((states, SEGS, width), jnp.float32), pltpu.VMEM((SEGS, width), jnp.float32)]


def relay_scratch():
    def kept(*dims):
        return pltpu.VMEM((PARTS,) + dims + (SEGS, LANES), jnp.float32)

    return [
        kept(GRID, GRID),
        kept(GRID, GRID),
        kept(GRID, GRID + 1),
        kept(GRID, GRID + 1),
        kept(GRID + 1),
        kept(GRID, GRID + 1),
        kept(GRID, GRID),
        kept(GRID, GRID),
        pltpu.SemaphoreType.DMA((PARTS, 3, GRID)),
        pltpu.SemaphoreType.DMA((PARTS, 3, GRID)),
    ]


def mixer(tokens, upstream, tap_bias, step_bias, skip, gain, second_gain, in_weight, taps, select, step_weight, decay_log, out_weight, router, routes, seats):
    rows, model = tokens.shape
    states, width = decay_log.shape
    reach = (taps.shape[0] - 1) * SEGS
    bf16, f32 = jnp.bfloat16, jnp.float32
    anywhere = pl.BlockSpec(memory_space=pl.ANY)
    results = [
        ((rows, model), bf16),
        ((rows, width), f32),
        ((rows + reach, width), f32),
        ((rows, width), f32),
        ((rows, width), f32),
        ((rows, width), f32),
        ((rows, width), f32),
        ((rows, LANES), f32),
        ((states, SEGS, width), f32),
        ((rows, width), f32),
        ((rows, width), bf16),
        ((rows, model), f32),
        ((rows, model), bf16),
        ((rows, EXPERTS), f32),
        ((rows, LANES), f32),
        ((seats, model + LANES), bf16),
        ((rows, LANES), f32),
        ((seats, model), bf16),
        ((rows, model), bf16),
        ((rows, model), bf16),
        ((SEGS, width), f32),
    ]
    kept = [pltpu.VMEM(dims, dtype) for dims, dtype in results]
    weights = [pltpu.VMEM((2 * width // CUT, model, CUT), bf16), pltpu.VMEM(out_weight.shape, bf16)]
    relayed = relay_scratch()
    return pl.pallas_call(
        mixer_kernel,
        out_shape=tuple(shaped(*dims, dtype=dtype) for dims, dtype in results),
        in_specs=[WHOLE] * 7 + [anywhere] + [WHOLE] * 4 + [anywhere] + [WHOLE] * 2,
        out_specs=(anywhere,) * len(results),
        scratch_shapes=kept[:1]
        + weights
        + [kept[2], kept[1]]
        + kept[3:]
        + [pltpu.VMEM((SEGS, width), f32)] * 2
        + chain_scratch(states, width)
        + [wide_scratch(rows, states)] * 2
        + [
            pltpu.SemaphoreType.DMA((2 * width // CUT + 1,)),
            pltpu.SemaphoreType.DMA((len(results),)),
            pltpu.SemaphoreType.DMA((2,)),
            pltpu.SemaphoreType.DMA((EXPERTS,)),
            pltpu.SemaphoreType.DMA((EXPERTS,)),
        ]
        + relayed,
        compiler_params=roomy(60, collective_id=0, has_side_effects=True),
        cost_estimate=busy(rows * states * width),
        name="mixer",
    )(tokens, upstream, tap_bias, step_bias, skip, gain, second_gain, in_weight, taps, select, step_weight, decay_log, out_weight, router, routes)


def mixer_back(
    back, slots, probs, chosen, normed, router, middle, up, out_weight, gate, mixed, conv, step, raw, selection, pre, padded, entry,
    decay_log, step_weight, select, taps, packed, in_weight, tokens, value,
):
    rows, width = step.shape
    model = tokens.shape[1]
    states = decay_log.shape[0]
    bf16, f32 = jnp.bfloat16, jnp.float32
    anywhere = pl.BlockSpec(memory_space=pl.ANY)
    held = width // CUT
    tall = ((rows, width), f32)
    results = [
        ((rows, model), bf16),
        ((rows, width), bf16),
        ((rows, width), bf16),
        ((width, LANES), f32),
        ((width, LANES), f32),
        ((16, model), f32),
        ((rows, model), f32),
        (value.shape, bf16),
    ]
    streamed = (0, 8, 9, 10, 11, 12, 13, 15, 16, 17, 23, 25)
    kept = (
        [(back.shape, bf16), (out_weight.shape, bf16)]
        + [tall] * 5
        + [(padded.shape, f32), (entry.shape, f32), ((held, model, CUT), bf16)]
        + results[:6]
        + [((rows, model), f32), tall, ((rows, width), bf16), ((rows, LANES), bf16), ((states, width), f32), ((1, width), f32)]
        + [((rows, model), f32), ((SEGS, width), f32), ((SEGS, width), f32), ((24, LANES), f32)]
    )
    return pl.pallas_call(
        mixer_back_kernel,
        out_shape=tuple(shaped(*dims, dtype=dtype) for dims, dtype in results),
        in_specs=[anywhere if k in streamed else WHOLE for k in range(26)],
        out_specs=(anywhere,) * len(results),
        scratch_shapes=[pltpu.VMEM(dims, dtype) for dims, dtype in kept]
        + chain_scratch(states, width)
        + [wide_scratch(rows, states)] * 4
        + [wide_scratch(rows, states, 1), wide_scratch(rows, states)]
        + [pltpu.VMEM((rows, LANES), f32)] * 2
        + [pltpu.SemaphoreType.DMA((10 + 2 * held,)), pltpu.SemaphoreType.DMA((len(results),)), pltpu.SemaphoreType.DMA((2,))]
        + [pltpu.SemaphoreType.DMA((EXPERTS,))] * 2
        + relay_scratch(),
        compiler_params=roomy(62, collective_id=1, has_side_effects=True),
        cost_estimate=busy(rows * states * width),
        name="mixer_back",
    )(
        back, slots, probs, chosen, normed, router, middle, up, out_weight, gate, mixed, conv, step, raw, selection, pre, padded, entry,
        decay_log, step_weight, select, taps, packed, in_weight, tokens, value,
    )


def segmented(block):
    rows = block.shape[0]
    return block.reshape(SEGS, rows // SEGS, -1).transpose(1, 0, 2).reshape(rows, -1)


def in_order(block):
    rows = block.shape[0]
    return block.reshape(rows // SEGS, SEGS, -1).transpose(1, 0, 2).reshape(rows, -1)


def rms_scale(stream):
    return lax.rsqrt(jnp.mean(stream * stream, axis=-1, keepdims=True) + 1e-05)


def rms_back(stream, scale, gain, grad):
    grown = grad * gain
    along = jnp.mean(stream * grown, axis=-1, keepdims=True)
    return scale * grown - stream * (scale * scale * scale * along), jnp.sum(grad * stream * scale, axis=0)


def silu_slope(value):
    gate = jax.nn.sigmoid(value)
    return gate * (1.0 + value * (1.0 - gate))


def product(left, right):
    return jnp.dot(left, right, preferred_element_type=jnp.float32)


def across(left, right):
    return jnp.einsum("tk,dk->td", left, right, preferred_element_type=jnp.float32)


def summed_rows(left, right):
    return jnp.einsum("tk,td->kd", left, right, preferred_element_type=jnp.float32)


CHUNK = 512
GELU_OUT = math.sqrt(2.0 / math.pi)
GELU_IN = 0.044715


def transposed_dot(left, right):
    return lax.dot_general(left, right, (((1,), (1,)), ((), ())), preferred_element_type=jnp.float32)


def column_dot(left, right):
    return lax.dot_general(left, right, (((0,), (0,)), ((), ())), preferred_element_type=jnp.float32)


def three_parts(value):
    parts, left = [], value
    for unused in range(3):
        part = left.astype(jnp.bfloat16)
        left = left - part.astype(jnp.float32)
        parts.append(part)
    return parts


def experts_kernel(
    leaving_hbm, up_ref, first_hbm, second_hbm, back_out, value_out, sums_out,
    received, first, second, pull, active, grad, value, sent, back, scaled_received, scaled_up, staged_sums,
    loads, saves, goes, comes, returns, arrives,
):
    rows, width = up_ref.shape
    hidden = second.shape[0]
    barrier = pltpu.get_barrier_semaphore()
    for peer in expert_peers():
        pl.semaphore_signal(barrier, inc=1, device_id={"expert": peer}, device_id_type=pl.DeviceIdType.MESH)
    loading = [
        pltpu.make_async_copy(second_hbm, second, loads.at[0]),
        pltpu.make_async_copy(first_hbm, first, loads.at[1]),
    ]
    for copy in loading:
        copy.start()
    pl.semaphore_wait(barrier, EXPERTS - 1)
    arriving = trade(leaving_hbm, received, goes, comes)
    loading[0].wait()

    def pulled(i, unused):
        cols = pl.ds(pl.multiple_of(i * CHUNK, CHUNK), CHUNK)
        pull[:, cols] = transposed_dot(up_ref[...], second[cols, :]).astype(jnp.bfloat16)
        return unused

    lax.fori_loop(0, hidden // CHUNK, pulled, 0)
    loading[1].wait()
    for copy in arriving:
        copy.wait()

    def layer(i, unused):
        cols = pl.ds(pl.multiple_of(i * CHUNK, CHUNK), CHUNK)
        pre = jnp.dot(received[:, :width], first[:, cols], preferred_element_type=jnp.float32)
        square = pre * pre
        bent = jnp.tanh(pre * (GELU_OUT + GELU_OUT * GELU_IN * square))
        share = 0.5 + 0.5 * bent
        slope = share + pre * (0.5 - 0.5 * bent * bent) * (GELU_OUT + 3.0 * GELU_OUT * GELU_IN * square)
        active[:, cols] = (pre * share).astype(jnp.bfloat16)
        grad[:, cols] = (slope * pull[:, cols].astype(jnp.float32)).astype(jnp.bfloat16)
        return unused

    lax.fori_loop(0, hidden // CHUNK, layer, 0)
    value[...] = jnp.dot(active[...], second[...], preferred_element_type=jnp.float32).astype(jnp.bfloat16)
    saving = [pltpu.make_async_copy(value, value_out, saves.at[0])]
    saving[0].start()
    sent[:, :width] = transposed_dot(grad[...], first[...]).astype(jnp.bfloat16)
    along = jnp.sum(value[...].astype(jnp.float32) * up_ref[...].astype(jnp.float32), axis=1, keepdims=True)
    place = lax.broadcasted_iota(jnp.int32, (rows, LANES), 1)
    tail = jnp.zeros(place.shape, jnp.float32)
    for k, part in enumerate(three_parts(along)):
        tail = jnp.where(place == k, part.astype(jnp.float32), tail)
    sent[:, width:] = tail.astype(jnp.bfloat16)
    returning = trade(sent, back, returns, arrives)

    parts = received[:, width:].astype(jnp.float32)
    gate = parts[:, 0:1] + parts[:, 1:2] + parts[:, 2:3]
    scaled_received[...] = (received[:, :width].astype(jnp.float32) * gate).astype(jnp.bfloat16)
    scaled_up[...] = (up_ref[...].astype(jnp.float32) * gate).astype(jnp.bfloat16)
    half = sums_out.shape[2]
    pairs = hidden // half // 2

    def stored(i, slot):
        return pltpu.make_async_copy(staged_sums.at[slot], sums_out.at[pl.ds(2 * i, 2)], saves.at[1 + slot])

    def sums(i, unused):
        slot = lax.rem(i, 2)
        cols = pl.ds(pl.multiple_of(i * 2 * half, 2 * half), 2 * half)

        @pl.when(i >= 2)
        def free():
            stored(i - 2, slot).wait()

        for which, (left, right) in enumerate(((grad, scaled_received), (active, scaled_up))):
            total = column_dot(left[:, cols], right[...]).astype(jnp.bfloat16)
            for k in range(2):
                staged_sums[slot, k, which] = total[k * half : (k + 1) * half]
        stored(i, slot).start()
        return unused

    lax.fori_loop(0, pairs, sums, 0)
    for i in (pairs - 2, pairs - 1):
        stored(i, i % 2).wait()
    for copy in returning:
        copy.wait()
    last = pltpu.make_async_copy(back, back_out, saves.at[3])
    last.start()
    last.wait()
    saving[0].wait()


def expert_pass(leaving, upstream, first, second, owners):
    rows, width = upstream.shape
    hidden = second.shape[0]
    wide = leaving.shape[1]
    bf16 = jnp.bfloat16
    half = hidden // owners
    anywhere = pl.BlockSpec(memory_space=pl.ANY)

    def kept(*dims):
        return pltpu.VMEM(dims, bf16)

    return pl.pallas_call(
        experts_kernel,
        out_shape=(
            shaped(rows, wide, dtype=bf16),
            shaped(rows, width, dtype=bf16),
            shaped(owners, 2, half, width, dtype=bf16),
        ),
        in_specs=[anywhere, WHOLE, anywhere, anywhere],
        out_specs=(anywhere,) * 3,
        scratch_shapes=[
            kept(rows, wide),
            kept(width, hidden),
            kept(hidden, width),
            kept(rows, hidden),
            kept(rows, hidden),
            kept(rows, hidden),
            kept(rows, width),
            kept(rows, wide),
            kept(rows, wide),
            kept(rows, width),
            kept(rows, width),
            kept(2, 2, 2, half, width),
            pltpu.SemaphoreType.DMA((2,)),
            pltpu.SemaphoreType.DMA((4,)),
        ]
        + [pltpu.SemaphoreType.DMA((EXPERTS,))] * 4,
        compiler_params=roomy(60, collective_id=3, has_side_effects=True),
        cost_estimate=pl.CostEstimate(flops=12 * rows * hidden * width, bytes_accessed=8 * hidden * width, transcendentals=rows * hidden),
        name="experts",
    )(leaving, upstream, first, second)


ORDERS = ("xyz", "yzx", "zxy")
PIECE = 16
TURNS = (0, 2, 1, 3)


def shares_kernel(
    conv_cols, gate_cols, token_ref, out_cols, middle_ref, left_ref, right_ref, narrow_ref,
    in_out, out_out, left_out, right_out, narrow_out, sum_ref, in_ref, out_ref, made, taken,
    half_a, half_b, half_c, one_a, one_b, one_c, sends, arrivals):
    seq, expert = lax.axis_index("seq"), lax.axis_index("expert")
    core = lax.rem(expert, 2)
    place = {"y": lax.div(seq, 4), "z": lax.rem(seq, 4), "x": lax.div(expert, 2)}
    third = token_ref.shape[1] // len(ORDERS)
    streams = [(L, q) for q in TURNS for L in range(len(ORDERS))]

    def flip(i):
        return i + 1 - 2 * lax.rem(i, 2)

    def device(**moved):
        at = dict(place, **moved)
        return {"seq": at["y"] * 4 + at["z"], "expert": at["x"] * 2 + at.get("core", core)}

    partners = [device(core=1 - core)]
    for axis in "xyz":
        partners += [device(**{axis: flip(place[axis])}), device(**{axis: 3 - place[axis]})]
    barrier = pltpu.get_barrier_semaphore()
    for partner in partners:
        pl.semaphore_signal(barrier, inc=1, device_id=partner, device_id_type=pl.DeviceIdType.MESH)
    pl.semaphore_wait(barrier, len(partners))

    def send(source, target, partner, stream, number):
        k = streams.index(stream)
        copy = pltpu.make_async_remote_copy(
            src_ref=source, dst_ref=target, send_sem=sends.at[k, number], recv_sem=arrivals.at[k, number],
            device_id=partner, device_id_type=pl.DeviceIdType.MESH,
        )
        copy.start()
        return copy

    def add(target, source, unit):
        def step(i, unused):
            target[i] = target[i] + source[i]
            return unused

        lax.fori_loop(0, unit, step, 0, unroll=min(unit, 8))

    inner = out_cols.shape[1]
    for source, target, base in ((conv_cols, in_ref, 0), (gate_cols, in_ref, inner), (out_cols, out_ref, 0)):

        def turn_over(k, unused, source=source, target=target, base=base):
            spot = pl.ds(pl.multiple_of(k * LANES, LANES), LANES)
            target[pl.ds(pl.multiple_of(base + k * LANES, LANES), LANES), :] = source[:, spot].T
            return unused

        lax.fori_loop(0, source.shape[1] // LANES, turn_over, 0)

    halves, ones = (half_a, half_b, half_c), (one_a, one_b, one_c)
    pending, holding = {}, {}

    def set_out(L):
        for q in TURNS:
            for copy in pending[L, q]:
                copy.wait()
            add(taken.at[L, q], made.at[L, 4 * core + q], 64)
            holding[L, q] = taken.at[L, q]
            pending[L, q] = start_halves(L, q, 0, holding[L, q], halves, place, flip, device, send)

    for L, order in enumerate(ORDERS):
        lanes = pl.ds(L * third, third)
        narrow = narrow_ref[:, lanes].astype(jnp.bfloat16)

        def block(s, unused):
            y, z = lax.div(s, 4), lax.rem(s, 4)
            by_in = jnp.dot(
                in_ref[pl.ds(pl.multiple_of(s * 288, 16), 288), :], token_ref[:, lanes], preferred_element_type=jnp.float32
            ).astype(jnp.bfloat16)
            here = pl.ds(pl.multiple_of(s * 144, 16), 144)
            by_out = jnp.dot(out_ref[here, :], middle_ref[:, lanes], preferred_element_type=jnp.float32)
            left, right = left_ref[here, :], right_ref[here, :]
            for x in range(4):
                at = {"x": x, "y": y, "z": z}
                slot = (at[order[0]] * 4 + at[order[1]]) * 4 + at[order[2]]
                rows = by_in[72 * x : 72 * x + 72]
                more = by_out[36 * x : 36 * x + 36].astype(jnp.bfloat16)
                for q in range(4):
                    made[L, q, slot] = rows[16 * q : 16 * q + 16]
                made[L, 4, slot, 0:8] = rows[64:]
                made[L, 4, slot, 8:16] = more[:8]
                made[L, 5, slot] = more[8:24]
                made[L, 6, slot, 0:12] = more[24:]
                made[L, 6, slot, 12:16] = narrow[8:12]
                made[L, 7, slot, 8:16] = narrow[0:8]
                last = jnp.concatenate([left[36 * x : 36 * x + 36], right[36 * x : 36 * x + 36]], axis=0)
                for part in range(third // LANES):
                    k = 8 * (L * (third // LANES) + part)
                    made[L, 7, slot, 0:8, part * LANES : (part + 1) * LANES] = last[k : k + 8].astype(jnp.bfloat16)
            return unused

        lax.fori_loop(0, 16, block, 0, unroll=2)
        for q in TURNS:
            pending[L, q] = [
                send(made.at[L, 4 * (1 - core) + q], taken.at[L, q], device(core=1 - core), (L, q), 0)
            ]

        if L:
            set_out(L - 1)
    set_out(len(ORDERS) - 1)
    for turn in range(3):
        unit = 16 >> (2 * turn)
        for L, q in streams:
            axis = ORDERS[L][turn]
            i = place[axis]
            for copy in pending[L, q]:
                copy.wait()
            other = 3 - i if q < 2 else flip(i)
            got = halves[turn].at[L, q]
            add(got.at[0], holding[L, q].at[pl.ds(i * unit, unit)], unit)
            add(got.at[1], holding[L, q].at[pl.ds(other * unit, unit)], unit)
            partner = device(**{axis: other})
            pending[L, q] = [send(got.at[1], ones[turn].at[L, q], partner, (L, q), 3 + 3 * turn)]
        for L, q in streams:
            for copy in pending[L, q]:
                copy.wait()
            got = ones[turn].at[L, q]
            if turn < 2:
                add(got, halves[turn].at[L, q, 0], unit)
                holding[L, q] = got
                pending[L, q] = start_halves(L, q, turn + 1, got, halves, place, flip, device, send)
            else:
                whole = got[0].astype(jnp.float32) + halves[turn][L, q, 0, 0].astype(jnp.float32)
                sum_ref[4 * core + q, :, L * third : (L + 1) * third] = whole
    here = sum_ref.at[pl.ds(4 * core, 4)]
    send(here, here, device(core=1 - core), (0, 0), 10).wait()
    whole = jnp.concatenate([sum_ref[q] for q in range(8)], axis=0)
    last = [whole[112:120, k * LANES : (k + 1) * LANES] for k in range(whole.shape[1] // LANES)]
    last = jnp.concatenate(last + [jnp.zeros((8, LANES), jnp.float32)], axis=0)
    narrow_out[...] = jnp.concatenate([whole[120:128], whole[108:112], whole[108:112]], axis=0)
    for c in range(2):

        @pl.when(core == c)
        def pick(c=c):
            in_out[...] = whole[36 * c : 36 * c + 40]
            out_out[...] = whole[72 + 18 * c : 90 + 18 * c]
            left_out[...] = last[18 * c : 18 * c + 24]
            right_out[...] = last[36 + 18 * c : 60 + 18 * c]


def start_halves(L, q, turn, source, halves, place, flip, device, send):
    axis = ORDERS[L][turn]
    unit = 16 >> (2 * turn)
    i = place[axis]
    partner = flip(i) if q < 2 else 3 - i
    second = 3 - partner if q < 2 else flip(partner)
    target = halves[turn].at[L, q]
    return [
        send(source.at[pl.ds(partner * unit, unit)], target.at[0], device(**{axis: partner}), (L, q), 1 + 3 * turn),
        send(source.at[pl.ds(second * unit, unit)], target.at[1], device(**{axis: partner}), (L, q), 2 + 3 * turn),
    ]


def shares(conv_cols, gate_cols, tokens, out_cols, middle, left, right, narrow):
    width = tokens.shape[1]
    rows, inner = out_cols.shape
    third = width // len(ORDERS)

    def slots(*lead):
        return pltpu.VMEM((len(ORDERS),) + lead + (PIECE, third), jnp.bfloat16)

    return pl.pallas_call(
        shares_kernel,
        out_shape=(shaped(40, width), shaped(18, width), shaped(24, LANES), shaped(24, LANES), shaped(16, width)),
        in_specs=[WHOLE] * 8,
        out_specs=(WHOLE,) * 5,
        scratch_shapes=[pltpu.VMEM((8, PIECE, width), jnp.float32)]
        + [pltpu.VMEM((2 * inner, rows), jnp.bfloat16), pltpu.VMEM((inner, rows), jnp.bfloat16)]
        + [slots(8, 64), slots(4, 64)]
        + [slots(4, 2, 16 >> (2 * turn)) for turn in range(3)]
        + [slots(4, 16 >> (2 * turn)) for turn in range(3)]
        + [pltpu.SemaphoreType.DMA((12, 11))] * 2,
        compiler_params=roomy(60, collective_id=2, has_side_effects=True),
        name="shares",
    )(conv_cols, gate_cols, tokens, out_cols, middle, left, right, narrow)


def finish_kernel(
    in_ref, left_ref, right_ref, narrow_ref, expert_ref,
    in_out, tap_out, tap_bias_out, select_out, step_out, step_bias_out, decay_out, skip_out, gain_out, second_out, router_out,
    expert_first_out, expert_second_out,
):
    def turned(value):
        size = value.shape[0]
        same = lax.broadcasted_iota(jnp.int32, (size, size), 0) == lax.broadcasted_iota(jnp.int32, (size, size), 1)
        ones = jnp.where(same, 1.0, 0.0).astype(jnp.bfloat16)
        return sum(column_dot(part, ones) for part in three_parts(value))

    each, taps, states = tap_out.shape[1], tap_out.shape[0], decay_out.shape[0]
    in_out[...] = in_ref[: in_out.shape[0], :]
    select_out[...] = left_ref[:each, : select_out.shape[1]]
    sums = turned(left_ref[...])[SELECTED:, :each]
    decay_out[...] = sums[:states]
    tap_out[...] = sums[states : states + taps]
    tap_bias_out[...] = sums[states + taps : states + taps + 1]
    step_bias_out[...] = sums[states + taps + 1 : states + taps + 2]
    skip_out[...] = sums[states + taps + 2 : states + taps + 3]
    step_out[...] = right_ref[:each, : step_out.shape[1]]
    fewer = router_out.shape[1]
    owner = lax.axis_index("seq") * EXPERTS + lax.axis_index("expert")
    shape = (narrow_ref.shape[1], LANES)
    mine = lax.broadcasted_iota(jnp.int32, shape, 0) == lax.broadcasted_iota(jnp.int32, shape, 1) + owner * fewer
    ones = jnp.where(mine, 1.0, 0.0).astype(jnp.bfloat16)
    parts = three_parts(narrow_ref[...])
    picked = sum(jnp.dot(part, ones, preferred_element_type=jnp.float32) for part in parts)
    gain_out[...] = picked[EXPERTS : EXPERTS + 1, :fewer]
    second_out[...] = picked[EXPERTS + 1 : EXPERTS + 2, :fewer]
    router_out[...] = picked[:EXPERTS, :fewer]
    expert_first_out[...] = expert_ref[0].astype(jnp.float32)
    expert_second_out[...] = expert_ref[1].astype(jnp.float32)


def finish(in_share, left, right, narrow, expert_share, devices, taps, states, rank, inner):
    model = in_share.shape[1]
    each, fewer, hidden = inner // devices, model // devices, expert_share.shape[1]
    dims = (
        (2 * each, model), (taps, each), (1, each), (each, rank + 2 * states), (each, rank), (1, each), (states, each), (1, each),
        (1, fewer), (1, fewer), (EXPERTS, fewer), (hidden, model), (hidden, model),
    )
    return pl.pallas_call(
        finish_kernel,
        out_shape=tuple(shaped(*size) for size in dims),
        in_specs=[WHOLE] * 5,
        out_specs=(WHOLE,) * len(dims),
        compiler_params=roomy(32),
        name="finish",
    )(in_share, left, right, narrow, expert_share)


def local(
    tokens,
    expert_index,
    cotangent,
    first_gain,
    in_weight,
    conv_weight,
    conv_bias,
    select_weight,
    step_weight,
    step_bias,
    decay_log,
    skip_gain,
    out_weight,
    second_gain,
    router_weight,
    expert_first,
    expert_second,
):
    bf16, f32 = jnp.bfloat16, jnp.float32
    row_count, model_width = tokens.shape[1:]
    seat_count = 2 * row_count
    inner = conv_bias.shape[0]
    rank = step_weight.shape[0]
    states = decay_log.shape[0]
    taps = conv_weight.shape[0]
    seqs, experts = lax.axis_size("seq"), lax.axis_size("expert")
    (
        normed_in, gate_input, padded, preact, conv_out, step_raw, step_size, selection, first, mixer_out, gated,
        middle, normed_mid, router_probs, gate_wide, leaving, slots, upstream_there, stream, upstream, packed,
    ) = mixer(
        tokens[0], cotangent[0], conv_bias, step_bias, skip_gain, first_gain, second_gain, in_weight, conv_weight, select_weight.T, step_weight, decay_log, out_weight, router_weight.T, expert_index[:, :, 0], seat_count
    )
    back, value_there, expert_grads = expert_pass(leaving, upstream_there, expert_first[0], expert_second[0], seqs)
    expert_share = lax.psum_scatter(
        expert_grads.reshape(-1, model_width), "seq", scatter_dimension=0, tiled=True
    ).reshape(2, -1, model_width)
    middle_low, grad_gate_input, grad_conv_input, left, right, narrow, grad_tokens, value_home = mixer_back(
        back, slots, router_probs, gate_wide, normed_mid, router_weight.T, middle, upstream, out_weight, gate_input, mixer_out, conv_out,
        step_size, step_raw, selection, preact, padded, first, decay_log, step_weight, select_weight.T, conv_weight, packed, in_weight, stream, value_there,
    )
    placing = (slots[:, 0:1] == jnp.arange(seat_count, dtype=f32)[None, :]).astype(bf16)
    mixed = middle + gate_wide[:, 0:1] * product(placing, value_home)

    devices = seqs * experts
    each, fewer = inner // devices, model_width // devices
    in_share, out_share, left, right, narrow = shares(
        grad_conv_input, grad_gate_input, normed_in, gated, middle_low, left, right, narrow
    )
    in_grad, tap_grad, tap_bias_grad, select_grad, step_grad, step_bias_grad, decay_grad, skip_grad, gain_grad, second_grad, router_grad, first_grad, second_hidden = finish(
        in_share, left, right, narrow, expert_share, devices, taps, states, rank, inner
    )
    return (
        in_order(mixed.astype(bf16))[None],
        grad_tokens[None],
        gain_grad[0],
        in_grad.T,
        tap_grad,
        tap_bias_grad[0],
        select_grad,
        step_grad.T,
        step_bias_grad[0],
        decay_grad,
        skip_grad[0],
        out_share,
        second_grad[0],
        router_grad.T,
        first_grad.T[None],
        second_hidden[None],
    )


def solution(mesh):
    return jax.shard_map(
        local,
        mesh=mesh,
        in_specs=(
            P("expert", "seq", None),
            P("expert", "seq", None),
            P("expert", "seq", None),
            P(),
            P(),
            P(),
            P(),
            P(),
            P(),
            P(),
            P(),
            P(),
            P(),
            P(),
            P(),
            P("expert", None, None),
            P("expert", None, None),
        ),
        out_specs=(
            P("expert", "seq", None),
            P("expert", "seq", None),
            P(("seq", "expert")),
            P(None, ("seq", "expert")),
            P(None, ("seq", "expert")),
            P(("seq", "expert")),
            P(("seq", "expert"), None),
            P(None, ("seq", "expert")),
            P(("seq", "expert")),
            P(None, ("seq", "expert")),
            P(("seq", "expert")),
            P(("seq", "expert"), None),
            P(("seq", "expert")),
            P(("seq", "expert"), None),
            P("expert", None, "seq"),
            P("expert", "seq", None),
        ),
        check_vma=False,
    )
```

```python
import functools
import math

import jax
import jax.numpy as jnp
from jax import lax
from jax.experimental import pallas as pl
from jax.experimental.pallas import tpu as pltpu
from jax.sharding import PartitionSpec as P

LANES = 128
SEGS = 8
LOG2E = math.log2(math.e)
PARTS = 3
SELECTED = 104
EXPERTS = 8
CAPACITY = 64
CUT = 768
GRID = 4


def spread_ones(states):
    row = lax.broadcasted_iota(jnp.int32, (LANES, states * LANES), 0)
    lane = lax.broadcasted_iota(jnp.int32, (LANES, states * LANES), 1)
    return row, lane // LANES


def fill_maps(sel_ref, wide_ref, column):
    steps, states = wide_ref.shape[:2]
    row, block = spread_ones(states)
    ones = jnp.where(row == block + column, 1.0, 0.0).astype(jnp.bfloat16)
    left, total = sel_ref[...], None
    for unused in range(3):
        part = left.astype(jnp.bfloat16)
        left = left - part.astype(jnp.float32)
        spread = jnp.dot(part, ones, preferred_element_type=jnp.float32)
        total = spread if total is None else total + spread
    for n in range(states):
        wide_ref[:, n] = total[:, n * LANES : (n + 1) * LANES].reshape(steps, SEGS, LANES)


def gather_maps(sum_ref, column):
    steps, states = sum_ref.shape[:2]
    row, block = spread_ones(states)
    ones = jnp.where(row == block + column, 1.0, 0.0).astype(jnp.bfloat16)
    left = jnp.concatenate([sum_ref[:, n].reshape(steps * SEGS, LANES) for n in range(states)], axis=1)
    total = None
    for unused in range(3):
        part = left.astype(jnp.bfloat16)
        left = left - part.astype(jnp.float32)
        summed = transposed_dot(part, ones)
        total = summed if total is None else total + summed
    return total


def lanes_of(block):
    return pl.ds(pl.multiple_of(block * LANES, LANES), LANES)


def rows_of(j):
    return pl.ds(pl.multiple_of(j * SEGS, SEGS), SEGS)


def rates_of(log_ref, lanes):
    states = log_ref.shape[0]
    rate = -LOG2E * jnp.exp(log_ref[:, lanes])
    return jnp.stack([jnp.broadcast_to(rate[n : n + 1], (SEGS, LANES)) for n in range(states)])


def neighbour(value, hop, later, fill):
    axis = value.ndim - 2
    place = lax.broadcasted_iota(jnp.int32, value.shape, axis)
    if later:
        return jnp.where(place < SEGS - hop, pltpu.roll(value, SEGS - hop, axis), fill)
    return jnp.where(place >= hop, pltpu.roll(value, hop, axis), fill)


def summarize(later, part, step_ref, other_ref, wide, log_ref, part_ref, span_ref, message):
    steps, states = wide.shape[:2]
    blocks = step_ref.shape[1] // LANES // PARTS

    def block(i, unused):
        lanes = lanes_of(part * blocks + i)
        rate = rates_of(log_ref, lanes)

        def advance(turn, carry):
            span, memory = carry
            j = steps - 1 - turn if later else turn
            step = step_ref[rows_of(j), lanes]
            other = other_ref[rows_of(j), lanes]
            decay = jnp.exp2(step * rate)
            if later:
                memory = decay * (memory + wide[j] * other)
            else:
                memory = decay * memory + wide[j] * (step * other)
            return span + step, memory

        zero = jnp.zeros((SEGS, LANES), jnp.float32)
        span, memory = lax.fori_loop(0, steps, advance, (zero, jnp.zeros(rate.shape, jnp.float32)), unroll=16)
        hop = 1
        while hop < SEGS:
            memory = memory + jnp.exp2(rate * span) * neighbour(memory, hop, later, 0.0)
            span = span + neighbour(span, hop, later, 0.0)
            hop *= 2
        span_ref[:, lanes] = span
        part_ref[:, :, lanes] = memory
        end = 0 if later else SEGS - 1
        for n in range(states):
            message[n // GRID, n % GRID, pl.ds(i, 1), :] = memory[n, end : end + 1]
        for q in range(GRID):
            message[q, GRID, pl.ds(i, 1), :] = span[end : end + 1]
        return unused

    lax.fori_loop(0, blocks, block, 0)


def entering(later, part_ref, span_ref, rate, lanes, carried):
    ends = part_ref[:, :, lanes] + jnp.exp2(rate * span_ref[:, lanes]) * carried
    return neighbour(ends, 1, later, carried)


def carried_at(in_ref, part, i):
    states = GRID * GRID
    return jnp.stack(
        [jnp.broadcast_to(in_ref[n // GRID, n % GRID, pl.ds(i, 1), :], (SEGS, LANES)) for n in range(states)]
    )


def scan_part(part, step_ref, conv_ref, wide_in, wide_out, log_ref, part_ref, span_ref, in_ref, y_ref, entry_ref):
    steps = wide_in.shape[0]
    blocks = step_ref.shape[1] // LANES // PARTS

    def block(i, unused):
        lanes = lanes_of(part * blocks + i)
        rate = rates_of(log_ref, lanes)
        first = entering(False, part_ref, span_ref, rate, lanes, carried_at(in_ref, part, i))
        entry_ref[:, :, lanes] = first

        def advance(j, memory):
            step = step_ref[rows_of(j), lanes]
            memory = jnp.exp2(step * rate) * memory + wide_in[j] * (step * conv_ref[rows_of(j), lanes])
            y_ref[rows_of(j), lanes] = jnp.sum(wide_out[j] * memory, axis=0)
            return memory

        lax.fori_loop(0, steps, advance, first, unroll=16)
        return unused

    lax.fori_loop(0, blocks, block, 0)


def retreat_part(
    part, step_ref, conv_ref, grad_ref, raw_ref, wide_in, wide_out, log_ref, pull_ref, entry_ref, part_ref, span_ref, in_ref,
    low_ref, gconv_ref, glog_ref, gbias_ref, sum_in, sum_out, states_ref, decays_ref, raw_sum, raw_rows,
):
    steps = wide_in.shape[0]
    blocks = step_ref.shape[1] // LANES // PARTS

    def block(i, unused):
        lanes = lanes_of(part * blocks + i)
        rate = rates_of(log_ref, lanes)

        def advance(j, memory):
            step = step_ref[rows_of(j), lanes]
            decay = jnp.exp2(step * rate)
            memory = decay * memory + wide_in[j] * (step * conv_ref[rows_of(j), lanes])
            decays_ref[j] = decay
            states_ref[j + 1] = memory
            return memory

        first = entry_ref[:, :, lanes]
        states_ref[0] = first
        lax.fori_loop(0, steps, advance, first, unroll=8)

        def retreat(turn, carry):
            j = steps - 1 - turn
            mu, slow = carry
            step = step_ref[rows_of(j), lanes]
            conv = conv_ref[rows_of(j), lanes]
            grad = grad_ref[rows_of(j), lanes]
            lam = wide_out[j] * grad + mu
            sum_out[j] += grad * states_ref[j + 1]
            sum_in[j] += lam * (step * conv)
            by_in = jnp.sum(lam * wide_in[j], axis=0)
            mu = lam * decays_ref[j]
            kept = mu * states_ref[j]
            by_rate = jnp.sum(kept * rate, axis=0)
            grad_step = by_in * conv + (1.0 / LOG2E) * by_rate
            raw_rows[rows_of(j), :] = grad_step * jax.nn.sigmoid(raw_ref[rows_of(j), lanes])
            gconv_ref[rows_of(j), lanes] = by_in * step
            return mu, slow + kept * step

        last = entering(True, part_ref, span_ref, rate, lanes, carried_at(in_ref, part, i))
        unused_mu, slow = lax.fori_loop(0, steps, retreat, (last, jnp.zeros(rate.shape, jnp.float32)), unroll=8)
        glog_ref[:, lanes] = (1.0 / LOG2E) * jnp.sum(slow * rate, axis=1)
        raw_steps = raw_rows[...]
        gbias_ref[:, lanes] = jnp.sum(raw_steps, axis=0, keepdims=True)
        low = raw_steps.astype(jnp.bfloat16)
        low_ref[:, lanes] = low
        raw_sum[:, : pull_ref.shape[0]] += transposed_dot(low, pull_ref[:, lanes])
        return unused

    lax.fori_loop(0, blocks, block, 0)


def expert_peers():
    me = lax.axis_index("expert")
    return [lax.rem(me + k, EXPERTS) for k in range(1, EXPERTS)]


def seats_of(device):
    return pl.ds(pl.multiple_of(device * CAPACITY, CAPACITY), CAPACITY)


def trade(source, target, send_sems, recv_sems):
    me = lax.axis_index("expert")
    copies = [
        pltpu.make_async_remote_copy(
            src_ref=source.at[seats_of(peer)], dst_ref=target.at[seats_of(me)], send_sem=send_sems.at[k], recv_sem=recv_sems.at[k],
            device_id={"expert": peer}, device_id_type=pl.DeviceIdType.MESH,
        )
        for k, peer in enumerate(expert_peers())
    ]
    copies.append(pltpu.make_async_copy(source.at[seats_of(me)], target.at[seats_of(me)], send_sems.at[EXPERTS - 1]))
    for copy in copies:
        copy.start()
    return copies


class Relay:
    def __init__(self, later, log_ref, log_rows, in_ref, message, got, row, rows_got, above, made, sends, arrivals, others=()):
        self.later, self.log_rows, self.message, self.got = later, log_rows, message, got
        self.row, self.rows_got, self.above, self.made, self.in_ref = row, rows_got, above, made, in_ref
        self.sends, self.arrivals = sends, arrivals
        seq = lax.axis_index("seq")
        self.y, self.z = lax.div(seq, GRID), lax.rem(seq, GRID)
        blocks = log_ref.shape[1] // LANES // PARTS
        log_rows[...] = jnp.zeros_like(log_rows)
        for part in range(PARTS):
            for b in range(blocks):
                lanes = pl.ds((part * blocks + b) * LANES, LANES)
                for n in range(GRID * GRID):
                    log_rows[part, n // GRID, n % GRID, b : b + 1, :] = log_ref[n : n + 1, lanes]
        self.flying = {}
        barrier = pltpu.get_barrier_semaphore()
        peers = [self.across(k) for k in range(1, GRID)] + [self.along(k) for k in range(1, GRID)]
        peers += [self.onward(1), self.onward(-1)] + list(others)
        for peer in peers:
            pl.semaphore_signal(barrier, inc=1, device_id=peer, device_id_type=pl.DeviceIdType.MESH)
        self.peers = len(peers)

    def onward(self, k):
        size = GRID * GRID
        return {"seq": lax.rem(self.y * GRID + self.z + k + size, size)}

    def across(self, k):
        return {"seq": self.y * GRID + lax.rem(self.z + k, GRID)}

    def along(self, k):
        return {"seq": lax.rem(self.y + k, GRID) * GRID + self.z}

    def meet(self):
        pl.semaphore_wait(pltpu.get_barrier_semaphore(), self.peers)

    def send(self, part, phase, k, source, target, peer):
        copy = pltpu.make_async_remote_copy(
            src_ref=source, dst_ref=target, send_sem=self.sends.at[part, phase, k], recv_sem=self.arrivals.at[part, phase, k],
            device_id=peer, device_id_type=pl.DeviceIdType.MESH,
        )
        copy.start()
        self.flying.setdefault((part, phase), []).append(copy)

    def land(self, part, phase):
        for copy in self.flying[part, phase]:
            copy.wait()

    def order(self):
        return range(GRID - 1, -1, -1) if self.later else range(GRID)

    def rate(self, part):
        return -LOG2E * jnp.exp(self.log_rows[part, self.z])

    def first(self, part):
        for k in range(1, GRID):
            peer = lax.rem(self.z + k, GRID)
            self.send(part, 0, k, self.message.at[part, peer], self.got.at[part, k], self.across(k))
        self.got[part, 0] = self.message[part, self.z]

    def second(self, part):
        self.land(part, 0)
        rate = self.rate(part)
        state, span = jnp.zeros(rate.shape, jnp.float32), jnp.zeros(rate.shape[1:], jnp.float32)
        for z in self.order():
            block = self.got[part, lax.rem(self.z - z + GRID, GRID)]
            state = jnp.exp2(rate * block[GRID]) * state + block[:GRID]
            span = span + block[GRID]
        self.row[part, :GRID] = state
        self.row[part, GRID] = span
        for k in range(1, GRID):
            self.send(part, 1, k, self.row.at[part], self.rows_got.at[part, k], self.along(k))
        self.rows_got[part, 0] = self.row[part]

    def third(self, part):
        self.land(part, 1)
        rate = self.rate(part)
        state = jnp.zeros(rate.shape, jnp.float32)
        for y in self.order():
            self.above[part, y] = state
            block = self.rows_got[part, lax.rem(self.y - y + GRID, GRID)]
            state = jnp.exp2(rate * block[GRID]) * state + block[:GRID]
        state = self.above[part, self.y]
        for z in self.order():
            self.made[part, z] = state
            block = self.got[part, lax.rem(self.z - z + GRID, GRID)]
            state = jnp.exp2(rate * block[GRID]) * state + block[:GRID]
        for k in range(1, GRID):
            peer = lax.rem(self.z + k, GRID)
            self.send(part, 2, k, self.made.at[part, peer], self.in_ref.at[part, self.z], self.across(k))
        self.in_ref[part, self.z] = self.made[part, self.z]

    def done(self, part):
        self.land(part, 2)


def staged(relay, summary, extra, scan):
    summary(0)
    relay.first(0)
    summary(1)
    relay.first(1)
    relay.second(0)
    summary(2)
    relay.first(2)
    relay.third(0)
    relay.second(1)
    extra()
    relay.second(2)
    relay.third(1)
    relay.done(0)
    scan(0)
    relay.third(2)
    relay.done(1)
    scan(1)
    relay.done(2)
    scan(2)


def named_experts(slots, rows):
    first = (lax.broadcasted_iota(jnp.int32, (rows, EXPERTS), 1) * CAPACITY).astype(jnp.float32)
    return jnp.where((slots >= first) & (slots < first + CAPACITY), 1.0, 0.0)


def seated_rows(slots, rows, seats):
    seat = lax.broadcasted_iota(jnp.int32, (rows, seats), 1).astype(jnp.float32)
    return jnp.where(seat == slots, 1.0, 0.0).astype(jnp.bfloat16)


def order_ones(rows, back):
    row, token = lax.broadcasted_iota(jnp.int32, (rows, rows), 0), lax.broadcasted_iota(jnp.int32, (rows, rows), 1)
    if back:
        row, token = token, row
    same = token == lax.rem(row, SEGS) * (rows // SEGS) + lax.div(row, SEGS)
    return jnp.where(same, 1.0, 0.0).astype(jnp.bfloat16)


def slots_of(routes, rows):
    expert = lax.broadcasted_iota(jnp.int32, (rows, EXPERTS), 1)
    named = jnp.where(lax.broadcasted_iota(jnp.int32, (EXPERTS, rows), 0) == routes, 1.0, 0.0).astype(jnp.bfloat16)
    named = transposed_dot(order_ones(rows, False), named)
    later = lax.broadcasted_iota(jnp.int32, (rows, rows), 0) > lax.broadcasted_iota(jnp.int32, (rows, rows), 1)
    ahead = jnp.dot(jnp.where(later, 1.0, 0.0).astype(jnp.bfloat16), named.astype(jnp.bfloat16), preferred_element_type=jnp.float32)
    return jnp.sum(named * (ahead + (expert * CAPACITY).astype(jnp.float32)), axis=1, keepdims=True)


def mixer_kernel(
    token_in, up_in, tap_bias_in, step_bias_in, skip_in, gain_in, second_gain_in, in_hbm, tap_ref, select_ref, step_weight_ref, log_ref, out_hbm, router_ref, route_ref,
    normed_out, gate_out, padded_out, pre_out, conv_out, raw_out, step_out, sel_out, entry_out, mixer_out, gated_out,
    middle_out, normed_mid_out, probs_out, chosen_out, leaving_out, slot_out, up_out, token_out, up_order_out, row_out,
    normed, in_ref, out_ref, padded, gate, pre, conv, raw, step, sel, entry, mixer, gated, middle, normed_mid, probs, chosen, leaving, slots, up_seated, token_ref, up_ref, row_ref,
    tail, tail_got, part_ref, span_ref, wide_in, wide_out, loads, saves, passing, goes, comes, log_rows, relay_in, *relayed
):
    rows, width = step.shape
    model = token_ref.shape[1]
    tap_bias_ref, step_bias_ref, skip_ref = (row_ref.at[k : k + 1] for k in range(3))
    gain_ref, second_gain_ref = row_ref.at[3:4, :model], row_ref.at[3:4, model:]
    taps, states = tap_ref.shape[0], log_ref.shape[0]
    reach = (taps - 1) * SEGS
    rank = SELECTED - 2 * states
    pieces = in_ref.shape[0]
    cut = in_ref.shape[2]
    blocks = width // LANES

    loading = [pltpu.make_async_copy(in_hbm.at[:, pl.ds(k * cut, cut)], in_ref.at[k], loads.at[k]) for k in range(pieces)]
    loading.append(pltpu.make_async_copy(out_hbm, out_ref, loads.at[pieces]))
    for copy in loading:
        copy.start()
    saving = []

    def save(source, target):
        copy = pltpu.make_async_copy(source, target, saves.at[len(saving)])
        copy.start()
        saving.append(copy)

    relay = Relay(False, log_ref, log_rows, relay_in, *relayed, others=[{"expert": peer} for peer in expert_peers()])

    for k, vector in enumerate((tap_bias_in, step_bias_in, skip_in)):
        row_ref[k : k + 1, :] = vector[...][None, :]
    row_ref[3:4, :model] = gain_in[...][None, :]
    row_ref[3:4, model:] = second_gain_in[...][None, :]
    row_ref[4:, :] = jnp.zeros_like(row_ref[4:, :])
    save(row_ref, row_out)
    ordering = order_ones(rows, False)
    stream = jnp.dot(ordering, token_in[...], preferred_element_type=jnp.float32)
    token_ref[...] = stream.astype(jnp.bfloat16)
    save(token_ref, token_out)
    normed[...] = (stream * rms_scale(stream) * gain_ref[...]).astype(jnp.bfloat16)
    save(normed, normed_out)
    for k in range(pieces // 2):
        loading[k].wait()
        padded[reach:, k * cut : (k + 1) * cut] = jnp.dot(normed[...], in_ref[k], preferred_element_type=jnp.float32)
    tail[...] = jnp.zeros_like(tail)
    for k in range(taps - 1):
        row = reach + rows - (taps - 1 - k) * SEGS + SEGS - 1
        tail[k : k + 1, :] = padded[row : row + 1, :]
    slot = slots_of(route_ref[...], rows)
    slots[...] = jnp.broadcast_to(slot, slots.shape)
    save(slots, slot_out)
    seating = seated_rows(slot, rows, leaving.shape[0])
    up_ref[...] = jnp.dot(ordering, up_in[...], preferred_element_type=jnp.float32).astype(jnp.bfloat16)
    save(up_ref, up_order_out)
    up_seated[...] = column_dot(seating, up_ref[...]).astype(jnp.bfloat16)
    relay.meet()
    handing = pltpu.make_async_remote_copy(
        src_ref=tail, dst_ref=tail_got, send_sem=passing.at[0], recv_sem=passing.at[1],
        device_id=relay.onward(1), device_id_type=pl.DeviceIdType.MESH,
    )
    handing.start()
    trading = trade(up_seated, up_out, goes, comes)
    for k in range(pieces // 2, pieces):
        loading[k].wait()
        spot = slice((k - pieces // 2) * cut, (k - pieces // 2 + 1) * cut)
        gate[:, spot] = jnp.dot(normed[...], in_ref[k], preferred_element_type=jnp.float32)
    save(gate, gate_out)
    handing.wait()
    started = jnp.where(lax.axis_index("seq") > 0, 1.0, 0.0)
    for k in range(taps - 1):
        row = rows + k * SEGS
        segment = lax.broadcasted_iota(jnp.int32, (SEGS, width), 0)
        before = pltpu.roll(padded[row : row + SEGS, :], 1, 0)
        padded[k * SEGS : (k + 1) * SEGS, :] = jnp.where(segment == 0, started * tail_got[k : k + 1, :], before)
    save(padded, padded_out)

    sel[...] = jnp.zeros_like(sel)

    def convolve(b, unused):
        lanes = lanes_of(b)
        value = tap_bias_ref[:, lanes]
        for k in range(taps):
            value = value + tap_ref[k : k + 1, lanes] * padded[k * SEGS : k * SEGS + rows, lanes]
        pre[:, lanes] = value
        value = value * jax.nn.sigmoid(value)
        conv[:, lanes] = value
        sel[:, :SELECTED] += transposed_dot(value.astype(jnp.bfloat16), select_ref[:, lanes])
        return unused

    lax.fori_loop(0, blocks, convolve, 0)
    save(pre, pre_out)
    save(conv, conv_out)
    save(sel, sel_out)
    step_low = sel[:, :rank].astype(jnp.bfloat16)

    def size(b, unused):
        lanes = lanes_of(b)
        value = jnp.dot(step_low, step_weight_ref[:, lanes], preferred_element_type=jnp.float32) + step_bias_ref[:, lanes]
        raw[:, lanes] = value
        step[:, lanes] = jnp.maximum(value, 0.0) + jnp.log1p(jnp.exp(-jnp.abs(value)))
        return unused

    lax.fori_loop(0, blocks, size, 0)
    save(raw, raw_out)
    save(step, step_out)
    fill_maps(sel, wide_in, rank)

    def summary(part):
        summarize(False, part, step, conv, wide_in, log_ref, part_ref, span_ref, relay.message.at[part])

    def scan(part):
        scan_part(part, step, conv, wide_in, wide_out, log_ref, part_ref, span_ref, relay_in.at[part], mixer, entry)

    staged(relay, summary, lambda: fill_maps(sel, wide_out, rank + states), scan)
    save(entry, entry_out)

    def blend(b, unused):
        lanes = lanes_of(b)
        value = mixer[:, lanes] + skip_ref[:, lanes] * conv[:, lanes]
        mixer[:, lanes] = value
        opening = gate[:, lanes]
        gated[:, lanes] = (value * (opening * jax.nn.sigmoid(opening))).astype(jnp.bfloat16)
        return unused

    lax.fori_loop(0, blocks, blend, 0)
    save(mixer, mixer_out)
    save(gated, gated_out)
    loading[pieces].wait()
    value = token_ref[...].astype(jnp.float32) + jnp.dot(gated[...], out_ref[...], preferred_element_type=jnp.float32)
    middle[...] = value
    save(middle, middle_out)
    normed_mid[...] = (value * rms_scale(value) * second_gain_ref[...]).astype(jnp.bfloat16)
    save(normed_mid, normed_mid_out)
    logits = transposed_dot(normed_mid[...], router_ref[...])
    grown = jnp.exp(logits - jnp.max(logits, axis=1, keepdims=True))
    probs[...] = grown / jnp.sum(grown, axis=1, keepdims=True)
    save(probs, probs_out)
    gate_value = jnp.sum(named_experts(slots[:, 0:1], rows) * probs[...], axis=1, keepdims=True)
    chosen[...] = jnp.broadcast_to(gate_value, (rows, LANES))
    save(chosen, chosen_out)
    place = lax.broadcasted_iota(jnp.int32, (rows, LANES), 1)
    parts = jnp.zeros((rows, LANES), jnp.float32)
    for k, piece in enumerate(three_parts(gate_value)):
        parts = jnp.where(place == k, piece.astype(jnp.float32), parts)
    seating = seated_rows(slots[:, 0:1], rows, leaving.shape[0])
    leaving[:, :model] = column_dot(seating, normed_mid[...]).astype(jnp.bfloat16)
    leaving[:, model:] = column_dot(seating, parts.astype(jnp.bfloat16)).astype(jnp.bfloat16)
    save(leaving, leaving_out)
    for copy in saving + trading:
        copy.wait()


def mixer_back_kernel(
    back_hbm, slot_ref, probs_ref, chosen_ref, normed_ref, router_ref, middle_ref, up_ref, out_hbm, gate_hbm,
    mixer_hbm, conv_hbm, step_hbm, raw_hbm, sel_ref, pre_hbm, padded_hbm, entry_hbm, log_ref, step_weight_ref, select_ref,
    tap_ref, packed_ref, in_hbm, token_ref, value_hbm,
    low_out, gate_out, conv_out, left_out, right_out, narrow_out, token_out, value_out,
    back, out_ref, gate, mixer, conv, step, raw, padded, entry, in_ref,
    middle_low, grad_gate, grad_conv, left, right, narrow, grad_middle, mixed, low, gsel, glog, gbias, total, tail, tail_got, row_ref,
    part_ref, span_ref, wide_in, wide_out, sum_in, sum_out, states_ref, decays_ref, raw_sum, raw_rows,
    loads, saves, passing, goes, comes, log_rows, relay_in, *relayed
):
    rows, width = step.shape
    model = up_ref.shape[1]
    skip_ref, gain_ref, second_gain_ref = packed_ref.at[2:3], packed_ref.at[3:4, :model], packed_ref.at[3:4, model:]
    taps, states = tap_ref.shape[0], log_ref.shape[0]
    rank = SELECTED - 2 * states
    held, cut = in_ref.shape[0], in_ref.shape[2]
    blocks = width // LANES
    saving, numbers = [], iter(range(64))

    def load(source, target):
        copy = pltpu.make_async_copy(source, target, loads.at[next(numbers)])
        copy.start()
        return copy

    def save(source, target):
        copy = pltpu.make_async_copy(source, target, saves.at[len(saving)])
        copy.start()
        saving.append(copy)

    def weight(k):
        return load(in_hbm.at[:, pl.ds(k * cut, cut)], in_ref.at[k % held])

    early = [load(back_hbm, back), load(out_hbm, out_ref), load(gate_hbm, gate), load(mixer_hbm, mixer)]
    scanning = [load(step_hbm, step), load(conv_hbm, conv), load(raw_hbm, raw), load(entry_hbm, entry)]
    padding = load(padded_hbm, padded)
    weights = {k: weight(k) for k in range(held, 2 * held)}
    relay = Relay(True, log_ref, log_rows, relay_in, *relayed, others=[{"expert": peer} for peer in expert_peers()])

    early[0].wait()
    slots = slot_ref[:, 0:1]
    seating = seated_rows(slots, rows, back.shape[0])
    chosen = chosen_ref[:, 0:1]
    along = jnp.sum(jnp.dot(seating, back[:, model:], preferred_element_type=jnp.float32), axis=1, keepdims=True)
    place = lax.broadcasted_iota(jnp.int32, (rows, LANES), 1)
    logits = (along * chosen * (named_experts(slots, rows) - probs_ref[...])).astype(jnp.bfloat16)
    grad = jnp.dot(logits, router_ref[...], preferred_element_type=jnp.float32) + chosen * jnp.dot(seating, back[:, :model], preferred_element_type=jnp.float32)
    narrow[...] = jnp.zeros_like(narrow)
    narrow[:EXPERTS, :] = column_dot(logits, normed_ref[...])
    value = middle_ref[...]
    returned, gained = rms_back(value, rms_scale(value), second_gain_ref[...], grad)
    narrow[EXPERTS + 1 : EXPERTS + 2, :] = gained[None, :]
    value = up_ref[...].astype(jnp.float32) + returned
    grad_middle[...] = value
    middle_low[...] = value.astype(jnp.bfloat16)
    save(middle_low, low_out)
    for copy in early[1:]:
        copy.wait()

    def open_gate(b, unused):
        lanes = lanes_of(b)
        grown = transposed_dot(middle_low[...], out_ref[lanes, :])
        opening = gate[:, lanes]
        mixed[:, lanes] = grown * (opening * jax.nn.sigmoid(opening))
        grad_gate[:, lanes] = (grown * mixer[:, lanes] * silu_slope(opening)).astype(jnp.bfloat16)
        return unused

    lax.fori_loop(0, blocks, open_gate, 0)
    save(grad_gate, gate_out)
    pre, gconv = gate, mixer
    activating = load(pre_hbm, pre)
    for copy in scanning:
        copy.wait()

    fill_maps(sel_ref, wide_out, rank + states)

    def summary(part):
        summarize(True, part, step, mixed, wide_out, log_ref, part_ref, span_ref, relay.message.at[part])

    def prepare():
        fill_maps(sel_ref, wide_in, rank)
        sum_in[...] = jnp.zeros_like(sum_in)
        sum_out[...] = jnp.zeros_like(sum_out)
        raw_sum[...] = jnp.zeros_like(raw_sum)

    def scan(part):
        retreat_part(
            part, step, conv, mixed, raw, wide_in, wide_out, log_ref, step_weight_ref, entry, part_ref, span_ref,
            relay_in.at[part], low, gconv, glog, gbias, sum_in, sum_out, states_ref, decays_ref, raw_sum, raw_rows,
        )

    relay.meet()
    trading = trade(value_hbm, value_out, goes, comes)
    staged(relay, summary, prepare, scan)
    maps = gather_maps(sum_in, rank) + gather_maps(sum_out, rank + states)
    gsel[...] = (raw_sum[...] + maps).astype(jnp.bfloat16)

    activating.wait()
    padding.wait()
    step_low = jnp.where(place < rank, sel_ref[...], 0.0).astype(jnp.bfloat16)
    tall = lax.broadcasted_iota(jnp.int32, (row_ref.shape[0], LANES), 0)
    spots = jnp.where(lax.broadcasted_iota(jnp.int32, tall.shape, 1) == tall + SELECTED, 1.0, 0.0).astype(jnp.bfloat16)
    row_ref[...] = jnp.zeros_like(row_ref)

    def convolve_back(b, unused):
        lanes = lanes_of(b)
        around, kept = mixed[:, lanes], conv[:, lanes]
        grown = jnp.dot(gsel[:, :SELECTED], select_ref[:, lanes], preferred_element_type=jnp.float32) + gconv[:, lanes] + skip_ref[:, lanes] * around
        grown = grown * silu_slope(pre[:, lanes])
        gconv[:, lanes] = grown
        row_ref[:states, :] = glog[:, lanes]
        for k in range(taps):
            row_ref[states + k : states + k + 1, :] = jnp.sum(
                grown * padded[k * SEGS : k * SEGS + rows, lanes], axis=0, keepdims=True
            )
        row_ref[states + taps : states + taps + 1, :] = jnp.sum(grown, axis=0, keepdims=True)
        row_ref[states + taps + 1 : states + taps + 2, :] = gbias[:, lanes]
        row_ref[states + taps + 2 : states + taps + 3, :] = jnp.sum(around * kept, axis=0, keepdims=True)
        summed = column_dot(kept.astype(jnp.bfloat16), gsel[...])
        for piece in three_parts(row_ref[...]):
            summed = summed + column_dot(piece, spots)
        left[lanes, :] = summed
        right[lanes, :] = column_dot(low[:, lanes], step_low)
        return unused

    lax.fori_loop(0, blocks, convolve_back, 0)
    save(left, left_out)
    save(right, right_out)

    tail[...] = jnp.zeros_like(tail)
    for k in range(taps - 1):
        tail[k : k + 1, :] = gconv[k * SEGS : k * SEGS + 1, :]
    handing = pltpu.make_async_remote_copy(
        src_ref=tail, dst_ref=tail_got, send_sem=passing.at[0], recv_sem=passing.at[1],
        device_id=relay.onward(-1), device_id_type=pl.DeviceIdType.MESH,
    )
    handing.start()
    for k in range(held):
        weights[held + k].wait()
        summed = transposed_dot(grad_gate[:, k * cut : (k + 1) * cut], in_ref[k])
        total[...] = summed if k == 0 else total[...] + summed
        weights[k] = weight(k)
    handing.wait()
    goes_on = jnp.where(lax.axis_index("seq") < GRID * GRID - 1, 1.0, 0.0)
    segment = lax.broadcasted_iota(jnp.int32, (SEGS, cut), 0)
    for k in range(held):
        spot = slice(k * cut, (k + 1) * cut)
        grown = None
        for t in range(taps):
            late = taps - 1 - t
            shifted = gconv[late * SEGS :, spot]
            if late:
                wrapped = [
                    jnp.where(
                        segment == SEGS - 1,
                        goes_on * tail_got[j : j + 1, spot],
                        pltpu.roll(gconv[j * SEGS : (j + 1) * SEGS, spot], SEGS - 1, 0),
                    )
                    for j in range(late)
                ]
                shifted = jnp.concatenate([shifted] + wrapped, axis=0)
            term = tap_ref[t : t + 1, spot] * shifted
            grown = term if grown is None else grown + term
        grad_conv[:, spot] = grown.astype(jnp.bfloat16)
        weights[k].wait()
        total[...] += transposed_dot(grad_conv[:, spot], in_ref[k])
    save(grad_conv, conv_out)
    stream = token_ref[...].astype(jnp.float32)
    returned, gained = rms_back(stream, rms_scale(stream), gain_ref[...], total[...])
    narrow[EXPERTS : EXPERTS + 1, :] = gained[None, :]
    save(narrow, narrow_out)
    value = grad_middle[...] + returned
    ordering = order_ones(rows, True)
    total[...] = sum(jnp.dot(ordering, part, preferred_element_type=jnp.float32) for part in three_parts(value))
    save(total, token_out)
    for copy in saving + trading:
        copy.wait()


WHOLE = pl.BlockSpec(memory_space=pltpu.VMEM)


def shaped(*dims, dtype=jnp.float32):
    return jax.ShapeDtypeStruct(dims, dtype)


def roomy(mebibytes, **more):
    return pltpu.CompilerParams(vmem_limit_bytes=mebibytes << 20, **more)


def busy(elements):
    return pl.CostEstimate(flops=4096 * elements, bytes_accessed=16 * elements, transcendentals=4 * elements)


def wide_scratch(rows, states, extra=0):
    return pltpu.VMEM((rows // SEGS + extra, states, SEGS, LANES), jnp.float32)


def chain_scratch(states, width):
    return [pltpu.VMEM((states, SEGS, width), jnp.float32), pltpu.VMEM((SEGS, width), jnp.float32)]


def relay_scratch():
    def kept(*dims):
        return pltpu.VMEM((PARTS,) + dims + (SEGS, LANES), jnp.float32)

    return [
        kept(GRID, GRID),
        kept(GRID, GRID),
        kept(GRID, GRID + 1),
        kept(GRID, GRID + 1),
        kept(GRID + 1),
        kept(GRID, GRID + 1),
        kept(GRID, GRID),
        kept(GRID, GRID),
        pltpu.SemaphoreType.DMA((PARTS, 3, GRID)),
        pltpu.SemaphoreType.DMA((PARTS, 3, GRID)),
    ]


def mixer(tokens, upstream, tap_bias, step_bias, skip, gain, second_gain, in_weight, taps, select, step_weight, decay_log, out_weight, router, routes, seats):
    rows, model = tokens.shape
    states, width = decay_log.shape
    reach = (taps.shape[0] - 1) * SEGS
    bf16, f32 = jnp.bfloat16, jnp.float32
    anywhere = pl.BlockSpec(memory_space=pl.ANY)
    results = [
        ((rows, model), bf16),
        ((rows, width), f32),
        ((rows + reach, width), f32),
        ((rows, width), f32),
        ((rows, width), f32),
        ((rows, width), f32),
        ((rows, width), f32),
        ((rows, LANES), f32),
        ((states, SEGS, width), f32),
        ((rows, width), f32),
        ((rows, width), bf16),
        ((rows, model), f32),
        ((rows, model), bf16),
        ((rows, EXPERTS), f32),
        ((rows, LANES), f32),
        ((seats, model + LANES), bf16),
        ((rows, LANES), f32),
        ((seats, model), bf16),
        ((rows, model), bf16),
        ((rows, model), bf16),
        ((SEGS, width), f32),
    ]
    kept = [pltpu.VMEM(dims, dtype) for dims, dtype in results]
    weights = [pltpu.VMEM((2 * width // CUT, model, CUT), bf16), pltpu.VMEM(out_weight.shape, bf16)]
    relayed = relay_scratch()
    return pl.pallas_call(
        mixer_kernel,
        out_shape=tuple(shaped(*dims, dtype=dtype) for dims, dtype in results),
        in_specs=[WHOLE] * 7 + [anywhere] + [WHOLE] * 4 + [anywhere] + [WHOLE] * 2,
        out_specs=(anywhere,) * len(results),
        scratch_shapes=kept[:1]
        + weights
        + [kept[2], kept[1]]
        + kept[3:]
        + [pltpu.VMEM((SEGS, width), f32)] * 2
        + chain_scratch(states, width)
        + [wide_scratch(rows, states)] * 2
        + [
            pltpu.SemaphoreType.DMA((2 * width // CUT + 1,)),
            pltpu.SemaphoreType.DMA((len(results),)),
            pltpu.SemaphoreType.DMA((2,)),
            pltpu.SemaphoreType.DMA((EXPERTS,)),
            pltpu.SemaphoreType.DMA((EXPERTS,)),
        ]
        + relayed,
        compiler_params=roomy(60, collective_id=0, has_side_effects=True),
        cost_estimate=busy(rows * states * width),
        name="mixer",
    )(tokens, upstream, tap_bias, step_bias, skip, gain, second_gain, in_weight, taps, select, step_weight, decay_log, out_weight, router, routes)


def mixer_back(
    back, slots, probs, chosen, normed, router, middle, up, out_weight, gate, mixed, conv, step, raw, selection, pre, padded, entry,
    decay_log, step_weight, select, taps, packed, in_weight, tokens, value,
):
    rows, width = step.shape
    model = tokens.shape[1]
    states = decay_log.shape[0]
    bf16, f32 = jnp.bfloat16, jnp.float32
    anywhere = pl.BlockSpec(memory_space=pl.ANY)
    held = width // CUT
    tall = ((rows, width), f32)
    results = [
        ((rows, model), bf16),
        ((rows, width), bf16),
        ((rows, width), bf16),
        ((width, LANES), f32),
        ((width, LANES), f32),
        ((16, model), f32),
        ((rows, model), f32),
        (value.shape, bf16),
    ]
    streamed = (0, 8, 9, 10, 11, 12, 13, 15, 16, 17, 23, 25)
    kept = (
        [(back.shape, bf16), (out_weight.shape, bf16)]
        + [tall] * 5
        + [(padded.shape, f32), (entry.shape, f32), ((held, model, CUT), bf16)]
        + results[:6]
        + [((rows, model), f32), tall, ((rows, width), bf16), ((rows, LANES), bf16), ((states, width), f32), ((1, width), f32)]
        + [((rows, model), f32), ((SEGS, width), f32), ((SEGS, width), f32), ((24, LANES), f32)]
    )
    return pl.pallas_call(
        mixer_back_kernel,
        out_shape=tuple(shaped(*dims, dtype=dtype) for dims, dtype in results),
        in_specs=[anywhere if k in streamed else WHOLE for k in range(26)],
        out_specs=(anywhere,) * len(results),
        scratch_shapes=[pltpu.VMEM(dims, dtype) for dims, dtype in kept]
        + chain_scratch(states, width)
        + [wide_scratch(rows, states)] * 4
        + [wide_scratch(rows, states, 1), wide_scratch(rows, states)]
        + [pltpu.VMEM((rows, LANES), f32)] * 2
        + [pltpu.SemaphoreType.DMA((10 + 2 * held,)), pltpu.SemaphoreType.DMA((len(results),)), pltpu.SemaphoreType.DMA((2,))]
        + [pltpu.SemaphoreType.DMA((EXPERTS,))] * 2
        + relay_scratch(),
        compiler_params=roomy(62, collective_id=1, has_side_effects=True),
        cost_estimate=busy(rows * states * width),
        name="mixer_back",
    )(
        back, slots, probs, chosen, normed, router, middle, up, out_weight, gate, mixed, conv, step, raw, selection, pre, padded, entry,
        decay_log, step_weight, select, taps, packed, in_weight, tokens, value,
    )


def segmented(block):
    rows = block.shape[0]
    return block.reshape(SEGS, rows // SEGS, -1).transpose(1, 0, 2).reshape(rows, -1)


def in_order(block):
    rows = block.shape[0]
    return block.reshape(rows // SEGS, SEGS, -1).transpose(1, 0, 2).reshape(rows, -1)


def rms_scale(stream):
    return lax.rsqrt(jnp.mean(stream * stream, axis=-1, keepdims=True) + 1e-05)


def rms_back(stream, scale, gain, grad):
    grown = grad * gain
    along = jnp.mean(stream * grown, axis=-1, keepdims=True)
    return scale * grown - stream * (scale * scale * scale * along), jnp.sum(grad * stream * scale, axis=0)


def silu_slope(value):
    gate = jax.nn.sigmoid(value)
    return gate * (1.0 + value * (1.0 - gate))


def product(left, right):
    return jnp.dot(left, right, preferred_element_type=jnp.float32)


def across(left, right):
    return jnp.einsum("tk,dk->td", left, right, preferred_element_type=jnp.float32)


def summed_rows(left, right):
    return jnp.einsum("tk,td->kd", left, right, preferred_element_type=jnp.float32)


CHUNK = 512
GELU_OUT = math.sqrt(2.0 / math.pi)
GELU_IN = 0.044715


def transposed_dot(left, right):
    return lax.dot_general(left, right, (((1,), (1,)), ((), ())), preferred_element_type=jnp.float32)


def column_dot(left, right):
    return lax.dot_general(left, right, (((0,), (0,)), ((), ())), preferred_element_type=jnp.float32)


def three_parts(value):
    parts, left = [], value
    for unused in range(3):
        part = left.astype(jnp.bfloat16)
        left = left - part.astype(jnp.float32)
        parts.append(part)
    return parts


def experts_kernel(
    leaving_hbm, up_ref, first_hbm, second_hbm, back_out, value_out, sums_out,
    received, first, second, pull, active, grad, value, sent, dots, scaled_received, scaled_up, staged_sums,
    loads, saves, goes, comes, returns, arrives,
):
    rows, width = up_ref.shape
    hidden = second.shape[0]
    barrier = pltpu.get_barrier_semaphore()
    for peer in expert_peers():
        pl.semaphore_signal(barrier, inc=1, device_id={"expert": peer}, device_id_type=pl.DeviceIdType.MESH)
    loading = [
        pltpu.make_async_copy(second_hbm, second, loads.at[0]),
        pltpu.make_async_copy(first_hbm, first, loads.at[1]),
    ]
    for copy in loading:
        copy.start()
    pl.semaphore_wait(barrier, EXPERTS - 1)
    arriving = trade(leaving_hbm, received, goes, comes)
    loading[0].wait()

    def pulled(i, unused):
        cols = pl.ds(pl.multiple_of(i * CHUNK, CHUNK), CHUNK)
        pull[:, cols] = transposed_dot(up_ref[...], second[cols, :]).astype(jnp.bfloat16)
        return unused

    lax.fori_loop(0, hidden // CHUNK, pulled, 0)
    loading[1].wait()
    for copy in arriving:
        copy.wait()

    dots[...] = jnp.zeros_like(dots)

    def layer(i, unused):
        cols = pl.ds(pl.multiple_of(i * CHUNK, CHUNK), CHUNK)
        pre = jnp.dot(received[:, :width], first[:, cols], preferred_element_type=jnp.float32)
        square = pre * pre
        bent = jnp.tanh(pre * (GELU_OUT + GELU_OUT * GELU_IN * square))
        share = 0.5 + 0.5 * bent
        slope = share + pre * (0.5 - 0.5 * bent * bent) * (GELU_OUT + 3.0 * GELU_OUT * GELU_IN * square)
        low = (pre * share).astype(jnp.bfloat16)
        active[:, cols] = low
        drawn = pull[:, cols].astype(jnp.float32)
        grad[:, cols] = (slope * drawn).astype(jnp.bfloat16)
        met = low.astype(jnp.float32) * drawn
        dots[...] += sum(met[:, k * LANES : (k + 1) * LANES] for k in range(CHUNK // LANES))
        return unused

    lax.fori_loop(0, hidden // CHUNK, layer, 0)
    sent[:, :width] = transposed_dot(grad[...], first[...]).astype(jnp.bfloat16)
    along = jnp.sum(dots[...], axis=1, keepdims=True)
    place = lax.broadcasted_iota(jnp.int32, (rows, LANES), 1)
    tail = jnp.zeros(place.shape, jnp.float32)
    for k, part in enumerate(three_parts(along)):
        tail = jnp.where(place == k, part.astype(jnp.float32), tail)
    sent[:, width:] = tail.astype(jnp.bfloat16)
    returning = trade(sent, back_out, returns, arrives)

    value[...] = jnp.dot(active[...], second[...], preferred_element_type=jnp.float32).astype(jnp.bfloat16)
    saving = [pltpu.make_async_copy(value, value_out, saves.at[0])]
    saving[0].start()
    parts = received[:, width:].astype(jnp.float32)
    gate = parts[:, 0:1] + parts[:, 1:2] + parts[:, 2:3]
    scaled_received[...] = (received[:, :width].astype(jnp.float32) * gate).astype(jnp.bfloat16)
    scaled_up[...] = (up_ref[...].astype(jnp.float32) * gate).astype(jnp.bfloat16)
    half = sums_out.shape[2]
    pairs = hidden // half // 2

    def stored(i, slot):
        return pltpu.make_async_copy(staged_sums.at[slot], sums_out.at[pl.ds(2 * i, 2)], saves.at[1 + slot])

    def sums(i, unused):
        slot = lax.rem(i, 2)
        cols = pl.ds(pl.multiple_of(i * 2 * half, 2 * half), 2 * half)

        @pl.when(i >= 2)
        def free():
            stored(i - 2, slot).wait()

        for which, (left, right) in enumerate(((grad, scaled_received), (active, scaled_up))):
            total = column_dot(left[:, cols], right[...]).astype(jnp.bfloat16)
            for k in range(2):
                staged_sums[slot, k, which] = total[k * half : (k + 1) * half]
        stored(i, slot).start()
        return unused

    lax.fori_loop(0, pairs, sums, 0)
    for i in (pairs - 2, pairs - 1):
        stored(i, i % 2).wait()
    for copy in returning:
        copy.wait()
    saving[0].wait()


def expert_pass(leaving, upstream, first, second, owners):
    rows, width = upstream.shape
    hidden = second.shape[0]
    wide = leaving.shape[1]
    bf16 = jnp.bfloat16
    half = hidden // owners
    anywhere = pl.BlockSpec(memory_space=pl.ANY)

    def kept(*dims):
        return pltpu.VMEM(dims, bf16)

    return pl.pallas_call(
        experts_kernel,
        out_shape=(
            shaped(rows, wide, dtype=bf16),
            shaped(rows, width, dtype=bf16),
            shaped(owners, 2, half, width, dtype=bf16),
        ),
        in_specs=[anywhere, WHOLE, anywhere, anywhere],
        out_specs=(anywhere,) * 3,
        scratch_shapes=[
            kept(rows, wide),
            kept(width, hidden),
            kept(hidden, width),
            kept(rows, hidden),
            kept(rows, hidden),
            kept(rows, hidden),
            kept(rows, width),
            kept(rows, wide),
            pltpu.VMEM((rows, LANES), jnp.float32),
            kept(rows, width),
            kept(rows, width),
            kept(2, 2, 2, half, width),
            pltpu.SemaphoreType.DMA((2,)),
            pltpu.SemaphoreType.DMA((3,)),
        ]
        + [pltpu.SemaphoreType.DMA((EXPERTS,))] * 4,
        compiler_params=roomy(60, collective_id=3, has_side_effects=True),
        cost_estimate=pl.CostEstimate(flops=12 * rows * hidden * width, bytes_accessed=8 * hidden * width, transcendentals=rows * hidden),
        name="experts",
    )(leaving, upstream, first, second)


ORDERS = ("xyz", "yzx", "zxy")
PIECE = 16
TURNS = (0, 2, 1, 3)


def shares_kernel(
    conv_cols, gate_cols, token_ref, out_cols, middle_ref, left_ref, right_ref, narrow_ref,
    in_out, out_out, left_out, right_out, narrow_out, sum_ref, in_ref, out_ref, made, taken,
    half_a, half_b, half_c, one_a, one_b, one_c, sends, arrivals):
    seq, expert = lax.axis_index("seq"), lax.axis_index("expert")
    core = lax.rem(expert, 2)
    place = {"y": lax.div(seq, 4), "z": lax.rem(seq, 4), "x": lax.div(expert, 2)}
    third = token_ref.shape[1] // len(ORDERS)
    streams = [(L, q) for q in TURNS for L in range(len(ORDERS))]

    def flip(i):
        return i + 1 - 2 * lax.rem(i, 2)

    def device(**moved):
        at = dict(place, **moved)
        return {"seq": at["y"] * 4 + at["z"], "expert": at["x"] * 2 + at.get("core", core)}

    partners = [device(core=1 - core)]
    for axis in "xyz":
        partners += [device(**{axis: flip(place[axis])}), device(**{axis: 3 - place[axis]})]
    barrier = pltpu.get_barrier_semaphore()
    for partner in partners:
        pl.semaphore_signal(barrier, inc=1, device_id=partner, device_id_type=pl.DeviceIdType.MESH)
    pl.semaphore_wait(barrier, len(partners))

    def send(source, target, partner, stream, number):
        k = streams.index(stream)
        copy = pltpu.make_async_remote_copy(
            src_ref=source, dst_ref=target, send_sem=sends.at[k, number], recv_sem=arrivals.at[k, number],
            device_id=partner, device_id_type=pl.DeviceIdType.MESH,
        )
        copy.start()
        return copy

    def add(target, source, unit):
        def step(i, unused):
            target[i] = target[i] + source[i]
            return unused

        lax.fori_loop(0, unit, step, 0, unroll=min(unit, 8))

    inner = out_cols.shape[1]
    for source, target, base in ((conv_cols, in_ref, 0), (gate_cols, in_ref, inner), (out_cols, out_ref, 0)):

        def turn_over(k, unused, source=source, target=target, base=base):
            spot = pl.ds(pl.multiple_of(k * LANES, LANES), LANES)
            target[pl.ds(pl.multiple_of(base + k * LANES, LANES), LANES), :] = source[:, spot].T
            return unused

        lax.fori_loop(0, source.shape[1] // LANES, turn_over, 0)

    halves, ones = (half_a, half_b, half_c), (one_a, one_b, one_c)
    pending, holding = {}, {}

    def set_out(L):
        for q in TURNS:
            for copy in pending[L, q]:
                copy.wait()
            add(taken.at[L, q], made.at[L, 4 * core + q], 64)
            holding[L, q] = taken.at[L, q]
            pending[L, q] = start_halves(L, q, 0, holding[L, q], halves, place, flip, device, send)

    for L, order in enumerate(ORDERS):
        lanes = pl.ds(L * third, third)
        narrow = narrow_ref[:, lanes].astype(jnp.bfloat16)

        def block(s, unused):
            y, z = lax.div(s, 4), lax.rem(s, 4)
            by_in = jnp.dot(
                in_ref[pl.ds(pl.multiple_of(s * 288, 16), 288), :], token_ref[:, lanes], preferred_element_type=jnp.float32
            ).astype(jnp.bfloat16)
            here = pl.ds(pl.multiple_of(s * 144, 16), 144)
            by_out = jnp.dot(out_ref[here, :], middle_ref[:, lanes], preferred_element_type=jnp.float32)
            left, right = left_ref[here, :], right_ref[here, :]
            for x in range(4):
                at = {"x": x, "y": y, "z": z}
                slot = (at[order[0]] * 4 + at[order[1]]) * 4 + at[order[2]]
                rows = by_in[72 * x : 72 * x + 72]
                more = by_out[36 * x : 36 * x + 36].astype(jnp.bfloat16)
                for q in range(4):
                    made[L, q, slot] = rows[16 * q : 16 * q + 16]
                made[L, 4, slot, 0:8] = rows[64:]
                made[L, 4, slot, 8:16] = more[:8]
                made[L, 5, slot] = more[8:24]
                made[L, 6, slot, 0:12] = more[24:]
                made[L, 6, slot, 12:16] = narrow[8:12]
                made[L, 7, slot, 8:16] = narrow[0:8]
                last = jnp.concatenate([left[36 * x : 36 * x + 36], right[36 * x : 36 * x + 36]], axis=0)
                for part in range(third // LANES):
                    k = 8 * (L * (third // LANES) + part)
                    made[L, 7, slot, 0:8, part * LANES : (part + 1) * LANES] = last[k : k + 8].astype(jnp.bfloat16)
            return unused

        lax.fori_loop(0, 16, block, 0, unroll=2)
        for q in TURNS:
            pending[L, q] = [
                send(made.at[L, 4 * (1 - core) + q], taken.at[L, q], device(core=1 - core), (L, q), 0)
            ]

        if L:
            set_out(L - 1)
    set_out(len(ORDERS) - 1)
    for turn in range(3):
        unit = 16 >> (2 * turn)
        for L, q in streams:
            axis = ORDERS[L][turn]
            i = place[axis]
            for copy in pending[L, q]:
                copy.wait()
            other = 3 - i if q < 2 else flip(i)
            got = halves[turn].at[L, q]
            add(got.at[0], holding[L, q].at[pl.ds(i * unit, unit)], unit)
            add(got.at[1], holding[L, q].at[pl.ds(other * unit, unit)], unit)
            partner = device(**{axis: other})
            pending[L, q] = [send(got.at[1], ones[turn].at[L, q], partner, (L, q), 3 + 3 * turn)]
        for L, q in streams:
            for copy in pending[L, q]:
                copy.wait()
            got = ones[turn].at[L, q]
            if turn < 2:
                add(got, halves[turn].at[L, q, 0], unit)
                holding[L, q] = got
                pending[L, q] = start_halves(L, q, turn + 1, got, halves, place, flip, device, send)
            else:
                whole = got[0].astype(jnp.float32) + halves[turn][L, q, 0, 0].astype(jnp.float32)
                sum_ref[4 * core + q, :, L * third : (L + 1) * third] = whole
    here = sum_ref.at[pl.ds(4 * core, 4)]
    send(here, here, device(core=1 - core), (0, 0), 10).wait()
    whole = jnp.concatenate([sum_ref[q] for q in range(8)], axis=0)
    last = [whole[112:120, k * LANES : (k + 1) * LANES] for k in range(whole.shape[1] // LANES)]
    last = jnp.concatenate(last + [jnp.zeros((8, LANES), jnp.float32)], axis=0)
    narrow_out[...] = jnp.concatenate([whole[120:128], whole[108:112], whole[108:112]], axis=0)
    for c in range(2):

        @pl.when(core == c)
        def pick(c=c):
            in_out[...] = whole[36 * c : 36 * c + 40]
            out_out[...] = whole[72 + 18 * c : 90 + 18 * c]
            left_out[...] = last[18 * c : 18 * c + 24]
            right_out[...] = last[36 + 18 * c : 60 + 18 * c]


def start_halves(L, q, turn, source, halves, place, flip, device, send):
    axis = ORDERS[L][turn]
    unit = 16 >> (2 * turn)
    i = place[axis]
    partner = flip(i) if q < 2 else 3 - i
    second = 3 - partner if q < 2 else flip(partner)
    target = halves[turn].at[L, q]
    return [
        send(source.at[pl.ds(partner * unit, unit)], target.at[0], device(**{axis: partner}), (L, q), 1 + 3 * turn),
        send(source.at[pl.ds(second * unit, unit)], target.at[1], device(**{axis: partner}), (L, q), 2 + 3 * turn),
    ]


def shares(conv_cols, gate_cols, tokens, out_cols, middle, left, right, narrow):
    width = tokens.shape[1]
    rows, inner = out_cols.shape
    third = width // len(ORDERS)

    def slots(*lead):
        return pltpu.VMEM((len(ORDERS),) + lead + (PIECE, third), jnp.bfloat16)

    return pl.pallas_call(
        shares_kernel,
        out_shape=(shaped(40, width), shaped(18, width), shaped(24, LANES), shaped(24, LANES), shaped(16, width)),
        in_specs=[WHOLE] * 8,
        out_specs=(WHOLE,) * 5,
        scratch_shapes=[pltpu.VMEM((8, PIECE, width), jnp.float32)]
        + [pltpu.VMEM((2 * inner, rows), jnp.bfloat16), pltpu.VMEM((inner, rows), jnp.bfloat16)]
        + [slots(8, 64), slots(4, 64)]
        + [slots(4, 2, 16 >> (2 * turn)) for turn in range(3)]
        + [slots(4, 16 >> (2 * turn)) for turn in range(3)]
        + [pltpu.SemaphoreType.DMA((12, 11))] * 2,
        compiler_params=roomy(60, collective_id=2, has_side_effects=True),
        name="shares",
    )(conv_cols, gate_cols, tokens, out_cols, middle, left, right, narrow)


def finish_kernel(
    in_ref, left_ref, right_ref, narrow_ref, expert_ref,
    in_out, tap_out, tap_bias_out, select_out, step_out, step_bias_out, decay_out, skip_out, gain_out, second_out, router_out,
    expert_first_out, expert_second_out,
):
    def turned(value):
        size = value.shape[0]
        same = lax.broadcasted_iota(jnp.int32, (size, size), 0) == lax.broadcasted_iota(jnp.int32, (size, size), 1)
        ones = jnp.where(same, 1.0, 0.0).astype(jnp.bfloat16)
        return sum(column_dot(part, ones) for part in three_parts(value))

    each, taps, states = tap_out.shape[1], tap_out.shape[0], decay_out.shape[0]
    in_out[...] = in_ref[: in_out.shape[0], :]
    select_out[...] = left_ref[:each, : select_out.shape[1]]
    sums = turned(left_ref[...])[SELECTED:, :each]
    decay_out[...] = sums[:states]
    tap_out[...] = sums[states : states + taps]
    tap_bias_out[...] = sums[states + taps : states + taps + 1]
    step_bias_out[...] = sums[states + taps + 1 : states + taps + 2]
    skip_out[...] = sums[states + taps + 2 : states + taps + 3]
    step_out[...] = right_ref[:each, : step_out.shape[1]]
    fewer = router_out.shape[1]
    owner = lax.axis_index("seq") * EXPERTS + lax.axis_index("expert")
    shape = (narrow_ref.shape[1], LANES)
    mine = lax.broadcasted_iota(jnp.int32, shape, 0) == lax.broadcasted_iota(jnp.int32, shape, 1) + owner * fewer
    ones = jnp.where(mine, 1.0, 0.0).astype(jnp.bfloat16)
    parts = three_parts(narrow_ref[...])
    picked = sum(jnp.dot(part, ones, preferred_element_type=jnp.float32) for part in parts)
    gain_out[...] = picked[EXPERTS : EXPERTS + 1, :fewer]
    second_out[...] = picked[EXPERTS + 1 : EXPERTS + 2, :fewer]
    router_out[...] = picked[:EXPERTS, :fewer]
    expert_first_out[...] = expert_ref[0].astype(jnp.float32)
    expert_second_out[...] = expert_ref[1].astype(jnp.float32)


def finish(in_share, left, right, narrow, expert_share, devices, taps, states, rank, inner):
    model = in_share.shape[1]
    each, fewer, hidden = inner // devices, model // devices, expert_share.shape[1]
    dims = (
        (2 * each, model), (taps, each), (1, each), (each, rank + 2 * states), (each, rank), (1, each), (states, each), (1, each),
        (1, fewer), (1, fewer), (EXPERTS, fewer), (hidden, model), (hidden, model),
    )
    return pl.pallas_call(
        finish_kernel,
        out_shape=tuple(shaped(*size) for size in dims),
        in_specs=[WHOLE] * 5,
        out_specs=(WHOLE,) * len(dims),
        compiler_params=roomy(32),
        name="finish",
    )(in_share, left, right, narrow, expert_share)


def local(
    tokens,
    expert_index,
    cotangent,
    first_gain,
    in_weight,
    conv_weight,
    conv_bias,
    select_weight,
    step_weight,
    step_bias,
    decay_log,
    skip_gain,
    out_weight,
    second_gain,
    router_weight,
    expert_first,
    expert_second,
):
    bf16, f32 = jnp.bfloat16, jnp.float32
    row_count, model_width = tokens.shape[1:]
    seat_count = 2 * row_count
    inner = conv_bias.shape[0]
    rank = step_weight.shape[0]
    states = decay_log.shape[0]
    taps = conv_weight.shape[0]
    seqs, experts = lax.axis_size("seq"), lax.axis_size("expert")
    (
        normed_in, gate_input, padded, preact, conv_out, step_raw, step_size, selection, first, mixer_out, gated,
        middle, normed_mid, router_probs, gate_wide, leaving, slots, upstream_there, stream, upstream, packed,
    ) = mixer(
        tokens[0], cotangent[0], conv_bias, step_bias, skip_gain, first_gain, second_gain, in_weight, conv_weight, select_weight.T, step_weight, decay_log, out_weight, router_weight.T, expert_index[:, :, 0], seat_count
    )
    back, value_there, expert_grads = expert_pass(leaving, upstream_there, expert_first[0], expert_second[0], seqs)
    expert_share = lax.psum_scatter(
        expert_grads.reshape(-1, model_width), "seq", scatter_dimension=0, tiled=True
    ).reshape(2, -1, model_width)
    middle_low, grad_gate_input, grad_conv_input, left, right, narrow, grad_tokens, value_home = mixer_back(
        back, slots, router_probs, gate_wide, normed_mid, router_weight.T, middle, upstream, out_weight, gate_input, mixer_out, conv_out,
        step_size, step_raw, selection, preact, padded, first, decay_log, step_weight, select_weight.T, conv_weight, packed, in_weight, stream, value_there,
    )
    placing = (slots[:, 0:1] == jnp.arange(seat_count, dtype=f32)[None, :]).astype(bf16)
    mixed = middle + gate_wide[:, 0:1] * product(placing, value_home)

    devices = seqs * experts
    each, fewer = inner // devices, model_width // devices
    in_share, out_share, left, right, narrow = shares(
        grad_conv_input, grad_gate_input, normed_in, gated, middle_low, left, right, narrow
    )
    in_grad, tap_grad, tap_bias_grad, select_grad, step_grad, step_bias_grad, decay_grad, skip_grad, gain_grad, second_grad, router_grad, first_grad, second_hidden = finish(
        in_share, left, right, narrow, expert_share, devices, taps, states, rank, inner
    )
    return (
        in_order(mixed.astype(bf16))[None],
        grad_tokens[None],
        gain_grad[0],
        in_grad.T,
        tap_grad,
        tap_bias_grad[0],
        select_grad,
        step_grad.T,
        step_bias_grad[0],
        decay_grad,
        skip_grad[0],
        out_share,
        second_grad[0],
        router_grad.T,
        first_grad.T[None],
        second_hidden[None],
    )


def solution(mesh):
    return jax.shard_map(
        local,
        mesh=mesh,
        in_specs=(
            P("expert", "seq", None),
            P("expert", "seq", None),
            P("expert", "seq", None),
            P(),
            P(),
            P(),
            P(),
            P(),
            P(),
            P(),
            P(),
            P(),
            P(),
            P(),
            P(),
            P("expert", None, None),
            P("expert", None, None),
        ),
        out_specs=(
            P("expert", "seq", None),
            P("expert", "seq", None),
            P(("seq", "expert")),
            P(None, ("seq", "expert")),
            P(None, ("seq", "expert")),
            P(("seq", "expert")),
            P(("seq", "expert"), None),
            P(None, ("seq", "expert")),
            P(("seq", "expert")),
            P(None, ("seq", "expert")),
            P(("seq", "expert")),
            P(("seq", "expert"), None),
            P(("seq", "expert")),
            P(("seq", "expert"), None),
            P("expert", None, "seq"),
            P("expert", "seq", None),
        ),
        check_vma=False,
    )
```
